32 devices in a mesh: dp: 4 (over y, core), wide: 8 (over z, x).
Axes of the slice: x: 2, y: 2, z: 4, core: 2. Of those that a mesh axis runs over, the one named last changes fastest.
Arguments:
- tokens: bfloat16 [32768, 768], P(('dp', 'wide')), may hold values from -6 to 6
- segments: int32 [32768], P(('dp', 'wide')), may hold values from 0 to 15, as said below
- counts: int32 [32], P(('dp', 'wide')), may hold values from 256 to 1024, as said below
- out_grad: bfloat16 [32768, 768], P(('dp', 'wide')), may hold values from -6 to 6
- attn_param: float32 [2363136], P(('dp', 'wide')), may hold values from -2.5 to 2.5
- attn_moment: float32 [2363136], P(('dp', 'wide')), may hold values from -0.03125 to 0.03125
- attn_square: float32 [2363136], P(('dp', 'wide')), may hold values from 1e-09 to 1e-07
- attn_shadow: float32 [2363136], P(('dp', 'wide')), may hold values from -0.75 to 0.75
- ffn_param: float32 [4723968], P(('dp', 'wide')), may hold values from -1.5 to 1.5
- ffn_moment: float32 [4723968], P(('dp', 'wide')), may hold values from -0.03125 to 0.03125
- ffn_square: float32 [4723968], P(('dp', 'wide')), may hold values from 1e-09 to 1e-07
- ffn_shadow: float32 [4723968], P(('dp', 'wide')), may hold values from -0.75 to 0.75
Outputs:
- activations: bfloat16 [32768, 768], P(('dp', 'wide'))
- pooled: float32 [512, 768], P(('dp', 'wide'))
- token_grad: bfloat16 [32768, 768], P(('dp', 'wide'))
- attn_grad: float32 [2363136], P(('dp', 'wide'))
- ffn_grad: float32 [4723968], P(('dp', 'wide'))
- attn_change: float32 [2363136], P(('dp', 'wide'))
- ffn_change: float32 [4723968], P(('dp', 'wide'))
- moment_attn: float32 [2363136], P(('dp', 'wide'))
- moment_ffn: float32 [4723968], P(('dp', 'wide'))
- square_attn: float32 [2363136], P(('dp', 'wide'))
- square_ffn: float32 [4723968], P(('dp', 'wide'))
- drift_attn: float32 [2363136], P(('dp', 'wide'))
- drift_ffn: float32 [4723968], P(('dp', 'wide'))
The draws below stay inside these ranges and needn't reach their ends.
Inputs may be any that keep to these rules, and one draw needn't show every extreme that they name: `counts`: true tokens of each row of 1024 positions; the later positions of the row are padding. `segments`: starts at 0 and never falls within each row of 1024 positions; a run of one number is 64 to 256 positions long, the last run of a row possibly shorter.
All inputs are finite; a program needn't handle non-finite values.
Results may differ from the reference program's by a relative error of at most 0.012.
The reference program's roundings to bfloat16 on the way count: a program that leaves them out, or rounds other values in their place, can miss the bound.
Values may be sent and summed in bfloat16 or wider, within the bound.
No kernel may reach another device: no remote copies, remote signals or barrier semaphores. Data moves between devices by JAX's collectives and lax.ppermute only.
A program may use at most 256 MiB of HBM per device.

```python
import math
import jax
import jax.numpy as jnp
from jax import lax

D = 768
FF = 3072
HEAD = 64
HEADS = 12
ROW = 1024
CROP_MIN = 64
CROP_MAX = 256
STEP = 10
CROPS = 16
NROWS = 32
TOKENS = 32768
PA = 2363136
PF = 4723968


def piece_scale(length_all, extents, factors):
    position = jnp.arange(length_all)
    result = jnp.full((length_all,), 0.02, jnp.float32)
    offset = 0
    for extent, factor in zip(extents, factors):
        result = jnp.where((position >= offset) & (position < offset + extent), factor, result)
        offset = offset + extent
    return (result, position)


def draw_attn_param(key, part):
    key = jax.random.fold_in(key, 11)
    noise_key, gain_key = jax.random.split(key)
    extents = [3 * D * D, D * D, 3 * D, D, D]
    factors = [D ** (-0.5), 6.0 * D ** (-0.5), 0.5, 0.0, 0.5]
    scale, position = piece_scale(PA, extents, factors)
    noise = jax.random.truncated_normal(noise_key, -3.0, 3.0, (PA,), jnp.float32) * scale
    gains = jax.random.uniform(gain_key, (PA,), jnp.float32, 0.8, 1.2)
    gain_start = 4 * D * D + 3 * D
    is_gain = (position >= gain_start) & (position < gain_start + D)
    return jnp.where(is_gain, gains, noise).astype(jnp.float32)


def draw_ffn_param(key, part):
    key = jax.random.fold_in(key, 13)
    noise_key, gain_key = jax.random.split(key)
    extents = [D * FF, FF * D, FF, D, D, D]
    factors = [D ** (-0.5), FF ** (-0.5), 0.5, 0.5, 0.0, 0.5]
    scale, position = piece_scale(PF, extents, factors)
    noise = jax.random.truncated_normal(noise_key, -3.0, 3.0, (PF,), jnp.float32) * scale
    gains = jax.random.uniform(gain_key, (PF,), jnp.float32, 0.8, 1.2)
    gain_start = 2 * D * FF + FF + D
    is_gain = (position >= gain_start) & (position < gain_start + D)
    return jnp.where(is_gain, gains, noise).astype(jnp.float32)


def draw_counts(key, part):
    key = jax.random.fold_in(key, 23)
    row_ids = jnp.arange(NROWS, dtype=jnp.int32)
    low_end = ROW // 3
    base = low_end + (ROW - low_end) * row_ids // max(NROWS - 1, 1)
    jitter = jax.random.randint(key, (NROWS,), 0, max(ROW // 8, 1), dtype=jnp.int32)
    counted = jnp.maximum(base - jitter, ROW // 4)
    counted = jnp.where(row_ids == 0, ROW // 4, counted)
    return jnp.where(row_ids == NROWS - 1, ROW, counted).astype(jnp.int32)


def draw_segments(key, part):
    key = jax.random.fold_in(key, 37)
    length_key, row_key = jax.random.split(key)
    lengths = jax.random.randint(length_key, (NROWS, CROPS), CROP_MIN, CROP_MAX + 1, dtype=jnp.int32)
    chosen = jax.random.randint(row_key, (), 0, NROWS, dtype=jnp.int32)
    lengths = jnp.where((jnp.arange(NROWS, dtype=jnp.int32) == chosen)[:, None], CROP_MIN, lengths)
    crop_ends = jnp.cumsum(lengths, axis=1)
    position = jnp.arange(ROW, dtype=jnp.int32)
    numbers = jnp.sum((crop_ends[:, None, :] <= position[None, :, None]).astype(jnp.int32), axis=2)
    return numbers.reshape(TOKENS).astype(jnp.int32)


def shard_levels(own_key, dims, pieces, smallest, top_value):
    def one(dim, blocks):
        draws = jax.random.uniform(jax.random.fold_in(jax.random.fold_in(own_key, 6), dim), (blocks,), jnp.float32, smallest / len(pieces), top_value / len(pieces))
        return jnp.repeat(jnp.exp(draws), dims[dim] // blocks).reshape((-1,) + (1,) * (len(dims) - dim - 1))

    factor_of = one(*pieces[0])
    for cut in pieces[1:]:
        factor_of = factor_of * one(*cut)
    return factor_of


def scatter_about(rng, dims, deviation, most, cuts=(), held_as=jnp.bfloat16):
    entries = jax.random.normal(rng, dims, jnp.float32) * deviation
    if len(cuts) > 0:
        entries = shard_levels(rng, dims, cuts, -0.22, 0.18) * entries
    return jnp.clip(entries, min=-most, max=most).astype(held_as)


def setup_inputs(seed: int = 0) -> dict:
    streams_of = jax.random.split(jax.random.key(seed), 13)
    tokens = scatter_about(streams_of[0], (TOKENS, D), 1.0, 6.0, ((0, 32),))
    segments = draw_segments(jax.random.fold_in(streams_of[12], 71), 0)
    counts = draw_counts(jax.random.fold_in(streams_of[12], 71), 0)
    out_grad = scatter_about(streams_of[3], (TOKENS, D), 1.0, 6.0, ((0, 32),))
    attn_param = draw_attn_param(jax.random.fold_in(streams_of[12], 71), 0)
    attn_moment = scatter_about(streams_of[5], (PA,), 0.002, 0.03125, ((0, 32),), jnp.float32)
    attn_square = jnp.clip(jnp.exp(math.log(1.0000000116860974e-07) - 4.6051702 * jax.random.uniform(streams_of[6], (PA,), jnp.float32) ** shard_levels(streams_of[6], (PA,), ((0, 32),), -0.2, 0.2)), 9.999999717180685e-10, 1.0000000116860974e-07)
    attn_shadow = scatter_about(streams_of[7], (PA,), 0.05, 0.75, ((0, 32),), jnp.float32)
    ffn_param = draw_ffn_param(jax.random.fold_in(streams_of[12], 71), 0)
    ffn_moment = scatter_about(streams_of[9], (PF,), 0.002, 0.03125, ((0, 32),), jnp.float32)
    ffn_square = jnp.clip(jnp.exp(math.log(1.0000000116860974e-07) - 4.6051702 * jax.random.uniform(streams_of[10], (PF,), jnp.float32) ** shard_levels(streams_of[10], (PF,), ((0, 32),), -0.2, 0.2)), 9.999999717180685e-10, 1.0000000116860974e-07)
    ffn_shadow = scatter_about(streams_of[11], (PF,), 0.05, 0.75, ((0, 32),), jnp.float32)
    return dict(tokens=tokens, segments=segments, counts=counts, out_grad=out_grad, attn_param=attn_param, attn_moment=attn_moment, attn_square=attn_square, attn_shadow=attn_shadow, ffn_param=ffn_param, ffn_moment=ffn_moment, ffn_square=ffn_square, ffn_shadow=ffn_shadow)


@jax.custom_vjp
def low(v):
    return lax.optimization_barrier(v.astype(jnp.bfloat16)).astype(jnp.float32)

@jax.custom_vjp
def low_back(v):
    return v

def low_keep(v):
    return (low(v), None)

def low_pass(kept, grad):
    return (grad,)

def back_keep(v):
    return (v, None)

def back_low(kept, grad):
    return (low(grad),)
low.defvjp(low_keep, low_pass)
low_back.defvjp(back_keep, back_low)
HIGHEST = lax.Precision.HIGHEST
NORM_EPSILON = 1e-12
NEGATIVE = -1e+30
MOMENT_DECAY = 0.9
SQUARE_DECAY = 0.999
LEARN_RATE = 0.001
WEIGHT_DECAY = 0.01
ADAM_EPSILON = 1e-08
SHADOW_RATE = 0.9995

def split_attn(flat):
    matrix_size = D * D
    w_query = flat[0:matrix_size].reshape(D, D)
    w_key = flat[matrix_size:2 * matrix_size].reshape(D, D)
    w_value = flat[2 * matrix_size:3 * matrix_size].reshape(D, D)
    w_out = flat[3 * matrix_size:4 * matrix_size].reshape(D, D)
    offset = 4 * matrix_size
    b_query = flat[offset:offset + D]
    b_value = flat[offset + D:offset + 2 * D]
    b_out = flat[offset + 2 * D:offset + 3 * D]
    gain_one = flat[offset + 3 * D:offset + 4 * D]
    shift_one = flat[offset + 4 * D:offset + 5 * D]
    return (w_query, w_key, w_value, w_out, b_query, b_value, b_out, gain_one, shift_one)

def split_ffn(flat):
    matrix_size = D * FF
    w_up = flat[0:matrix_size].reshape(D, FF)
    w_down = flat[matrix_size:2 * matrix_size].reshape(FF, D)
    offset = 2 * matrix_size
    b_up = flat[offset:offset + FF]
    b_down = flat[offset + FF:offset + FF + D]
    gain_two = flat[offset + FF + D:offset + FF + 2 * D]
    shift_two = flat[offset + FF + 2 * D:offset + FF + 3 * D]
    return (w_up, w_down, b_up, b_down, gain_two, shift_two)

def layer_norm(resid, gain, shift):
    centred = resid - lax.optimization_barrier(jnp.mean(resid, axis=-1, keepdims=True))
    spread = lax.optimization_barrier(jnp.mean(centred * centred, axis=-1, keepdims=True))
    return centred * lax.rsqrt(spread + NORM_EPSILON) * gain + shift

def attend_row(query_row, key_row, value_row, segment_row, valid_row):
    scores = jnp.einsum('qhe,khe->hqk', query_row, key_row, precision=HIGHEST) * HEAD ** (-0.5)
    scores = low_back(scores)
    position = jnp.arange(ROW, dtype=jnp.int32)
    allowed = (segment_row[:, None] == segment_row[None, :]) & valid_row[None, :] | (position[:, None] == position[None, :])
    scores = jnp.where(allowed[None], scores, NEGATIVE)
    att_prob = low(jax.nn.softmax(scores, axis=-1))
    return jnp.einsum('hqk,khe->qhe', att_prob, value_row, precision=HIGHEST)

def layer_forward(inputs, attn_flat, ffn_flat, segments, is_valid):
    w_query, w_key, w_value, w_out, b_query, b_value, b_out, gain_one, shift_one = split_attn(low(attn_flat))
    w_up, w_down, b_up, b_down, gain_two, shift_two = split_ffn(low(ffn_flat))
    queries = low(low_back(jnp.dot(inputs, w_query, precision=HIGHEST) + b_query))
    keys = low(low_back(jnp.dot(inputs, w_key, precision=HIGHEST)))
    values = low(low_back(jnp.dot(inputs, w_value, precision=HIGHEST) + b_value))
    shape = (NROWS, ROW, HEADS, HEAD)
    row_attend = jax.checkpoint(attend_row)

    def one_row(group):
        return row_attend(group[0], group[1], group[2], group[3], group[4])
    mixed = lax.map(one_row, (queries.reshape(shape), keys.reshape(shape), values.reshape(shape), segments.reshape(NROWS, ROW), is_valid.reshape(NROWS, ROW)))
    mixed = low(low_back(mixed.reshape(TOKENS, D)))
    attn_proj = low_back(jnp.dot(mixed, w_out, precision=HIGHEST) + b_out)
    hidden_one = layer_norm(inputs + attn_proj, gain_one, shift_one)
    pre_act = low_back(jnp.dot(low(hidden_one), w_up, precision=HIGHEST) + b_up)
    activated = low(jax.nn.gelu(pre_act, approximate=False))
    ffn_proj = low_back(jnp.dot(activated, w_down, precision=HIGHEST) + b_down)
    return layer_norm(hidden_one + ffn_proj, gain_two, shift_two)

def adam_update(param, gradient, moment, square, shadow):
    step_float = float(STEP)
    moment_next = MOMENT_DECAY * moment + (1.0 - MOMENT_DECAY) * gradient
    square_next = SQUARE_DECAY * square + (1.0 - SQUARE_DECAY) * gradient * gradient
    moment_hat = moment_next / (1.0 - MOMENT_DECAY ** step_float)
    square_hat = square_next / (1.0 - SQUARE_DECAY ** step_float)
    change = -LEARN_RATE * (moment_hat / (jnp.sqrt(square_hat) + ADAM_EPSILON) + WEIGHT_DECAY * param)
    updated = param + change
    drift = (1.0 - SHADOW_RATE) * (updated - shadow)
    return (change, moment_next, square_next, drift)

def reference(tokens, segments, counts, out_grad, attn_param, attn_moment, attn_square, attn_shadow, ffn_param, ffn_moment, ffn_square, ffn_shadow):
    position = jnp.arange(ROW, dtype=jnp.int32)
    is_valid = (position[None, :] < counts[:, None]).reshape(TOKENS)

    def layer_fn(inputs, attn_flat, ffn_flat):
        return layer_forward(inputs, attn_flat, ffn_flat, segments, is_valid)
    final_out, pullback = jax.vjp(layer_fn, tokens.astype(jnp.float32), attn_param, ffn_param)
    valid_float = is_valid.astype(jnp.float32)
    cotangent = out_grad.astype(jnp.float32) * valid_float[:, None]
    grad_tokens, grad_attn_sum, grad_ffn_sum = pullback(cotangent)
    token_total = jnp.sum(counts).astype(jnp.float32)
    attn_grad = grad_attn_sum / token_total
    ffn_grad = grad_ffn_sum / token_total
    row_ids = jnp.arange(NROWS, dtype=jnp.int32)[:, None] * CROPS
    slot_ids = (row_ids + segments.reshape(NROWS, ROW).astype(jnp.int32)).reshape(TOKENS).astype(jnp.int32)
    crop_sums = jax.ops.segment_sum(final_out * valid_float[:, None], slot_ids, num_segments=NROWS * CROPS)
    crop_sizes = jax.ops.segment_sum(valid_float, slot_ids, num_segments=NROWS * CROPS)
    pooled = crop_sums / jnp.maximum(crop_sizes, 1.0)[:, None]
    attn_change, moment_attn, square_attn, drift_attn = adam_update(attn_param, attn_grad, attn_moment, attn_square, attn_shadow)
    ffn_change, moment_ffn, square_ffn, drift_ffn = adam_update(ffn_param, ffn_grad, ffn_moment, ffn_square, ffn_shadow)
    return (final_out.astype(jnp.bfloat16), pooled, grad_tokens.astype(jnp.bfloat16), attn_grad, ffn_grad, attn_change, ffn_change, moment_attn, moment_ffn, square_attn, square_ffn, drift_attn, drift_ffn)
```

```python
import functools

import jax
import jax.numpy as jnp
from jax import lax
from jax.experimental import pallas as pl
from jax.experimental.pallas import tpu as pltpu
from jax.sharding import PartitionSpec as P

D = 768
FF = 3072
HEAD = 64
HEADS = 12
ROW = 1024
STEP = 10
CROPS = 16

NORM_EPSILON = 1e-12
NEGATIVE = -1e30
MOMENT_DECAY = 0.9
SQUARE_DECAY = 0.999
LEARN_RATE = 0.001
WEIGHT_DECAY = 0.01
ADAM_EPSILON = 1e-08
SHADOW_RATE = 0.9995
SCALE = HEAD ** (-0.5)

AXES = ("dp", "wide")
BF = jnp.bfloat16
F32 = jnp.float32
UP_CHUNKS = FF // D
ATTN_ROWS = 4 * D
FFN_ROWS = 2 * FF
ATTN_TAIL = 5 * D
FFN_TAIL = FF + 3 * D
VEC_ROWS = 16
COUNT_ROW = 12
MIB = 1 << 20


def dot(left, right, left_dim, right_dim):
    return lax.dot_general(
        left, right, (((left_dim,), (right_dim,)), ((), ())), preferred_element_type=F32
    )


class Places:
    def __init__(self, mesh):
        self.dp, self.wide = mesh.shape["dp"], mesh.shape["wide"]
        self.count = self.dp * self.wide
        self.size = {"c": 2, "y": self.dp // 2}
        self.size["x"] = self.size["y"]
        self.size["z"] = self.wide // self.size["x"]

    def staged(self):
        exact = self.dp % 2 == 0 and self.wide % self.size["x"] == 0
        return exact and ATTN_ROWS % (32 * self.count) == 0

    def index(self, y, c, z, x):
        return (y * 2 + c) * self.wide + z * self.size["x"] + x

    def rotation(self, axis, step):
        pairs = []
        extent = self.size
        for y in range(extent["y"]):
            for c in range(2):
                for z in range(extent["z"]):
                    for x in range(extent["x"]):
                        at = {"y": y, "c": c, "z": z, "x": x}
                        to = dict(at)
                        to[axis] = (at[axis] + step) % extent[axis]
                        pairs.append((self.index(**at), self.index(**to)))
        return pairs

    def send(self, array, axis, step):
        return lax.ppermute(array, AXES, self.rotation(axis, step))

    def here(self):
        outer, inner = lax.axis_index("dp"), lax.axis_index("wide")
        extent = self.size["x"]
        return {"y": outer // 2, "c": outer % 2, "z": inner // extent, "x": inner % extent}


def pick(array, index, axis):
    return lax.dynamic_index_in_dim(array, index, axis, keepdims=False)


def small_sum(places, array):
    for axis in ("c", "z", "x", "y"):
        total = array
        for step in range(1, places.size[axis]):
            total = total + places.send(array, axis, step)
        array = total
    return array


def gather_pieces(places, own):
    extent = places.size
    rows = own.shape[0]
    half_rows = rows // 2
    blocks = [own] + [places.send(own, "z", k) for k in range(1, extent["z"])]
    pieces = []
    for half, (first, second) in enumerate((("x", "y"), ("y", "x"))):
        held = jnp.concatenate([b[half * half_rows : (half + 1) * half_rows] for b in blocks], 0)
        where = [{"z": k} for k in range(extent["z"])]
        near, near_where = [held], list(where)
        for k in range(1, extent[first]):
            near.append(places.send(held, first, k))
            near_where += [dict(w, **{first: k}) for w in where]
        near = jnp.concatenate(near, 0)
        groups = [(near, near_where)]
        for k in range(1, extent[second]):
            groups.append((places.send(near, second, k), [dict(w, **{second: k}) for w in near_where]))
        groups += [(places.send(g, "c", 1), [dict(w, c=1) for w in ws]) for g, ws in groups]
        pieces += [
            (g, [(w.get("z", 0), w.get("x", 0), w.get("y", 0), w.get("c", 0), half) for w in ws])
            for g, ws in groups
        ]
    return pieces


def owner_index(places, here, offsets):
    extent = places.size
    dz, dx, dy, dc, _ = offsets
    return places.index(
        lax.rem(here["y"] + (extent["y"] - dy), extent["y"]),
        lax.rem(here["c"] + (2 - dc), 2),
        lax.rem(here["z"] + (extent["z"] - dz), extent["z"]),
        lax.rem(here["x"] + (extent["x"] - dx), extent["x"]),
    )


def assemble(places, me, pieces, rows, cut, place):
    def kernel(me_ref, *refs):
        out, sem = refs[-2:]
        here = {"y": me_ref[0], "c": me_ref[1], "z": me_ref[2], "x": me_ref[3]}
        for (_, offsets), ref in zip(pieces, refs):
            step = ref.shape[0] // len(offsets)
            part_rows = step // cut
            for i, off in enumerate(offsets):
                owner = owner_index(places, here, off)
                for part in range(cut):
                    start = pl.multiple_of(place(owner, off[4], part), 16)
                    pltpu.make_async_copy(
                        ref.at[pl.ds(i * step + part * part_rows, part_rows)],
                        out.at[pl.ds(start, part_rows)],
                        sem,
                    ).start()
        pltpu.make_async_copy(out, out, sem).wait()

    return pl.pallas_call(
        kernel,
        in_specs=[pl.BlockSpec(memory_space=pltpu.SMEM)]
        + [pl.BlockSpec(memory_space=pl.ANY)] * len(pieces),
        out_specs=pl.BlockSpec(memory_space=pl.ANY),
        out_shape=jax.ShapeDtypeStruct((rows, D), BF),
        scratch_shapes=[pltpu.SemaphoreType.DMA],
        name="assemble",
    )(me, *[p for p, _ in pieces])


def scatter_sum(places, here, parts):
    extent = places.size

    def add(own, arrived):
        total = own.astype(F32)
        for a in arrived:
            total = total + a.astype(F32)
        return total

    def reduce_axis(array, axis, dim):
        arrived = [
            places.send(pick(array, lax.rem(here[axis] + k, extent[axis]), dim), axis, k)
            for k in range(1, extent[axis])
        ]
        return add(pick(array, here[axis], dim), arrived)

    summed = jnp.stack([reduce_axis(p, "c", 0).astype(BF) for p in parts])
    half_rows = summed.shape[3] // 2
    first = summed[:, :, :, :half_rows]
    second = summed[:, :, :, half_rows:]
    first = reduce_axis(first, "y", 0).astype(BF)
    second = reduce_axis(second, "x", 2).astype(BF)
    first = reduce_axis(first, "x", 1).astype(BF)
    second = reduce_axis(second, "y", 0).astype(BF)
    return reduce_axis(jnp.concatenate([first, second], 1), "z", 0)


def to_rows(places, me, flat, rows, tail):
    count = places.count
    block = rows // count * D
    slack = tail // count
    before = lax.ppermute(flat[-tail:], AXES, [(i, i + 1) for i in range(count - 1)])
    joined = jnp.concatenate([before, flat])
    return lax.dynamic_slice_in_dim(joined, tail - me * slack, block).reshape(rows // count, D)


def to_flat(places, me, block, vectors, tail):
    count = places.count
    slack = tail // count
    after = lax.ppermute(block[: tail // D], AXES, [(i + 1, i) for i in range(count - 1)])
    after = jnp.where(me == count - 1, vectors, after)
    joined = jnp.concatenate([block, after], 0).reshape(-1)
    return lax.dynamic_slice_in_dim(joined, me * slack, block.size + slack)


def project_kernel(tokens, weights, vec, query, key, value):
    held = tokens[...]
    query[...] = (dot(held, weights[0], 1, 0) + vec[0:1]).astype(BF)
    key[...] = dot(held, weights[1], 1, 0).astype(BF)
    value[...] = (dot(held, weights[2], 1, 0) + vec[1:2]).astype(BF)


def project(tokens, weights, vec):
    rows = tokens.shape[0]
    step = 256
    tile = pl.BlockSpec((step, D), lambda i: (i, 0))
    return pl.pallas_call(
        project_kernel,
        grid=(rows // step,),
        in_specs=[
            tile,
            pl.BlockSpec((3, D, D), lambda i: (0, 0, 0), pipeline_mode=pl.Buffered(1)),
            pl.BlockSpec((VEC_ROWS, D), lambda i: (0, 0)),
        ],
        out_specs=[tile] * 3,
        out_shape=[jax.ShapeDtypeStruct((rows, D), BF)] * 3,
        compiler_params=pltpu.CompilerParams(vmem_limit_bytes=40 * MIB),
        name="project",
    )(tokens, weights, vec)


QUERY_BLOCK = 256
QUERY_BLOCKS = ROW // QUERY_BLOCK


def window(block):
    low = max(0, block - 1) * QUERY_BLOCK
    return low, min(QUERY_BLOCKS, block + 2) * QUERY_BLOCK


def fill_bias(bias, seg_column, seg_row, count):
    for block in range(QUERY_BLOCKS):
        low, high = window(block)
        at = slice(block * QUERY_BLOCK, (block + 1) * QUERY_BLOCK)
        shape = (high - low, QUERY_BLOCK)
        key_pos = low + lax.broadcasted_iota(jnp.int32, shape, 0)
        query_pos = block * QUERY_BLOCK + lax.broadcasted_iota(jnp.int32, shape, 1)
        same = seg_column[low:high, 0:1] == seg_row[0:1, at]
        allowed = (same & (key_pos < count)) | (key_pos == query_pos)
        bias[0 : high - low, at] = jnp.where(allowed, 0.0, NEGATIVE).astype(F32)


def one_head(transposed):
    zero = jnp.zeros((HEAD, transposed.shape[1]), transposed.dtype)
    return (
        jnp.concatenate([transposed[:HEAD], zero], 0),
        jnp.concatenate([zero, transposed[HEAD:]], 0),
    )


def attend_kernel(count, seg_column, seg_row, query, key, value, mixed, log_total, bias):
    @pl.when(pl.program_id(0) == 0)
    def _():
        fill_bias(bias, seg_column, seg_row, count[0])

    value_t = value[...].T
    query_t = one_head((query[...] * jnp.asarray(SCALE, BF)).T)
    for block in range(QUERY_BLOCKS):
        low, high = window(block)
        at = slice(block * QUERY_BLOCK, (block + 1) * QUERY_BLOCK)
        parts = []
        for h in range(2):
            scores = dot(key[low:high, :], query_t[h][:, at], 1, 0) + bias[0 : high - low, at]
            top = jnp.max(scores, axis=0, keepdims=True)
            shifted = jnp.exp(scores - top)
            total = jnp.sum(shifted, axis=0, keepdims=True)
            part = dot(value_t[h * HEAD : (h + 1) * HEAD, low:high], shifted.astype(BF), 1, 0)
            parts.append(part * (1.0 / total))
            log_total[0, h : h + 1, at] = top + jnp.log(total)
        mixed[at, :] = jnp.concatenate(parts, 0).T.astype(BF)


def attend_specs():
    return [
        pl.BlockSpec(memory_space=pltpu.SMEM),
        pl.BlockSpec((ROW, 1), lambda h: (0, 0)),
        pl.BlockSpec((1, ROW), lambda h: (0, 0)),
    ]


def attend(query, key, value, segments, count):
    pair = pl.BlockSpec((ROW, 2 * HEAD), lambda h: (0, h))
    return pl.pallas_call(
        attend_kernel,
        grid=(HEADS // 2,),
        in_specs=attend_specs() + [pair] * 3,
        out_specs=[pair, pl.BlockSpec((1, 8, ROW), lambda h: (h, 0, 0))],
        out_shape=[
            jax.ShapeDtypeStruct((ROW, D), BF),
            jax.ShapeDtypeStruct((HEADS // 2, 8, ROW), F32),
        ],
        scratch_shapes=[pltpu.VMEM((3 * QUERY_BLOCK, ROW), F32)],
        compiler_params=pltpu.CompilerParams(vmem_limit_bytes=40 * MIB),
        name="attend",
    )(count, segments.reshape(ROW, 1), segments.reshape(1, ROW), query, key, value)


def attend_back_kernel(
    count, seg_column, seg_row, query, key, value, grad, log_total, grad_query, grad_key, grad_value, bias, key_sum, value_sum
):
    @pl.when(pl.program_id(0) == 0)
    def _():
        fill_bias(bias, seg_column, seg_row, count[0])

    query_t = (query[...] * jnp.asarray(SCALE, BF)).T
    key_t = key[...].T
    grad_t = grad[...].T
    query_one, grad_one = one_head(query_t), one_head(grad_t)
    key_sum[...] = jnp.zeros_like(key_sum)
    value_sum[...] = jnp.zeros_like(value_sum)
    for block in range(QUERY_BLOCKS):
        low, high = window(block)
        at = slice(block * QUERY_BLOCK, (block + 1) * QUERY_BLOCK)
        parts = []
        for h in range(2):
            rows = slice(h * HEAD, (h + 1) * HEAD)
            scores = dot(key[low:high, :], query_one[h][:, at], 1, 0) + bias[0 : high - low, at]
            probs = jnp.exp(scores - log_total[0, h : h + 1, at])
            grad_probs = dot(value[low:high, :], grad_one[h][:, at], 1, 0)
            weighted = probs * grad_probs
            total = jnp.sum(weighted, axis=0, keepdims=True)
            grad_scores = (weighted - probs * total).astype(BF)
            parts.append(dot(key_t[rows, low:high], grad_scores, 1, 0))
            key_sum[rows, low:high] += dot(query_t[rows, at], grad_scores, 1, 1)
            value_sum[rows, low:high] += dot(grad_t[rows, at], probs.astype(BF), 1, 1)
        grad_query[at, :] = (jnp.concatenate(parts, 0) * SCALE).T.astype(BF)
    grad_key[...] = key_sum[...].T.astype(BF)
    grad_value[...] = value_sum[...].T.astype(BF)


def attend_back(query, key, value, grad, log_total, segments, count):
    pair = pl.BlockSpec((ROW, 2 * HEAD), lambda h: (0, h))
    return pl.pallas_call(
        attend_back_kernel,
        grid=(HEADS // 2,),
        in_specs=attend_specs() + [pair] * 4 + [pl.BlockSpec((1, 8, ROW), lambda h: (h, 0, 0))],
        out_specs=[pair] * 3,
        out_shape=[jax.ShapeDtypeStruct((ROW, D), BF)] * 3,
        scratch_shapes=[
            pltpu.VMEM((3 * QUERY_BLOCK, ROW), F32),
            pltpu.VMEM((2 * HEAD, ROW), F32),
            pltpu.VMEM((2 * HEAD, ROW), F32),
        ],
        compiler_params=pltpu.CompilerParams(vmem_limit_bytes=48 * MIB),
        name="attend_back",
    )(count, segments.reshape(ROW, 1), segments.reshape(1, ROW), query, key, value, grad, log_total)


def normalise(resid):
    centred = resid - jnp.mean(resid, axis=-1, keepdims=True)
    spread = jnp.mean(centred * centred, axis=-1, keepdims=True)
    inverse = lax.rsqrt(spread + NORM_EPSILON)
    return centred * inverse, inverse


def normalise_back(cotangent, gain, normal, inverse):
    scaled = cotangent * gain
    mean = jnp.mean(scaled, axis=-1, keepdims=True)
    aligned = jnp.mean(scaled * normal, axis=-1, keepdims=True)
    return inverse * (scaled - mean - normal * aligned)


def column_sum(array):
    return jnp.sum(array, axis=0, keepdims=True)


MIDDLE_ROWS = 256


def middle_kernel(
    count,
    seg_row,
    mixed,
    tokens,
    out_grad,
    w_out,
    w_ffn,
    vec,
    final_low,
    hidden_low,
    activated,
    grad_pre,
    grad_ffn_out,
    grad_attn_out,
    grad_mixed,
    grad_resid,
    vec_grad,
    crop_sums,
    slope,
):
    step = pl.program_id(0)

    @pl.when(step == 0)
    def _():
        vec_grad[...] = jnp.zeros_like(vec_grad)
        crop_sums[...] = jnp.zeros_like(crop_sums)

    def row(i):
        return vec[i : i + 1]

    def note(i, value):
        vec_grad[i : i + 1] += value

    resid_one = tokens[...].astype(F32) + (dot(mixed[...], w_out[...], 1, 0) + row(2))
    normal_one, inverse_one = normalise(resid_one)
    hidden = normal_one * row(3) + row(4)
    low = hidden.astype(BF)
    hidden_low[...] = low
    total = hidden + row(9)
    for j in range(UP_CHUNKS):
        at = slice(j * D, (j + 1) * D)
        pre = dot(low, w_ffn[j], 1, 0) + row(5 + j)
        share = 0.5 + 0.5 * lax.erf(pre * (0.5**0.5))
        density = jnp.exp(-0.5 * pre * pre) * 0.3989422804014327
        slope[:, at] = share + pre * density
        act = (pre * share).astype(BF)
        activated[:, at] = act
        total = total + dot(act, w_ffn[UP_CHUNKS + j], 1, 0)
    normal_two, inverse_two = normalise(total)
    final = normal_two * row(10) + row(11)
    final_low[...] = final.astype(BF)

    first = step * MIDDLE_ROWS
    across = (CROPS, MIDDLE_ROWS)
    position = first + lax.broadcasted_iota(jnp.int32, across, 1)
    crop = lax.broadcasted_iota(jnp.int32, across, 0)
    member = ((seg_row[...] == crop) & (position < count[0])).astype(BF)
    high = final.astype(BF)
    rest = final - high.astype(F32)
    mid = rest.astype(BF)
    tiny = (rest - mid.astype(F32)).astype(BF)
    crop_sums[...] += dot(member, high, 1, 0) + (dot(member, mid, 1, 0) + dot(member, tiny, 1, 0))

    position = first + lax.broadcasted_iota(jnp.int32, (MIDDLE_ROWS, 1), 0)
    valid = (position < count[0]).astype(F32)
    cotangent = out_grad[...].astype(F32) * valid
    note(10, column_sum(cotangent * normal_two))
    note(11, column_sum(cotangent))
    grad_two = normalise_back(cotangent, row(10), normal_two, inverse_two)
    grad_out = grad_two.astype(BF)
    grad_ffn_out[...] = grad_out
    note(9, column_sum(grad_out.astype(F32)))
    grad_hidden = grad_two
    for j in range(UP_CHUNKS):
        at = slice(j * D, (j + 1) * D)
        back = (dot(grad_out, w_ffn[UP_CHUNKS + j], 1, 1) * slope[:, at]).astype(BF)
        grad_pre[:, at] = back
        note(5 + j, column_sum(back.astype(F32)))
        grad_hidden = grad_hidden + dot(back, w_ffn[j], 1, 1)
    note(3, column_sum(grad_hidden * normal_one))
    note(4, column_sum(grad_hidden))
    grad_one = normalise_back(grad_hidden, row(3), normal_one, inverse_one)
    grad_resid[...] = grad_one
    grad_proj = grad_one.astype(BF)
    grad_attn_out[...] = grad_proj
    note(2, column_sum(grad_proj.astype(F32)))
    grad_mixed[...] = dot(grad_proj, w_out[...], 1, 1).astype(BF)


def middle(count, segments, mixed, tokens, out_grad, w_out, w_ffn, vec):
    rows = tokens.shape[0]
    tile = pl.BlockSpec((MIDDLE_ROWS, D), lambda i: (i, 0))
    wide = pl.BlockSpec((MIDDLE_ROWS, FF), lambda i: (i, 0))
    small = pl.BlockSpec((VEC_ROWS, D), lambda i: (0, 0))

    def shape(width, kind):
        return jax.ShapeDtypeStruct((rows, width), kind)

    return pl.pallas_call(
        middle_kernel,
        grid=(rows // MIDDLE_ROWS,),
        in_specs=[
            pl.BlockSpec(memory_space=pltpu.SMEM),
            pl.BlockSpec((1, MIDDLE_ROWS), lambda i: (0, i)),
            tile,
            tile,
            tile,
            pl.BlockSpec((D, D), lambda i: (0, 0), pipeline_mode=pl.Buffered(1)),
            pl.BlockSpec((2 * UP_CHUNKS, D, D), lambda i: (0, 0, 0), pipeline_mode=pl.Buffered(1)),
            small,
        ],
        out_specs=[tile, tile, wide, wide, tile, tile, tile, tile, small, small],
        out_shape=[
            shape(D, BF),
            shape(D, BF),
            shape(FF, BF),
            shape(FF, BF),
            shape(D, BF),
            shape(D, BF),
            shape(D, BF),
            shape(D, F32),
            jax.ShapeDtypeStruct((VEC_ROWS, D), F32),
            jax.ShapeDtypeStruct((CROPS, D), F32),
        ],
        scratch_shapes=[pltpu.VMEM((MIDDLE_ROWS, FF), F32)],
        compiler_params=pltpu.CompilerParams(vmem_limit_bytes=56 * MIB),
        name="middle",
    )(count, segments.reshape(1, rows), mixed, tokens, out_grad, w_out, w_ffn, vec)


def adam_update(param, gradient, moment, square, shadow):
    step_float = float(STEP)
    moment_next = MOMENT_DECAY * moment + (1.0 - MOMENT_DECAY) * gradient
    square_next = SQUARE_DECAY * square + (1.0 - SQUARE_DECAY) * gradient * gradient
    moment_hat = moment_next / (1.0 - MOMENT_DECAY**step_float)
    square_hat = square_next / (1.0 - SQUARE_DECAY**step_float)
    change = -LEARN_RATE * (
        moment_hat / (jnp.sqrt(square_hat) + ADAM_EPSILON) + WEIGHT_DECAY * param
    )
    updated = param + change
    drift = (1.0 - SHADOW_RATE) * (updated - shadow)
    return (change, moment_next, square_next, drift)


def contract_rows(left, right):
    return dot(left, right, 0, 0)


def on_device(
    places,
    tokens,
    segments,
    counts,
    out_grad,
    attn_param,
    attn_moment,
    attn_square,
    attn_shadow,
    ffn_param,
    ffn_moment,
    ffn_square,
    ffn_shadow,
):
    assert counts.shape[0] == 1 and tokens.shape[0] == ROW
    number = places.count
    here = places.here()
    place_list = jnp.stack([here[a] for a in ("y", "c", "z", "x")]).astype(jnp.int32)
    me = lax.axis_index("dp") * places.wide + lax.axis_index("wide")
    staged = places.staged()
    attn_rows, ffn_rows = ATTN_ROWS // number, FFN_ROWS // number
    up_rows = ffn_rows // UP_CHUNKS
    holds_up = me < number // 2

    last = (me == number - 1).astype(F32)
    ends = jnp.concatenate([attn_param[-ATTN_TAIL:], ffn_param[-FFN_TAIL:]]) * last
    count_row = jnp.full((D,), counts[0].astype(F32), F32)
    small = jnp.concatenate(
        [ends, count_row, jnp.zeros(((VEC_ROWS - COUNT_ROW - 1) * D,), F32)]
    ).reshape(VEC_ROWS, D)
    if staged:
        small = small_sum(places, small)
    else:
        small = lax.psum(small, AXES)
    token_total = small[COUNT_ROW, 0]
    vec = small.astype(BF).astype(F32)

    if staged:
        attn_own = to_rows(places, me, attn_param, ATTN_ROWS, ATTN_TAIL).astype(BF)
        ffn_own = to_rows(places, me, ffn_param, FFN_ROWS, FFN_TAIL).astype(BF)
        by_chunk = ffn_own.reshape(up_rows, UP_CHUNKS, D).transpose(1, 0, 2).reshape(ffn_rows, D)
        ffn_own = jnp.where(holds_up, by_chunk, ffn_own)
        attn_whole = assemble(
            places,
            place_list,
            gather_pieces(places, attn_own),
            ATTN_ROWS,
            1,
            lambda owner, half, part: owner * attn_rows + half * (attn_rows // 2),
        ).reshape(4, D, D)

        def ffn_place(owner, half, part):
            chunk = half * (UP_CHUNKS // 2) + part
            return jnp.where(
                owner < number // 2,
                chunk * D + owner * up_rows,
                FF + (owner - number // 2) * ffn_rows + chunk * up_rows,
            )

        w_ffn = assemble(
            places,
            place_list,
            gather_pieces(places, ffn_own),
            FFN_ROWS,
            UP_CHUNKS // 2,
            ffn_place,
        ).reshape(2 * UP_CHUNKS, D, D)
    else:
        flat = lax.all_gather(attn_param.astype(BF), AXES, axis=0, tiled=True)
        attn_whole = flat[: ATTN_ROWS * D].reshape(4, D, D)
        flat = lax.all_gather(ffn_param.astype(BF), AXES, axis=0, tiled=True)
        w_up = flat[: FF * D].reshape(D, UP_CHUNKS, D).transpose(1, 0, 2)
        w_down = flat[FF * D : FFN_ROWS * D].reshape(UP_CHUNKS, D, D)
        w_ffn = jnp.concatenate([w_up, w_down], 0)

    query, key, value = project(tokens, attn_whole, vec)
    mixed, log_total = attend(query, key, value, segments, counts)
    (
        final_low,
        hidden_low,
        activated,
        grad_pre,
        grad_ffn_out,
        grad_attn_out,
        grad_mixed,
        grad_resid,
        vec_grad,
        crop_sums,
    ) = middle(counts, segments, mixed, tokens, out_grad, attn_whole[3], w_ffn, vec)
    is_valid = jnp.arange(ROW, dtype=jnp.int32) < counts[0]
    member = (segments[None, :] == jnp.arange(CROPS, dtype=jnp.int32)[:, None]) & is_valid[None, :]
    crop_sizes = jnp.sum(member.astype(F32), axis=1)
    pooled = crop_sums / jnp.maximum(crop_sizes, 1.0)[:, None]

    grad_w_down = contract_rows(activated, grad_ffn_out)
    grad_w_up = [
        contract_rows(hidden_low, grad_pre[:, j * D : (j + 1) * D]) for j in range(UP_CHUNKS)
    ]
    if staged:
        extent = places.size
        split = (extent["y"] // 2, 2, extent["z"], extent["x"])
        up = jnp.stack(
            [g.astype(BF).reshape(number // 2, up_rows, D) for g in grad_w_up], 1
        ).reshape(split + (ffn_rows, D))
        down = grad_w_down.astype(BF).reshape(split + (ffn_rows, D))
        ffn_parts = [up[y] for y in range(split[0])] + [down[y] for y in range(split[0])]
        ffn_block = scatter_sum(places, here, ffn_parts)
        by_row = ffn_block.reshape(UP_CHUNKS, up_rows, D).transpose(1, 0, 2).reshape(ffn_rows, D)
        ffn_block = jnp.where(holds_up, by_row, ffn_block)

    grad_w_out = contract_rows(mixed, grad_attn_out)
    grad_query, grad_key, grad_value = attend_back(
        query, key, value, grad_mixed, log_total, segments, counts
    )
    grad_w_query = contract_rows(tokens, grad_query)
    grad_w_key = contract_rows(tokens, grad_key)
    grad_w_value = contract_rows(tokens, grad_value)
    grad_b_query = jnp.sum(grad_query.astype(F32), axis=0)
    grad_b_value = jnp.sum(grad_value.astype(F32), axis=0)
    token_grad = (
        grad_resid
        + dot(grad_query, attn_whole[0], 1, 1)
        + dot(grad_key, attn_whole[1], 1, 1)
        + dot(grad_value, attn_whole[2], 1, 1)
    ).astype(BF)
    vec_grad = jnp.concatenate([jnp.stack([grad_b_query, grad_b_value]), vec_grad[2:]], 0)
    if staged:
        vec_sum = small_sum(places, vec_grad)
        mats = [grad_w_query, grad_w_key, grad_w_value, grad_w_out]
        mats = jnp.stack([m.astype(BF) for m in mats]).reshape(
            extent["y"], 2, extent["z"], extent["x"], attn_rows, D
        )
        attn_block = scatter_sum(places, here, [mats[y] for y in range(extent["y"])])
        attn_summed = to_flat(places, me, attn_block, vec_sum[:5], ATTN_TAIL)
        ffn_summed = to_flat(places, me, ffn_block, vec_sum[5:12], FFN_TAIL)
    else:
        attn_full = jnp.concatenate(
            [g.reshape(-1) for g in (grad_w_query, grad_w_key, grad_w_value, grad_w_out, vec_grad[:5])]
        )
        up = jnp.stack(grad_w_up, 1)
        ffn_full = jnp.concatenate([g.reshape(-1) for g in (up, grad_w_down, vec_grad[5:12])])
        attn_summed = lax.psum_scatter(attn_full, AXES, scatter_dimension=0, tiled=True)
        ffn_summed = lax.psum_scatter(ffn_full, AXES, scatter_dimension=0, tiled=True)
    attn_grad = attn_summed / token_total
    ffn_grad = ffn_summed / token_total
    attn_change, moment_attn, square_attn, drift_attn = adam_update(
        attn_param, attn_grad, attn_moment, attn_square, attn_shadow
    )
    ffn_change, moment_ffn, square_ffn, drift_ffn = adam_update(
        ffn_param, ffn_grad, ffn_moment, ffn_square, ffn_shadow
    )
    return (
        final_low,
        pooled,
        token_grad,
        attn_grad,
        ffn_grad,
        attn_change,
        ffn_change,
        moment_attn,
        moment_ffn,
        square_attn,
        square_ffn,
        drift_attn,
        drift_ffn,
    )


def solution(mesh):
    rows, flat = P(AXES, None), P(AXES)
    return jax.shard_map(
        functools.partial(on_device, Places(mesh)),
        mesh=mesh,
        in_specs=(rows, flat, flat, rows) + (flat,) * 8,
        out_specs=(rows, rows, rows) + (flat,) * 10,
        check_vma=False,
    )
```

```python
import functools

import jax
import jax.numpy as jnp
from jax import lax
from jax.experimental import pallas as pl
from jax.experimental.pallas import tpu as pltpu
from jax.sharding import PartitionSpec as P

D = 768
FF = 3072
HEAD = 64
HEADS = 12
ROW = 1024
STEP = 10
CROPS = 16

NORM_EPSILON = 1e-12
NEGATIVE = -1e30
MOMENT_DECAY = 0.9
SQUARE_DECAY = 0.999
LEARN_RATE = 0.001
WEIGHT_DECAY = 0.01
ADAM_EPSILON = 1e-08
SHADOW_RATE = 0.9995
SCALE = HEAD ** (-0.5)

AXES = ("dp", "wide")
BF = jnp.bfloat16
F32 = jnp.float32
UP_CHUNKS = FF // D
ATTN_ROWS = 4 * D
FFN_ROWS = 2 * FF
ATTN_TAIL = 5 * D
FFN_TAIL = FF + 3 * D
FFN_SETS = 2
ATTEND_CALLS = 3
VEC_ROWS = 16
COUNT_ROW = 12
MIB = 1 << 20


def dot(left, right, left_dim, right_dim):
    return lax.dot_general(
        left, right, (((left_dim,), (right_dim,)), ((), ())), preferred_element_type=F32
    )


class Places:
    def __init__(self, mesh):
        self.dp, self.wide = mesh.shape["dp"], mesh.shape["wide"]
        self.count = self.dp * self.wide
        self.size = {"c": 2, "y": self.dp // 2}
        self.size["x"] = self.size["y"]
        self.size["z"] = self.wide // self.size["x"]

    def staged(self):
        exact = self.dp == 4 and self.wide % self.size["x"] == 0
        return exact and D % (16 * UP_CHUNKS * self.wide // 2) == 0

    def index(self, y, c, z, x):
        return (y * 2 + c) * self.wide + z * self.size["x"] + x

    def rotation(self, axis, step):
        pairs = []
        extent = self.size
        for y in range(extent["y"]):
            for c in range(2):
                along = axis if len(axis) == 1 else axis[c]
                for z in range(extent["z"]):
                    for x in range(extent["x"]):
                        at = {"y": y, "c": c, "z": z, "x": x}
                        to = dict(at)
                        to[along] = (at[along] + step) % extent[along]
                        pairs.append((self.index(**at), self.index(**to)))
        return pairs

    def send(self, array, axis, step):
        return lax.ppermute(array, AXES, self.rotation(axis, step))

    def here(self):
        outer, inner = lax.axis_index("dp"), lax.axis_index("wide")
        extent = self.size["x"]
        return {"y": outer // 2, "c": outer % 2, "z": inner // extent, "x": inner % extent}


def pick(array, index, axis):
    return lax.dynamic_index_in_dim(array, index, axis, keepdims=False)


def order(array, *before):
    return lax.optimization_barrier((array,) + before)[0]


class Gathered:
    def __init__(self, places, rows):
        self.places, self.rows = places, rows
        self.deep = places.size["z"] * rows

    def along_z(self, here, own):
        places, rows, extent = self.places, self.rows, self.places.size
        blocks = [own] + [places.send(own, "z", k) for k in range(1, extent["z"])]
        near = jnp.zeros((self.deep, D), BF)
        for k, block in enumerate(blocks):
            at = lax.rem(here["z"] + (extent["z"] - k), extent["z"]) * rows
            near = lax.dynamic_update_slice_in_dim(near, block[:rows], at, 0)
        if own.shape[0] > rows:
            near = jnp.concatenate([near, self.total([b[rows:] for b in blocks])], 0)
        return near

    def along_first(self, near):
        places, extent = self.places, self.places.size
        blocks = [near] + [places.send(near, "xy", k) for k in range(1, extent["x"])]
        parts = [b[: self.deep] for b in blocks]
        if near.shape[0] > self.deep:
            parts.append(self.total([b[self.deep :] for b in blocks]))
        return jnp.concatenate(parts, 0)

    def along_second(self, near):
        return [self.places.send(near, "yx", k) for k in range(1, self.places.size["x"])]

    def from_core(self, groups):
        return [self.places.send(g, "c", 1) for g in groups]

    def total(self, arrays):
        result = arrays[0].astype(F32)
        for a in arrays[1:]:
            result = result + a.astype(F32)
        return result.astype(BF)

    def columns(self, here):
        extent = self.places.size

        def back(axis, step):
            return lax.rem(here[axis] + (extent[axis] - step), extent[axis])

        for g in range(2 * extent["x"]):
            far, second = divmod(g, extent["x"])
            core = here["c"] if far == 0 else 1 - here["c"]
            for first in range(extent["x"]):
                y = jnp.where(core == 0, back("y", second), back("y", first))
                x = jnp.where(core == 0, back("x", first), back("x", second))
                yield g, first, y, core, x


def read_here(me_ref):
    return {"y": me_ref[0], "c": me_ref[1], "z": me_ref[2], "x": me_ref[3]}


class Scattered:
    def __init__(self, places, here):
        self.places, self.here, self.extent = places, here, places.size
        self.core_zero = here["c"] == 0

    def add(self, own, arrived):
        total = own.astype(F32)
        for a in arrived:
            total = total + a.astype(F32)
        return total

    def shifted(self, axis, k):
        return lax.rem(self.here[axis] + k, self.extent[axis])

    def core(self, give):
        return [self.places.send(give, "c", 1)]

    def first_cut(self, held, k):
        along_x = pick(held, self.shifted("x", k), 2).transpose(1, 0, 2, 3)
        return jnp.where(self.core_zero, along_x, pick(held, self.shifted("y", k), 0))

    def first(self, held):
        steps = range(1, self.extent["x"])
        return [self.places.send(self.first_cut(held, k), "xy", k) for k in steps]

    def second_cut(self, line, k):
        index = jnp.where(self.core_zero, self.shifted("y", k), self.shifted("x", k))
        return pick(line, index, 1)

    def second(self, line):
        steps = range(1, self.extent["x"])
        return [self.places.send(self.second_cut(line, k), "yx", k) for k in steps]

    def along_z(self, column):
        steps = range(1, self.extent["z"])
        return [self.places.send(pick(column, self.shifted("z", k), 0), "z", k) for k in steps]

    def held(self, keep, arrived):
        return self.add(keep, arrived).astype(BF)

    def line(self, held, arrived):
        return self.add(self.first_cut(held, 0), arrived).astype(BF)

    def column(self, line, arrived):
        return self.add(self.second_cut(line, 0), arrived).astype(BF)

    def result(self, column, arrived):
        return self.add(pick(column, self.here["z"], 0), arrived)


def to_rows(places, me, flat, rows, tail):
    count = places.count
    block = rows // count * D
    slack = tail // count
    before = lax.ppermute(flat[-tail:], AXES, [(i, i + 1) for i in range(count - 1)])
    joined = jnp.concatenate([before, flat])
    return lax.dynamic_slice_in_dim(joined, tail - me * slack, block).reshape(rows // count, D)


def to_flat(places, me, block, vectors, tail):
    count = places.count
    slack = tail // count
    after = lax.ppermute(block[: tail // D], AXES, [(i + 1, i) for i in range(count - 1)])
    after = jnp.where(me == count - 1, vectors, after)
    joined = jnp.concatenate([block, after], 0).reshape(-1)
    return lax.dynamic_slice_in_dim(joined, me * slack, block.size + slack)


def project_body(step, tokens, weights, vec, query, key, value):
    held = tokens[...]
    query[...] = (dot(held, weights[0:D], 1, 0) + vec[0:1]).astype(BF)
    key[...] = dot(held, weights[D : 2 * D], 1, 0).astype(BF)
    value[...] = (dot(held, weights[2 * D : 3 * D], 1, 0) + vec[1:2]).astype(BF)


def project_kernel(gathered, number, after, me, tokens, *refs):
    groups = refs[:number]
    query, key, value, vec, whole, weights, extras, sem, extra_sem, out_sem = refs[number + after :]
    step = pl.program_id(0)
    extent = gathered.places.size
    rows, deep = gathered.rows, gathered.rows * extent["z"]

    @pl.when(step == 0)
    def _():
        here = read_here(me)
        for g, ref in enumerate(groups):
            pltpu.make_async_copy(
                ref.at[pl.ds(extent["x"] * deep, VEC_ROWS)], extras.at[g], extra_sem
            ).start()
        shape = (extent["y"], 2, extent["z"], extent["x"], rows, D)
        for g, first, y, core, x in gathered.columns(here):
            pltpu.make_async_copy(
                groups[g].at[pl.ds(first * deep, deep)].reshape(extent["z"], rows, D),
                weights.reshape(*shape).at[y, core, :, x],
                sem,
            ).start()
        pltpu.make_async_copy(extras, extras, extra_sem).wait()
        total = extras[0].astype(F32)
        for g in range(1, number):
            total = total + extras[g].astype(F32)
        vec[...] = total
        pltpu.make_async_copy(weights, weights, sem).wait()
        pltpu.make_async_copy(weights, whole, out_sem).start()

    project_body(step, tokens, weights, vec, query, key, value)

    @pl.when(step == pl.num_programs(0) - 1)
    def _():
        pltpu.make_async_copy(weights, whole, out_sem).wait()


PROJECT_ROWS = 256


def project(tokens, me, gathered, groups, after):
    rows = tokens.shape[0]
    tile = pl.BlockSpec((PROJECT_ROWS, D), lambda i: (i, 0))
    number = len(groups)
    return pl.pallas_call(
        functools.partial(project_kernel, gathered, number, len(after)),
        grid=(rows // PROJECT_ROWS,),
        in_specs=[pl.BlockSpec(memory_space=pltpu.SMEM), tile]
        + [pl.BlockSpec(memory_space=pl.ANY)] * (number + len(after)),
        out_specs=[tile] * 3
        + [pl.BlockSpec((VEC_ROWS, D), lambda i: (0, 0)), pl.BlockSpec(memory_space=pl.ANY)],
        out_shape=[jax.ShapeDtypeStruct((rows, D), BF)] * 3
        + [jax.ShapeDtypeStruct((VEC_ROWS, D), F32), jax.ShapeDtypeStruct((ATTN_ROWS, D), BF)],
        scratch_shapes=[
            pltpu.VMEM((ATTN_ROWS, D), BF),
            pltpu.VMEM((number, VEC_ROWS, D), BF),
            pltpu.SemaphoreType.DMA,
            pltpu.SemaphoreType.DMA,
            pltpu.SemaphoreType.DMA,
        ],
        compiler_params=pltpu.CompilerParams(vmem_limit_bytes=24 * MIB),
        cost_estimate=cost(8),
        name="project",
    )(me, tokens, *groups, *after)


def project_whole(tokens, weights, vec):
    rows = tokens.shape[0]
    tile = pl.BlockSpec((PROJECT_ROWS, D), lambda i: (i, 0))
    return pl.pallas_call(
        lambda *refs: project_body(None, *refs),
        grid=(rows // PROJECT_ROWS,),
        in_specs=[
            tile,
            pl.BlockSpec((ATTN_ROWS, D), lambda i: (0, 0), pipeline_mode=pl.Buffered(1)),
            pl.BlockSpec((VEC_ROWS, D), lambda i: (0, 0)),
        ],
        out_specs=[tile] * 3,
        out_shape=[jax.ShapeDtypeStruct((rows, D), BF)] * 3,
        compiler_params=pltpu.CompilerParams(vmem_limit_bytes=24 * MIB),
        name="project",
    )(tokens, weights, vec)


QUERY_BLOCK = 256
QUERY_BLOCKS = ROW // QUERY_BLOCK


def window(block):
    low = max(0, block - 1) * QUERY_BLOCK
    return low, min(QUERY_BLOCKS, block + 2) * QUERY_BLOCK


def fill_bias(bias, seg_column, seg_row, count):
    for block in range(QUERY_BLOCKS):
        low, high = window(block)
        at = slice(block * QUERY_BLOCK, (block + 1) * QUERY_BLOCK)
        shape = (high - low, QUERY_BLOCK)
        key_pos = low + lax.broadcasted_iota(jnp.int32, shape, 0)
        query_pos = block * QUERY_BLOCK + lax.broadcasted_iota(jnp.int32, shape, 1)
        same = seg_column[low:high, 0:1] == seg_row[0:1, at]
        allowed = (same & (key_pos < count)) | (key_pos == query_pos)
        bias[0 : high - low, at] = jnp.where(allowed, 0.0, NEGATIVE).astype(F32)


def one_head(transposed):
    zero = jnp.zeros((HEAD, transposed.shape[1]), transposed.dtype)
    return (
        jnp.concatenate([transposed[:HEAD], zero], 0),
        jnp.concatenate([zero, transposed[HEAD:]], 0),
    )


def attend_kernel(count, seg_column, seg_row, query, key, value, *refs):
    mixed, log_total, bias = refs[-3:]

    @pl.when(pl.program_id(0) == 0)
    def _():
        fill_bias(bias, seg_column, seg_row, count[0])

    value_t = value[...].T
    query_t = one_head((query[...] * jnp.asarray(SCALE, BF)).T)
    for block in range(QUERY_BLOCKS):
        low, high = window(block)
        at = slice(block * QUERY_BLOCK, (block + 1) * QUERY_BLOCK)
        parts = []
        for h in range(2):
            scores = dot(key[low:high, :], query_t[h][:, at], 1, 0) + bias[0 : high - low, at]
            top = jnp.max(scores, axis=0, keepdims=True)
            shifted = jnp.exp(scores - top)
            total = jnp.sum(shifted, axis=0, keepdims=True)
            part = dot(value_t[h * HEAD : (h + 1) * HEAD, low:high], shifted.astype(BF), 1, 0)
            parts.append(part * (1.0 / total))
            log_total[0, h : h + 1, at] = top + jnp.log(total)
        mixed[at, :] = jnp.concatenate(parts, 0).T.astype(BF)


def attend_specs():
    return [
        pl.BlockSpec(memory_space=pltpu.SMEM),
        pl.BlockSpec((ROW, 1), lambda h: (0, 0)),
        pl.BlockSpec((1, ROW), lambda h: (0, 0)),
    ]


def attend(query, key, value, segments, count, first, pairs, after):
    pair = pl.BlockSpec((ROW, 2 * HEAD), lambda h: (0, h + first))
    return pl.pallas_call(
        attend_kernel,
        grid=(pairs,),
        in_specs=attend_specs() + [pair] * 3 + [pl.BlockSpec(memory_space=pl.ANY)] * len(after),
        out_specs=[
            pl.BlockSpec((ROW, 2 * HEAD), lambda h: (0, h)),
            pl.BlockSpec((1, 8, ROW), lambda h: (h, 0, 0)),
        ],
        out_shape=[
            jax.ShapeDtypeStruct((ROW, pairs * 2 * HEAD), BF),
            jax.ShapeDtypeStruct((pairs, 8, ROW), F32),
        ],
        scratch_shapes=[pltpu.VMEM((3 * QUERY_BLOCK, ROW), F32)],
        compiler_params=pltpu.CompilerParams(vmem_limit_bytes=24 * MIB),
        cost_estimate=cost(25 * pairs / 6),
        name="attend",
    )(count, segments.reshape(ROW, 1), segments.reshape(1, ROW), query, key, value, *after)


def attend_back_kernel(
    count, seg_column, seg_row, query, key, value, grad, log_total, *refs
):
    grads, sums, bias, key_sum, value_sum = refs[-5:]

    @pl.when(pl.program_id(0) == 0)
    def _():
        fill_bias(bias, seg_column, seg_row, count[0])

    query_t = (query[...] * jnp.asarray(SCALE, BF)).T
    key_t = key[...].T
    grad_t = grad[...].T
    query_one, grad_one = one_head(query_t), one_head(grad_t)
    key_sum[...] = jnp.zeros_like(key_sum)
    value_sum[...] = jnp.zeros_like(value_sum)
    for block in range(QUERY_BLOCKS):
        low, high = window(block)
        at = slice(block * QUERY_BLOCK, (block + 1) * QUERY_BLOCK)
        parts = []
        for h in range(2):
            rows = slice(h * HEAD, (h + 1) * HEAD)
            scores = dot(key[low:high, :], query_one[h][:, at], 1, 0) + bias[0 : high - low, at]
            probs = jnp.exp(scores - log_total[0, h : h + 1, at])
            grad_probs = dot(value[low:high, :], grad_one[h][:, at], 1, 0)
            weighted = probs * grad_probs
            total = jnp.sum(weighted, axis=0, keepdims=True)
            grad_scores = (weighted - probs * total).astype(BF)
            parts.append(dot(key_t[rows, low:high], grad_scores, 1, 0))
            key_sum[rows, low:high] += dot(query_t[rows, at], grad_scores, 1, 1)
            value_sum[rows, low:high] += dot(grad_t[rows, at], probs.astype(BF), 1, 1)
        grads[0, at, :] = (jnp.concatenate(parts, 0) * SCALE).T.astype(BF)
    grads[1] = key_sum[...].T.astype(BF)
    grads[2] = value_sum[...].T.astype(BF)
    sums[...] = jnp.zeros_like(sums)
    sums[0:1] = column_sum(grads[0].astype(F32))
    sums[1:2] = column_sum(grads[2].astype(F32))


def attend_back(query, key, value, grad, log_total, segments, count, first, pairs, after):
    pair = pl.BlockSpec((ROW, 2 * HEAD), lambda h: (0, h + first))
    return pl.pallas_call(
        attend_back_kernel,
        grid=(pairs,),
        in_specs=attend_specs()
        + [pair] * 4
        + [pl.BlockSpec((1, 8, ROW), lambda h: (h, 0, 0))]
        + [pl.BlockSpec(memory_space=pl.ANY)] * len(after),
        out_specs=[
            pl.BlockSpec((3, ROW, 2 * HEAD), lambda h: (0, 0, h)),
            pl.BlockSpec((8, 2 * HEAD), lambda h: (0, h)),
        ],
        out_shape=[
            jax.ShapeDtypeStruct((3, ROW, pairs * 2 * HEAD), BF),
            jax.ShapeDtypeStruct((8, pairs * 2 * HEAD), F32),
        ],
        scratch_shapes=[
            pltpu.VMEM((3 * QUERY_BLOCK, ROW), F32),
            pltpu.VMEM((2 * HEAD, ROW), F32),
            pltpu.VMEM((2 * HEAD, ROW), F32),
        ],
        compiler_params=pltpu.CompilerParams(vmem_limit_bytes=24 * MIB),
        cost_estimate=cost(33 * pairs / 6),
        name="attend_back",
    )(
        count,
        segments.reshape(ROW, 1),
        segments.reshape(1, ROW),
        query,
        key,
        value,
        grad,
        log_total,
        *after,
    )


def normalise(resid):
    centred = resid - jnp.mean(resid, axis=-1, keepdims=True)
    spread = jnp.mean(centred * centred, axis=-1, keepdims=True)
    inverse = lax.rsqrt(spread + NORM_EPSILON)
    return centred * inverse, inverse


def normalise_back(cotangent, gain, normal, inverse):
    scaled = cotangent * gain
    mean = jnp.mean(scaled, axis=-1, keepdims=True)
    aligned = jnp.mean(scaled * normal, axis=-1, keepdims=True)
    return inverse * (scaled - mean - normal * aligned)


def cost(micros):
    return pl.CostEstimate(flops=int(micros * 1.1e9), bytes_accessed=MIB, transcendentals=0)


def column_sum(array):
    return jnp.sum(array, axis=0, keepdims=True)


MIDDLE_ROWS = 256


def middle_kernel(
    fetch,
    groups,
    count,
    me,
    seg_row,
    tokens,
    out_grad,
    w_out,
    vec,
    *refs,
):
    mixed = jnp.concatenate([ref[...] for ref in refs[:ATTEND_CALLS]], 1)
    refs = refs[ATTEND_CALLS:]
    (
        final_low,
        hidden_low,
        activated,
        grad_pre,
        grad_ffn_out,
        grad_attn_out,
        grad_mixed,
        grad_resid,
        vec_grad,
        crop_sums,
        slope,
        weights,
        sem,
    ) = refs[groups:]
    step = pl.program_id(0)

    @pl.when(step == 0)
    def _():
        vec_grad[...] = jnp.zeros_like(vec_grad)
        crop_sums[...] = jnp.zeros_like(crop_sums)
        fetch(read_here(me), refs[:groups], weights, sem)

    def row(i):
        return vec[i : i + 1]

    def chunk(j):
        return weights[j * D : (j + 1) * D]

    def note(i, value):
        vec_grad[i : i + 1] += value

    resid_one = tokens[...].astype(F32) + (dot(mixed, w_out[...], 1, 0) + row(2))
    normal_one, inverse_one = normalise(resid_one)
    hidden = normal_one * row(3) + row(4)
    low = hidden.astype(BF)
    hidden_low[...] = low
    total = hidden + row(9)

    def arrived(first, chunks, which):
        @pl.when(step == 0)
        def _():
            part = weights.at[pl.ds(first * D, chunks * D)]
            pltpu.make_async_copy(part, part, sem.at[which]).wait()

    for j in range(UP_CHUNKS):
        at = slice(j * D, (j + 1) * D)
        arrived(j, 1, j)
        pre = dot(low, chunk(j), 1, 0) + row(5 + j)
        share = 0.5 + 0.5 * lax.erf(pre * (0.5**0.5))
        density = jnp.exp(-0.5 * pre * pre) * 0.3989422804014327
        slope[:, at] = share + pre * density
        act = (pre * share).astype(BF)
        activated[:, at] = act
        if j == 0:
            arrived(UP_CHUNKS, UP_CHUNKS, UP_CHUNKS)
        total = total + dot(act, chunk(UP_CHUNKS + j), 1, 0)
    normal_two, inverse_two = normalise(total)
    final = normal_two * row(10) + row(11)
    final_low[...] = final.astype(BF)

    first = step * MIDDLE_ROWS
    across = (CROPS, MIDDLE_ROWS)
    position = first + lax.broadcasted_iota(jnp.int32, across, 1)
    crop = lax.broadcasted_iota(jnp.int32, across, 0)
    member = ((seg_row[...] == crop) & (position < count[0])).astype(BF)
    high = final.astype(BF)
    rest = final - high.astype(F32)
    mid = rest.astype(BF)
    tiny = (rest - mid.astype(F32)).astype(BF)
    crop_sums[...] += dot(member, high, 1, 0) + (dot(member, mid, 1, 0) + dot(member, tiny, 1, 0))

    position = first + lax.broadcasted_iota(jnp.int32, (MIDDLE_ROWS, 1), 0)
    valid = (position < count[0]).astype(F32)
    cotangent = out_grad[...].astype(F32) * valid
    note(10, column_sum(cotangent * normal_two))
    note(11, column_sum(cotangent))
    grad_two = normalise_back(cotangent, row(10), normal_two, inverse_two)
    grad_out = grad_two.astype(BF)
    grad_ffn_out[...] = grad_out
    note(9, column_sum(grad_out.astype(F32)))
    grad_hidden = grad_two
    for j in range(UP_CHUNKS):
        at = slice(j * D, (j + 1) * D)
        back = (dot(grad_out, chunk(UP_CHUNKS + j), 1, 1) * slope[:, at]).astype(BF)
        grad_pre[:, at] = back
        note(5 + j, column_sum(back.astype(F32)))
        grad_hidden = grad_hidden + dot(back, chunk(j), 1, 1)
    note(3, column_sum(grad_hidden * normal_one))
    note(4, column_sum(grad_hidden))
    grad_one = normalise_back(grad_hidden, row(3), normal_one, inverse_one)
    grad_resid[...] = grad_one
    grad_proj = grad_one.astype(BF)
    grad_attn_out[...] = grad_proj
    note(2, column_sum(grad_proj.astype(F32)))
    grad_mixed[...] = dot(grad_proj, w_out[...], 1, 1).astype(BF)


def middle(count, me, segments, mixed, tokens, out_grad, attn_whole, sources, fetch, vec):
    rows = tokens.shape[0]
    tile = pl.BlockSpec((MIDDLE_ROWS, D), lambda i: (i, 0))
    wide = pl.BlockSpec((MIDDLE_ROWS, FF), lambda i: (i, 0))
    small = pl.BlockSpec((VEC_ROWS, D), lambda i: (0, 0))

    def shape(width, kind):
        return jax.ShapeDtypeStruct((rows, width), kind)

    return pl.pallas_call(
        functools.partial(middle_kernel, fetch, len(sources)),
        grid=(rows // MIDDLE_ROWS,),
        in_specs=[
            pl.BlockSpec(memory_space=pltpu.SMEM),
            pl.BlockSpec(memory_space=pltpu.SMEM),
            pl.BlockSpec((1, MIDDLE_ROWS), lambda i: (0, i)),
            tile,
            tile,
            pl.BlockSpec((D, D), lambda i: (3, 0), pipeline_mode=pl.Buffered(1)),
            small,
        ]
        + [pl.BlockSpec((MIDDLE_ROWS, D // ATTEND_CALLS), lambda i: (i, 0))] * ATTEND_CALLS
        + [pl.BlockSpec(memory_space=pl.ANY)] * len(sources),
        out_specs=[tile, tile, wide, wide, tile, tile, tile, tile, small, small],
        out_shape=[
            shape(D, BF),
            shape(D, BF),
            shape(FF, BF),
            shape(FF, BF),
            shape(D, BF),
            shape(D, BF),
            shape(D, BF),
            shape(D, F32),
            jax.ShapeDtypeStruct((VEC_ROWS, D), F32),
            jax.ShapeDtypeStruct((CROPS, D), F32),
        ],
        scratch_shapes=[
            pltpu.VMEM((MIDDLE_ROWS, FF), F32),
            pltpu.VMEM((FFN_ROWS, D), BF),
            pltpu.SemaphoreType.DMA((UP_CHUNKS + 1,)),
        ],
        compiler_params=pltpu.CompilerParams(vmem_limit_bytes=44 * MIB),
        cost_estimate=cost(40),
        name="middle",
    )(count, me, segments.reshape(1, rows), tokens, out_grad, attn_whole, vec, *mixed, *sources)


WIDTH = 2 * HEAD * (HEADS // 2 // 3)


def ffn_terms_kernel(shares, me, hidden, activated, *refs):
    pre, out = refs[:shares], refs[shares : 2 * shares]
    keep, give, hidden_t, block, sem = refs[-5:]
    step = pl.program_id(0)
    slot = lax.rem(step, 2)
    owners, rows = keep.shape[1], keep.shape[2]
    up_rows = rows // UP_CHUNKS
    per_chunk = D // rows

    @pl.when(step == 0)
    def _():
        hidden_t[...] = hidden[...].T

    @pl.when(step >= 2)
    def _():
        pltpu.make_async_copy(block.at[slot], block.at[slot], sem.at[slot]).wait()

    def to(core, y, start):
        @pl.when(core == me[1])
        def _():
            start(keep.at[y])

        @pl.when(core != me[1])
        def _():
            start(give.at[y])

    @pl.when(step < UP_CHUNKS)
    def _():
        right = jnp.concatenate([ref[...] for ref in pre], 1)
        block[slot] = dot(hidden_t[...], right, 1, 0).astype(BF)
        for core in range(2):
            source = block.at[slot, pl.ds(core * (D // 2), D // 2)]
            source = source.reshape(owners, up_rows, block.shape[2])

            def start(target):
                at = pl.ds(pl.multiple_of(step * up_rows, 16), up_rows)
                pltpu.make_async_copy(source, target.at[:, at], sem.at[slot]).start()

            to(core, 0, start)

    @pl.when(step >= UP_CHUNKS)
    def _():
        right = jnp.concatenate([ref[...] for ref in out], 1)
        block[slot] = dot(activated[...], right, 0, 0).astype(BF)
        chunk = step - UP_CHUNKS
        source = block.at[slot].reshape(per_chunk, rows, block.shape[2])

        def start(target):
            at = pl.ds(lax.rem(chunk, 2) * per_chunk, per_chunk)
            pltpu.make_async_copy(source, target.at[at], sem.at[slot]).start()

        to(lax.div(chunk, 2), 1, start)

    @pl.when(step == pl.num_programs(0) - 1)
    def _():
        for s in range(2):
            pltpu.make_async_copy(block.at[s], block.at[s], sem.at[s]).wait()


def ffn_terms(places, me, hidden, activated, grad_pre, grad_out, thirds, after):
    owners = places.wide
    rows = FFN_ROWS // places.count
    shares = len(thirds)
    width = shares * WIDTH
    shape = jax.ShapeDtypeStruct((2, owners, rows, width), BF)

    def pre_spec(third):
        return pl.BlockSpec((ROW, WIDTH), lambda i: (0, 3 * jnp.minimum(i, UP_CHUNKS - 1) + third))

    def out_spec(third):
        return pl.BlockSpec((ROW, WIDTH), lambda i: (0, third))

    def kernel(me_ref, hidden_ref, activated_ref, *refs):
        used = refs[: 2 * shares] + refs[2 * shares + len(after) :]
        ffn_terms_kernel(shares, me_ref, hidden_ref, activated_ref, *used)

    return pl.pallas_call(
        kernel,
        grid=(2 * UP_CHUNKS,),
        in_specs=[
            pl.BlockSpec(memory_space=pltpu.SMEM),
            pl.BlockSpec((ROW, D), lambda i: (0, 0), pipeline_mode=pl.Buffered(1)),
            pl.BlockSpec((ROW, D), lambda i: (0, jnp.maximum(i - UP_CHUNKS, 0))),
        ]
        + [pre_spec(t) for t in thirds]
        + [out_spec(t) for t in thirds]
        + [pl.BlockSpec(memory_space=pl.ANY)] * len(after),
        out_specs=[pl.BlockSpec(memory_space=pl.ANY)] * 2,
        out_shape=[shape] * 2,
        scratch_shapes=[
            pltpu.VMEM((D, ROW), BF),
            pltpu.VMEM((2, D, width), BF),
            pltpu.SemaphoreType.DMA((2,)),
        ],
        compiler_params=pltpu.CompilerParams(vmem_limit_bytes=32 * MIB),
        cost_estimate=cost(5 * shares),
        name="ffn_terms",
    )(me, hidden, activated, *([grad_pre] * shares), *([grad_out] * shares), *after)


def attn_terms(places, me, tokens, mixed, grads, grad_proj, thirds, vectors, after):
    owners = places.wide
    rows = ATTN_ROWS // places.count
    shares, extra = len(thirds), vectors.shape[0]
    width = shares * WIDTH
    shape = jax.ShapeDtypeStruct((2, owners, rows + extra, width), BF)

    def kernel(me_ref, tokens_ref, vectors_ref, *refs):
        mixed_refs, refs = refs[:ATTEND_CALLS], refs[ATTEND_CALLS:]
        grad_refs, proj_refs, refs = refs[:shares], refs[shares : 2 * shares], refs[2 * shares :]
        keep, give, tokens_t, block, below, sem, below_sem = refs[len(after) :]
        step = pl.program_id(0)
        slot = lax.rem(step, 2)

        @pl.when(step == 0)
        def _():
            tokens_t[...] = tokens_ref[...].T
            below[...] = jnp.broadcast_to(vectors_ref[...][None], below.shape)
            for target in (keep, give):
                for y in range(2):
                    pltpu.make_async_copy(
                        below, target.at[y, :, pl.ds(rows, extra)], below_sem
                    ).start()

        @pl.when(step >= 2)
        def _():
            pltpu.make_async_copy(block.at[slot], block.at[slot], sem.at[slot]).wait()

        @pl.when(step < 3)
        def _():
            right = jnp.concatenate([ref[0] for ref in grad_refs], 1)
            block[slot] = dot(tokens_t[...], right, 1, 0).astype(BF)

        @pl.when(step == 3)
        def _():
            left = jnp.concatenate([ref[...] for ref in mixed_refs], 1)
            right = jnp.concatenate([ref[...] for ref in proj_refs], 1)
            block[slot] = dot(left, right, 0, 0).astype(BF)

        source = block.at[slot].reshape(owners, rows, width)
        y, core = lax.div(step, 2), lax.rem(step, 2)

        @pl.when(core == me_ref[1])
        def _():
            pltpu.make_async_copy(source, keep.at[y, :, pl.ds(0, rows)], sem.at[slot]).start()

        @pl.when(core != me_ref[1])
        def _():
            pltpu.make_async_copy(source, give.at[y, :, pl.ds(0, rows)], sem.at[slot]).start()

        @pl.when(step == 3)
        def _():
            for s in range(2):
                pltpu.make_async_copy(block.at[s], block.at[s], sem.at[s]).wait()
            for _ in range(4):
                pltpu.make_async_copy(below, below, below_sem).wait()

    def third_spec(third):
        return pl.BlockSpec((ROW, WIDTH), lambda i: (0, third))

    return pl.pallas_call(
        kernel,
        grid=(4,),
        in_specs=[
            pl.BlockSpec(memory_space=pltpu.SMEM),
            pl.BlockSpec((ROW, D), lambda i: (0, 0), pipeline_mode=pl.Buffered(1)),
            pl.BlockSpec((extra, width), lambda i: (0, 0)),
        ]
        + [pl.BlockSpec((ROW, WIDTH), lambda i: (0, 0), pipeline_mode=pl.Buffered(1))] * ATTEND_CALLS
        + [pl.BlockSpec((1, ROW, WIDTH), lambda i: (jnp.minimum(i, 2), 0, 0))] * shares
        + [third_spec(t) for t in thirds]
        + [pl.BlockSpec(memory_space=pl.ANY)] * len(after),
        out_specs=[pl.BlockSpec(memory_space=pl.ANY)] * 2,
        out_shape=[shape] * 2,
        scratch_shapes=[
            pltpu.VMEM((D, ROW), BF),
            pltpu.VMEM((2, D, width), BF),
            pltpu.VMEM((owners, extra, width), BF),
            pltpu.SemaphoreType.DMA((2,)),
            pltpu.SemaphoreType.DMA,
        ],
        compiler_params=pltpu.CompilerParams(vmem_limit_bytes=24 * MIB),
        cost_estimate=cost(1.5 * shares + 1),
        name="attn_terms",
    )(me, tokens, vectors, *mixed, *grads, *([grad_proj] * shares), *after)


def token_grad_kernel(resid, weights, *refs):
    out = refs[-1]
    total = resid[...]
    for i, ref in enumerate(refs[:ATTEND_CALLS]):
        for m in range(3):
            held = weights[m * D : (m + 1) * D, i * WIDTH : (i + 1) * WIDTH]
            total = total + dot(ref[m], held, 1, 1)
    out[...] = total.astype(BF)


def token_gradient(resid, weights, grads, after):
    step = 256
    tile = pl.BlockSpec((step, D), lambda i: (i, 0))
    return pl.pallas_call(
        token_grad_kernel,
        grid=(ROW // step,),
        in_specs=[tile, pl.BlockSpec((3 * D, D), lambda i: (0, 0), pipeline_mode=pl.Buffered(1))]
        + [pl.BlockSpec((3, step, WIDTH), lambda i: (0, i, 0))] * ATTEND_CALLS
        + [pl.BlockSpec(memory_space=pl.ANY)] * len(after),
        out_specs=tile,
        out_shape=jax.ShapeDtypeStruct((ROW, D), BF),
        compiler_params=pltpu.CompilerParams(vmem_limit_bytes=24 * MIB),
        cost_estimate=cost(5),
        name="token_grad",
    )(resid, weights, *grads, *after)


def adam_update(param, gradient, moment, square, shadow):
    step_float = float(STEP)
    moment_next = MOMENT_DECAY * moment + (1.0 - MOMENT_DECAY) * gradient
    square_next = SQUARE_DECAY * square + (1.0 - SQUARE_DECAY) * gradient * gradient
    moment_hat = moment_next / (1.0 - MOMENT_DECAY**step_float)
    square_hat = square_next / (1.0 - SQUARE_DECAY**step_float)
    change = -LEARN_RATE * (
        moment_hat / (jnp.sqrt(square_hat) + ADAM_EPSILON) + WEIGHT_DECAY * param
    )
    updated = param + change
    drift = (1.0 - SHADOW_RATE) * (updated - shadow)
    return (change, moment_next, square_next, drift)


def contract_rows(left, right):
    return dot(left, right, 0, 0)


def on_device(
    places,
    tokens,
    segments,
    counts,
    out_grad,
    attn_param,
    attn_moment,
    attn_square,
    attn_shadow,
    ffn_param,
    ffn_moment,
    ffn_square,
    ffn_shadow,
):
    assert counts.shape[0] == 1 and tokens.shape[0] == ROW
    number = places.count
    here = places.here()
    place_list = jnp.stack([here[a] for a in ("y", "c", "z", "x")]).astype(jnp.int32)
    me = lax.axis_index("dp") * places.wide + lax.axis_index("wide")
    staged = places.staged()
    attn_rows, ffn_rows = ATTN_ROWS // number, FFN_ROWS // number
    up_rows = ffn_rows // UP_CHUNKS
    holds_up = me < number // 2

    last = me == number - 1
    ends = jnp.concatenate([attn_param[-ATTN_TAIL:], ffn_param[-FFN_TAIL:]]).astype(BF)
    ends = jnp.where(last, ends, jnp.zeros_like(ends))
    if staged:
        digits = [lax.rem(lax.shift_right_logical(counts[0], 3 * i), 8) for i in range(4)]
        count_row = jnp.concatenate([jnp.stack(digits).astype(BF), jnp.zeros((D - 4,), BF)])
        filler = jnp.zeros(((VEC_ROWS - COUNT_ROW - 1) * D,), BF)
        extra = jnp.concatenate([ends, count_row, filler]).reshape(VEC_ROWS, D)
        attn_own = to_rows(places, me, attn_param, ATTN_ROWS, ATTN_TAIL).astype(BF)
        attn_set = Gathered(places, attn_rows)
        column = attn_set.along_z(here, jnp.concatenate([attn_own, extra], 0))
        ffn_own = to_rows(places, me, order(ffn_param, column), FFN_ROWS, FFN_TAIL).astype(BF)
        by_chunk = ffn_own.reshape(up_rows, UP_CHUNKS, D).transpose(1, 0, 2).reshape(ffn_rows, D)
        ffn_own = jnp.where(holds_up, by_chunk, ffn_own)
        plane = attn_set.along_first(column)
        groups = [plane] + attn_set.along_second(plane)
        attn_groups = groups + attn_set.from_core(groups)
        set_rows = ffn_rows // FFN_SETS
        per_set = UP_CHUNKS // FFN_SETS
        ffn_set = Gathered(places, set_rows)
        columns = [
            ffn_set.along_z(here, ffn_own[i * set_rows : (i + 1) * set_rows])
            for i in range(FFN_SETS)
        ]
        query, key, value, vec, attn_whole = project(
            tokens, place_list, attn_set, attn_groups, columns
        )
        token_total = sum(vec[COUNT_ROW, i] * float(8**i) for i in range(4))
        planes = [order(ffn_set.along_first(c), query) for c in columns]
        groups = [[p] + [order(g, query) for g in ffn_set.from_core([p])] for p in planes]
        far = [ffn_set.along_second(p) for p in planes]
        attend_after = [[planes[0]], [planes[1]], []]
        extent = places.size
        piece = (extent["x"], extent["z"], per_set, up_rows, D)
        half = extent["y"] // 2

        def fetch(place, refs, weights, sem):
            side = (half, 2, extent["z"], extent["x"])
            up = weights.at[pl.ds(0, FF)].reshape(*((UP_CHUNKS,) + side + (up_rows, D)))
            down = weights.at[pl.ds(FF, FF)].reshape(*(side + (UP_CHUNKS, up_rows, D)))
            number = 2 * extent["x"]
            for s in range(FFN_SETS):
                own = refs[s * number : (s + 1) * number]
                chunks = pl.ds(s * per_set, per_set)
                for g, first, y, core, x in ffn_set.columns(place):

                    @pl.when(y < half)
                    def _():
                        for part in range(per_set):
                            chunk = s * per_set + part
                            pltpu.make_async_copy(
                                own[g].at[first, :, part],
                                up.at[chunk, y, core, :, x],
                                sem.at[chunk],
                            ).start()

                    @pl.when(y >= half)
                    def _():
                        pltpu.make_async_copy(
                            own[g].at[first],
                            down.at[y - half, core, :, x, chunks],
                            sem.at[UP_CHUNKS],
                        ).start()

    else:
        token_total = lax.psum(counts[0].astype(F32), AXES)
        vec = lax.psum(ends.astype(F32), AXES).reshape(COUNT_ROW, D)
        vec = jnp.concatenate([vec, jnp.zeros((VEC_ROWS - COUNT_ROW, D), F32)], 0)
        flat = lax.all_gather(attn_param.astype(BF), AXES, axis=0, tiled=True)
        attn_whole = flat[: ATTN_ROWS * D].reshape(ATTN_ROWS, D)
        flat = lax.all_gather(ffn_param.astype(BF), AXES, axis=0, tiled=True)
        w_up = flat[: FF * D].reshape(D, UP_CHUNKS, D).transpose(1, 0, 2).reshape(FF, D)
        w_down = flat[FF * D : FFN_ROWS * D].reshape(FF, D)
        sources = [w_up, w_down]

        def fetch(place, refs, weights, sem):
            w_up, w_down = refs
            for j in range(UP_CHUNKS):
                rows = pl.ds(j * D, D)
                pltpu.make_async_copy(w_up.at[rows], weights.at[rows], sem.at[j]).start()
            down = weights.at[pl.ds(FF, FF)]
            pltpu.make_async_copy(w_down, down, sem.at[UP_CHUNKS]).start()

        query, key, value = project_whole(tokens, attn_whole, vec)
        attend_after = [[]] * ATTEND_CALLS

    pairs = HEADS // 2 // ATTEND_CALLS
    ahead = [
        attend(query, key, value, segments, counts, i * pairs, pairs, attend_after[i])
        for i in range(ATTEND_CALLS)
    ]
    mixed = [a[0] for a in ahead]
    if staged:
        sources = []
        for s in range(FFN_SETS):
            near, crossed = groups[s]
            others = [order(f, mixed[s + 1]) for f in far[s]]
            arrays = [near] + others + [crossed] + ffn_set.from_core(others)
            sources += [g.reshape(piece) for g in arrays]
    (
        final_low,
        hidden_low,
        activated,
        grad_pre,
        grad_ffn_out,
        grad_attn_out,
        grad_mixed,
        grad_resid,
        vec_grad,
        crop_sums,
    ) = middle(
        counts,
        place_list,
        segments,
        mixed,
        tokens,
        out_grad,
        attn_whole,
        sources,
        fetch,
        vec,
    )
    is_valid = jnp.arange(ROW, dtype=jnp.int32) < counts[0]
    member = (segments[None, :] == jnp.arange(CROPS, dtype=jnp.int32)[:, None]) & is_valid[None, :]
    crop_sizes = jnp.sum(member.astype(F32), axis=1)
    pooled = crop_sums / jnp.maximum(crop_sizes, 1.0)[:, None]

    def back(i, after):
        return attend_back(
            query,
            key,
            value,
            grad_mixed,
            ahead[i][1],
            segments,
            counts,
            i * pairs,
            pairs,
            after,
        )

    if staged:
        sums = Scattered(places, here)

        def spread(terms):
            return terms.reshape(2, extent["z"], extent["x"], *terms.shape[2:])

        def ffn_side(thirds, after):
            operands = (hidden_low, activated, grad_pre, grad_ffn_out)
            terms = ffn_terms(places, place_list, *operands, thirds, after)
            return [spread(t) for t in terms]

        def attn_side(thirds, grads, vectors, after):
            width = len(thirds) * WIDTH
            vectors = vectors.astype(BF).reshape(-1)
            filled = -(-vectors.shape[0] // (16 * width)) * 16
            vectors = jnp.pad(vectors, (0, filled * width - vectors.shape[0]))
            vectors = vectors.reshape(filled, width)
            operands = (tokens, mixed, grads, grad_attn_out)
            terms = attn_terms(places, place_list, *operands, thirds, vectors, after)
            return [spread(t) for t in terms]

        def later(arrays, *before):
            return [order(a, *before) for a in arrays]

        keep_a, give_a = ffn_side([0, 1], [])
        core_a = sums.core(give_a)
        keep_b, give_b = ffn_side([2], [give_a])
        core_b = sums.core(give_b)
        held_a = sums.held(keep_a, later(core_a, give_b))
        first_a = sums.first(held_a)
        held_b = sums.held(keep_b, later(core_b, held_a))
        first_b = sums.first(held_b)
        back_0 = back(0, [held_a, held_b])
        line_a = sums.line(held_a, later(first_a, back_0[0]))
        line_b = sums.line(held_b, later(first_b, back_0[0]))
        second_a, second_b = sums.second(line_a), sums.second(line_b)
        back_1 = back(1, [line_a, line_b])
        column_a = sums.column(line_a, later(second_a, back_1[0]))
        column_b = sums.column(line_b, later(second_b, back_1[0]))
        up_z_a, up_z_b = sums.along_z(column_a), sums.along_z(column_b)
        grads = [back_0[0], back_1[0]]
        keep_c, give_c = attn_side([0, 1], grads, vec_grad[2:12], [column_a, column_b])
        core_c = sums.core(give_c)
        back_2 = back(2, [give_c])
        held_c = sums.held(keep_c, later(core_c, back_2[0]))
        first_c = sums.first(held_c)
        vectors = jnp.stack(
            [jnp.concatenate([b[1][i] for b in (back_0, back_1, back_2)]) for i in range(2)]
        )
        grads = [b[0] for b in (back_0, back_1, back_2)]
        keep_d, give_d = attn_side([2], grads[2:], vectors, [held_c])
        core_d = sums.core(give_d)
        token_grad = token_gradient(grad_resid, attn_whole, grads, [give_d])
        held_d = sums.held(keep_d, core_d)
        first_d = sums.first(held_d)
        line_c = sums.line(held_c, later(first_c, give_d))
        second_c = sums.second(line_c)
        line_d = sums.line(held_d, first_d)
        second_d = sums.second(line_d)
        column_c = sums.column(line_c, second_c)
        up_z_c = sums.along_z(column_c)
        column_d = sums.column(line_d, second_d)
        up_z_d = sums.along_z(column_d)
        ffn_block = jnp.concatenate(
            [
                sums.result(column_a, later(up_z_a, give_d)),
                sums.result(column_b, later(up_z_b, give_d)),
            ],
            1,
        )
        block_c, block_d = sums.result(column_c, up_z_c), sums.result(column_d, up_z_d)
        attn_block = jnp.concatenate([block_c[:attn_rows], block_d[:attn_rows]], 1)
        early_vec = block_c[attn_rows:].reshape(-1)[: 10 * D].reshape(10, D)
        late_vec = block_d[attn_rows:].reshape(-1)[: 2 * D].reshape(2, D)
        by_row = ffn_block.reshape(UP_CHUNKS, up_rows, D).transpose(1, 0, 2).reshape(ffn_rows, D)
        ffn_block = jnp.where(holds_up, by_row, ffn_block)
        ffn_summed = to_flat(places, me, ffn_block, early_vec[3:], FFN_TAIL)
        attn_tail = jnp.concatenate([late_vec, early_vec[:3]], 0)
        attn_summed = to_flat(places, me, attn_block, attn_tail, ATTN_TAIL)
    else:
        backs = [back(i, []) for i in range(ATTEND_CALLS)]
        grads = [b[0] for b in backs]
        token_grad = token_gradient(grad_resid, attn_whole, grads, [])
        grads = jnp.concatenate(grads, 2)
        mats = [contract_rows(tokens, grads[i]) for i in range(3)]
        mats.append(contract_rows(jnp.concatenate(mixed, 1), grad_attn_out))
        vectors = jnp.concatenate([b[1] for b in backs], 1)[:2]
        vec_grad = jnp.concatenate([vectors, vec_grad[2:]], 0)
        attn_full = jnp.concatenate([g.reshape(-1) for g in mats + [vec_grad[:5]]])
        up = contract_rows(hidden_low, grad_pre)
        down = contract_rows(activated, grad_ffn_out)
        ffn_full = jnp.concatenate([g.reshape(-1) for g in (up, down, vec_grad[5:12])])
        attn_summed = lax.psum_scatter(attn_full, AXES, scatter_dimension=0, tiled=True)
        ffn_summed = lax.psum_scatter(ffn_full, AXES, scatter_dimension=0, tiled=True)
    attn_grad = attn_summed / token_total
    ffn_grad = ffn_summed / token_total
    attn_change, moment_attn, square_attn, drift_attn = adam_update(
        attn_param, attn_grad, attn_moment, attn_square, attn_shadow
    )
    ffn_change, moment_ffn, square_ffn, drift_ffn = adam_update(
        ffn_param, ffn_grad, ffn_moment, ffn_square, ffn_shadow
    )
    return (
        final_low,
        pooled,
        token_grad,
        attn_grad,
        ffn_grad,
        attn_change,
        ffn_change,
        moment_attn,
        moment_ffn,
        square_attn,
        square_ffn,
        drift_attn,
        drift_ffn,
    )


def solution(mesh):
    rows, flat = P(AXES, None), P(AXES)
    return jax.shard_map(
        functools.partial(on_device, Places(mesh)),
        mesh=mesh,
        in_specs=(rows, flat, flat, rows) + (flat,) * 8,
        out_specs=(rows, rows, rows) + (flat,) * 10,
        check_vma=False,
    )
```

```python
import functools

import jax
import jax.numpy as jnp
from jax import lax
from jax.experimental import pallas as pl
from jax.experimental.pallas import tpu as pltpu
from jax.sharding import PartitionSpec as P

D = 768
FF = 3072
HEAD = 64
HEADS = 12
ROW = 1024
STEP = 10
CROPS = 16

NORM_EPSILON = 1e-12
NEGATIVE = -1e30
MOMENT_DECAY = 0.9
SQUARE_DECAY = 0.999
LEARN_RATE = 0.001
WEIGHT_DECAY = 0.01
ADAM_EPSILON = 1e-08
SHADOW_RATE = 0.9995
SCALE = HEAD ** (-0.5)

AXES = ("dp", "wide")
BF = jnp.bfloat16
F32 = jnp.float32
UP_CHUNKS = FF // D
ATTN_ROWS = 4 * D
FFN_ROWS = 2 * FF
ATTN_TAIL = 5 * D
FFN_TAIL = FF + 3 * D
BACK_CALLS = 3
VEC_ROWS = 16
COUNT_ROW = 12
MIB = 1 << 20
BACK_VMEM = 24 * MIB


def dot(left, right, left_dim, right_dim):
    return lax.dot_general(
        left, right, (((left_dim,), (right_dim,)), ((), ())), preferred_element_type=F32
    )


class Places:
    def __init__(self, mesh):
        self.dp, self.wide = mesh.shape["dp"], mesh.shape["wide"]
        self.count = self.dp * self.wide
        self.size = {"c": 2, "y": self.dp // 2}
        self.size["x"] = self.size["y"]
        self.size["z"] = self.wide // self.size["x"]

    def staged(self):
        exact = self.dp == 4 and self.wide % self.size["x"] == 0
        return exact and D % (16 * UP_CHUNKS * self.wide // 2) == 0

    def index(self, y, c, z, x):
        return (y * 2 + c) * self.wide + z * self.size["x"] + x

    def rotation(self, axis, step):
        pairs = []
        extent = self.size
        for y in range(extent["y"]):
            for c in range(2):
                along = axis if len(axis) == 1 else axis[c]
                for z in range(extent["z"]):
                    for x in range(extent["x"]):
                        at = {"y": y, "c": c, "z": z, "x": x}
                        to = dict(at)
                        to[along] = (at[along] + step) % extent[along]
                        pairs.append((self.index(**at), self.index(**to)))
        return pairs

    def send(self, array, axis, step):
        return lax.ppermute(array, AXES, self.rotation(axis, step))

    def here(self):
        outer, inner = lax.axis_index("dp"), lax.axis_index("wide")
        extent = self.size["x"]
        return {"y": outer // 2, "c": outer % 2, "z": inner // extent, "x": inner % extent}


def order(array, *before):
    return lax.optimization_barrier((array,) + before)[0]


class Gathered:
    def __init__(self, places, rows):
        self.places, self.rows = places, rows
        self.deep = places.size["z"] * rows

    def start_z(self, own):
        extent = self.places.size["z"]
        return [own] + [self.places.send(own, "z", k) for k in range(1, extent)]

    def join_z(self, here, blocks):
        rows, extent = self.rows, self.places.size["z"]
        near = jnp.zeros((self.deep, D), BF)
        for k, block in enumerate(blocks):
            at = lax.rem(here["z"] + (extent - k), extent) * rows
            near = lax.dynamic_update_slice_in_dim(near, block[:rows], at, 0)
        return jnp.concatenate([near, self.total([b[rows:] for b in blocks])], 0)

    def join_parts(self, me, parts):
        extent, count = self.places.size["z"], len(parts)
        share = self.rows // count

        def kernel(me_ref, *refs):
            out, sem = refs[-2:]
            for p in range(count):
                for k in range(extent):
                    at = lax.rem(me_ref[2] + (extent - k), extent)
                    pltpu.make_async_copy(
                        refs[p * extent + k], out.at[at, pl.ds(p * share, share)], sem
                    ).start()
            pltpu.make_async_copy(out, out, sem).wait()

        blocks = [b for part in parts for b in part]
        return pl.pallas_call(
            kernel,
            in_specs=[pl.BlockSpec(memory_space=pltpu.SMEM)]
            + [pl.BlockSpec(memory_space=pltpu.VMEM)] * len(blocks),
            out_specs=pl.BlockSpec(memory_space=pltpu.VMEM),
            out_shape=jax.ShapeDtypeStruct((extent, self.rows, D), BF),
            scratch_shapes=[pltpu.SemaphoreType.DMA],
            compiler_params=pltpu.CompilerParams(vmem_limit_bytes=16 * MIB),
            cost_estimate=cost(2),
            name="join",
        )(me, *blocks).reshape(self.deep, D)

    def along_first(self, near):
        places, extent = self.places, self.places.size
        blocks = [near] + [places.send(near, "xy", k) for k in range(1, extent["x"])]
        parts = [b[: self.deep] for b in blocks]
        if near.shape[0] > self.deep:
            parts.append(self.total([b[self.deep :] for b in blocks]))
        return jnp.concatenate(parts, 0)

    def along_second(self, near):
        return [self.places.send(near, "yx", k) for k in range(1, self.places.size["x"])]

    def from_core(self, groups):
        return [self.places.send(g, "c", 1) for g in groups]

    def total(self, arrays):
        result = arrays[0].astype(F32)
        for a in arrays[1:]:
            result = result + a.astype(F32)
        return result.astype(BF)

    def place(self, here, far, first, second):
        extent = self.places.size

        def back(axis, step):
            return lax.rem(here[axis] + (extent[axis] - step), extent[axis])

        core = here["c"] if far == 0 else 1 - here["c"]
        y = jnp.where(core == 0, back("y", second), back("y", first))
        x = jnp.where(core == 0, back("x", first), back("x", second))
        return y, core, x


def read_here(me_ref):
    return {"y": me_ref[0], "c": me_ref[1], "z": me_ref[2], "x": me_ref[3]}


def add_routed(me, keep, arrived, grid, routes, micros):
    rows, width = keep.shape[-2:]
    lead = len(keep.shape) - 2

    def kernel(me_ref, *refs):
        for i in range(len(routes)):
            total = refs[2 * i][...].astype(F32) + refs[2 * i + 1][...].astype(F32)
            refs[2 * len(routes) + i][...] = total.astype(BF)

    def source(route):
        return pl.BlockSpec((None,) * lead + (rows, width), lambda *at: route(*at) + (0, 0))

    target = pl.BlockSpec(
        (None,) * len(grid) + (rows, width), lambda *at: at[: len(grid)] + (0, 0)
    )
    return pl.pallas_call(
        kernel,
        grid_spec=pltpu.PrefetchScalarGridSpec(
            num_scalar_prefetch=1,
            grid=grid,
            in_specs=[source(r) for r in routes for _ in range(2)],
            out_specs=[target] * len(routes),
        ),
        out_shape=[jax.ShapeDtypeStruct(grid + (rows, width), BF)] * len(routes),
        compiler_params=pltpu.CompilerParams(vmem_limit_bytes=24 * MIB),
        cost_estimate=cost(micros),
        name="add_routed",
    )(me, *([keep, arrived] * len(routes)))


class Scattered:
    def __init__(self, places, me, micros):
        self.places, self.me, self.micros = places, me, micros
        self.z = places.size["z"]

    def core(self, give):
        return self.places.send(give, "c", 1)

    def first(self, keep, arrived):
        def route(far):
            def pick_block(z, e, me):
                y, x = jnp.abs(me[0] - far), jnp.abs(me[3] - far)
                return jnp.where(me[1] == 0, e, y), z, jnp.where(me[1] == 0, x, e)

            return pick_block

        routes = [route(0), route(1)]
        own, cut = add_routed(self.me, keep, arrived, (self.z, 2), routes, 4 * self.micros)
        return own, cut, self.places.send(cut, "xy", 1)

    def second(self, keep, arrived):
        def route(far):
            return lambda z, me: (z, jnp.abs(jnp.where(me[1] == 0, me[0], me[3]) - far))

        routes = [route(0), route(1)]
        own, cut = add_routed(self.me, keep, arrived, (self.z,), routes, 2 * self.micros)
        return own, cut, self.places.send(cut, "yx", 1)

    def along_z(self, keep, arrived):
        def route(k):
            return lambda i, me: (lax.rem(me[2] + k, self.z),)

        routes = [route(k) for k in range(self.z)]
        own, *cuts = add_routed(self.me, keep, arrived, (1,), routes, self.micros)
        return own, cuts, [self.places.send(c, "z", k + 1) for k, c in enumerate(cuts)]

    def result(self, own, arrived):
        total = own[0].astype(F32)
        for a in arrived:
            total = total + a[0].astype(F32)
        return total


def to_rows(places, me, flat, rows, tail):
    count = places.count
    block = rows // count * D
    slack = tail // count
    before = lax.ppermute(flat[-tail:], AXES, [(i, i + 1) for i in range(count - 1)])
    joined = jnp.concatenate([before, flat])
    return lax.dynamic_slice_in_dim(joined, tail - me * slack, block).reshape(rows // count, D)


def to_flat(places, me, block, vectors, tail):
    count = places.count
    slack = tail // count
    after = lax.ppermute(block[: tail // D], AXES, [(i + 1, i) for i in range(count - 1)])
    after = jnp.where(me == count - 1, vectors, after)
    joined = jnp.concatenate([block, after], 0).reshape(-1)
    return lax.dynamic_slice_in_dim(joined, me * slack, block.size + slack)


def project_body(step, tokens, weights, vec, query, key, value):
    held = tokens[...]
    query[...] = (dot(held, weights[0:D], 1, 0) + vec[0:1]).astype(BF)
    key[...] = dot(held, weights[D : 2 * D], 1, 0).astype(BF)
    value[...] = (dot(held, weights[2 * D : 3 * D], 1, 0) + vec[1:2]).astype(BF)


def project_kernel(gathered, number, after, me, tokens, *refs):
    groups = refs[:number]
    query, key, value, vec, whole, weights, extras, sem, extra_sem, out_sem = refs[number + after :]
    step = pl.program_id(0)
    extent = gathered.places.size
    rows, deep = gathered.rows, gathered.rows * extent["z"]

    @pl.when(step == 0)
    def _():
        here = read_here(me)
        for g, ref in enumerate(groups):
            pltpu.make_async_copy(
                ref.at[pl.ds(extent["x"] * deep, VEC_ROWS)], extras.at[g], extra_sem
            ).start()
        shape = (extent["y"], 2, extent["z"], extent["x"], rows, D)
        for g, ref in enumerate(groups):
            far, second = divmod(g, extent["x"])
            for first in range(extent["x"]):
                y, core, x = gathered.place(here, far, first, second)
                pltpu.make_async_copy(
                    ref.at[pl.ds(first * deep, deep)].reshape(extent["z"], rows, D),
                    weights.reshape(*shape).at[y, core, :, x],
                    sem,
                ).start()
        pltpu.make_async_copy(extras, extras, extra_sem).wait()
        total = extras[0].astype(F32)
        for g in range(1, number):
            total = total + extras[g].astype(F32)
        vec[...] = total
        pltpu.make_async_copy(weights, weights, sem).wait()
        pltpu.make_async_copy(weights, whole, out_sem).start()

    project_body(step, tokens, weights, vec, query, key, value)

    @pl.when(step == pl.num_programs(0) - 1)
    def _():
        pltpu.make_async_copy(weights, whole, out_sem).wait()


PROJECT_ROWS = 256


def project(tokens, me, gathered, groups, after):
    rows = tokens.shape[0]
    tile = pl.BlockSpec((PROJECT_ROWS, D), lambda i: (i, 0))
    number = len(groups)
    return pl.pallas_call(
        functools.partial(project_kernel, gathered, number, len(after)),
        grid=(rows // PROJECT_ROWS,),
        in_specs=[pl.BlockSpec(memory_space=pltpu.SMEM), tile]
        + [pl.BlockSpec(memory_space=pl.ANY)] * (number + len(after)),
        out_specs=[tile] * 3
        + [pl.BlockSpec((VEC_ROWS, D), lambda i: (0, 0)), pl.BlockSpec(memory_space=pl.ANY)],
        out_shape=[jax.ShapeDtypeStruct((rows, D), BF)] * 3
        + [jax.ShapeDtypeStruct((VEC_ROWS, D), F32), jax.ShapeDtypeStruct((ATTN_ROWS, D), BF)],
        scratch_shapes=[
            pltpu.VMEM((ATTN_ROWS, D), BF),
            pltpu.VMEM((number, VEC_ROWS, D), BF),
            pltpu.SemaphoreType.DMA,
            pltpu.SemaphoreType.DMA,
            pltpu.SemaphoreType.DMA,
        ],
        compiler_params=pltpu.CompilerParams(vmem_limit_bytes=24 * MIB),
        cost_estimate=cost(8),
        name="project",
    )(me, tokens, *groups, *after)


def project_whole(tokens, weights, vec):
    rows = tokens.shape[0]
    tile = pl.BlockSpec((PROJECT_ROWS, D), lambda i: (i, 0))
    return pl.pallas_call(
        lambda *refs: project_body(None, *refs),
        grid=(rows // PROJECT_ROWS,),
        in_specs=[
            tile,
            pl.BlockSpec((ATTN_ROWS, D), lambda i: (0, 0), pipeline_mode=pl.Buffered(1)),
            pl.BlockSpec((VEC_ROWS, D), lambda i: (0, 0)),
        ],
        out_specs=[tile] * 3,
        out_shape=[jax.ShapeDtypeStruct((rows, D), BF)] * 3,
        compiler_params=pltpu.CompilerParams(vmem_limit_bytes=24 * MIB),
        name="project",
    )(tokens, weights, vec)


QUERY_BLOCK = 256
QUERY_BLOCKS = ROW // QUERY_BLOCK


def window(block):
    low = max(0, block - 1) * QUERY_BLOCK
    return low, min(QUERY_BLOCKS, block + 2) * QUERY_BLOCK


def fill_bias(bias, seg_column, seg_row, count):
    for block in range(QUERY_BLOCKS):
        low, high = window(block)
        at = slice(block * QUERY_BLOCK, (block + 1) * QUERY_BLOCK)
        shape = (high - low, QUERY_BLOCK)
        key_pos = low + lax.broadcasted_iota(jnp.int32, shape, 0)
        query_pos = block * QUERY_BLOCK + lax.broadcasted_iota(jnp.int32, shape, 1)
        same = seg_column[low:high, 0:1] == seg_row[0:1, at]
        allowed = (same & (key_pos < count)) | (key_pos == query_pos)
        bias[0 : high - low, at] = jnp.where(allowed, 0.0, NEGATIVE).astype(F32)


def one_head(transposed):
    zero = jnp.zeros((HEAD, transposed.shape[1]), transposed.dtype)
    return (
        jnp.concatenate([transposed[:HEAD], zero], 0),
        jnp.concatenate([zero, transposed[HEAD:]], 0),
    )


def attend_kernel(count, seg_column, seg_row, query, key, value, *refs):
    mixed, log_total, bias = refs[-3:]

    @pl.when(pl.program_id(0) == 0)
    def _():
        fill_bias(bias, seg_column, seg_row, count[0])

    value_t = value[...].T
    query_t = one_head((query[...] * jnp.asarray(SCALE, BF)).T)
    for block in range(QUERY_BLOCKS):
        low, high = window(block)
        at = slice(block * QUERY_BLOCK, (block + 1) * QUERY_BLOCK)
        parts = []
        for h in range(2):
            scores = dot(key[low:high, :], query_t[h][:, at], 1, 0) + bias[0 : high - low, at]
            top = jnp.max(scores, axis=0, keepdims=True)
            shifted = jnp.exp(scores - top)
            total = jnp.sum(shifted, axis=0, keepdims=True)
            part = dot(value_t[h * HEAD : (h + 1) * HEAD, low:high], shifted.astype(BF), 1, 0)
            parts.append(part * (1.0 / total))
            log_total[0, h : h + 1, at] = top + jnp.log(total)
        mixed[at, :] = jnp.concatenate(parts, 0).T.astype(BF)


def attend_specs():
    return [
        pl.BlockSpec(memory_space=pltpu.SMEM),
        pl.BlockSpec((ROW, 1), lambda h: (0, 0)),
        pl.BlockSpec((1, ROW), lambda h: (0, 0)),
    ]


def attend(query, key, value, segments, count, after):
    pair = pl.BlockSpec((ROW, 2 * HEAD), lambda h: (0, h))
    return pl.pallas_call(
        attend_kernel,
        grid=(HEADS // 2,),
        in_specs=attend_specs() + [pair] * 3 + [pl.BlockSpec(memory_space=pl.ANY)] * len(after),
        out_specs=[pair, pl.BlockSpec((1, 8, ROW), lambda h: (h, 0, 0))],
        out_shape=[
            jax.ShapeDtypeStruct((ROW, D), BF),
            jax.ShapeDtypeStruct((HEADS // 2, 8, ROW), F32),
        ],
        scratch_shapes=[pltpu.VMEM((3 * QUERY_BLOCK, ROW), F32)],
        compiler_params=pltpu.CompilerParams(vmem_limit_bytes=24 * MIB),
        cost_estimate=cost(25),
        name="attend",
    )(count, segments.reshape(ROW, 1), segments.reshape(1, ROW), query, key, value, *after)


def attend_back_kernel(
    count, seg_column, seg_row, query, key, value, grad, log_total, *refs
):
    grads, sums, bias, key_sum, value_sum = refs[-5:]

    @pl.when(pl.program_id(0) == 0)
    def _():
        fill_bias(bias, seg_column, seg_row, count[0])

    query_t = (query[...] * jnp.asarray(SCALE, BF)).T
    key_t = key[...].T
    grad_t = grad[...].T
    query_one, grad_one = one_head(query_t), one_head(grad_t)
    key_sum[...] = jnp.zeros_like(key_sum)
    value_sum[...] = jnp.zeros_like(value_sum)
    for block in range(QUERY_BLOCKS):
        low, high = window(block)
        at = slice(block * QUERY_BLOCK, (block + 1) * QUERY_BLOCK)
        parts = []
        for h in range(2):
            rows = slice(h * HEAD, (h + 1) * HEAD)
            scores = dot(key[low:high, :], query_one[h][:, at], 1, 0) + bias[0 : high - low, at]
            probs = jnp.exp(scores - log_total[0, h : h + 1, at])
            grad_probs = dot(value[low:high, :], grad_one[h][:, at], 1, 0)
            weighted = probs * grad_probs
            total = jnp.sum(weighted, axis=0, keepdims=True)
            grad_scores = (weighted - probs * total).astype(BF)
            parts.append(dot(key_t[rows, low:high], grad_scores, 1, 0))
            key_sum[rows, low:high] += dot(query_t[rows, at], grad_scores, 1, 1)
            value_sum[rows, low:high] += dot(grad_t[rows, at], probs.astype(BF), 1, 1)
        grads[0, at, :] = (jnp.concatenate(parts, 0) * SCALE).T.astype(BF)
    grads[1] = key_sum[...].T.astype(BF)
    grads[2] = value_sum[...].T.astype(BF)
    sums[...] = jnp.zeros_like(sums)
    sums[0:1] = column_sum(grads[0].astype(F32))
    sums[1:2] = column_sum(grads[2].astype(F32))


def attend_back(query, key, value, grad, log_total, segments, count, first, pairs, after, micros):
    pair = pl.BlockSpec((ROW, 2 * HEAD), lambda h: (0, h + first))
    return pl.pallas_call(
        attend_back_kernel,
        grid=(pairs,),
        in_specs=attend_specs()
        + [pair] * 4
        + [pl.BlockSpec((1, 8, ROW), lambda h: (h + first, 0, 0))]
        + [pl.BlockSpec(memory_space=pl.ANY)] * len(after),
        out_specs=[
            pl.BlockSpec((3, ROW, 2 * HEAD), lambda h: (0, 0, h)),
            pl.BlockSpec((8, 2 * HEAD), lambda h: (0, h)),
        ],
        out_shape=[
            jax.ShapeDtypeStruct((3, ROW, pairs * 2 * HEAD), BF),
            jax.ShapeDtypeStruct((8, pairs * 2 * HEAD), F32),
        ],
        scratch_shapes=[
            pltpu.VMEM((3 * QUERY_BLOCK, ROW), F32),
            pltpu.VMEM((2 * HEAD, ROW), F32),
            pltpu.VMEM((2 * HEAD, ROW), F32),
        ],
        compiler_params=pltpu.CompilerParams(vmem_limit_bytes=BACK_VMEM),
        cost_estimate=cost(micros),
        name="attend_back",
    )(
        count,
        segments.reshape(ROW, 1),
        segments.reshape(1, ROW),
        query,
        key,
        value,
        grad,
        log_total,
        *after,
    )


def normalise(resid):
    centred = resid - jnp.mean(resid, axis=-1, keepdims=True)
    spread = jnp.mean(centred * centred, axis=-1, keepdims=True)
    inverse = lax.rsqrt(spread + NORM_EPSILON)
    return centred * inverse, inverse


def normalise_back(cotangent, gain, normal, inverse):
    scaled = cotangent * gain
    mean = jnp.mean(scaled, axis=-1, keepdims=True)
    aligned = jnp.mean(scaled * normal, axis=-1, keepdims=True)
    return inverse * (scaled - mean - normal * aligned)


def cost(micros):
    return pl.CostEstimate(flops=int(micros * 1.1e9), bytes_accessed=MIB, transcendentals=0)


def column_sum(array):
    return jnp.sum(array, axis=0, keepdims=True)


MIDDLE_ROWS = 256


def middle_kernel(
    fetch,
    groups,
    count,
    me,
    seg_row,
    mixed,
    tokens,
    out_grad,
    w_out,
    vec,
    *refs,
):

    (
        final_low,
        hidden_low,
        activated,
        grad_pre,
        grad_ffn_out,
        grad_attn_out,
        grad_mixed,
        grad_resid,
        vec_grad,
        crop_sums,
        slope,
        weights,
        sem,
    ) = refs[groups:]
    step = pl.program_id(0)

    @pl.when(step == 0)
    def _():
        vec_grad[...] = jnp.zeros_like(vec_grad)
        crop_sums[...] = jnp.zeros_like(crop_sums)
        fetch(read_here(me), refs[:groups], weights, sem)

    def row(i):
        return vec[i : i + 1]

    def chunk(j):
        return weights[j * D : (j + 1) * D]

    def note(i, value):
        vec_grad[i : i + 1] += value

    resid_one = tokens[...].astype(F32) + (dot(mixed[...], w_out[...], 1, 0) + row(2))
    normal_one, inverse_one = normalise(resid_one)
    hidden = normal_one * row(3) + row(4)
    low = hidden.astype(BF)
    hidden_low[...] = low
    total = hidden + row(9)

    def arrived(first, chunks, which):
        @pl.when(step == 0)
        def _():
            part = weights.at[pl.ds(first * D, chunks * D)]
            pltpu.make_async_copy(part, part, sem.at[which]).wait()

    for j in range(UP_CHUNKS):
        at = slice(j * D, (j + 1) * D)
        arrived(j, 1, j)
        pre = dot(low, chunk(j), 1, 0) + row(5 + j)
        share = 0.5 + 0.5 * lax.erf(pre * (0.5**0.5))
        density = jnp.exp(-0.5 * pre * pre) * 0.3989422804014327
        slope[:, at] = share + pre * density
        act = (pre * share).astype(BF)
        activated[:, at] = act
        if j == 0:
            arrived(UP_CHUNKS, UP_CHUNKS, UP_CHUNKS)
        total = total + dot(act, chunk(UP_CHUNKS + j), 1, 0)
    normal_two, inverse_two = normalise(total)
    final = normal_two * row(10) + row(11)
    final_low[...] = final.astype(BF)

    first = step * MIDDLE_ROWS
    across = (CROPS, MIDDLE_ROWS)
    position = first + lax.broadcasted_iota(jnp.int32, across, 1)
    crop = lax.broadcasted_iota(jnp.int32, across, 0)
    member = ((seg_row[...] == crop) & (position < count[0])).astype(BF)
    high = final.astype(BF)
    rest = final - high.astype(F32)
    mid = rest.astype(BF)
    tiny = (rest - mid.astype(F32)).astype(BF)
    crop_sums[...] += dot(member, high, 1, 0) + (dot(member, mid, 1, 0) + dot(member, tiny, 1, 0))

    position = first + lax.broadcasted_iota(jnp.int32, (MIDDLE_ROWS, 1), 0)
    valid = (position < count[0]).astype(F32)
    cotangent = out_grad[...].astype(F32) * valid
    note(10, column_sum(cotangent * normal_two))
    note(11, column_sum(cotangent))
    grad_two = normalise_back(cotangent, row(10), normal_two, inverse_two)
    grad_out = grad_two.astype(BF)
    grad_ffn_out[...] = grad_out
    note(9, column_sum(grad_out.astype(F32)))
    grad_hidden = grad_two
    for j in range(UP_CHUNKS):
        at = slice(j * D, (j + 1) * D)
        back = (dot(grad_out, chunk(UP_CHUNKS + j), 1, 1) * slope[:, at]).astype(BF)
        grad_pre[:, at] = back
        note(5 + j, column_sum(back.astype(F32)))
        grad_hidden = grad_hidden + dot(back, chunk(j), 1, 1)
    note(3, column_sum(grad_hidden * normal_one))
    note(4, column_sum(grad_hidden))
    grad_one = normalise_back(grad_hidden, row(3), normal_one, inverse_one)
    grad_resid[...] = grad_one
    grad_proj = grad_one.astype(BF)
    grad_attn_out[...] = grad_proj
    note(2, column_sum(grad_proj.astype(F32)))
    grad_mixed[...] = dot(grad_proj, w_out[...], 1, 1).astype(BF)


def middle(count, me, segments, mixed, tokens, out_grad, attn_whole, sources, fetch, vec):
    rows = tokens.shape[0]
    tile = pl.BlockSpec((MIDDLE_ROWS, D), lambda i: (i, 0))
    wide = pl.BlockSpec((MIDDLE_ROWS, FF), lambda i: (i, 0))
    small = pl.BlockSpec((VEC_ROWS, D), lambda i: (0, 0))

    def shape(width, kind):
        return jax.ShapeDtypeStruct((rows, width), kind)

    return pl.pallas_call(
        functools.partial(middle_kernel, fetch, len(sources)),
        grid=(rows // MIDDLE_ROWS,),
        in_specs=[
            pl.BlockSpec(memory_space=pltpu.SMEM),
            pl.BlockSpec(memory_space=pltpu.SMEM),
            pl.BlockSpec((1, MIDDLE_ROWS), lambda i: (0, i)),
            tile,
            tile,
            tile,
            pl.BlockSpec((D, D), lambda i: (3, 0), pipeline_mode=pl.Buffered(1)),
            small,
        ]
        + [pl.BlockSpec(memory_space=pl.ANY)] * len(sources),
        out_specs=[tile, tile, wide, wide, tile, tile, tile, tile, small, small],
        out_shape=[
            shape(D, BF),
            shape(D, BF),
            shape(FF, BF),
            shape(FF, BF),
            shape(D, BF),
            shape(D, BF),
            shape(D, BF),
            shape(D, F32),
            jax.ShapeDtypeStruct((VEC_ROWS, D), F32),
            jax.ShapeDtypeStruct((CROPS, D), F32),
        ],
        scratch_shapes=[
            pltpu.VMEM((MIDDLE_ROWS, FF), F32),
            pltpu.VMEM((FFN_ROWS, D), BF),
            pltpu.SemaphoreType.DMA((UP_CHUNKS + 1,)),
        ],
        compiler_params=pltpu.CompilerParams(vmem_limit_bytes=44 * MIB),
        cost_estimate=cost(40),
        name="middle",
    )(count, me, segments.reshape(1, rows), mixed, tokens, out_grad, attn_whole, vec, *sources)


WIDTH = 2 * HEAD * (HEADS // 2 // 3)


def ffn_terms_kernel(shares, me, hidden, activated, *refs):
    pre, out = refs[:shares], refs[shares : 2 * shares]
    keep, give, hidden_t, block, sem = refs[-5:]
    step = pl.program_id(0)
    slot = lax.rem(step, 2)
    owners, rows = keep.shape[1], keep.shape[2]
    up_rows = rows // UP_CHUNKS
    per_chunk = D // rows

    @pl.when(step == 0)
    def _():
        hidden_t[...] = hidden[...].T

    @pl.when(step >= 2)
    def _():
        pltpu.make_async_copy(block.at[slot], block.at[slot], sem.at[slot]).wait()

    def to(core, y, start):
        @pl.when(core == me[1])
        def _():
            start(keep.at[y])

        @pl.when(core != me[1])
        def _():
            start(give.at[y])

    @pl.when(step < UP_CHUNKS)
    def _():
        right = jnp.concatenate([ref[...] for ref in pre], 1)
        block[slot] = dot(hidden_t[...], right, 1, 0).astype(BF)
        for core in range(2):
            source = block.at[slot, pl.ds(core * (D // 2), D // 2)]
            source = source.reshape(owners, up_rows, block.shape[2])

            def start(target):
                at = pl.ds(pl.multiple_of(step * up_rows, 16), up_rows)
                pltpu.make_async_copy(source, target.at[:, at], sem.at[slot]).start()

            to(core, 0, start)

    @pl.when(step >= UP_CHUNKS)
    def _():
        right = jnp.concatenate([ref[...] for ref in out], 1)
        block[slot] = dot(activated[...], right, 0, 0).astype(BF)
        chunk = step - UP_CHUNKS
        source = block.at[slot].reshape(per_chunk, rows, block.shape[2])

        def start(target):
            at = pl.ds(lax.rem(chunk, 2) * per_chunk, per_chunk)
            pltpu.make_async_copy(source, target.at[at], sem.at[slot]).start()

        to(lax.div(chunk, 2), 1, start)

    @pl.when(step == pl.num_programs(0) - 1)
    def _():
        for s in range(2):
            pltpu.make_async_copy(block.at[s], block.at[s], sem.at[s]).wait()


def ffn_terms(places, me, hidden, activated, grad_pre, grad_out, thirds, after):
    owners = places.wide
    rows = FFN_ROWS // places.count
    shares = len(thirds)
    width = shares * WIDTH
    shape = jax.ShapeDtypeStruct((2, owners, rows, width), BF)

    def pre_spec(third):
        return pl.BlockSpec((ROW, WIDTH), lambda i: (0, 3 * jnp.minimum(i, UP_CHUNKS - 1) + third))

    def out_spec(third):
        return pl.BlockSpec((ROW, WIDTH), lambda i: (0, third))

    def kernel(me_ref, hidden_ref, activated_ref, *refs):
        used = refs[: 2 * shares] + refs[2 * shares + len(after) :]
        ffn_terms_kernel(shares, me_ref, hidden_ref, activated_ref, *used)

    return pl.pallas_call(
        kernel,
        grid=(2 * UP_CHUNKS,),
        in_specs=[
            pl.BlockSpec(memory_space=pltpu.SMEM),
            pl.BlockSpec((ROW, D), lambda i: (0, 0), pipeline_mode=pl.Buffered(1)),
            pl.BlockSpec((ROW, D), lambda i: (0, jnp.maximum(i - UP_CHUNKS, 0))),
        ]
        + [pre_spec(t) for t in thirds]
        + [out_spec(t) for t in thirds]
        + [pl.BlockSpec(memory_space=pl.ANY)] * len(after),
        out_specs=[pl.BlockSpec(memory_space=pl.ANY)] * 2,
        out_shape=[shape] * 2,
        scratch_shapes=[
            pltpu.VMEM((D, ROW), BF),
            pltpu.VMEM((2, D, width), BF),
            pltpu.SemaphoreType.DMA((2,)),
        ],
        compiler_params=pltpu.CompilerParams(vmem_limit_bytes=56 * MIB),
        cost_estimate=cost(5 * shares),
        name="ffn_terms",
    )(me, hidden, activated, *([grad_pre] * shares), *([grad_out] * shares), *after)


def attn_terms(places, me, tokens, mixed, grads, grad_proj, thirds, vectors, after):
    owners = places.wide
    rows = ATTN_ROWS // places.count
    shares, extra = len(thirds), vectors.shape[0]
    width = shares * WIDTH
    shape = jax.ShapeDtypeStruct((2, owners, rows + extra, width), BF)

    def kernel(me_ref, tokens_ref, vectors_ref, *refs):
        mixed_ref, refs = refs[0], refs[1:]
        grad_refs, proj_refs, refs = refs[:shares], refs[shares : 2 * shares], refs[2 * shares :]
        keep, give, tokens_t, block, below, sem, below_sem = refs[len(after) :]
        step = pl.program_id(0)
        slot = lax.rem(step, 2)

        @pl.when(step == 0)
        def _():
            tokens_t[...] = tokens_ref[...].T
            below[...] = jnp.broadcast_to(vectors_ref[...][None], below.shape)
            for target in (keep, give):
                for y in range(2):
                    pltpu.make_async_copy(
                        below, target.at[y, :, pl.ds(rows, extra)], below_sem
                    ).start()

        @pl.when(step >= 2)
        def _():
            pltpu.make_async_copy(block.at[slot], block.at[slot], sem.at[slot]).wait()

        @pl.when(step < 3)
        def _():
            right = jnp.concatenate([ref[0] for ref in grad_refs], 1)
            block[slot] = dot(tokens_t[...], right, 1, 0).astype(BF)

        @pl.when(step == 3)
        def _():
            right = jnp.concatenate([ref[...] for ref in proj_refs], 1)
            block[slot] = dot(mixed_ref[...], right, 0, 0).astype(BF)

        source = block.at[slot].reshape(owners, rows, width)
        y, core = lax.div(step, 2), lax.rem(step, 2)

        @pl.when(core == me_ref[1])
        def _():
            pltpu.make_async_copy(source, keep.at[y, :, pl.ds(0, rows)], sem.at[slot]).start()

        @pl.when(core != me_ref[1])
        def _():
            pltpu.make_async_copy(source, give.at[y, :, pl.ds(0, rows)], sem.at[slot]).start()

        @pl.when(step == 3)
        def _():
            for s in range(2):
                pltpu.make_async_copy(block.at[s], block.at[s], sem.at[s]).wait()
            for _ in range(4):
                pltpu.make_async_copy(below, below, below_sem).wait()

    def third_spec(third):
        return pl.BlockSpec((ROW, WIDTH), lambda i: (0, third))

    return pl.pallas_call(
        kernel,
        grid=(4,),
        in_specs=[
            pl.BlockSpec(memory_space=pltpu.SMEM),
            pl.BlockSpec((ROW, D), lambda i: (0, 0), pipeline_mode=pl.Buffered(1)),
            pl.BlockSpec((extra, width), lambda i: (0, 0)),
        ]
        + [pl.BlockSpec((ROW, D), lambda i: (0, 0), pipeline_mode=pl.Buffered(1))]
        + [pl.BlockSpec((1, ROW, WIDTH), lambda i: (jnp.minimum(i, 2), 0, 0))] * shares
        + [third_spec(t) for t in thirds]
        + [pl.BlockSpec(memory_space=pl.ANY)] * len(after),
        out_specs=[pl.BlockSpec(memory_space=pl.ANY)] * 2,
        out_shape=[shape] * 2,
        scratch_shapes=[
            pltpu.VMEM((D, ROW), BF),
            pltpu.VMEM((2, D, width), BF),
            pltpu.VMEM((owners, extra, width), BF),
            pltpu.SemaphoreType.DMA((2,)),
            pltpu.SemaphoreType.DMA,
        ],
        compiler_params=pltpu.CompilerParams(vmem_limit_bytes=BACK_VMEM),
        cost_estimate=cost(2),
        name="attn_terms",
    )(me, tokens, vectors, mixed, *grads, *([grad_proj] * shares), *after)


def token_grad_kernel(resid, weights, *refs):
    out = refs[-1]
    total = resid[...]
    for i, ref in enumerate(refs[:BACK_CALLS]):
        for m in range(3):
            held = weights[m * D : (m + 1) * D, i * WIDTH : (i + 1) * WIDTH]
            total = total + dot(ref[m], held, 1, 1)
    out[...] = total.astype(BF)


def token_gradient(resid, weights, grads, after):
    step = 256
    tile = pl.BlockSpec((step, D), lambda i: (i, 0))
    return pl.pallas_call(
        token_grad_kernel,
        grid=(ROW // step,),
        in_specs=[tile, pl.BlockSpec((3 * D, D), lambda i: (0, 0), pipeline_mode=pl.Buffered(1))]
        + [pl.BlockSpec((3, step, WIDTH), lambda i: (0, i, 0))] * BACK_CALLS
        + [pl.BlockSpec(memory_space=pl.ANY)] * len(after),
        out_specs=tile,
        out_shape=jax.ShapeDtypeStruct((ROW, D), BF),
        compiler_params=pltpu.CompilerParams(vmem_limit_bytes=BACK_VMEM),
        cost_estimate=cost(2),
        name="token_grad",
    )(resid, weights, *grads, *after)


def adam_update(param, gradient, moment, square, shadow):
    step_float = float(STEP)
    moment_next = MOMENT_DECAY * moment + (1.0 - MOMENT_DECAY) * gradient
    square_next = SQUARE_DECAY * square + (1.0 - SQUARE_DECAY) * gradient * gradient
    moment_hat = moment_next / (1.0 - MOMENT_DECAY**step_float)
    square_hat = square_next / (1.0 - SQUARE_DECAY**step_float)
    change = -LEARN_RATE * (
        moment_hat / (jnp.sqrt(square_hat) + ADAM_EPSILON) + WEIGHT_DECAY * param
    )
    updated = param + change
    drift = (1.0 - SHADOW_RATE) * (updated - shadow)
    return (change, moment_next, square_next, drift)


def contract_rows(left, right):
    return dot(left, right, 0, 0)


def on_device(
    places,
    tokens,
    segments,
    counts,
    out_grad,
    attn_param,
    attn_moment,
    attn_square,
    attn_shadow,
    ffn_param,
    ffn_moment,
    ffn_square,
    ffn_shadow,
):
    assert counts.shape[0] == 1 and tokens.shape[0] == ROW
    number = places.count
    here = places.here()
    place_list = jnp.stack([here[a] for a in ("y", "c", "z", "x")]).astype(jnp.int32)
    me = lax.axis_index("dp") * places.wide + lax.axis_index("wide")
    staged = places.staged()
    attn_rows, ffn_rows = ATTN_ROWS // number, FFN_ROWS // number
    up_rows = ffn_rows // UP_CHUNKS
    holds_up = me < number // 2

    last = me == number - 1
    ends = jnp.concatenate([attn_param[-ATTN_TAIL:], ffn_param[-FFN_TAIL:]]).astype(BF)
    ends = jnp.where(last, ends, jnp.zeros_like(ends))
    if staged:
        digits = [lax.rem(lax.shift_right_logical(counts[0], 3 * i), 8) for i in range(4)]
        count_row = jnp.concatenate([jnp.stack(digits).astype(BF), jnp.zeros((D - 4,), BF)])
        filler = jnp.zeros(((VEC_ROWS - COUNT_ROW - 1) * D,), BF)
        extra = jnp.concatenate([ends, count_row, filler]).reshape(VEC_ROWS, D)
        attn_own = to_rows(places, me, attn_param, ATTN_ROWS, ATTN_TAIL).astype(BF)
        attn_set = Gathered(places, attn_rows)
        blocks = attn_set.start_z(jnp.concatenate([attn_own, extra], 0))
        ffn_own = to_rows(places, me, order(ffn_param, blocks[1]), FFN_ROWS, FFN_TAIL).astype(BF)
        by_chunk = ffn_own.reshape(up_rows, UP_CHUNKS, D).transpose(1, 0, 2).reshape(ffn_rows, D)
        ffn_own = jnp.where(holds_up, by_chunk, ffn_own)
        column = attn_set.join_z(here, blocks)
        ffn_set = Gathered(places, ffn_rows)
        half = ffn_rows // 2
        first_half = ffn_set.start_z(order(ffn_own[:half], column))
        plane = order(attn_set.along_first(column), *first_half)
        second_half = ffn_set.start_z(order(ffn_own[half:], plane))
        groups = [plane] + [order(g, *second_half) for g in attn_set.along_second(plane)]
        attn_groups = groups + attn_set.from_core(groups)
        near = ffn_set.join_parts(place_list, [first_half, second_half])
        query, key, value, vec, attn_whole = project(
            tokens, place_list, attn_set, attn_groups, [near]
        )
        token_total = sum(vec[COUNT_ROW, i] * float(8**i) for i in range(4))
        steps = range(1, places.size["x"])
        arrays = {(0, 0, 0): near}
        for k in steps:
            arrays[0, k, 0] = order(places.send(near, "xy", k), query)
        late = order(near, query)
        arrays[1, 0, 0] = places.send(late, "c", 1)
        for k in steps:
            arrays[0, 0, k] = places.send(late, "yx", k)
            arrays[1, k, 0] = places.send(arrays[0, k, 0], "c", 1)
            for m in steps:
                arrays[0, k, m] = places.send(arrays[0, k, 0], "yx", m)
        attend_after = [arrays[0, k, 0] for k in steps]
        extent = places.size
        piece = (extent["z"], UP_CHUNKS, up_rows, D)
        half = extent["y"] // 2

        def fetch(place, refs, weights, sem):
            side = (half, 2, extent["z"], extent["x"])
            up = weights.at[pl.ds(0, FF)].reshape(*((UP_CHUNKS,) + side + (up_rows, D)))
            down = weights.at[pl.ds(FF, FF)].reshape(*(side + (UP_CHUNKS, up_rows, D)))
            for ref, steps in zip(refs, sorted(arrays)):
                y, core, x = ffn_set.place(place, *steps)

                @pl.when(y < half)
                def _():
                    for chunk in range(UP_CHUNKS):
                        pltpu.make_async_copy(
                            ref.at[:, chunk], up.at[chunk, y, core, :, x], sem.at[chunk]
                        ).start()

                @pl.when(y >= half)
                def _():
                    pltpu.make_async_copy(
                        ref, down.at[y - half, core, :, x], sem.at[UP_CHUNKS]
                    ).start()

    else:
        token_total = lax.psum(counts[0].astype(F32), AXES)
        vec = lax.psum(ends.astype(F32), AXES).reshape(COUNT_ROW, D)
        vec = jnp.concatenate([vec, jnp.zeros((VEC_ROWS - COUNT_ROW, D), F32)], 0)
        flat = lax.all_gather(attn_param.astype(BF), AXES, axis=0, tiled=True)
        attn_whole = flat[: ATTN_ROWS * D].reshape(ATTN_ROWS, D)
        flat = lax.all_gather(ffn_param.astype(BF), AXES, axis=0, tiled=True)
        w_up = flat[: FF * D].reshape(D, UP_CHUNKS, D).transpose(1, 0, 2).reshape(FF, D)
        w_down = flat[FF * D : FFN_ROWS * D].reshape(FF, D)
        sources = [w_up, w_down]

        def fetch(place, refs, weights, sem):
            w_up, w_down = refs
            for j in range(UP_CHUNKS):
                rows = pl.ds(j * D, D)
                pltpu.make_async_copy(w_up.at[rows], weights.at[rows], sem.at[j]).start()
            down = weights.at[pl.ds(FF, FF)]
            pltpu.make_async_copy(w_down, down, sem.at[UP_CHUNKS]).start()

        query, key, value = project_whole(tokens, attn_whole, vec)
        attend_after = []

    mixed, log_total = attend(query, key, value, segments, counts, attend_after)
    if staged:
        for first in range(places.size["x"]):
            for second in steps:
                arrays[0, first, second] = order(arrays[0, first, second], mixed)
                arrays[1, first, second] = places.send(arrays[0, first, second], "c", 1)
        sources = [arrays[key].reshape(piece) for key in sorted(arrays)]
    (
        final_low,
        hidden_low,
        activated,
        grad_pre,
        grad_ffn_out,
        grad_attn_out,
        grad_mixed,
        grad_resid,
        vec_grad,
        crop_sums,
    ) = middle(
        counts,
        place_list,
        segments,
        mixed,
        tokens,
        out_grad,
        attn_whole,
        sources,
        fetch,
        vec,
    )
    is_valid = jnp.arange(ROW, dtype=jnp.int32) < counts[0]
    member = (segments[None, :] == jnp.arange(CROPS, dtype=jnp.int32)[:, None]) & is_valid[None, :]
    crop_sizes = jnp.sum(member.astype(F32), axis=1)
    pooled = crop_sums / jnp.maximum(crop_sizes, 1.0)[:, None]

    pairs = HEADS // 2 // BACK_CALLS

    def back(i, after, micros=11):
        return attend_back(
            query,
            key,
            value,
            grad_mixed,
            log_total,
            segments,
            counts,
            i * pairs,
            pairs,
            after,
            micros,
        )

    if staged:
        ffn_sums, attn_sums = Scattered(places, place_list, 1.2), Scattered(places, place_list, 0.5)

        def spread(terms):
            return terms.reshape(2, extent["z"], extent["x"], *terms.shape[2:])

        def ffn_side(thirds, after):
            operands = (hidden_low, activated, grad_pre, grad_ffn_out)
            terms = ffn_terms(places, place_list, *operands, thirds, after)
            return [spread(t) for t in terms]

        def attn_side(thirds, grads, vectors, after):
            width = len(thirds) * WIDTH
            vectors = vectors.astype(BF).reshape(-1)
            filled = -(-vectors.shape[0] // (16 * width)) * 16
            vectors = jnp.pad(vectors, (0, filled * width - vectors.shape[0]))
            vectors = vectors.reshape(filled, width)
            operands = (tokens, mixed, grads, grad_attn_out)
            terms = attn_terms(places, place_list, *operands, thirds, vectors, after)
            return [spread(t) for t in terms]

        keep_a, give_a = ffn_side([0, 1, 2], [])
        core_a = ffn_sums.core(give_a)
        back_0 = back(0, [give_a])
        own_a, cut_a, first_a = ffn_sums.first(keep_a, order(core_a, back_0[0]))
        back_1 = back(1, [cut_a], 3)
        grads = [back_0[0], back_1[0]]
        keep_c, give_c = attn_side([0, 1], grads, vec_grad[2:12], [])
        core_c = attn_sums.core(give_c)
        own_a, cut_a, second_a = ffn_sums.second(own_a, order(first_a, give_c))
        back_2 = back(2, [give_c, cut_a])
        own_c, cut_c, first_c = attn_sums.first(keep_c, order(core_c, back_2[0]))
        vectors = jnp.stack(
            [jnp.concatenate([b[1][i] for b in (back_0, back_1, back_2)]) for i in range(2)]
        )
        grads = [b[0] for b in (back_0, back_1, back_2)]
        keep_d, give_d = attn_side([2], grads[2:], vectors, [cut_c])
        core_d = attn_sums.core(give_d)
        own_a, cuts_a, up_z_a = ffn_sums.along_z(own_a, order(second_a, give_d))
        own_d, cut_d, first_d = attn_sums.first(keep_d, order(core_d, *cuts_a))
        token_grad = token_gradient(grad_resid, attn_whole, grads, cuts_a + [cut_d])
        own_c, cut_c, second_c = attn_sums.second(own_c, order(first_c, token_grad))
        own_d, cut_d, second_d = attn_sums.second(own_d, order(first_d, cut_c))
        own_c, cuts_c, up_z_c = attn_sums.along_z(own_c, order(second_c, cut_d))
        own_d, cuts_d, up_z_d = attn_sums.along_z(own_d, order(second_d, *cuts_c))
        ffn_block = ffn_sums.result(own_a, up_z_a)
        block_c, block_d = attn_sums.result(own_c, up_z_c), attn_sums.result(own_d, up_z_d)
        attn_block = jnp.concatenate([block_c[:attn_rows], block_d[:attn_rows]], 1)
        early_vec = block_c[attn_rows:].reshape(-1)[: 10 * D].reshape(10, D)
        late_vec = block_d[attn_rows:].reshape(-1)[: 2 * D].reshape(2, D)
        by_row = ffn_block.reshape(UP_CHUNKS, up_rows, D).transpose(1, 0, 2).reshape(ffn_rows, D)
        ffn_block = jnp.where(holds_up, by_row, ffn_block)
        ffn_summed = to_flat(places, me, ffn_block, early_vec[3:], FFN_TAIL)
        attn_tail = jnp.concatenate([late_vec, early_vec[:3]], 0)
        attn_summed = to_flat(places, me, attn_block, attn_tail, ATTN_TAIL)
    else:
        backs = [back(i, []) for i in range(BACK_CALLS)]
        grads = [b[0] for b in backs]
        token_grad = token_gradient(grad_resid, attn_whole, grads, [])
        grads = jnp.concatenate(grads, 2)
        mats = [contract_rows(tokens, grads[i]) for i in range(3)]
        mats.append(contract_rows(mixed, grad_attn_out))
        vectors = jnp.concatenate([b[1] for b in backs], 1)[:2]
        vec_grad = jnp.concatenate([vectors, vec_grad[2:]], 0)
        attn_full = jnp.concatenate([g.reshape(-1) for g in mats + [vec_grad[:5]]])
        up = contract_rows(hidden_low, grad_pre)
        down = contract_rows(activated, grad_ffn_out)
        ffn_full = jnp.concatenate([g.reshape(-1) for g in (up, down, vec_grad[5:12])])
        attn_summed = lax.psum_scatter(attn_full, AXES, scatter_dimension=0, tiled=True)
        ffn_summed = lax.psum_scatter(ffn_full, AXES, scatter_dimension=0, tiled=True)
    attn_grad = attn_summed / token_total
    ffn_grad = ffn_summed / token_total
    attn_change, moment_attn, square_attn, drift_attn = adam_update(
        attn_param, attn_grad, attn_moment, attn_square, attn_shadow
    )
    ffn_change, moment_ffn, square_ffn, drift_ffn = adam_update(
        ffn_param, ffn_grad, ffn_moment, ffn_square, ffn_shadow
    )
    return (
        final_low,
        pooled,
        token_grad,
        attn_grad,
        ffn_grad,
        attn_change,
        ffn_change,
        moment_attn,
        moment_ffn,
        square_attn,
        square_ffn,
        drift_attn,
        drift_ffn,
    )


def solution(mesh):
    rows, flat = P(AXES, None), P(AXES)
    return jax.shard_map(
        functools.partial(on_device, Places(mesh)),
        mesh=mesh,
        in_specs=(rows, flat, flat, rows) + (flat,) * 8,
        out_specs=(rows, rows, rows) + (flat,) * 10,
        check_vma=False,
    )
```

```python
import functools

import jax
import jax.numpy as jnp
from jax import lax
from jax.experimental import pallas as pl
from jax.experimental.pallas import tpu as pltpu
from jax.sharding import PartitionSpec as P

D = 768
FF = 3072
HEAD = 64
HEADS = 12
ROW = 1024
STEP = 10
CROPS = 16

NORM_EPSILON = 1e-12
NEGATIVE = -1e30
MOMENT_DECAY = 0.9
SQUARE_DECAY = 0.999
LEARN_RATE = 0.001
WEIGHT_DECAY = 0.01
ADAM_EPSILON = 1e-08
SHADOW_RATE = 0.9995
SCALE = HEAD ** (-0.5)

AXES = ("dp", "wide")
BF = jnp.bfloat16
F32 = jnp.float32
UP_CHUNKS = FF // D
ATTN_ROWS = 4 * D
FFN_ROWS = 2 * FF
ATTN_TAIL = 5 * D
FFN_TAIL = FF + 3 * D
AHEAD_PAIRS = (2, 2, 2)
PAIRS = (2, 4)
VEC_ROWS = 16
COUNT_ROW = 12
MIB = 1 << 20
BACK_VMEM = 24 * MIB
TERMS_VMEM = 24 * MIB
TOKEN_VMEM = 24 * MIB
FFN_VMEM = 56 * MIB
ADD_VMEM = 24 * MIB


def dot(left, right, left_dim, right_dim):
    return lax.dot_general(
        left, right, (((left_dim,), (right_dim,)), ((), ())), preferred_element_type=F32
    )


class Places:
    def __init__(self, mesh):
        self.dp, self.wide = mesh.shape["dp"], mesh.shape["wide"]
        self.count = self.dp * self.wide
        self.size = {"c": 2, "y": self.dp // 2}
        self.size["x"] = self.size["y"]
        self.size["z"] = self.wide // self.size["x"]

    def staged(self):
        exact = self.dp == 4 and self.wide % self.size["x"] == 0
        return exact and D % (16 * UP_CHUNKS * self.wide // 2) == 0

    def index(self, y, c, z, x):
        return (y * 2 + c) * self.wide + z * self.size["x"] + x

    def rotation(self, axis, step):
        pairs = []
        extent = self.size
        for y in range(extent["y"]):
            for c in range(2):
                along = axis if len(axis) == 1 else axis[c]
                for z in range(extent["z"]):
                    for x in range(extent["x"]):
                        at = {"y": y, "c": c, "z": z, "x": x}
                        to = dict(at)
                        to[along] = (at[along] + step) % extent[along]
                        pairs.append((self.index(**at), self.index(**to)))
        return pairs

    def send(self, array, axis, step):
        return lax.ppermute(array, AXES, self.rotation(axis, step))

    def here(self):
        outer, inner = lax.axis_index("dp"), lax.axis_index("wide")
        extent = self.size["x"]
        return {"y": outer // 2, "c": outer % 2, "z": inner // extent, "x": inner % extent}


def order(array, *before):
    return lax.optimization_barrier((array,) + before)[0]


class Gathered:
    def __init__(self, places, rows):
        self.places, self.rows = places, rows
        self.deep = places.size["z"] * rows

    def start_z(self, own):
        extent = self.places.size["z"]
        return [own] + [self.places.send(own, "z", k) for k in range(1, extent)]

    def join_z(self, here, blocks):
        rows, extent = self.rows, self.places.size["z"]
        near = jnp.zeros((self.deep, D), BF)
        for k, block in enumerate(blocks):
            at = lax.rem(here["z"] + (extent - k), extent) * rows
            near = lax.dynamic_update_slice_in_dim(near, block[:rows], at, 0)
        return jnp.concatenate([near, self.total([b[rows:] for b in blocks])], 0)

    def join_parts(self, me, parts):
        extent, count = self.places.size["z"], len(parts)
        share = self.rows // count

        def kernel(me_ref, *refs):
            out, sem = refs[-2:]
            for p in range(count):
                for k in range(extent):
                    at = lax.rem(me_ref[2] + (extent - k), extent)
                    pltpu.make_async_copy(
                        refs[p * extent + k], out.at[at, pl.ds(p * share, share)], sem
                    ).start()
            pltpu.make_async_copy(out, out, sem).wait()

        blocks = [b for part in parts for b in part]
        return pl.pallas_call(
            kernel,
            in_specs=[pl.BlockSpec(memory_space=pltpu.SMEM)]
            + [pl.BlockSpec(memory_space=pl.ANY)] * len(blocks),
            out_specs=pl.BlockSpec(memory_space=pltpu.VMEM),
            out_shape=jax.ShapeDtypeStruct((extent, self.rows, D), BF),
            scratch_shapes=[pltpu.SemaphoreType.DMA],
            compiler_params=pltpu.CompilerParams(vmem_limit_bytes=16 * MIB),
            cost_estimate=cost(2),
            name="join",
        )(me, *blocks).reshape(self.deep, D)

    def along_first(self, near):
        places, extent = self.places, self.places.size
        blocks = [near] + [places.send(near, "xy", k) for k in range(1, extent["x"])]
        parts = [b[: self.deep] for b in blocks]
        if near.shape[0] > self.deep:
            parts.append(self.total([b[self.deep :] for b in blocks]))
        return jnp.concatenate(parts, 0)

    def along_second(self, near):
        return [self.places.send(near, "yx", k) for k in range(1, self.places.size["x"])]

    def from_core(self, groups):
        return [self.places.send(g, "c", 1) for g in groups]

    def total(self, arrays):
        result = arrays[0].astype(F32)
        for a in arrays[1:]:
            result = result + a.astype(F32)
        return result.astype(BF)

    def place(self, here, far, first, second):
        extent = self.places.size

        def back(axis, step):
            return lax.rem(here[axis] + (extent[axis] - step), extent[axis])

        core = here["c"] if far == 0 else 1 - here["c"]
        y = jnp.where(core == 0, back("y", second), back("y", first))
        x = jnp.where(core == 0, back("x", first), back("x", second))
        return y, core, x


def read_here(me_ref):
    return {"y": me_ref[0], "c": me_ref[1], "z": me_ref[2], "x": me_ref[3]}


def add_routed(me, keep, arrived, grid, routes, source_block, target_block, target_lead, micros):
    rows, width = keep.shape[-2:]

    def kernel(me_ref, *refs):
        for i in range(len(routes)):
            total = refs[2 * i][...].astype(F32) + refs[2 * i + 1][...].astype(F32)
            refs[2 * len(routes) + i][...] = total.astype(BF)

    def source(route):
        return pl.BlockSpec(source_block + (rows, width), lambda *at: route(*at) + (0, 0))

    target = pl.BlockSpec(target_block[0] + (rows, width), lambda *at: target_block[1](*at) + (0, 0))
    return pl.pallas_call(
        kernel,
        grid_spec=pltpu.PrefetchScalarGridSpec(
            num_scalar_prefetch=1,
            grid=grid,
            in_specs=[source(r) for r in routes for _ in range(2)],
            out_specs=[target] * len(routes),
        ),
        out_shape=[jax.ShapeDtypeStruct(target_lead + (rows, width), BF)] * len(routes),
        compiler_params=pltpu.CompilerParams(vmem_limit_bytes=ADD_VMEM),
        cost_estimate=cost(micros),
        name="add_routed",
    )(me, *([keep, arrived] * len(routes)))


class Scattered:
    def __init__(self, places, me, micros):
        self.places, self.me, self.micros = places, me, micros
        self.z = places.size["z"]

    def core(self, give):
        return self.places.send(give, "c", 1)

    def first(self, keep, arrived):
        deep = 2

        def route(far):
            def pick_block(z, e, me):
                y, x = jnp.abs(me[0] - far), jnp.abs(me[3] - far)
                return jnp.where(me[1] == 0, e, y), z, jnp.where(me[1] == 0, x, e)

            return pick_block

        own, cut = add_routed(
            self.me,
            keep,
            arrived,
            (self.z // deep, 2),
            [route(0), route(1)],
            (None, deep, None),
            ((deep, None), lambda z, e, me: (z, e)),
            (self.z, 2),
            4 * self.micros,
        )
        return own, cut

    def second(self, keep, arrived):
        deep = 2

        def route(far):
            return lambda z, me: (z, jnp.abs(jnp.where(me[1] == 0, me[0], me[3]) - far))

        own, cut = add_routed(
            self.me,
            keep,
            arrived,
            (self.z // deep,),
            [route(0), route(1)],
            (deep, None),
            ((deep,), lambda z, me: (z,)),
            (self.z,),
            2 * self.micros,
        )
        return own, cut

    def along_z(self, keep, arrived):
        def route(k):
            return lambda i, me: (lax.rem(me[2] + k, self.z),)

        own, *cuts = add_routed(
            self.me,
            keep,
            arrived,
            (1,),
            [route(k) for k in range(self.z)],
            (None,),
            ((None,), lambda i, me: (0,)),
            (1,),
            self.micros,
        )
        return own, cuts

    def send(self, cut, *before):
        return self.places.send(order(cut, *before), "xy", 1)

    def send_second(self, cut, *before):
        return self.places.send(order(cut, *before), "yx", 1)

    def send_z(self, cuts, *before):
        return [self.places.send(order(c, *before), "z", k + 1) for k, c in enumerate(cuts)]

    def result(self, own, arrived):
        total = own[0].astype(F32)
        for a in arrived:
            total = total + a[0].astype(F32)
        return total


def to_rows(places, me, flat, rows, tail):
    count = places.count
    block = rows // count * D
    slack = tail // count
    before = lax.ppermute(flat[-tail:], AXES, [(i, i + 1) for i in range(count - 1)])
    joined = jnp.concatenate([before, flat])
    return lax.dynamic_slice_in_dim(joined, tail - me * slack, block).reshape(rows // count, D)


def to_flat(places, me, block, vectors, tail):
    count = places.count
    slack = tail // count
    after = lax.ppermute(block[: tail // D], AXES, [(i + 1, i) for i in range(count - 1)])
    after = jnp.where(me == count - 1, vectors, after)
    joined = jnp.concatenate([block, after], 0).reshape(-1)
    return lax.dynamic_slice_in_dim(joined, me * slack, block.size + slack)


def project_body(step, tokens, weights, vec, query, key, value):
    held = tokens[...]
    query[...] = (dot(held, weights[0:D], 1, 0) + vec[0:1]).astype(BF)
    key[...] = dot(held, weights[D : 2 * D], 1, 0).astype(BF)
    value[...] = (dot(held, weights[2 * D : 3 * D], 1, 0) + vec[1:2]).astype(BF)


def project_kernel(gathered, number, after, me, tokens, *refs):
    groups = refs[:number]
    query, key, value, vec, whole, weights, extras, sem, extra_sem, out_sem = refs[number + after :]
    step = pl.program_id(0)
    extent = gathered.places.size
    rows, deep = gathered.rows, gathered.rows * extent["z"]

    @pl.when(step == 0)
    def _():
        here = read_here(me)
        for g, ref in enumerate(groups):
            pltpu.make_async_copy(
                ref.at[pl.ds(extent["x"] * deep, VEC_ROWS)], extras.at[g], extra_sem
            ).start()
        shape = (extent["y"], 2, extent["z"], extent["x"], rows, D)
        for g, ref in enumerate(groups):
            far, second = divmod(g, extent["x"])
            for first in range(extent["x"]):
                y, core, x = gathered.place(here, far, first, second)
                pltpu.make_async_copy(
                    ref.at[pl.ds(first * deep, deep)].reshape(extent["z"], rows, D),
                    weights.reshape(*shape).at[y, core, :, x],
                    sem,
                ).start()
        pltpu.make_async_copy(extras, extras, extra_sem).wait()
        total = extras[0].astype(F32)
        for g in range(1, number):
            total = total + extras[g].astype(F32)
        vec[...] = total
        pltpu.make_async_copy(weights, weights, sem).wait()
        pltpu.make_async_copy(weights, whole, out_sem).start()

    project_body(step, tokens, weights, vec, query, key, value)

    @pl.when(step == pl.num_programs(0) - 1)
    def _():
        pltpu.make_async_copy(weights, whole, out_sem).wait()


PROJECT_ROWS = 256


def project(tokens, me, gathered, groups, after):
    rows = tokens.shape[0]
    tile = pl.BlockSpec((PROJECT_ROWS, D), lambda i: (i, 0))
    number = len(groups)
    return pl.pallas_call(
        functools.partial(project_kernel, gathered, number, len(after)),
        grid=(rows // PROJECT_ROWS,),
        in_specs=[pl.BlockSpec(memory_space=pltpu.SMEM), tile]
        + [pl.BlockSpec(memory_space=pl.ANY)] * (number + len(after)),
        out_specs=[tile] * 3
        + [pl.BlockSpec((VEC_ROWS, D), lambda i: (0, 0)), pl.BlockSpec(memory_space=pl.ANY)],
        out_shape=[jax.ShapeDtypeStruct((rows, D), BF)] * 3
        + [jax.ShapeDtypeStruct((VEC_ROWS, D), F32), jax.ShapeDtypeStruct((ATTN_ROWS, D), BF)],
        scratch_shapes=[
            pltpu.VMEM((ATTN_ROWS, D), BF),
            pltpu.VMEM((number, VEC_ROWS, D), BF),
            pltpu.SemaphoreType.DMA,
            pltpu.SemaphoreType.DMA,
            pltpu.SemaphoreType.DMA,
        ],
        compiler_params=pltpu.CompilerParams(vmem_limit_bytes=24 * MIB),
        cost_estimate=cost(8),
        name="project",
    )(me, tokens, *groups, *after)


def project_whole(tokens, weights, vec):
    rows = tokens.shape[0]
    tile = pl.BlockSpec((PROJECT_ROWS, D), lambda i: (i, 0))
    return pl.pallas_call(
        lambda *refs: project_body(None, *refs),
        grid=(rows // PROJECT_ROWS,),
        in_specs=[
            tile,
            pl.BlockSpec((ATTN_ROWS, D), lambda i: (0, 0), pipeline_mode=pl.Buffered(1)),
            pl.BlockSpec((VEC_ROWS, D), lambda i: (0, 0)),
        ],
        out_specs=[tile] * 3,
        out_shape=[jax.ShapeDtypeStruct((rows, D), BF)] * 3,
        compiler_params=pltpu.CompilerParams(vmem_limit_bytes=24 * MIB),
        name="project",
    )(tokens, weights, vec)


QUERY_BLOCK = 256
QUERY_BLOCKS = ROW // QUERY_BLOCK


def window(block):
    low = max(0, block - 1) * QUERY_BLOCK
    return low, min(QUERY_BLOCKS, block + 2) * QUERY_BLOCK


def fill_bias(bias, seg_column, seg_row, count):
    for block in range(QUERY_BLOCKS):
        low, high = window(block)
        at = slice(block * QUERY_BLOCK, (block + 1) * QUERY_BLOCK)
        shape = (high - low, QUERY_BLOCK)
        key_pos = low + lax.broadcasted_iota(jnp.int32, shape, 0)
        query_pos = block * QUERY_BLOCK + lax.broadcasted_iota(jnp.int32, shape, 1)
        same = seg_column[low:high, 0:1] == seg_row[0:1, at]
        allowed = (same & (key_pos < count)) | (key_pos == query_pos)
        bias[0 : high - low, at] = jnp.where(allowed, 0.0, NEGATIVE).astype(F32)


def one_head(transposed):
    zero = jnp.zeros((HEAD, transposed.shape[1]), transposed.dtype)
    return (
        jnp.concatenate([transposed[:HEAD], zero], 0),
        jnp.concatenate([zero, transposed[HEAD:]], 0),
    )


def attend_kernel(count, seg_column, seg_row, query, key, value, *refs):
    mixed, log_total, bias = refs[-3:]

    @pl.when(pl.program_id(0) == 0)
    def _():
        fill_bias(bias, seg_column, seg_row, count[0])

    value_t = value[...].T
    query_t = one_head((query[...] * jnp.asarray(SCALE, BF)).T)
    for block in range(QUERY_BLOCKS):
        low, high = window(block)
        at = slice(block * QUERY_BLOCK, (block + 1) * QUERY_BLOCK)
        parts = []
        for h in range(2):
            scores = dot(key[low:high, :], query_t[h][:, at], 1, 0) + bias[0 : high - low, at]
            top = jnp.max(scores, axis=0, keepdims=True)
            shifted = jnp.exp(scores - top)
            total = jnp.sum(shifted, axis=0, keepdims=True)
            part = dot(value_t[h * HEAD : (h + 1) * HEAD, low:high], shifted.astype(BF), 1, 0)
            parts.append(part * (1.0 / total))
            log_total[0, h : h + 1, at] = top + jnp.log(total)
        mixed[at, :] = jnp.concatenate(parts, 0).T.astype(BF)


def attend_specs():
    return [
        pl.BlockSpec(memory_space=pltpu.SMEM),
        pl.BlockSpec((ROW, 1), lambda h: (0, 0)),
        pl.BlockSpec((1, ROW), lambda h: (0, 0)),
    ]


def attend(query, key, value, segments, count, first, pairs, after):
    pair = pl.BlockSpec((ROW, 2 * HEAD), lambda h: (0, h + first))
    return pl.pallas_call(
        attend_kernel,
        grid=(pairs,),
        in_specs=attend_specs() + [pair] * 3 + [pl.BlockSpec(memory_space=pl.ANY)] * len(after),
        out_specs=[
            pl.BlockSpec((ROW, 2 * HEAD), lambda h: (0, h)),
            pl.BlockSpec((1, 8, ROW), lambda h: (h, 0, 0)),
        ],
        out_shape=[
            jax.ShapeDtypeStruct((ROW, pairs * 2 * HEAD), BF),
            jax.ShapeDtypeStruct((pairs, 8, ROW), F32),
        ],
        scratch_shapes=[pltpu.VMEM((3 * QUERY_BLOCK, ROW), F32)],
        compiler_params=pltpu.CompilerParams(vmem_limit_bytes=24 * MIB),
        cost_estimate=cost(25 * pairs / 6),
        name="attend",
    )(count, segments.reshape(ROW, 1), segments.reshape(1, ROW), query, key, value, *after)


def attend_back_kernel(
    count, seg_column, seg_row, query, key, value, grad, log_total, *refs
):
    grads, sums, bias, key_sum, value_sum = refs[-5:]

    @pl.when(pl.program_id(0) == 0)
    def _():
        fill_bias(bias, seg_column, seg_row, count[0])

    query_t = (query[...] * jnp.asarray(SCALE, BF)).T
    key_t = key[...].T
    grad_t = grad[...].T
    query_one, grad_one = one_head(query_t), one_head(grad_t)
    key_sum[...] = jnp.zeros_like(key_sum)
    value_sum[...] = jnp.zeros_like(value_sum)
    for block in range(QUERY_BLOCKS):
        low, high = window(block)
        at = slice(block * QUERY_BLOCK, (block + 1) * QUERY_BLOCK)
        parts = []
        for h in range(2):
            rows = slice(h * HEAD, (h + 1) * HEAD)
            scores = dot(key[low:high, :], query_one[h][:, at], 1, 0) + bias[0 : high - low, at]
            probs = jnp.exp(scores - log_total[0, h : h + 1, at])
            grad_probs = dot(value[low:high, :], grad_one[h][:, at], 1, 0)
            weighted = probs * grad_probs
            total = jnp.sum(weighted, axis=0, keepdims=True)
            grad_scores = (weighted - probs * total).astype(BF)
            parts.append(dot(key_t[rows, low:high], grad_scores, 1, 0))
            key_sum[rows, low:high] += dot(query_t[rows, at], grad_scores, 1, 1)
            value_sum[rows, low:high] += dot(grad_t[rows, at], probs.astype(BF), 1, 1)
        grads[0, at, :] = (jnp.concatenate(parts, 0) * SCALE).T.astype(BF)
    grads[1] = key_sum[...].T.astype(BF)
    grads[2] = value_sum[...].T.astype(BF)
    sums[...] = jnp.zeros_like(sums)
    sums[0:1] = column_sum(grads[0].astype(F32))
    sums[1:2] = column_sum(grads[2].astype(F32))


def attend_back(query, key, value, grad, log_total, segments, count, first, pairs, after, micros):
    pair = pl.BlockSpec((ROW, 2 * HEAD), lambda h: (0, h + first))
    return pl.pallas_call(
        attend_back_kernel,
        grid=(pairs,),
        in_specs=attend_specs()
        + [pair] * 4
        + [pl.BlockSpec((1, 8, ROW), lambda h: (h + first, 0, 0))]
        + [pl.BlockSpec(memory_space=pl.ANY)] * len(after),
        out_specs=[
            pl.BlockSpec((3, ROW, 2 * HEAD), lambda h: (0, 0, h)),
            pl.BlockSpec((8, 2 * HEAD), lambda h: (0, h)),
        ],
        out_shape=[
            jax.ShapeDtypeStruct((3, ROW, pairs * 2 * HEAD), BF),
            jax.ShapeDtypeStruct((8, pairs * 2 * HEAD), F32),
        ],
        scratch_shapes=[
            pltpu.VMEM((3 * QUERY_BLOCK, ROW), F32),
            pltpu.VMEM((2 * HEAD, ROW), F32),
            pltpu.VMEM((2 * HEAD, ROW), F32),
        ],
        compiler_params=pltpu.CompilerParams(vmem_limit_bytes=BACK_VMEM),
        cost_estimate=cost(micros),
        name="attend_back",
    )(
        count,
        segments.reshape(ROW, 1),
        segments.reshape(1, ROW),
        query,
        key,
        value,
        grad,
        log_total,
        *after,
    )


def normalise(resid):
    centred = resid - jnp.mean(resid, axis=-1, keepdims=True)
    spread = jnp.mean(centred * centred, axis=-1, keepdims=True)
    inverse = lax.rsqrt(spread + NORM_EPSILON)
    return centred * inverse, inverse


def normalise_back(cotangent, gain, normal, inverse):
    scaled = cotangent * gain
    mean = jnp.mean(scaled, axis=-1, keepdims=True)
    aligned = jnp.mean(scaled * normal, axis=-1, keepdims=True)
    return inverse * (scaled - mean - normal * aligned)


def cost(micros):
    return pl.CostEstimate(flops=int(micros * 1.1e9), bytes_accessed=MIB, transcendentals=0)


def column_sum(array):
    return jnp.sum(array, axis=0, keepdims=True)


MIDDLE_ROWS = 256


def middle_kernel(
    fetch,
    groups,
    count,
    me,
    seg_row,
    tokens,
    out_grad,
    w_out,
    vec,
    *refs,
):
    mixed = jnp.concatenate([ref[...] for ref in refs[: len(AHEAD_PAIRS)]], 1)
    refs = refs[len(AHEAD_PAIRS) :]

    (
        final_low,
        hidden_low,
        activated,
        grad_pre,
        grad_ffn_out,
        grad_attn_out,
        grad_mixed,
        grad_resid,
        vec_grad,
        crop_sums,
        slope,
        weights,
        sem,
    ) = refs[groups:]
    step = pl.program_id(0)

    @pl.when(step == 0)
    def _():
        vec_grad[...] = jnp.zeros_like(vec_grad)
        crop_sums[...] = jnp.zeros_like(crop_sums)
        fetch(read_here(me), refs[:groups], weights, sem)

    def row(i):
        return vec[i : i + 1]

    def chunk(j):
        return weights[j * D : (j + 1) * D]

    def note(i, value):
        vec_grad[i : i + 1] += value

    resid_one = tokens[...].astype(F32) + (dot(mixed, w_out[...], 1, 0) + row(2))
    normal_one, inverse_one = normalise(resid_one)
    hidden = normal_one * row(3) + row(4)
    low = hidden.astype(BF)
    hidden_low[...] = low
    total = hidden + row(9)

    def arrived(first, chunks, which):
        @pl.when(step == 0)
        def _():
            part = weights.at[pl.ds(first * D, chunks * D)]
            pltpu.make_async_copy(part, part, sem.at[which]).wait()

    for j in range(UP_CHUNKS):
        at = slice(j * D, (j + 1) * D)
        arrived(j, 1, j)
        pre = dot(low, chunk(j), 1, 0) + row(5 + j)
        share = 0.5 + 0.5 * lax.erf(pre * (0.5**0.5))
        density = jnp.exp(-0.5 * pre * pre) * 0.3989422804014327
        slope[:, at] = share + pre * density
        act = (pre * share).astype(BF)
        activated[:, at] = act
        if j == 0:
            arrived(UP_CHUNKS, UP_CHUNKS, UP_CHUNKS)
        total = total + dot(act, chunk(UP_CHUNKS + j), 1, 0)
    normal_two, inverse_two = normalise(total)
    final = normal_two * row(10) + row(11)
    final_low[...] = final.astype(BF)

    first = step * MIDDLE_ROWS
    across = (CROPS, MIDDLE_ROWS)
    position = first + lax.broadcasted_iota(jnp.int32, across, 1)
    crop = lax.broadcasted_iota(jnp.int32, across, 0)
    member = ((seg_row[...] == crop) & (position < count[0])).astype(BF)
    high = final.astype(BF)
    rest = final - high.astype(F32)
    mid = rest.astype(BF)
    tiny = (rest - mid.astype(F32)).astype(BF)
    crop_sums[...] += dot(member, high, 1, 0) + (dot(member, mid, 1, 0) + dot(member, tiny, 1, 0))

    position = first + lax.broadcasted_iota(jnp.int32, (MIDDLE_ROWS, 1), 0)
    valid = (position < count[0]).astype(F32)
    cotangent = out_grad[...].astype(F32) * valid
    note(10, column_sum(cotangent * normal_two))
    note(11, column_sum(cotangent))
    grad_two = normalise_back(cotangent, row(10), normal_two, inverse_two)
    grad_out = grad_two.astype(BF)
    grad_ffn_out[...] = grad_out
    note(9, column_sum(grad_out.astype(F32)))
    grad_hidden = grad_two
    for j in range(UP_CHUNKS):
        at = slice(j * D, (j + 1) * D)
        back = (dot(grad_out, chunk(UP_CHUNKS + j), 1, 1) * slope[:, at]).astype(BF)
        grad_pre[:, at] = back
        note(5 + j, column_sum(back.astype(F32)))
        grad_hidden = grad_hidden + dot(back, chunk(j), 1, 1)
    note(3, column_sum(grad_hidden * normal_one))
    note(4, column_sum(grad_hidden))
    grad_one = normalise_back(grad_hidden, row(3), normal_one, inverse_one)
    grad_resid[...] = grad_one
    grad_proj = grad_one.astype(BF)
    grad_attn_out[...] = grad_proj
    note(2, column_sum(grad_proj.astype(F32)))
    grad_mixed[...] = dot(grad_proj, w_out[...], 1, 1).astype(BF)


def middle(count, me, segments, mixed, tokens, out_grad, attn_whole, sources, fetch, vec):
    rows = tokens.shape[0]
    tile = pl.BlockSpec((MIDDLE_ROWS, D), lambda i: (i, 0))
    wide = pl.BlockSpec((MIDDLE_ROWS, FF), lambda i: (i, 0))
    small = pl.BlockSpec((VEC_ROWS, D), lambda i: (0, 0))

    def shape(width, kind):
        return jax.ShapeDtypeStruct((rows, width), kind)

    return pl.pallas_call(
        functools.partial(middle_kernel, fetch, len(sources)),
        grid=(rows // MIDDLE_ROWS,),
        in_specs=[
            pl.BlockSpec(memory_space=pltpu.SMEM),
            pl.BlockSpec(memory_space=pltpu.SMEM),
            pl.BlockSpec((1, MIDDLE_ROWS), lambda i: (0, i)),
            tile,
            tile,
            pl.BlockSpec((D, D), lambda i: (3, 0), pipeline_mode=pl.Buffered(1)),
            small,
        ]
        + [pl.BlockSpec((MIDDLE_ROWS, 2 * HEAD * p), lambda i: (i, 0)) for p in AHEAD_PAIRS]
        + [pl.BlockSpec(memory_space=pl.ANY)] * len(sources),
        out_specs=[tile, tile, wide, wide, tile, tile, tile, tile, small, small],
        out_shape=[
            shape(D, BF),
            shape(D, BF),
            shape(FF, BF),
            shape(FF, BF),
            shape(D, BF),
            shape(D, BF),
            shape(D, BF),
            shape(D, F32),
            jax.ShapeDtypeStruct((VEC_ROWS, D), F32),
            jax.ShapeDtypeStruct((CROPS, D), F32),
        ],
        scratch_shapes=[
            pltpu.VMEM((MIDDLE_ROWS, FF), F32),
            pltpu.VMEM((FFN_ROWS, D), BF),
            pltpu.SemaphoreType.DMA((UP_CHUNKS + 1,)),
        ],
        compiler_params=pltpu.CompilerParams(vmem_limit_bytes=44 * MIB),
        cost_estimate=cost(40),
        name="middle",
    )(count, me, segments.reshape(1, rows), tokens, out_grad, attn_whole, vec, *mixed, *sources)


WIDTH = D // 3


def ffn_terms_kernel(shares, me, hidden, activated, *refs):
    pre, out = refs[:shares], refs[shares : 2 * shares]
    keep, give, hidden_t, block, sem = refs[-5:]
    step = pl.program_id(0)
    slot = lax.rem(step, 2)
    owners, rows = keep.shape[1], keep.shape[2]
    up_rows = rows // UP_CHUNKS
    per_chunk = D // rows

    @pl.when(step == 0)
    def _():
        hidden_t[...] = hidden[...].T

    @pl.when(step >= 2)
    def _():
        pltpu.make_async_copy(block.at[slot], block.at[slot], sem.at[slot]).wait()

    def to(core, y, start):
        @pl.when(core == me[1])
        def _():
            start(keep.at[y])

        @pl.when(core != me[1])
        def _():
            start(give.at[y])

    @pl.when(step < UP_CHUNKS)
    def _():
        right = jnp.concatenate([ref[...] for ref in pre], 1)
        block[slot] = dot(hidden_t[...], right, 1, 0).astype(BF)
        for core in range(2):
            source = block.at[slot, pl.ds(core * (D // 2), D // 2)]
            source = source.reshape(owners, up_rows, block.shape[2])

            def start(target):
                at = pl.ds(pl.multiple_of(step * up_rows, 16), up_rows)
                pltpu.make_async_copy(source, target.at[:, at], sem.at[slot]).start()

            to(core, 0, start)

    @pl.when(step >= UP_CHUNKS)
    def _():
        right = jnp.concatenate([ref[...] for ref in out], 1)
        block[slot] = dot(activated[...], right, 0, 0).astype(BF)
        chunk = step - UP_CHUNKS
        source = block.at[slot].reshape(per_chunk, rows, block.shape[2])

        def start(target):
            at = pl.ds(lax.rem(chunk, 2) * per_chunk, per_chunk)
            pltpu.make_async_copy(source, target.at[at], sem.at[slot]).start()

        to(lax.div(chunk, 2), 1, start)

    @pl.when(step == pl.num_programs(0) - 1)
    def _():
        for s in range(2):
            pltpu.make_async_copy(block.at[s], block.at[s], sem.at[s]).wait()


def ffn_terms(places, me, hidden, activated, grad_pre, grad_out, thirds, after):
    owners = places.wide
    rows = FFN_ROWS // places.count
    shares = len(thirds)
    width = shares * WIDTH
    shape = jax.ShapeDtypeStruct((2, owners, rows, width), BF)

    def pre_spec(third):
        return pl.BlockSpec((ROW, WIDTH), lambda i: (0, 3 * jnp.minimum(i, UP_CHUNKS - 1) + third))

    def out_spec(third):
        return pl.BlockSpec((ROW, WIDTH), lambda i: (0, third))

    def kernel(me_ref, hidden_ref, activated_ref, *refs):
        used = refs[: 2 * shares] + refs[2 * shares + len(after) :]
        ffn_terms_kernel(shares, me_ref, hidden_ref, activated_ref, *used)

    return pl.pallas_call(
        kernel,
        grid=(2 * UP_CHUNKS,),
        in_specs=[
            pl.BlockSpec(memory_space=pltpu.SMEM),
            pl.BlockSpec((ROW, D), lambda i: (0, 0), pipeline_mode=pl.Buffered(1)),
            pl.BlockSpec((ROW, D), lambda i: (0, jnp.maximum(i - UP_CHUNKS, 0))),
        ]
        + [pre_spec(t) for t in thirds]
        + [out_spec(t) for t in thirds]
        + [pl.BlockSpec(memory_space=pl.ANY)] * len(after),
        out_specs=[pl.BlockSpec(memory_space=pl.ANY)] * 2,
        out_shape=[shape] * 2,
        scratch_shapes=[
            pltpu.VMEM((D, ROW), BF),
            pltpu.VMEM((2, D, width), BF),
            pltpu.SemaphoreType.DMA((2,)),
        ],
        compiler_params=pltpu.CompilerParams(vmem_limit_bytes=FFN_VMEM),
        cost_estimate=cost(5 * shares),
        name="ffn_terms",
    )(me, hidden, activated, *([grad_pre] * shares), *([grad_out] * shares), *after)


def attn_terms(places, me, tokens, mixed, grads, grad_proj, vectors, after):
    owners = places.wide
    rows = ATTN_ROWS // places.count
    parts, extra = len(AHEAD_PAIRS), vectors.shape[0]
    shape = jax.ShapeDtypeStruct((2, owners, rows + extra, D), BF)

    def kernel(me_ref, tokens_ref, vectors_ref, proj_ref, *refs):
        mixed_refs, grad_refs, refs = refs[:parts], refs[parts : parts + len(PAIRS)], refs[parts + len(PAIRS) :]
        keep, give, tokens_t, block, below, sem, below_sem = refs[len(after) :]
        step = pl.program_id(0)
        slot = lax.rem(step, 2)

        @pl.when(step == 0)
        def _():
            tokens_t[...] = tokens_ref[...].T
            below[...] = jnp.broadcast_to(vectors_ref[...].astype(BF)[None], below.shape)
            for target in (keep, give):
                for y in range(2):
                    pltpu.make_async_copy(
                        below, target.at[y, :, pl.ds(rows, extra)], below_sem
                    ).start()

        @pl.when(step >= 2)
        def _():
            pltpu.make_async_copy(block.at[slot], block.at[slot], sem.at[slot]).wait()

        @pl.when(step < 3)
        def _():
            right = jnp.concatenate([ref[0] for ref in grad_refs], 1)
            block[slot] = dot(tokens_t[...], right, 1, 0).astype(BF)

        @pl.when(step == 3)
        def _():
            left = jnp.concatenate([ref[...] for ref in mixed_refs], 1)
            block[slot] = dot(left, proj_ref[...], 0, 0).astype(BF)

        source = block.at[slot].reshape(owners, rows, D)
        y, core = lax.div(step, 2), lax.rem(step, 2)

        @pl.when(core == me_ref[1])
        def _():
            pltpu.make_async_copy(source, keep.at[y, :, pl.ds(0, rows)], sem.at[slot]).start()

        @pl.when(core != me_ref[1])
        def _():
            pltpu.make_async_copy(source, give.at[y, :, pl.ds(0, rows)], sem.at[slot]).start()

        @pl.when(step == 3)
        def _():
            for s in range(2):
                pltpu.make_async_copy(block.at[s], block.at[s], sem.at[s]).wait()
            for _ in range(4):
                pltpu.make_async_copy(below, below, below_sem).wait()

    def whole(width):
        return pl.BlockSpec((ROW, width), lambda i: (0, 0), pipeline_mode=pl.Buffered(1))

    return pl.pallas_call(
        kernel,
        grid=(4,),
        in_specs=[
            pl.BlockSpec(memory_space=pltpu.SMEM),
            whole(D),
            pl.BlockSpec((extra, D), lambda i: (0, 0)),
            whole(D),
        ]
        + [whole(2 * HEAD * p) for p in AHEAD_PAIRS]
        + [pl.BlockSpec((1, ROW, 2 * HEAD * p), lambda i: (jnp.minimum(i, 2), 0, 0)) for p in PAIRS]
        + [pl.BlockSpec(memory_space=pl.ANY)] * len(after),
        out_specs=[pl.BlockSpec(memory_space=pl.ANY)] * 2,
        out_shape=[shape] * 2,
        scratch_shapes=[
            pltpu.VMEM((D, ROW), BF),
            pltpu.VMEM((2, D, D), BF),
            pltpu.VMEM((owners, extra, D), BF),
            pltpu.SemaphoreType.DMA((2,)),
            pltpu.SemaphoreType.DMA,
        ],
        compiler_params=pltpu.CompilerParams(vmem_limit_bytes=TERMS_VMEM),
        cost_estimate=cost(6),
        name="attn_terms",
    )(me, tokens, vectors, grad_proj, *mixed, *grads, *after)


def token_grad_kernel(resid, weights, *refs):
    out = refs[-1]
    total = resid[...]
    for m in range(3):
        grad = jnp.concatenate([ref[m] for ref in refs[: len(PAIRS)]], 1)
        total = total + dot(grad, weights[m * D : (m + 1) * D], 1, 1)
    out[...] = total.astype(BF)


def token_gradient(resid, weights, grads, after):
    step = 256
    tile = pl.BlockSpec((step, D), lambda i: (i, 0))
    return pl.pallas_call(
        token_grad_kernel,
        grid=(ROW // step,),
        in_specs=[tile, pl.BlockSpec((3 * D, D), lambda i: (0, 0), pipeline_mode=pl.Buffered(1))]
        + [pl.BlockSpec((3, step, 2 * HEAD * p), lambda i: (0, i, 0)) for p in PAIRS]
        + [pl.BlockSpec(memory_space=pl.ANY)] * len(after),
        out_specs=tile,
        out_shape=jax.ShapeDtypeStruct((ROW, D), BF),
        compiler_params=pltpu.CompilerParams(vmem_limit_bytes=TOKEN_VMEM),
        cost_estimate=cost(2),
        name="token_grad",
    )(resid, weights, *grads, *after)


def adam_update(param, gradient, moment, square, shadow):
    step_float = float(STEP)
    moment_next = MOMENT_DECAY * moment + (1.0 - MOMENT_DECAY) * gradient
    square_next = SQUARE_DECAY * square + (1.0 - SQUARE_DECAY) * gradient * gradient
    moment_hat = moment_next / (1.0 - MOMENT_DECAY**step_float)
    square_hat = square_next / (1.0 - SQUARE_DECAY**step_float)
    change = -LEARN_RATE * (
        moment_hat / (jnp.sqrt(square_hat) + ADAM_EPSILON) + WEIGHT_DECAY * param
    )
    updated = param + change
    drift = (1.0 - SHADOW_RATE) * (updated - shadow)
    return (change, moment_next, square_next, drift)


def contract_rows(left, right):
    return dot(left, right, 0, 0)


def on_device(
    places,
    tokens,
    segments,
    counts,
    out_grad,
    attn_param,
    attn_moment,
    attn_square,
    attn_shadow,
    ffn_param,
    ffn_moment,
    ffn_square,
    ffn_shadow,
):
    assert counts.shape[0] == 1 and tokens.shape[0] == ROW
    number = places.count
    here = places.here()
    place_list = jnp.stack([here[a] for a in ("y", "c", "z", "x")]).astype(jnp.int32)
    me = lax.axis_index("dp") * places.wide + lax.axis_index("wide")
    staged = places.staged()
    attn_rows, ffn_rows = ATTN_ROWS // number, FFN_ROWS // number
    up_rows = ffn_rows // UP_CHUNKS
    holds_up = me < number // 2

    last = me == number - 1
    ends = jnp.concatenate([attn_param[-ATTN_TAIL:], ffn_param[-FFN_TAIL:]]).astype(BF)
    ends = jnp.where(last, ends, jnp.zeros_like(ends))
    if staged:
        digits = [lax.rem(lax.shift_right_logical(counts[0], 3 * i), 8) for i in range(4)]
        count_row = jnp.concatenate([jnp.stack(digits).astype(BF), jnp.zeros((D - 4,), BF)])
        filler = jnp.zeros(((VEC_ROWS - COUNT_ROW - 1) * D,), BF)
        extra = jnp.concatenate([ends, count_row, filler]).reshape(VEC_ROWS, D)
        attn_own = to_rows(places, me, attn_param, ATTN_ROWS, ATTN_TAIL).astype(BF)
        attn_set = Gathered(places, attn_rows)
        blocks = attn_set.start_z(jnp.concatenate([attn_own, extra], 0))
        ffn_own = to_rows(places, me, order(ffn_param, blocks[1]), FFN_ROWS, FFN_TAIL).astype(BF)
        by_chunk = ffn_own.reshape(up_rows, UP_CHUNKS, D).transpose(1, 0, 2).reshape(ffn_rows, D)
        ffn_own = jnp.where(holds_up, by_chunk, ffn_own)
        column = attn_set.join_z(here, blocks)
        half_rows = ffn_rows // 2
        ffn_set = Gathered(places, half_rows)
        blocks = ffn_set.start_z(order(ffn_own[:half_rows], column))
        near = [ffn_set.join_parts(place_list, [blocks])]
        plane = order(attn_set.along_first(column), *blocks)
        blocks = ffn_set.start_z(order(ffn_own[half_rows:], plane, near[0]))
        aside = [places.send(near[0], "xy", 1)]
        crossed = [places.send(near[0], "c", 1)]
        groups = [plane]
        groups += [order(g, aside[0], *blocks) for g in attn_set.along_second(plane)]
        attn_groups = groups + attn_set.from_core(groups)
        near.append(ffn_set.join_parts(place_list, [blocks]))
        aside.append(places.send(near[1], "xy", 1))
        across = [places.send(near[0], "yx", 1)]
        corner = [places.send(aside[0], "yx", 1)]
        query, key, value, vec, attn_whole = project(
            tokens, place_list, attn_set, attn_groups, [aside[0], near[1], crossed[0]]
        )
        token_total = sum(vec[COUNT_ROW, i] * float(8**i) for i in range(4))
        aside = [order(a, query) for a in aside]
        near[1] = order(near[1], query)
        crossed += [places.send(near[1], "c", 1)] + [places.send(a, "c", 1) for a in aside]
        across.append(places.send(near[1], "yx", 1))
        corner.append(places.send(aside[1], "yx", 1))
        extent = places.size
        per_half = UP_CHUNKS // 2
        piece = (extent["z"], per_half, up_rows, D)
        half = extent["y"] // 2

        def fetch(place, refs, weights, sem):
            side = (half, 2, extent["z"], extent["x"])
            up = weights.at[pl.ds(0, FF)].reshape(*((UP_CHUNKS,) + side + (up_rows, D)))
            down = weights.at[pl.ds(FF, FF)].reshape(*(side + (UP_CHUNKS, up_rows, D)))
            ways = [(far, i, j) for far in range(2) for i in range(2) for j in range(2)]
            for i, ref in enumerate(refs):
                h, way = divmod(i, len(ways))
                y, core, x = ffn_set.place(place, *ways[way])

                @pl.when(y < half)
                def _():
                    for part in range(per_half):
                        chunk = h * per_half + part
                        pltpu.make_async_copy(
                            ref.at[:, part], up.at[chunk, y, core, :, x], sem.at[chunk]
                        ).start()

                @pl.when(y >= half)
                def _():
                    chunks = pl.ds(h * per_half, per_half)
                    pltpu.make_async_copy(
                        ref, down.at[y - half, core, :, x, chunks], sem.at[UP_CHUNKS]
                    ).start()

    else:
        token_total = lax.psum(counts[0].astype(F32), AXES)
        vec = lax.psum(ends.astype(F32), AXES).reshape(COUNT_ROW, D)
        vec = jnp.concatenate([vec, jnp.zeros((VEC_ROWS - COUNT_ROW, D), F32)], 0)
        flat = lax.all_gather(attn_param.astype(BF), AXES, axis=0, tiled=True)
        attn_whole = flat[: ATTN_ROWS * D].reshape(ATTN_ROWS, D)
        flat = lax.all_gather(ffn_param.astype(BF), AXES, axis=0, tiled=True)
        w_up = flat[: FF * D].reshape(D, UP_CHUNKS, D).transpose(1, 0, 2).reshape(FF, D)
        w_down = flat[FF * D : FFN_ROWS * D].reshape(FF, D)
        sources = [w_up, w_down]

        def fetch(place, refs, weights, sem):
            w_up, w_down = refs
            for j in range(UP_CHUNKS):
                rows = pl.ds(j * D, D)
                pltpu.make_async_copy(w_up.at[rows], weights.at[rows], sem.at[j]).start()
            down = weights.at[pl.ds(FF, FF)]
            pltpu.make_async_copy(w_down, down, sem.at[UP_CHUNKS]).start()

        query, key, value = project_whole(tokens, attn_whole, vec)

    ahead = []
    for i, pairs in enumerate(AHEAD_PAIRS):
        after = [aside[1]] if staged and i == 0 else []
        first = sum(AHEAD_PAIRS[:i])
        ahead.append(attend(query, key, value, segments, counts, first, pairs, after))
    mixed = [a[0] for a in ahead]
    log_total = jnp.concatenate([a[1] for a in ahead], 0)
    if staged:
        sources = []
        for h in range(2):
            across[h], corner[h] = order(across[h], mixed[h]), order(corner[h], mixed[h])
            mine = [near[h], across[h], aside[h], corner[h]]
            theirs = [crossed[h], places.send(across[h], "c", 1)]
            theirs += [crossed[2 + h], places.send(corner[h], "c", 1)]
            sources += [a.reshape(piece) for a in mine + theirs]
    (
        final_low,
        hidden_low,
        activated,
        grad_pre,
        grad_ffn_out,
        grad_attn_out,
        grad_mixed,
        grad_resid,
        vec_grad,
        crop_sums,
    ) = middle(
        counts,
        place_list,
        segments,
        mixed,
        tokens,
        out_grad,
        attn_whole,
        sources,
        fetch,
        vec,
    )
    is_valid = jnp.arange(ROW, dtype=jnp.int32) < counts[0]
    member = (segments[None, :] == jnp.arange(CROPS, dtype=jnp.int32)[:, None]) & is_valid[None, :]
    crop_sizes = jnp.sum(member.astype(F32), axis=1)
    pooled = crop_sums / jnp.maximum(crop_sizes, 1.0)[:, None]

    def back(i, after, micros):
        return attend_back(
            query,
            key,
            value,
            grad_mixed,
            log_total,
            segments,
            counts,
            sum(PAIRS[:i]),
            PAIRS[i],
            after,
            micros,
        )

    if staged:
        ffn_sums, attn_sums = Scattered(places, place_list, 1.2), Scattered(places, place_list, 0.5)

        def spread(terms):
            return terms.reshape(2, extent["z"], extent["x"], *terms.shape[2:])

        def ffn_side(thirds, after):
            operands = (hidden_low, activated, grad_pre, grad_ffn_out)
            terms = ffn_terms(places, place_list, *operands, thirds, after)
            return [spread(t) for t in terms]

        keep_a, give_a = ffn_side([0, 1, 2], [])
        core_a = ffn_sums.core(give_a)
        back_0 = back(0, [give_a], 12)
        own_a, cut_a = ffn_sums.first(keep_a, order(core_a, back_0[0]))
        first_a = ffn_sums.send(cut_a)
        back_1 = back(1, [cut_a], 15)
        vectors = jnp.concatenate([back_0[1], back_1[1]], 1)[:2]
        vec_grad = jnp.concatenate([vectors, vec_grad[2:]], 0)
        grads = [back_0[0], back_1[0]]
        operands = (tokens, mixed, grads, grad_attn_out, vec_grad)
        terms = attn_terms(places, place_list, *operands, [])
        keep_c, give_c = [spread(t) for t in terms]
        core_c = attn_sums.core(give_c)
        own_a, cut_a = ffn_sums.second(own_a, order(first_a, give_c))
        second_a = ffn_sums.send_second(cut_a)
        token_grad = token_gradient(grad_resid, attn_whole, grads, [give_c, cut_a])
        own_c, cut_c = attn_sums.first(keep_c, order(core_c, token_grad))
        own_a, cuts_a = ffn_sums.along_z(own_a, order(second_a, cut_c))
        up_z_a = ffn_sums.send_z(cuts_a)
        first_c = attn_sums.send(cut_c, *cuts_a)
        own_c, cut_c = attn_sums.second(own_c, order(first_c, up_z_a[1]))
        second_c = attn_sums.send_second(cut_c)
        own_c, cuts_c = attn_sums.along_z(own_c, second_c)
        up_z_c = attn_sums.send_z(cuts_c)
        ffn_block = ffn_sums.result(own_a, up_z_a)
        block_c = attn_sums.result(own_c, up_z_c)
        attn_block, vec_sum = block_c[:attn_rows], block_c[attn_rows:]
        by_row = ffn_block.reshape(UP_CHUNKS, up_rows, D).transpose(1, 0, 2).reshape(ffn_rows, D)
        ffn_block = jnp.where(holds_up, by_row, ffn_block)
        ffn_summed = to_flat(places, me, ffn_block, vec_sum[5:12], FFN_TAIL)
        attn_summed = to_flat(places, me, attn_block, vec_sum[:5], ATTN_TAIL)
    else:
        backs = [back(i, [], 12) for i in range(len(PAIRS))]
        grads = [b[0] for b in backs]
        token_grad = token_gradient(grad_resid, attn_whole, grads, [])
        grads = jnp.concatenate(grads, 2)
        mats = [contract_rows(tokens, grads[i]) for i in range(3)]
        mats.append(contract_rows(jnp.concatenate(mixed, 1), grad_attn_out))
        vectors = jnp.concatenate([b[1] for b in backs], 1)[:2]
        vec_grad = jnp.concatenate([vectors, vec_grad[2:]], 0)
        attn_full = jnp.concatenate([g.reshape(-1) for g in mats + [vec_grad[:5]]])
        up = contract_rows(hidden_low, grad_pre)
        down = contract_rows(activated, grad_ffn_out)
        ffn_full = jnp.concatenate([g.reshape(-1) for g in (up, down, vec_grad[5:12])])
        attn_summed = lax.psum_scatter(attn_full, AXES, scatter_dimension=0, tiled=True)
        ffn_summed = lax.psum_scatter(ffn_full, AXES, scatter_dimension=0, tiled=True)
    attn_grad = attn_summed / token_total
    ffn_grad = ffn_summed / token_total
    attn_change, moment_attn, square_attn, drift_attn = adam_update(
        attn_param, attn_grad, attn_moment, attn_square, attn_shadow
    )
    ffn_change, moment_ffn, square_ffn, drift_ffn = adam_update(
        ffn_param, ffn_grad, ffn_moment, ffn_square, ffn_shadow
    )
    return (
        final_low,
        pooled,
        token_grad,
        attn_grad,
        ffn_grad,
        attn_change,
        ffn_change,
        moment_attn,
        moment_ffn,
        square_attn,
        square_ffn,
        drift_attn,
        drift_ffn,
    )


def solution(mesh):
    rows, flat = P(AXES, None), P(AXES)
    return jax.shard_map(
        functools.partial(on_device, Places(mesh)),
        mesh=mesh,
        in_specs=(rows, flat, flat, rows) + (flat,) * 8,
        out_specs=(rows, rows, rows) + (flat,) * 10,
        check_vma=False,
    )
```

```python
import functools

import jax
import jax.numpy as jnp
from jax import lax
from jax.experimental import pallas as pl
from jax.experimental.pallas import tpu as pltpu
from jax.sharding import PartitionSpec as P

D = 768
FF = 3072
HEAD = 64
HEADS = 12
ROW = 1024
STEP = 10
CROPS = 16

NORM_EPSILON = 1e-12
NEGATIVE = -1e30
MOMENT_DECAY = 0.9
SQUARE_DECAY = 0.999
LEARN_RATE = 0.001
WEIGHT_DECAY = 0.01
ADAM_EPSILON = 1e-08
SHADOW_RATE = 0.9995
SCALE = HEAD ** (-0.5)

AXES = ("dp", "wide")
BF = jnp.bfloat16
F32 = jnp.float32
UP_CHUNKS = FF // D
ATTN_ROWS = 4 * D
FFN_ROWS = 2 * FF
ATTN_TAIL = 5 * D
FFN_TAIL = FF + 3 * D
AHEAD_PAIRS = (2, 2, 2)
PAIRS = (2, 4)
VEC_ROWS = 16
COUNT_ROW = 12
MIB = 1 << 20
BACK_VMEM = 24 * MIB
TERMS_VMEM = 24 * MIB
TOKEN_VMEM = 24 * MIB
FFN_VMEM = 56 * MIB
ADD_VMEM = 24 * MIB


def dot(left, right, left_dim, right_dim):
    return lax.dot_general(
        left, right, (((left_dim,), (right_dim,)), ((), ())), preferred_element_type=F32
    )


class Places:
    def __init__(self, mesh):
        self.dp, self.wide = mesh.shape["dp"], mesh.shape["wide"]
        self.count = self.dp * self.wide
        self.size = {"c": 2, "y": self.dp // 2}
        self.size["x"] = self.size["y"]
        self.size["z"] = self.wide // self.size["x"]

    def staged(self):
        exact = self.dp == 4 and self.wide % self.size["x"] == 0
        return exact and D % (16 * UP_CHUNKS * self.wide // 2) == 0

    def index(self, y, c, z, x):
        return (y * 2 + c) * self.wide + z * self.size["x"] + x

    def rotation(self, axis, step):
        pairs = []
        extent = self.size
        for y in range(extent["y"]):
            for c in range(2):
                along = axis if len(axis) == 1 else axis[c]
                for z in range(extent["z"]):
                    for x in range(extent["x"]):
                        at = {"y": y, "c": c, "z": z, "x": x}
                        to = dict(at)
                        to[along] = (at[along] + step) % extent[along]
                        pairs.append((self.index(**at), self.index(**to)))
        return pairs

    def send(self, array, axis, step):
        return lax.ppermute(array, AXES, self.rotation(axis, step))

    def here(self):
        outer, inner = lax.axis_index("dp"), lax.axis_index("wide")
        extent = self.size["x"]
        return {"y": outer // 2, "c": outer % 2, "z": inner // extent, "x": inner % extent}


def order(array, *before):
    return lax.optimization_barrier((array,) + before)[0]


class Gathered:
    def __init__(self, places, rows):
        self.places, self.rows = places, rows
        self.deep = places.size["z"] * rows

    def start_z(self, own):
        extent = self.places.size["z"]
        return [own] + [self.places.send(own, "z", k) for k in range(1, extent)]

    def join_z(self, here, blocks):
        rows, extent = self.rows, self.places.size["z"]
        near = jnp.zeros((self.deep, D), BF)
        for k, block in enumerate(blocks):
            at = lax.rem(here["z"] + (extent - k), extent) * rows
            near = lax.dynamic_update_slice_in_dim(near, block[:rows], at, 0)
        return jnp.concatenate([near, self.total([b[rows:] for b in blocks])], 0)

    def join_parts(self, me, parts):
        extent, count = self.places.size["z"], len(parts)
        share = self.rows // count

        def kernel(me_ref, *refs):
            out, sem = refs[-2:]
            for p in range(count):
                for k in range(extent):
                    at = lax.rem(me_ref[2] + (extent - k), extent)
                    pltpu.make_async_copy(
                        refs[p * extent + k], out.at[at, pl.ds(p * share, share)], sem
                    ).start()
            pltpu.make_async_copy(out, out, sem).wait()

        blocks = [b for part in parts for b in part]
        return pl.pallas_call(
            kernel,
            in_specs=[pl.BlockSpec(memory_space=pltpu.SMEM)]
            + [pl.BlockSpec(memory_space=pl.ANY)] * len(blocks),
            out_specs=pl.BlockSpec(memory_space=pltpu.VMEM),
            out_shape=jax.ShapeDtypeStruct((extent, self.rows, D), BF),
            scratch_shapes=[pltpu.SemaphoreType.DMA],
            compiler_params=pltpu.CompilerParams(vmem_limit_bytes=16 * MIB),
            cost_estimate=cost(2),
            name="join",
        )(me, *blocks).reshape(self.deep, D)

    def along_first(self, near):
        places, extent = self.places, self.places.size
        blocks = [near] + [places.send(near, "xy", k) for k in range(1, extent["x"])]
        parts = [b[: self.deep] for b in blocks]
        if near.shape[0] > self.deep:
            parts.append(self.total([b[self.deep :] for b in blocks]))
        return jnp.concatenate(parts, 0)

    def along_second(self, near):
        return [self.places.send(near, "yx", k) for k in range(1, self.places.size["x"])]

    def from_core(self, groups):
        return [self.places.send(g, "c", 1) for g in groups]

    def total(self, arrays):
        result = arrays[0].astype(F32)
        for a in arrays[1:]:
            result = result + a.astype(F32)
        return result.astype(BF)

    def place(self, here, far, first, second):
        extent = self.places.size

        def back(axis, step):
            return lax.rem(here[axis] + (extent[axis] - step), extent[axis])

        core = here["c"] if far == 0 else 1 - here["c"]
        y = jnp.where(core == 0, back("y", second), back("y", first))
        x = jnp.where(core == 0, back("x", first), back("x", second))
        return y, core, x


def read_here(me_ref):
    return {"y": me_ref[0], "c": me_ref[1], "z": me_ref[2], "x": me_ref[3]}


def add_routed(me, keep, arrived, grid, routes, source_block, target_block, target_lead, micros):
    rows, width = keep.shape[-2:]

    def kernel(me_ref, *refs):
        for i in range(len(routes)):
            total = refs[2 * i][...].astype(F32) + refs[2 * i + 1][...].astype(F32)
            refs[2 * len(routes) + i][...] = total.astype(BF)

    def source(route):
        return pl.BlockSpec(source_block + (rows, width), lambda *at: route(*at) + (0, 0))

    target = pl.BlockSpec(target_block[0] + (rows, width), lambda *at: target_block[1](*at) + (0, 0))
    return pl.pallas_call(
        kernel,
        grid_spec=pltpu.PrefetchScalarGridSpec(
            num_scalar_prefetch=1,
            grid=grid,
            in_specs=[source(r) for r in routes for _ in range(2)],
            out_specs=[target] * len(routes),
        ),
        out_shape=[jax.ShapeDtypeStruct(target_lead + (rows, width), BF)] * len(routes),
        compiler_params=pltpu.CompilerParams(vmem_limit_bytes=ADD_VMEM),
        cost_estimate=cost(micros),
        name="add_routed",
    )(me, *([keep, arrived] * len(routes)))


class Scattered:
    def __init__(self, places, me, micros):
        self.places, self.me, self.micros = places, me, micros
        self.z = places.size["z"]

    def core(self, give):
        return self.places.send(give, "c", 1)

    def first(self, keep, arrived):
        deep = 2

        def route(far):
            def pick_block(z, e, me):
                y, x = jnp.abs(me[0] - far), jnp.abs(me[3] - far)
                return jnp.where(me[1] == 0, e, y), z, jnp.where(me[1] == 0, x, e)

            return pick_block

        own, cut = add_routed(
            self.me,
            keep,
            arrived,
            (self.z // deep, 2),
            [route(0), route(1)],
            (None, deep, None),
            ((deep, None), lambda z, e, me: (z, e)),
            (self.z, 2),
            4 * self.micros,
        )
        return own, cut

    def second(self, keep, arrived):
        deep = 2

        def route(far):
            return lambda z, me: (z, jnp.abs(jnp.where(me[1] == 0, me[0], me[3]) - far))

        own, cut = add_routed(
            self.me,
            keep,
            arrived,
            (self.z // deep,),
            [route(0), route(1)],
            (deep, None),
            ((deep,), lambda z, me: (z,)),
            (self.z,),
            2 * self.micros,
        )
        return own, cut

    def along_z(self, keep, arrived):
        def route(k):
            return lambda i, me: (lax.rem(me[2] + k, self.z),)

        own, *cuts = add_routed(
            self.me,
            keep,
            arrived,
            (1,),
            [route(k) for k in range(self.z)],
            (None,),
            ((None,), lambda i, me: (0,)),
            (1,),
            self.micros,
        )
        return own, cuts

    def send(self, cut, *before):
        return self.places.send(order(cut, *before), "xy", 1)

    def send_second(self, cut, *before):
        return self.places.send(order(cut, *before), "yx", 1)

    def send_z(self, cuts, *before):
        return [self.places.send(order(c, *before), "z", k + 1) for k, c in enumerate(cuts)]

    def result(self, own, arrived):
        total = own[0].astype(F32)
        for a in arrived:
            total = total + a[0].astype(F32)
        return total


def to_rows(places, me, flat, rows, tail):
    count = places.count
    block = rows // count * D
    slack = tail // count
    before = lax.ppermute(flat[-tail:], AXES, [(i, i + 1) for i in range(count - 1)])
    joined = jnp.concatenate([before, flat])
    return lax.dynamic_slice_in_dim(joined, tail - me * slack, block).reshape(rows // count, D)


def to_flat(places, me, block, vectors, tail):
    count = places.count
    slack = tail // count
    after = lax.ppermute(block[: tail // D], AXES, [(i + 1, i) for i in range(count - 1)])
    after = jnp.where(me == count - 1, vectors, after)
    joined = jnp.concatenate([block, after], 0).reshape(-1)
    return lax.dynamic_slice_in_dim(joined, me * slack, block.size + slack)


def project_body(step, tokens, weights, vec, query, key, value):
    held = tokens[...]
    query[...] = (dot(held, weights[0:D], 1, 0) + vec[0:1]).astype(BF)
    key[...] = dot(held, weights[D : 2 * D], 1, 0).astype(BF)
    value[...] = (dot(held, weights[2 * D : 3 * D], 1, 0) + vec[1:2]).astype(BF)


def project_kernel(gathered, number, after, me, tokens, *refs):
    groups = refs[:number]
    query, key, value, vec, whole, weights, extras, sem, extra_sem, out_sem = refs[number + after :]
    step = pl.program_id(0)
    extent = gathered.places.size
    rows, deep = gathered.rows, gathered.rows * extent["z"]

    @pl.when(step == 0)
    def _():
        here = read_here(me)
        for g, ref in enumerate(groups):
            pltpu.make_async_copy(
                ref.at[pl.ds(extent["x"] * deep, VEC_ROWS)], extras.at[g], extra_sem
            ).start()
        shape = (extent["y"], 2, extent["z"], extent["x"], rows, D)
        for g, ref in enumerate(groups):
            far, second = divmod(g, extent["x"])
            for first in range(extent["x"]):
                y, core, x = gathered.place(here, far, first, second)
                pltpu.make_async_copy(
                    ref.at[pl.ds(first * deep, deep)].reshape(extent["z"], rows, D),
                    weights.reshape(*shape).at[y, core, :, x],
                    sem,
                ).start()
        pltpu.make_async_copy(extras, extras, extra_sem).wait()
        total = extras[0].astype(F32)
        for g in range(1, number):
            total = total + extras[g].astype(F32)
        vec[...] = total
        pltpu.make_async_copy(weights, weights, sem).wait()
        pltpu.make_async_copy(weights, whole, out_sem).start()

    project_body(step, tokens, weights, vec, query, key, value)

    @pl.when(step == pl.num_programs(0) - 1)
    def _():
        pltpu.make_async_copy(weights, whole, out_sem).wait()


PROJECT_ROWS = 256


def project(tokens, me, gathered, groups, after):
    rows = tokens.shape[0]
    tile = pl.BlockSpec((PROJECT_ROWS, D), lambda i: (i, 0))
    number = len(groups)
    return pl.pallas_call(
        functools.partial(project_kernel, gathered, number, len(after)),
        grid=(rows // PROJECT_ROWS,),
        in_specs=[pl.BlockSpec(memory_space=pltpu.SMEM), tile]
        + [pl.BlockSpec(memory_space=pl.ANY)] * (number + len(after)),
        out_specs=[tile] * 3
        + [pl.BlockSpec((VEC_ROWS, D), lambda i: (0, 0)), pl.BlockSpec(memory_space=pl.ANY)],
        out_shape=[jax.ShapeDtypeStruct((rows, D), BF)] * 3
        + [jax.ShapeDtypeStruct((VEC_ROWS, D), F32), jax.ShapeDtypeStruct((ATTN_ROWS, D), BF)],
        scratch_shapes=[
            pltpu.VMEM((ATTN_ROWS, D), BF),
            pltpu.VMEM((number, VEC_ROWS, D), BF),
            pltpu.SemaphoreType.DMA,
            pltpu.SemaphoreType.DMA,
            pltpu.SemaphoreType.DMA,
        ],
        compiler_params=pltpu.CompilerParams(vmem_limit_bytes=24 * MIB),
        cost_estimate=cost(8),
        name="project",
    )(me, tokens, *groups, *after)


def project_whole(tokens, weights, vec):
    rows = tokens.shape[0]
    tile = pl.BlockSpec((PROJECT_ROWS, D), lambda i: (i, 0))
    return pl.pallas_call(
        lambda *refs: project_body(None, *refs),
        grid=(rows // PROJECT_ROWS,),
        in_specs=[
            tile,
            pl.BlockSpec((ATTN_ROWS, D), lambda i: (0, 0), pipeline_mode=pl.Buffered(1)),
            pl.BlockSpec((VEC_ROWS, D), lambda i: (0, 0)),
        ],
        out_specs=[tile] * 3,
        out_shape=[jax.ShapeDtypeStruct((rows, D), BF)] * 3,
        compiler_params=pltpu.CompilerParams(vmem_limit_bytes=24 * MIB),
        name="project",
    )(tokens, weights, vec)


QUERY_BLOCK = 256
QUERY_BLOCKS = ROW // QUERY_BLOCK


def window(block):
    low = max(0, block - 1) * QUERY_BLOCK
    return low, min(QUERY_BLOCKS, block + 2) * QUERY_BLOCK


def fill_bias(bias, seg_column, seg_row, count):
    for block in range(QUERY_BLOCKS):
        low, high = window(block)
        at = slice(block * QUERY_BLOCK, (block + 1) * QUERY_BLOCK)
        shape = (high - low, QUERY_BLOCK)
        key_pos = low + lax.broadcasted_iota(jnp.int32, shape, 0)
        query_pos = block * QUERY_BLOCK + lax.broadcasted_iota(jnp.int32, shape, 1)
        same = seg_column[low:high, 0:1] == seg_row[0:1, at]
        allowed = (same & (key_pos < count)) | (key_pos == query_pos)
        bias[0 : high - low, at] = jnp.where(allowed, 0.0, NEGATIVE).astype(F32)


def one_head(transposed):
    zero = jnp.zeros((HEAD, transposed.shape[1]), transposed.dtype)
    return (
        jnp.concatenate([transposed[:HEAD], zero], 0),
        jnp.concatenate([zero, transposed[HEAD:]], 0),
    )


def attend_kernel(count, seg_column, seg_row, query, key, value, *refs):
    mixed, log_total, bias = refs[-3:]

    @pl.when(pl.program_id(0) == 0)
    def _():
        fill_bias(bias, seg_column, seg_row, count[0])

    value_t = value[...].T
    query_t = one_head((query[...] * jnp.asarray(SCALE, BF)).T)
    parts = []

    def score(block, h):
        low, high = window(block)
        at = slice(block * QUERY_BLOCK, (block + 1) * QUERY_BLOCK)
        return dot(key[low:high, :], query_t[h][:, at], 1, 0) + bias[0 : high - low, at]

    def mix(block, h, shifted, inverse):
        low, high = window(block)
        at = slice(block * QUERY_BLOCK, (block + 1) * QUERY_BLOCK)
        part = dot(value_t[h * HEAD : (h + 1) * HEAD, low:high], shifted, 1, 0)
        parts.append(part * inverse)
        if h == 1:
            mixed[at, :] = jnp.concatenate(parts, 0).T.astype(BF)
            parts.clear()

    items = [(block, h) for block in range(QUERY_BLOCKS) for h in range(2)]
    ahead, behind = score(*items[0]), None
    for n, (block, h) in enumerate(items):
        at = slice(block * QUERY_BLOCK, (block + 1) * QUERY_BLOCK)
        scores = ahead
        if n + 1 < len(items):
            ahead = score(*items[n + 1])
        if behind is not None:
            mix(*behind)
        top = jnp.max(scores, axis=0, keepdims=True)
        shifted = jnp.exp(scores - top)
        total = jnp.sum(shifted, axis=0, keepdims=True)
        log_total[0, h : h + 1, at] = top + jnp.log(total)
        behind = (block, h, shifted.astype(BF), 1.0 / total)
    mix(*behind)


def attend_specs():
    return [
        pl.BlockSpec(memory_space=pltpu.SMEM),
        pl.BlockSpec((ROW, 1), lambda h: (0, 0)),
        pl.BlockSpec((1, ROW), lambda h: (0, 0)),
    ]


def attend(query, key, value, segments, count, first, pairs, after):
    pair = pl.BlockSpec((ROW, 2 * HEAD), lambda h: (0, h + first))
    return pl.pallas_call(
        attend_kernel,
        grid=(pairs,),
        in_specs=attend_specs() + [pair] * 3 + [pl.BlockSpec(memory_space=pl.ANY)] * len(after),
        out_specs=[
            pl.BlockSpec((ROW, 2 * HEAD), lambda h: (0, h)),
            pl.BlockSpec((1, 8, ROW), lambda h: (h, 0, 0)),
        ],
        out_shape=[
            jax.ShapeDtypeStruct((ROW, pairs * 2 * HEAD), BF),
            jax.ShapeDtypeStruct((pairs, 8, ROW), F32),
        ],
        scratch_shapes=[pltpu.VMEM((3 * QUERY_BLOCK, ROW), F32)],
        compiler_params=pltpu.CompilerParams(vmem_limit_bytes=24 * MIB),
        cost_estimate=cost(25 * pairs / 6),
        name="attend",
    )(count, segments.reshape(ROW, 1), segments.reshape(1, ROW), query, key, value, *after)


def attend_back_kernel(
    count, seg_column, seg_row, query, key, value, grad, log_total, *refs
):
    grads, sums, bias, key_sum, value_sum = refs[-5:]

    @pl.when(pl.program_id(0) == 0)
    def _():
        fill_bias(bias, seg_column, seg_row, count[0])

    query_t = (query[...] * jnp.asarray(SCALE, BF)).T
    key_t = key[...].T
    grad_t = grad[...].T
    query_one, grad_one = one_head(query_t), one_head(grad_t)
    key_sum[...] = jnp.zeros_like(key_sum)
    value_sum[...] = jnp.zeros_like(value_sum)
    parts = []

    def score(block, h):
        low, high = window(block)
        at = slice(block * QUERY_BLOCK, (block + 1) * QUERY_BLOCK)
        scores = dot(key[low:high, :], query_one[h][:, at], 1, 0) + bias[0 : high - low, at]
        return scores, dot(value[low:high, :], grad_one[h][:, at], 1, 0)

    def spread(block, h, grad_scores, probs):
        low, high = window(block)
        at = slice(block * QUERY_BLOCK, (block + 1) * QUERY_BLOCK)
        rows = slice(h * HEAD, (h + 1) * HEAD)
        parts.append(dot(key_t[rows, low:high], grad_scores, 1, 0))
        key_sum[rows, low:high] += dot(query_t[rows, at], grad_scores, 1, 1)
        value_sum[rows, low:high] += dot(grad_t[rows, at], probs, 1, 1)
        if h == 1:
            grads[0, at, :] = (jnp.concatenate(parts, 0) * SCALE).T.astype(BF)
            parts.clear()

    items = [(block, h) for block in range(QUERY_BLOCKS) for h in range(2)]
    ahead, behind = score(*items[0]), None
    for n, (block, h) in enumerate(items):
        at = slice(block * QUERY_BLOCK, (block + 1) * QUERY_BLOCK)
        scores, grad_probs = ahead
        if n + 1 < len(items):
            ahead = score(*items[n + 1])
        if behind is not None:
            spread(*behind)
        probs = jnp.exp(scores - log_total[0, h : h + 1, at])
        weighted = probs * grad_probs
        total = jnp.sum(weighted, axis=0, keepdims=True)
        behind = (block, h, (weighted - probs * total).astype(BF), probs.astype(BF))
    spread(*behind)
    grads[1] = key_sum[...].T.astype(BF)
    grads[2] = value_sum[...].T.astype(BF)
    sums[...] = jnp.zeros_like(sums)
    sums[0:1] = column_sum(grads[0].astype(F32))
    sums[1:2] = column_sum(grads[2].astype(F32))


def attend_back(query, key, value, grad, log_total, segments, count, first, pairs, after, micros):
    pair = pl.BlockSpec((ROW, 2 * HEAD), lambda h: (0, h + first))
    return pl.pallas_call(
        attend_back_kernel,
        grid=(pairs,),
        in_specs=attend_specs()
        + [pair] * 4
        + [pl.BlockSpec((1, 8, ROW), lambda h: (h + first, 0, 0))]
        + [pl.BlockSpec(memory_space=pl.ANY)] * len(after),
        out_specs=[
            pl.BlockSpec((3, ROW, 2 * HEAD), lambda h: (0, 0, h)),
            pl.BlockSpec((8, 2 * HEAD), lambda h: (0, h)),
        ],
        out_shape=[
            jax.ShapeDtypeStruct((3, ROW, pairs * 2 * HEAD), BF),
            jax.ShapeDtypeStruct((8, pairs * 2 * HEAD), F32),
        ],
        scratch_shapes=[
            pltpu.VMEM((3 * QUERY_BLOCK, ROW), F32),
            pltpu.VMEM((2 * HEAD, ROW), F32),
            pltpu.VMEM((2 * HEAD, ROW), F32),
        ],
        compiler_params=pltpu.CompilerParams(vmem_limit_bytes=BACK_VMEM),
        cost_estimate=cost(micros),
        name="attend_back",
    )(
        count,
        segments.reshape(ROW, 1),
        segments.reshape(1, ROW),
        query,
        key,
        value,
        grad,
        log_total,
        *after,
    )


def normalise(resid):
    centred = resid - jnp.mean(resid, axis=-1, keepdims=True)
    spread = jnp.mean(centred * centred, axis=-1, keepdims=True)
    inverse = lax.rsqrt(spread + NORM_EPSILON)
    return centred * inverse, inverse


def normalise_back(cotangent, gain, normal, inverse):
    scaled = cotangent * gain
    mean = jnp.mean(scaled, axis=-1, keepdims=True)
    aligned = jnp.mean(scaled * normal, axis=-1, keepdims=True)
    return inverse * (scaled - mean - normal * aligned)


def cost(micros):
    return pl.CostEstimate(flops=int(micros * 1.1e9), bytes_accessed=MIB, transcendentals=0)


def column_sum(array):
    return jnp.sum(array, axis=0, keepdims=True)


MIDDLE_ROWS = 256


def middle_kernel(
    fetch,
    groups,
    count,
    me,
    seg_row,
    tokens,
    out_grad,
    w_out,
    vec,
    *refs,
):
    mixed, refs = refs[: len(AHEAD_PAIRS)], refs[len(AHEAD_PAIRS) :]
    (
        final_low,
        hidden_low,
        activated,
        grad_pre,
        grad_ffn_out,
        grad_attn_out,
        grad_mixed,
        grad_resid,
        vec_grad,
        crop_sums,
        slope,
        hidden_one,
        normals,
        inverses,
        weights,
        sem,
    ) = refs[groups:]
    step = pl.program_id(0)

    def row(i):
        return vec[i : i + 1]

    def chunk(j):
        return weights[j * D : (j + 1) * D]

    def note(i, value):
        vec_grad[i : i + 1] += value

    @pl.when(step == 0)
    def _():
        vec_grad[...] = jnp.zeros_like(vec_grad)
        crop_sums[...] = jnp.zeros_like(crop_sums)
        fetch(read_here(me), refs[:groups], weights, sem)
        for first in range(0, ROW, MIDDLE_ROWS):
            at = slice(first, first + MIDDLE_ROWS)
            held = jnp.concatenate([ref[at] for ref in mixed], 1)
            resid_one = tokens[at].astype(F32) + (dot(held, w_out[...], 1, 0) + row(2))
            normal, inverse = normalise(resid_one)
            hidden = normal * row(3) + row(4)
            hidden_one[at] = hidden
            hidden_low[at] = hidden.astype(BF)
            normals[at] = normal
            inverses[at] = jnp.broadcast_to(inverse, (MIDDLE_ROWS, 128))
        for j in range(UP_CHUNKS):
            part = weights.at[pl.ds(j * D, D)]
            pltpu.make_async_copy(part, part, sem.at[j]).wait()
        part = weights.at[pl.ds(FF, FF)]
        pltpu.make_async_copy(part, part, sem.at[UP_CHUNKS]).wait()

    @pl.when(step > 0)
    def _():
        middle_tile(
            step - 1,
            count,
            seg_row,
            out_grad,
            w_out,
            row,
            chunk,
            note,
            final_low,
            hidden_low,
            activated,
            grad_pre,
            grad_ffn_out,
            grad_attn_out,
            grad_mixed,
            grad_resid,
            crop_sums,
            slope,
            hidden_one,
            normals,
            inverses,
        )


def middle_tile(
    step,
    count,
    seg_row,
    out_grad,
    w_out,
    row,
    chunk,
    note,
    final_low,
    hidden_low,
    activated,
    grad_pre,
    grad_ffn_out,
    grad_attn_out,
    grad_mixed,
    grad_resid,
    crop_sums,
    slope,
    hidden_one,
    normals,
    inverses,
):
    at = pl.ds(pl.multiple_of(step * MIDDLE_ROWS, MIDDLE_ROWS), MIDDLE_ROWS)
    low = hidden_low[at, :]
    total = hidden_one[at, :] + row(9)
    normal_one, inverse_one = normals[at, :], inverses[at, 0:1]
    ahead, act = dot(low, chunk(0), 1, 0), None
    for j in range(UP_CHUNKS):
        at = slice(j * D, (j + 1) * D)
        pre = ahead + row(5 + j)
        if j + 1 < UP_CHUNKS:
            ahead = dot(low, chunk(j + 1), 1, 0)
        if act is not None:
            total = total + dot(act, chunk(UP_CHUNKS + j - 1), 1, 0)
        share = 0.5 + 0.5 * lax.erf(pre * (0.5**0.5))
        density = jnp.exp(-0.5 * pre * pre) * 0.3989422804014327
        slope[:, at] = share + pre * density
        act = (pre * share).astype(BF)
        activated[:, at] = act
    total = total + dot(act, chunk(2 * UP_CHUNKS - 1), 1, 0)
    normal_two, inverse_two = normalise(total)
    final = normal_two * row(10) + row(11)
    final_low[...] = final.astype(BF)

    first = step * MIDDLE_ROWS
    across = (CROPS, MIDDLE_ROWS)
    position = first + lax.broadcasted_iota(jnp.int32, across, 1)
    crop = lax.broadcasted_iota(jnp.int32, across, 0)
    member = ((seg_row[...] == crop) & (position < count[0])).astype(BF)
    high = final.astype(BF)
    rest = final - high.astype(F32)
    mid = rest.astype(BF)
    tiny = (rest - mid.astype(F32)).astype(BF)
    crop_sums[...] += dot(member, high, 1, 0) + (dot(member, mid, 1, 0) + dot(member, tiny, 1, 0))

    position = first + lax.broadcasted_iota(jnp.int32, (MIDDLE_ROWS, 1), 0)
    valid = (position < count[0]).astype(F32)
    cotangent = out_grad[...].astype(F32) * valid
    note(10, column_sum(cotangent * normal_two))
    note(11, column_sum(cotangent))
    grad_two = normalise_back(cotangent, row(10), normal_two, inverse_two)
    grad_out = grad_two.astype(BF)
    grad_ffn_out[...] = grad_out
    note(9, column_sum(grad_out.astype(F32)))
    grad_hidden = grad_two
    ahead, back = dot(grad_out, chunk(UP_CHUNKS), 1, 1), None
    for j in range(UP_CHUNKS):
        at = slice(j * D, (j + 1) * D)
        grad_act = ahead
        if j + 1 < UP_CHUNKS:
            ahead = dot(grad_out, chunk(UP_CHUNKS + j + 1), 1, 1)
        if back is not None:
            grad_hidden = grad_hidden + dot(back, chunk(j - 1), 1, 1)
        back = (grad_act * slope[:, at]).astype(BF)
        grad_pre[:, at] = back
        note(5 + j, column_sum(back.astype(F32)))
    grad_hidden = grad_hidden + dot(back, chunk(UP_CHUNKS - 1), 1, 1)
    note(3, column_sum(grad_hidden * normal_one))
    note(4, column_sum(grad_hidden))
    grad_one = normalise_back(grad_hidden, row(3), normal_one, inverse_one)
    grad_resid[...] = grad_one
    grad_proj = grad_one.astype(BF)
    grad_attn_out[...] = grad_proj
    note(2, column_sum(grad_proj.astype(F32)))
    grad_mixed[...] = dot(grad_proj, w_out[...], 1, 1).astype(BF)


def middle(count, me, segments, mixed, tokens, out_grad, attn_whole, sources, fetch, vec):
    rows = tokens.shape[0]

    def tile_of(i):
        return jnp.maximum(i - 1, 0)

    def whole(width):
        return pl.BlockSpec((rows, width), lambda i: (0, 0), pipeline_mode=pl.Buffered(1))

    tile = pl.BlockSpec((MIDDLE_ROWS, D), lambda i: (tile_of(i), 0))
    wide = pl.BlockSpec((MIDDLE_ROWS, FF), lambda i: (tile_of(i), 0))
    small = pl.BlockSpec((VEC_ROWS, D), lambda i: (0, 0))

    def shape(width, kind):
        return jax.ShapeDtypeStruct((rows, width), kind)

    return pl.pallas_call(
        functools.partial(middle_kernel, fetch, len(sources)),
        grid=(rows // MIDDLE_ROWS + 1,),
        in_specs=[
            pl.BlockSpec(memory_space=pltpu.SMEM),
            pl.BlockSpec(memory_space=pltpu.SMEM),
            pl.BlockSpec((1, MIDDLE_ROWS), lambda i: (0, tile_of(i))),
            whole(D),
            tile,
            pl.BlockSpec((D, D), lambda i: (3, 0), pipeline_mode=pl.Buffered(1)),
            small,
        ]
        + [whole(2 * HEAD * p) for p in AHEAD_PAIRS]
        + [pl.BlockSpec(memory_space=pl.ANY)] * len(sources),
        out_specs=[tile, whole(D), wide, wide, tile, tile, tile, tile, small, small],
        out_shape=[
            shape(D, BF),
            shape(D, BF),
            shape(FF, BF),
            shape(FF, BF),
            shape(D, BF),
            shape(D, BF),
            shape(D, BF),
            shape(D, F32),
            jax.ShapeDtypeStruct((VEC_ROWS, D), F32),
            jax.ShapeDtypeStruct((CROPS, D), F32),
        ],
        scratch_shapes=[
            pltpu.VMEM((MIDDLE_ROWS, FF), F32),
            pltpu.VMEM((rows, D), F32),
            pltpu.VMEM((rows, D), F32),
            pltpu.VMEM((rows, 128), F32),
            pltpu.VMEM((FFN_ROWS, D), BF),
            pltpu.SemaphoreType.DMA((UP_CHUNKS + 1,)),
        ],
        compiler_params=pltpu.CompilerParams(vmem_limit_bytes=40 * MIB),
        cost_estimate=cost(40),
        name="middle",
    )(count, me, segments.reshape(1, rows), tokens, out_grad, attn_whole, vec, *mixed, *sources)


WIDTH = D // 3


def ffn_terms_kernel(shares, me, hidden, activated, *refs):
    pre, out = refs[:shares], refs[shares : 2 * shares]
    keep, give, hidden_t, block, sem = refs[-5:]
    step = pl.program_id(0)
    slot = lax.rem(step, 2)
    owners, rows = keep.shape[1], keep.shape[2]
    up_rows = rows // UP_CHUNKS
    per_chunk = D // rows

    @pl.when(step == 0)
    def _():
        hidden_t[...] = hidden[...].T

    @pl.when(step >= 2)
    def _():
        pltpu.make_async_copy(block.at[slot], block.at[slot], sem.at[slot]).wait()

    def to(core, y, start):
        @pl.when(core == me[1])
        def _():
            start(keep.at[y])

        @pl.when(core != me[1])
        def _():
            start(give.at[y])

    @pl.when(step < UP_CHUNKS)
    def _():
        right = jnp.concatenate([ref[...] for ref in pre], 1)
        block[slot] = dot(hidden_t[...], right, 1, 0).astype(BF)
        for core in range(2):
            source = block.at[slot, pl.ds(core * (D // 2), D // 2)]
            source = source.reshape(owners, up_rows, block.shape[2])

            def start(target):
                at = pl.ds(pl.multiple_of(step * up_rows, 16), up_rows)
                pltpu.make_async_copy(source, target.at[:, at], sem.at[slot]).start()

            to(core, 0, start)

    @pl.when(step >= UP_CHUNKS)
    def _():
        right = jnp.concatenate([ref[...] for ref in out], 1)
        block[slot] = dot(activated[...], right, 0, 0).astype(BF)
        chunk = step - UP_CHUNKS
        source = block.at[slot].reshape(per_chunk, rows, block.shape[2])

        def start(target):
            at = pl.ds(lax.rem(chunk, 2) * per_chunk, per_chunk)
            pltpu.make_async_copy(source, target.at[at], sem.at[slot]).start()

        to(lax.div(chunk, 2), 1, start)

    @pl.when(step == pl.num_programs(0) - 1)
    def _():
        for s in range(2):
            pltpu.make_async_copy(block.at[s], block.at[s], sem.at[s]).wait()


def ffn_terms(places, me, hidden, activated, grad_pre, grad_out, thirds, after):
    owners = places.wide
    rows = FFN_ROWS // places.count
    shares = len(thirds)
    width = shares * WIDTH
    shape = jax.ShapeDtypeStruct((2, owners, rows, width), BF)

    def pre_spec(third):
        return pl.BlockSpec((ROW, WIDTH), lambda i: (0, 3 * jnp.minimum(i, UP_CHUNKS - 1) + third))

    def out_spec(third):
        return pl.BlockSpec((ROW, WIDTH), lambda i: (0, third))

    def kernel(me_ref, hidden_ref, activated_ref, *refs):
        used = refs[: 2 * shares] + refs[2 * shares + len(after) :]
        ffn_terms_kernel(shares, me_ref, hidden_ref, activated_ref, *used)

    return pl.pallas_call(
        kernel,
        grid=(2 * UP_CHUNKS,),
        in_specs=[
            pl.BlockSpec(memory_space=pltpu.SMEM),
            pl.BlockSpec((ROW, D), lambda i: (0, 0), pipeline_mode=pl.Buffered(1)),
            pl.BlockSpec((ROW, D), lambda i: (0, jnp.maximum(i - UP_CHUNKS, 0))),
        ]
        + [pre_spec(t) for t in thirds]
        + [out_spec(t) for t in thirds]
        + [pl.BlockSpec(memory_space=pl.ANY)] * len(after),
        out_specs=[pl.BlockSpec(memory_space=pl.ANY)] * 2,
        out_shape=[shape] * 2,
        scratch_shapes=[
            pltpu.VMEM((D, ROW), BF),
            pltpu.VMEM((2, D, width), BF),
            pltpu.SemaphoreType.DMA((2,)),
        ],
        compiler_params=pltpu.CompilerParams(vmem_limit_bytes=FFN_VMEM),
        cost_estimate=cost(5 * shares),
        name="ffn_terms",
    )(me, hidden, activated, *([grad_pre] * shares), *([grad_out] * shares), *after)


def attn_terms(places, me, tokens, mixed, grads, grad_proj, vectors, after):
    owners = places.wide
    rows = ATTN_ROWS // places.count
    parts, extra = len(AHEAD_PAIRS), vectors.shape[0]
    shape = jax.ShapeDtypeStruct((2, owners, rows + extra, D), BF)

    def kernel(me_ref, tokens_ref, vectors_ref, proj_ref, *refs):
        mixed_refs, grad_refs, refs = refs[:parts], refs[parts : parts + len(PAIRS)], refs[parts + len(PAIRS) :]
        keep, give, tokens_t, block, below, sem, below_sem = refs[len(after) :]
        step = pl.program_id(0)
        slot = lax.rem(step, 2)

        @pl.when(step == 0)
        def _():
            tokens_t[...] = tokens_ref[...].T
            below[...] = jnp.broadcast_to(vectors_ref[...].astype(BF)[None], below.shape)
            for target in (keep, give):
                for y in range(2):
                    pltpu.make_async_copy(
                        below, target.at[y, :, pl.ds(rows, extra)], below_sem
                    ).start()

        @pl.when(step >= 2)
        def _():
            pltpu.make_async_copy(block.at[slot], block.at[slot], sem.at[slot]).wait()

        @pl.when(step < 3)
        def _():
            right = jnp.concatenate([ref[0] for ref in grad_refs], 1)
            block[slot] = dot(tokens_t[...], right, 1, 0).astype(BF)

        @pl.when(step == 3)
        def _():
            left = jnp.concatenate([ref[...] for ref in mixed_refs], 1)
            block[slot] = dot(left, proj_ref[...], 0, 0).astype(BF)

        source = block.at[slot].reshape(owners, rows, D)
        y, core = lax.div(step, 2), lax.rem(step, 2)

        @pl.when(core == me_ref[1])
        def _():
            pltpu.make_async_copy(source, keep.at[y, :, pl.ds(0, rows)], sem.at[slot]).start()

        @pl.when(core != me_ref[1])
        def _():
            pltpu.make_async_copy(source, give.at[y, :, pl.ds(0, rows)], sem.at[slot]).start()

        @pl.when(step == 3)
        def _():
            for s in range(2):
                pltpu.make_async_copy(block.at[s], block.at[s], sem.at[s]).wait()
            for _ in range(4):
                pltpu.make_async_copy(below, below, below_sem).wait()

    def whole(width):
        return pl.BlockSpec((ROW, width), lambda i: (0, 0), pipeline_mode=pl.Buffered(1))

    return pl.pallas_call(
        kernel,
        grid=(4,),
        in_specs=[
            pl.BlockSpec(memory_space=pltpu.SMEM),
            whole(D),
            pl.BlockSpec((extra, D), lambda i: (0, 0)),
            whole(D),
        ]
        + [whole(2 * HEAD * p) for p in AHEAD_PAIRS]
        + [pl.BlockSpec((1, ROW, 2 * HEAD * p), lambda i: (jnp.minimum(i, 2), 0, 0)) for p in PAIRS]
        + [pl.BlockSpec(memory_space=pl.ANY)] * len(after),
        out_specs=[pl.BlockSpec(memory_space=pl.ANY)] * 2,
        out_shape=[shape] * 2,
        scratch_shapes=[
            pltpu.VMEM((D, ROW), BF),
            pltpu.VMEM((2, D, D), BF),
            pltpu.VMEM((owners, extra, D), BF),
            pltpu.SemaphoreType.DMA((2,)),
            pltpu.SemaphoreType.DMA,
        ],
        compiler_params=pltpu.CompilerParams(vmem_limit_bytes=TERMS_VMEM),
        cost_estimate=cost(6),
        name="attn_terms",
    )(me, tokens, vectors, grad_proj, *mixed, *grads, *after)


def token_grad_kernel(resid, weights, *refs):
    out = refs[-1]
    total = resid[...]
    for m in range(3):
        grad = jnp.concatenate([ref[m] for ref in refs[: len(PAIRS)]], 1)
        total = total + dot(grad, weights[m * D : (m + 1) * D], 1, 1)
    out[...] = total.astype(BF)


def token_gradient(resid, weights, grads, after):
    step = 256
    tile = pl.BlockSpec((step, D), lambda i: (i, 0))
    return pl.pallas_call(
        token_grad_kernel,
        grid=(ROW // step,),
        in_specs=[tile, pl.BlockSpec((3 * D, D), lambda i: (0, 0), pipeline_mode=pl.Buffered(1))]
        + [pl.BlockSpec((3, step, 2 * HEAD * p), lambda i: (0, i, 0)) for p in PAIRS]
        + [pl.BlockSpec(memory_space=pl.ANY)] * len(after),
        out_specs=tile,
        out_shape=jax.ShapeDtypeStruct((ROW, D), BF),
        compiler_params=pltpu.CompilerParams(vmem_limit_bytes=TOKEN_VMEM),
        cost_estimate=cost(2),
        name="token_grad",
    )(resid, weights, *grads, *after)


def adam_update(param, gradient, moment, square, shadow):
    step_float = float(STEP)
    moment_next = MOMENT_DECAY * moment + (1.0 - MOMENT_DECAY) * gradient
    square_next = SQUARE_DECAY * square + (1.0 - SQUARE_DECAY) * gradient * gradient
    moment_hat = moment_next / (1.0 - MOMENT_DECAY**step_float)
    square_hat = square_next / (1.0 - SQUARE_DECAY**step_float)
    change = -LEARN_RATE * (
        moment_hat / (jnp.sqrt(square_hat) + ADAM_EPSILON) + WEIGHT_DECAY * param
    )
    updated = param + change
    drift = (1.0 - SHADOW_RATE) * (updated - shadow)
    return (change, moment_next, square_next, drift)


def contract_rows(left, right):
    return dot(left, right, 0, 0)


def on_device(
    places,
    tokens,
    segments,
    counts,
    out_grad,
    attn_param,
    attn_moment,
    attn_square,
    attn_shadow,
    ffn_param,
    ffn_moment,
    ffn_square,
    ffn_shadow,
):
    assert counts.shape[0] == 1 and tokens.shape[0] == ROW
    number = places.count
    here = places.here()
    place_list = jnp.stack([here[a] for a in ("y", "c", "z", "x")]).astype(jnp.int32)
    me = lax.axis_index("dp") * places.wide + lax.axis_index("wide")
    staged = places.staged()
    attn_rows, ffn_rows = ATTN_ROWS // number, FFN_ROWS // number
    up_rows = ffn_rows // UP_CHUNKS
    holds_up = me < number // 2

    last = me == number - 1
    ends = jnp.concatenate([attn_param[-ATTN_TAIL:], ffn_param[-FFN_TAIL:]]).astype(BF)
    ends = jnp.where(last, ends, jnp.zeros_like(ends))
    if staged:
        digits = [lax.rem(lax.shift_right_logical(counts[0], 3 * i), 8) for i in range(4)]
        count_row = jnp.concatenate([jnp.stack(digits).astype(BF), jnp.zeros((D - 4,), BF)])
        filler = jnp.zeros(((VEC_ROWS - COUNT_ROW - 1) * D,), BF)
        extra = jnp.concatenate([ends, count_row, filler]).reshape(VEC_ROWS, D)
        attn_own = to_rows(places, me, attn_param, ATTN_ROWS, ATTN_TAIL).astype(BF)
        attn_set = Gathered(places, attn_rows)
        blocks = attn_set.start_z(jnp.concatenate([attn_own, extra], 0))
        ffn_own = to_rows(places, me, order(ffn_param, blocks[1]), FFN_ROWS, FFN_TAIL).astype(BF)
        by_chunk = ffn_own.reshape(up_rows, UP_CHUNKS, D).transpose(1, 0, 2).reshape(ffn_rows, D)
        ffn_own = jnp.where(holds_up, by_chunk, ffn_own)
        column = attn_set.join_z(here, blocks)
        half_rows = ffn_rows // 2
        ffn_set = Gathered(places, half_rows)
        blocks = ffn_set.start_z(order(ffn_own[:half_rows], column))
        near = [ffn_set.join_parts(place_list, [blocks])]
        plane = order(attn_set.along_first(column), *blocks)
        blocks = ffn_set.start_z(order(ffn_own[half_rows:], plane, near[0]))
        aside = [places.send(near[0], "xy", 1)]
        crossed = [places.send(near[0], "c", 1)]
        near.append(ffn_set.join_parts(place_list, [blocks]))
        groups = [plane]
        groups += [order(g, aside[0], near[1]) for g in attn_set.along_second(plane)]
        attn_groups = groups + attn_set.from_core(groups)
        aside.append(places.send(near[1], "xy", 1))
        across = [places.send(near[0], "yx", 1)]
        corner = [places.send(aside[0], "yx", 1)]
        query, key, value, vec, attn_whole = project(
            tokens, place_list, attn_set, attn_groups, [aside[0], near[1], crossed[0]]
        )
        token_total = sum(vec[COUNT_ROW, i] * float(8**i) for i in range(4))
        aside = [order(a, query) for a in aside]
        near[1] = order(near[1], query)
        crossed += [places.send(near[1], "c", 1)] + [places.send(a, "c", 1) for a in aside]
        across.append(places.send(near[1], "yx", 1))
        corner.append(places.send(aside[1], "yx", 1))
        extent = places.size
        per_half = UP_CHUNKS // 2
        piece = (extent["z"], per_half, up_rows, D)
        half = extent["y"] // 2

        def fetch(place, refs, weights, sem):
            side = (half, 2, extent["z"], extent["x"])
            up = weights.at[pl.ds(0, FF)].reshape(*((UP_CHUNKS,) + side + (up_rows, D)))
            down = weights.at[pl.ds(FF, FF)].reshape(*(side + (UP_CHUNKS, up_rows, D)))
            ways = [(far, i, j) for far in range(2) for i in range(2) for j in range(2)]
            for i, ref in enumerate(refs):
                h, way = divmod(i, len(ways))
                y, core, x = ffn_set.place(place, *ways[way])

                @pl.when(y < half)
                def _():
                    for part in range(per_half):
                        chunk = h * per_half + part
                        pltpu.make_async_copy(
                            ref.at[:, part], up.at[chunk, y, core, :, x], sem.at[chunk]
                        ).start()

                @pl.when(y >= half)
                def _():
                    chunks = pl.ds(h * per_half, per_half)
                    pltpu.make_async_copy(
                        ref, down.at[y - half, core, :, x, chunks], sem.at[UP_CHUNKS]
                    ).start()

    else:
        token_total = lax.psum(counts[0].astype(F32), AXES)
        vec = lax.psum(ends.astype(F32), AXES).reshape(COUNT_ROW, D)
        vec = jnp.concatenate([vec, jnp.zeros((VEC_ROWS - COUNT_ROW, D), F32)], 0)
        flat = lax.all_gather(attn_param.astype(BF), AXES, axis=0, tiled=True)
        attn_whole = flat[: ATTN_ROWS * D].reshape(ATTN_ROWS, D)
        flat = lax.all_gather(ffn_param.astype(BF), AXES, axis=0, tiled=True)
        w_up = flat[: FF * D].reshape(D, UP_CHUNKS, D).transpose(1, 0, 2).reshape(FF, D)
        w_down = flat[FF * D : FFN_ROWS * D].reshape(FF, D)
        sources = [w_up, w_down]

        def fetch(place, refs, weights, sem):
            w_up, w_down = refs
            for j in range(UP_CHUNKS):
                rows = pl.ds(j * D, D)
                pltpu.make_async_copy(w_up.at[rows], weights.at[rows], sem.at[j]).start()
            down = weights.at[pl.ds(FF, FF)]
            pltpu.make_async_copy(w_down, down, sem.at[UP_CHUNKS]).start()

        query, key, value = project_whole(tokens, attn_whole, vec)

    ahead = []
    for i, pairs in enumerate(AHEAD_PAIRS):
        after = [aside[1]] if staged and i == 0 else []
        first = sum(AHEAD_PAIRS[:i])
        ahead.append(attend(query, key, value, segments, counts, first, pairs, after))
    mixed = [a[0] for a in ahead]
    log_total = jnp.concatenate([a[1] for a in ahead], 0)
    if staged:
        sources = []
        for h in range(2):
            across[h], corner[h] = order(across[h], mixed[h]), order(corner[h], mixed[h])
            mine = [near[h], across[h], aside[h], corner[h]]
            theirs = [crossed[h], places.send(across[h], "c", 1)]
            theirs += [crossed[2 + h], places.send(corner[h], "c", 1)]
            sources += [a.reshape(piece) for a in mine + theirs]
    (
        final_low,
        hidden_low,
        activated,
        grad_pre,
        grad_ffn_out,
        grad_attn_out,
        grad_mixed,
        grad_resid,
        vec_grad,
        crop_sums,
    ) = middle(
        counts,
        place_list,
        segments,
        mixed,
        tokens,
        out_grad,
        attn_whole,
        sources,
        fetch,
        vec,
    )
    is_valid = jnp.arange(ROW, dtype=jnp.int32) < counts[0]
    member = (segments[None, :] == jnp.arange(CROPS, dtype=jnp.int32)[:, None]) & is_valid[None, :]
    crop_sizes = jnp.sum(member.astype(F32), axis=1)
    pooled = crop_sums / jnp.maximum(crop_sizes, 1.0)[:, None]

    def back(i, after, micros):
        return attend_back(
            query,
            key,
            value,
            grad_mixed,
            log_total,
            segments,
            counts,
            sum(PAIRS[:i]),
            PAIRS[i],
            after,
            micros,
        )

    if staged:
        ffn_sums, attn_sums = Scattered(places, place_list, 1.2), Scattered(places, place_list, 0.5)

        def spread(terms):
            return terms.reshape(2, extent["z"], extent["x"], *terms.shape[2:])

        def ffn_side(thirds, after):
            operands = (hidden_low, activated, grad_pre, grad_ffn_out)
            terms = ffn_terms(places, place_list, *operands, thirds, after)
            return [spread(t) for t in terms]

        keep_a, give_a = ffn_side([0, 1, 2], [])
        core_a = ffn_sums.core(give_a)
        back_0 = back(0, [give_a], 12)
        own_a, cut_a = ffn_sums.first(keep_a, order(core_a, back_0[0]))
        first_a = ffn_sums.send(cut_a)
        back_1 = back(1, [cut_a], 15)
        vectors = jnp.concatenate([back_0[1], back_1[1]], 1)[:2]
        vec_grad = jnp.concatenate([vectors, vec_grad[2:]], 0)
        grads = [back_0[0], back_1[0]]
        operands = (tokens, mixed, grads, grad_attn_out, vec_grad)
        terms = attn_terms(places, place_list, *operands, [])
        keep_c, give_c = [spread(t) for t in terms]
        core_c = attn_sums.core(give_c)
        own_a, cut_a = ffn_sums.second(own_a, order(first_a, give_c))
        second_a = ffn_sums.send_second(cut_a)
        token_grad = token_gradient(grad_resid, attn_whole, grads, [give_c, cut_a])
        own_c, cut_c = attn_sums.first(keep_c, order(core_c, token_grad))
        own_a, cuts_a = ffn_sums.along_z(own_a, order(second_a, cut_c))
        up_z_a = ffn_sums.send_z(cuts_a)
        first_c = attn_sums.send(cut_c, *cuts_a)
        own_c, cut_c = attn_sums.second(own_c, order(first_c, up_z_a[1]))
        second_c = attn_sums.send_second(cut_c)
        own_c, cuts_c = attn_sums.along_z(own_c, second_c)
        up_z_c = attn_sums.send_z(cuts_c)
        ffn_block = ffn_sums.result(own_a, up_z_a)
        block_c = attn_sums.result(own_c, up_z_c)
        attn_block, vec_sum = block_c[:attn_rows], block_c[attn_rows:]
        by_row = ffn_block.reshape(UP_CHUNKS, up_rows, D).transpose(1, 0, 2).reshape(ffn_rows, D)
        ffn_block = jnp.where(holds_up, by_row, ffn_block)
        ffn_summed = to_flat(places, me, ffn_block, vec_sum[5:12], FFN_TAIL)
        attn_summed = to_flat(places, me, attn_block, vec_sum[:5], ATTN_TAIL)
    else:
        backs = [back(i, [], 12) for i in range(len(PAIRS))]
        grads = [b[0] for b in backs]
        token_grad = token_gradient(grad_resid, attn_whole, grads, [])
        grads = jnp.concatenate(grads, 2)
        mats = [contract_rows(tokens, grads[i]) for i in range(3)]
        mats.append(contract_rows(jnp.concatenate(mixed, 1), grad_attn_out))
        vectors = jnp.concatenate([b[1] for b in backs], 1)[:2]
        vec_grad = jnp.concatenate([vectors, vec_grad[2:]], 0)
        attn_full = jnp.concatenate([g.reshape(-1) for g in mats + [vec_grad[:5]]])
        up = contract_rows(hidden_low, grad_pre)
        down = contract_rows(activated, grad_ffn_out)
        ffn_full = jnp.concatenate([g.reshape(-1) for g in (up, down, vec_grad[5:12])])
        attn_summed = lax.psum_scatter(attn_full, AXES, scatter_dimension=0, tiled=True)
        ffn_summed = lax.psum_scatter(ffn_full, AXES, scatter_dimension=0, tiled=True)
    attn_grad = attn_summed / token_total
    ffn_grad = ffn_summed / token_total
    attn_change, moment_attn, square_attn, drift_attn = adam_update(
        attn_param, attn_grad, attn_moment, attn_square, attn_shadow
    )
    ffn_change, moment_ffn, square_ffn, drift_ffn = adam_update(
        ffn_param, ffn_grad, ffn_moment, ffn_square, ffn_shadow
    )
    return (
        final_low,
        pooled,
        token_grad,
        attn_grad,
        ffn_grad,
        attn_change,
        ffn_change,
        moment_attn,
        moment_ffn,
        square_attn,
        square_ffn,
        drift_attn,
        drift_ffn,
    )


def solution(mesh):
    rows, flat = P(AXES, None), P(AXES)
    return jax.shard_map(
        functools.partial(on_device, Places(mesh)),
        mesh=mesh,
        in_specs=(rows, flat, flat, rows) + (flat,) * 8,
        out_specs=(rows, rows, rows) + (flat,) * 10,
        check_vma=False,
    )
```

```python
import functools

import jax
import jax.numpy as jnp
from jax import lax
from jax.experimental import pallas as pl
from jax.experimental.pallas import tpu as pltpu
from jax.sharding import PartitionSpec as P

D = 768
FF = 3072
HEAD = 64
HEADS = 12
ROW = 1024
STEP = 10
CROPS = 16

NORM_EPSILON = 1e-12
NEGATIVE = -1e30
MOMENT_DECAY = 0.9
SQUARE_DECAY = 0.999
LEARN_RATE = 0.001
WEIGHT_DECAY = 0.01
ADAM_EPSILON = 1e-08
SHADOW_RATE = 0.9995
SCALE = HEAD ** (-0.5)

AXES = ("dp", "wide")
BF = jnp.bfloat16
F32 = jnp.float32
UP_CHUNKS = FF // D
ATTN_ROWS = 4 * D
FFN_ROWS = 2 * FF
ATTN_TAIL = 5 * D
FFN_TAIL = FF + 3 * D
AHEAD_PAIRS = (2, 2, 2)
PAIRS = (1, 5)
VEC_ROWS = 16
COUNT_ROW = 12
MIB = 1 << 20
BACK_VMEM = 24 * MIB
TERMS_VMEM = 24 * MIB
TOKEN_VMEM = 24 * MIB
FFN_VMEM = 30 * MIB
ADD_VMEM = 24 * MIB


def dot(left, right, left_dim, right_dim):
    return lax.dot_general(
        left, right, (((left_dim,), (right_dim,)), ((), ())), preferred_element_type=F32
    )


class Places:
    def __init__(self, mesh):
        self.dp, self.wide = mesh.shape["dp"], mesh.shape["wide"]
        self.count = self.dp * self.wide
        self.size = {"c": 2, "y": self.dp // 2}
        self.size["x"] = self.size["y"]
        self.size["z"] = self.wide // self.size["x"]

    def staged(self):
        exact = self.dp == 4 and self.wide % self.size["x"] == 0
        return exact and D % (16 * UP_CHUNKS * self.wide // 2) == 0

    def index(self, y, c, z, x):
        return (y * 2 + c) * self.wide + z * self.size["x"] + x

    def rotation(self, axis, step):
        pairs = []
        extent = self.size
        for y in range(extent["y"]):
            for c in range(2):
                along = axis if len(axis) == 1 else axis[c]
                for z in range(extent["z"]):
                    for x in range(extent["x"]):
                        at = {"y": y, "c": c, "z": z, "x": x}
                        to = dict(at)
                        to[along] = (at[along] + step) % extent[along]
                        pairs.append((self.index(**at), self.index(**to)))
        return pairs

    def send(self, array, axis, step):
        return lax.ppermute(array, AXES, self.rotation(axis, step))

    def here(self):
        outer, inner = lax.axis_index("dp"), lax.axis_index("wide")
        extent = self.size["x"]
        return {"y": outer // 2, "c": outer % 2, "z": inner // extent, "x": inner % extent}


def order(array, *before):
    return lax.optimization_barrier((array,) + before)[0]


class Gathered:
    def __init__(self, places, rows):
        self.places, self.rows = places, rows
        self.deep = places.size["z"] * rows

    def start_z(self, own):
        extent = self.places.size["z"]
        return [own] + [self.places.send(own, "z", k) for k in range(1, extent)]

    def join_z(self, here, blocks):
        rows, extent = self.rows, self.places.size["z"]
        near = jnp.zeros((self.deep, D), BF)
        for k, block in enumerate(blocks):
            at = lax.rem(here["z"] + (extent - k), extent) * rows
            near = lax.dynamic_update_slice_in_dim(near, block[:rows], at, 0)
        return jnp.concatenate([near, self.total([b[rows:] for b in blocks])], 0)

    def join_parts(self, me, parts):
        extent, count = self.places.size["z"], len(parts)
        share = self.rows // count

        def kernel(me_ref, *refs):
            out, sem = refs[-2:]
            for p in range(count):
                for k in range(extent):
                    at = lax.rem(me_ref[2] + (extent - k), extent)
                    pltpu.make_async_copy(
                        refs[p * extent + k], out.at[at, pl.ds(p * share, share)], sem
                    ).start()
            pltpu.make_async_copy(out, out, sem).wait()

        blocks = [b for part in parts for b in part]
        return pl.pallas_call(
            kernel,
            in_specs=[pl.BlockSpec(memory_space=pltpu.SMEM)]
            + [pl.BlockSpec(memory_space=pl.ANY)] * len(blocks),
            out_specs=pl.BlockSpec(memory_space=pltpu.VMEM),
            out_shape=jax.ShapeDtypeStruct((extent, self.rows, D), BF),
            scratch_shapes=[pltpu.SemaphoreType.DMA],
            compiler_params=pltpu.CompilerParams(vmem_limit_bytes=16 * MIB),
            cost_estimate=cost(2),
            name="join",
        )(me, *blocks).reshape(self.deep, D)

    def along_first(self, near):
        places, extent = self.places, self.places.size
        blocks = [near] + [places.send(near, "xy", k) for k in range(1, extent["x"])]
        parts = [b[: self.deep] for b in blocks]
        if near.shape[0] > self.deep:
            parts.append(self.total([b[self.deep :] for b in blocks]))
        return jnp.concatenate(parts, 0)

    def along_second(self, near):
        return [self.places.send(near, "yx", k) for k in range(1, self.places.size["x"])]

    def from_core(self, groups):
        return [self.places.send(g, "c", 1) for g in groups]

    def total(self, arrays):
        result = arrays[0].astype(F32)
        for a in arrays[1:]:
            result = result + a.astype(F32)
        return result.astype(BF)

    def place(self, here, far, first, second):
        extent = self.places.size

        def back(axis, step):
            return lax.rem(here[axis] + (extent[axis] - step), extent[axis])

        core = here["c"] if far == 0 else 1 - here["c"]
        y = jnp.where(core == 0, back("y", second), back("y", first))
        x = jnp.where(core == 0, back("x", first), back("x", second))
        return y, core, x


def read_here(me_ref):
    return {"y": me_ref[0], "c": me_ref[1], "z": me_ref[2], "x": me_ref[3]}


def add_routed(me, keep, arrived, grid, routes, source_block, target_block, target_lead, micros):
    rows, width = keep.shape[-2:]

    def kernel(me_ref, *refs):
        for i in range(len(routes)):
            total = refs[2 * i][...].astype(F32) + refs[2 * i + 1][...].astype(F32)
            refs[2 * len(routes) + i][...] = total.astype(BF)

    def source(route):
        return pl.BlockSpec(source_block + (rows, width), lambda *at: route(*at) + (0, 0))

    target = pl.BlockSpec(target_block[0] + (rows, width), lambda *at: target_block[1](*at) + (0, 0))
    return pl.pallas_call(
        kernel,
        grid_spec=pltpu.PrefetchScalarGridSpec(
            num_scalar_prefetch=1,
            grid=grid,
            in_specs=[source(r) for r in routes for _ in range(2)],
            out_specs=[target] * len(routes),
        ),
        out_shape=[jax.ShapeDtypeStruct(target_lead + (rows, width), BF)] * len(routes),
        compiler_params=pltpu.CompilerParams(vmem_limit_bytes=ADD_VMEM),
        cost_estimate=cost(micros),
        name="add_routed",
    )(me, *([keep, arrived] * len(routes)))


class Scattered:
    def __init__(self, places, me, micros):
        self.places, self.me, self.micros = places, me, micros
        self.z = places.size["z"]

    def core(self, give):
        return self.places.send(give, "c", 1)

    def first(self, keep, arrived):
        deep = 2

        def route(far):
            def pick_block(z, e, me):
                y, x = jnp.abs(me[0] - far), jnp.abs(me[3] - far)
                return jnp.where(me[1] == 0, e, y), z, jnp.where(me[1] == 0, x, e)

            return pick_block

        own, cut = add_routed(
            self.me,
            keep,
            arrived,
            (self.z // deep, 2),
            [route(0), route(1)],
            (None, deep, None),
            ((deep, None), lambda z, e, me: (z, e)),
            (self.z, 2),
            4 * self.micros,
        )
        return own, cut

    def second(self, keep, arrived):
        deep = 2

        def route(far):
            return lambda z, me: (z, jnp.abs(jnp.where(me[1] == 0, me[0], me[3]) - far))

        own, cut = add_routed(
            self.me,
            keep,
            arrived,
            (self.z // deep,),
            [route(0), route(1)],
            (deep, None),
            ((deep,), lambda z, me: (z,)),
            (self.z,),
            2 * self.micros,
        )
        return own, cut

    def along_z(self, keep, arrived):
        def route(k):
            return lambda i, me: (lax.rem(me[2] + k, self.z),)

        own, *cuts = add_routed(
            self.me,
            keep,
            arrived,
            (1,),
            [route(k) for k in range(self.z)],
            (None,),
            ((None,), lambda i, me: (0,)),
            (1,),
            self.micros,
        )
        return own, cuts

    def send(self, cut, *before):
        return self.places.send(order(cut, *before), "xy", 1)

    def send_second(self, cut, *before):
        return self.places.send(order(cut, *before), "yx", 1)

    def send_z(self, cuts, *before):
        return [self.places.send(order(c, *before), "z", k + 1) for k, c in enumerate(cuts)]

    def result(self, own, arrived):
        total = own[0].astype(F32)
        for a in arrived:
            total = total + a[0].astype(F32)
        return total


def to_rows(places, me, flat, rows, tail):
    count = places.count
    block = rows // count * D
    slack = tail // count
    before = lax.ppermute(flat[-tail:], AXES, [(i, i + 1) for i in range(count - 1)])
    joined = jnp.concatenate([before, flat])
    return lax.dynamic_slice_in_dim(joined, tail - me * slack, block).reshape(rows // count, D)


def to_flat(places, me, block, vectors, tail):
    count = places.count
    slack = tail // count
    after = lax.ppermute(block[: tail // D], AXES, [(i + 1, i) for i in range(count - 1)])
    after = jnp.where(me == count - 1, vectors, after)
    joined = jnp.concatenate([block, after], 0).reshape(-1)
    return lax.dynamic_slice_in_dim(joined, me * slack, block.size + slack)


def project_body(step, tokens, weights, vec, query, key, value):
    held = tokens[...]
    query[...] = (dot(held, weights[0:D], 1, 0) + vec[0:1]).astype(BF)
    key[...] = dot(held, weights[D : 2 * D], 1, 0).astype(BF)
    value[...] = (dot(held, weights[2 * D : 3 * D], 1, 0) + vec[1:2]).astype(BF)


def project_kernel(gathered, number, after, me, tokens, *refs):
    groups = refs[:number]
    query, key, value, vec, whole, weights, extras, sem, extra_sem, out_sem = refs[number + after :]
    step = pl.program_id(0)
    extent = gathered.places.size
    rows, deep = gathered.rows, gathered.rows * extent["z"]

    @pl.when(step == 0)
    def _():
        here = read_here(me)
        for g, ref in enumerate(groups):
            pltpu.make_async_copy(
                ref.at[pl.ds(extent["x"] * deep, VEC_ROWS)], extras.at[g], extra_sem
            ).start()
        shape = (extent["y"], 2, extent["z"], extent["x"], rows, D)
        for g, ref in enumerate(groups):
            far, second = divmod(g, extent["x"])
            for first in range(extent["x"]):
                y, core, x = gathered.place(here, far, first, second)
                pltpu.make_async_copy(
                    ref.at[pl.ds(first * deep, deep)].reshape(extent["z"], rows, D),
                    weights.reshape(*shape).at[y, core, :, x],
                    sem,
                ).start()
        pltpu.make_async_copy(extras, extras, extra_sem).wait()
        total = extras[0].astype(F32)
        for g in range(1, number):
            total = total + extras[g].astype(F32)
        vec[...] = total
        pltpu.make_async_copy(weights, weights, sem).wait()
        pltpu.make_async_copy(weights, whole, out_sem).start()

    project_body(step, tokens, weights, vec, query, key, value)

    @pl.when(step == pl.num_programs(0) - 1)
    def _():
        pltpu.make_async_copy(weights, whole, out_sem).wait()


PROJECT_ROWS = 256


def project(tokens, me, gathered, groups, after):
    rows = tokens.shape[0]
    tile = pl.BlockSpec((PROJECT_ROWS, D), lambda i: (i, 0))
    number = len(groups)
    return pl.pallas_call(
        functools.partial(project_kernel, gathered, number, len(after)),
        grid=(rows // PROJECT_ROWS,),
        in_specs=[pl.BlockSpec(memory_space=pltpu.SMEM), tile]
        + [pl.BlockSpec(memory_space=pl.ANY)] * (number + len(after)),
        out_specs=[tile] * 3
        + [pl.BlockSpec((VEC_ROWS, D), lambda i: (0, 0)), pl.BlockSpec(memory_space=pl.ANY)],
        out_shape=[jax.ShapeDtypeStruct((rows, D), BF)] * 3
        + [jax.ShapeDtypeStruct((VEC_ROWS, D), F32), jax.ShapeDtypeStruct((ATTN_ROWS, D), BF)],
        scratch_shapes=[
            pltpu.VMEM((ATTN_ROWS, D), BF),
            pltpu.VMEM((number, VEC_ROWS, D), BF),
            pltpu.SemaphoreType.DMA,
            pltpu.SemaphoreType.DMA,
            pltpu.SemaphoreType.DMA,
        ],
        compiler_params=pltpu.CompilerParams(vmem_limit_bytes=24 * MIB),
        cost_estimate=cost(8),
        name="project",
    )(me, tokens, *groups, *after)


def project_whole(tokens, weights, vec):
    rows = tokens.shape[0]
    tile = pl.BlockSpec((PROJECT_ROWS, D), lambda i: (i, 0))
    return pl.pallas_call(
        lambda *refs: project_body(None, *refs),
        grid=(rows // PROJECT_ROWS,),
        in_specs=[
            tile,
            pl.BlockSpec((ATTN_ROWS, D), lambda i: (0, 0), pipeline_mode=pl.Buffered(1)),
            pl.BlockSpec((VEC_ROWS, D), lambda i: (0, 0)),
        ],
        out_specs=[tile] * 3,
        out_shape=[jax.ShapeDtypeStruct((rows, D), BF)] * 3,
        compiler_params=pltpu.CompilerParams(vmem_limit_bytes=24 * MIB),
        name="project",
    )(tokens, weights, vec)


QUERY_BLOCK = 256
QUERY_BLOCKS = ROW // QUERY_BLOCK


def window(block):
    low = max(0, block - 1) * QUERY_BLOCK
    return low, min(QUERY_BLOCKS, block + 2) * QUERY_BLOCK


def fill_bias(bias, seg_column, seg_row, count):
    for block in range(QUERY_BLOCKS):
        low, high = window(block)
        at = slice(block * QUERY_BLOCK, (block + 1) * QUERY_BLOCK)
        shape = (high - low, QUERY_BLOCK)
        key_pos = low + lax.broadcasted_iota(jnp.int32, shape, 0)
        query_pos = block * QUERY_BLOCK + lax.broadcasted_iota(jnp.int32, shape, 1)
        same = seg_column[low:high, 0:1] == seg_row[0:1, at]
        allowed = (same & (key_pos < count)) | (key_pos == query_pos)
        bias[0 : high - low, at] = jnp.where(allowed, 0.0, NEGATIVE).astype(F32)


def one_head(transposed):
    zero = jnp.zeros((HEAD, transposed.shape[1]), transposed.dtype)
    return (
        jnp.concatenate([transposed[:HEAD], zero], 0),
        jnp.concatenate([zero, transposed[HEAD:]], 0),
    )


def attend_kernel(count, seg_column, seg_row, query, key, value, *refs):
    mixed, log_total, bias = refs[-3:]

    @pl.when(pl.program_id(0) == 0)
    def _():
        fill_bias(bias, seg_column, seg_row, count[0])

    value_t = value[...].T
    query_t = one_head((query[...] * jnp.asarray(SCALE, BF)).T)
    parts = []

    def score(block, h):
        low, high = window(block)
        at = slice(block * QUERY_BLOCK, (block + 1) * QUERY_BLOCK)
        return dot(key[low:high, :], query_t[h][:, at], 1, 0) + bias[0 : high - low, at]

    def mix(block, h, shifted, inverse):
        low, high = window(block)
        at = slice(block * QUERY_BLOCK, (block + 1) * QUERY_BLOCK)
        part = dot(value_t[h * HEAD : (h + 1) * HEAD, low:high], shifted, 1, 0)
        parts.append(part * inverse)
        if h == 1:
            mixed[at, :] = jnp.concatenate(parts, 0).T.astype(BF)
            parts.clear()

    items = [(block, h) for block in range(QUERY_BLOCKS) for h in range(2)]
    ahead, behind = score(*items[0]), None
    for n, (block, h) in enumerate(items):
        at = slice(block * QUERY_BLOCK, (block + 1) * QUERY_BLOCK)
        scores = ahead
        if n + 1 < len(items):
            ahead = score(*items[n + 1])
        if behind is not None:
            mix(*behind)
        top = jnp.max(scores, axis=0, keepdims=True)
        shifted = jnp.exp(scores - top)
        total = jnp.sum(shifted, axis=0, keepdims=True)
        log_total[0, h : h + 1, at] = top + jnp.log(total)
        behind = (block, h, shifted.astype(BF), 1.0 / total)
    mix(*behind)


def attend_specs():
    return [
        pl.BlockSpec(memory_space=pltpu.SMEM),
        pl.BlockSpec((ROW, 1), lambda h: (0, 0)),
        pl.BlockSpec((1, ROW), lambda h: (0, 0)),
    ]


def attend(query, key, value, segments, count, first, pairs, after):
    pair = pl.BlockSpec((ROW, 2 * HEAD), lambda h: (0, h + first))
    return pl.pallas_call(
        attend_kernel,
        grid=(pairs,),
        in_specs=attend_specs() + [pair] * 3 + [pl.BlockSpec(memory_space=pl.ANY)] * len(after),
        out_specs=[
            pl.BlockSpec((ROW, 2 * HEAD), lambda h: (0, h)),
            pl.BlockSpec((1, 8, ROW), lambda h: (h, 0, 0)),
        ],
        out_shape=[
            jax.ShapeDtypeStruct((ROW, pairs * 2 * HEAD), BF),
            jax.ShapeDtypeStruct((pairs, 8, ROW), F32),
        ],
        scratch_shapes=[pltpu.VMEM((3 * QUERY_BLOCK, ROW), F32)],
        compiler_params=pltpu.CompilerParams(vmem_limit_bytes=24 * MIB),
        cost_estimate=cost(25 * pairs / 6),
        name="attend",
    )(count, segments.reshape(ROW, 1), segments.reshape(1, ROW), query, key, value, *after)


def attend_back_kernel(
    count, seg_column, seg_row, query, key, value, grad, log_total, *refs
):
    grads, sums, bias, key_sum, value_sum = refs[-5:]

    @pl.when(pl.program_id(0) == 0)
    def _():
        fill_bias(bias, seg_column, seg_row, count[0])

    query_t = (query[...] * jnp.asarray(SCALE, BF)).T
    key_t = key[...].T
    grad_t = grad[...].T
    query_one, grad_one = one_head(query_t), one_head(grad_t)
    key_sum[...] = jnp.zeros_like(key_sum)
    value_sum[...] = jnp.zeros_like(value_sum)
    parts = []

    def score(block, h):
        low, high = window(block)
        at = slice(block * QUERY_BLOCK, (block + 1) * QUERY_BLOCK)
        scores = dot(key[low:high, :], query_one[h][:, at], 1, 0) + bias[0 : high - low, at]
        return scores, dot(value[low:high, :], grad_one[h][:, at], 1, 0)

    def spread(block, h, grad_scores, probs):
        low, high = window(block)
        at = slice(block * QUERY_BLOCK, (block + 1) * QUERY_BLOCK)
        rows = slice(h * HEAD, (h + 1) * HEAD)
        parts.append(dot(key_t[rows, low:high], grad_scores, 1, 0))
        key_sum[rows, low:high] += dot(query_t[rows, at], grad_scores, 1, 1)
        value_sum[rows, low:high] += dot(grad_t[rows, at], probs, 1, 1)
        if h == 1:
            grads[0, at, :] = (jnp.concatenate(parts, 0) * SCALE).T.astype(BF)
            parts.clear()

    items = [(block, h) for block in range(QUERY_BLOCKS) for h in range(2)]
    ahead, behind = score(*items[0]), None
    for n, (block, h) in enumerate(items):
        at = slice(block * QUERY_BLOCK, (block + 1) * QUERY_BLOCK)
        scores, grad_probs = ahead
        if n + 1 < len(items):
            ahead = score(*items[n + 1])
        if behind is not None:
            spread(*behind)
        probs = jnp.exp(scores - log_total[0, h : h + 1, at])
        weighted = probs * grad_probs
        total = jnp.sum(weighted, axis=0, keepdims=True)
        behind = (block, h, (weighted - probs * total).astype(BF), probs.astype(BF))
    spread(*behind)
    grads[1] = key_sum[...].T.astype(BF)
    grads[2] = value_sum[...].T.astype(BF)
    sums[...] = jnp.zeros_like(sums)
    sums[0:1] = column_sum(grads[0].astype(F32))
    sums[1:2] = column_sum(grads[2].astype(F32))


def attend_back(query, key, value, grad, log_total, segments, count, first, pairs, after, micros):
    pair = pl.BlockSpec((ROW, 2 * HEAD), lambda h: (0, h + first))
    return pl.pallas_call(
        attend_back_kernel,
        grid=(pairs,),
        in_specs=attend_specs()
        + [pair] * 4
        + [pl.BlockSpec((1, 8, ROW), lambda h: (h + first, 0, 0))]
        + [pl.BlockSpec(memory_space=pl.ANY)] * len(after),
        out_specs=[
            pl.BlockSpec((3, ROW, 2 * HEAD), lambda h: (0, 0, h)),
            pl.BlockSpec((8, 2 * HEAD), lambda h: (0, h)),
        ],
        out_shape=[
            jax.ShapeDtypeStruct((3, ROW, pairs * 2 * HEAD), BF),
            jax.ShapeDtypeStruct((8, pairs * 2 * HEAD), F32),
        ],
        scratch_shapes=[
            pltpu.VMEM((3 * QUERY_BLOCK, ROW), F32),
            pltpu.VMEM((2 * HEAD, ROW), F32),
            pltpu.VMEM((2 * HEAD, ROW), F32),
        ],
        compiler_params=pltpu.CompilerParams(vmem_limit_bytes=BACK_VMEM),
        cost_estimate=cost(micros),
        name="attend_back",
    )(
        count,
        segments.reshape(ROW, 1),
        segments.reshape(1, ROW),
        query,
        key,
        value,
        grad,
        log_total,
        *after,
    )


def normalise(resid):
    centred = resid - jnp.mean(resid, axis=-1, keepdims=True)
    spread = jnp.mean(centred * centred, axis=-1, keepdims=True)
    inverse = lax.rsqrt(spread + NORM_EPSILON)
    return centred * inverse, inverse


def normalise_back(cotangent, gain, normal, inverse):
    scaled = cotangent * gain
    mean = jnp.mean(scaled, axis=-1, keepdims=True)
    aligned = jnp.mean(scaled * normal, axis=-1, keepdims=True)
    return inverse * (scaled - mean - normal * aligned)


def cost(micros):
    return pl.CostEstimate(flops=int(micros * 1.1e9), bytes_accessed=MIB, transcendentals=0)


def column_sum(array):
    return jnp.sum(array, axis=0, keepdims=True)


MIDDLE_ROWS = 256


def middle_kernel(
    fetch,
    groups,
    count,
    me,
    seg_row,
    tokens,
    out_grad,
    w_out,
    vec,
    *refs,
):
    mixed, refs = refs[: len(AHEAD_PAIRS)], refs[len(AHEAD_PAIRS) :]
    (
        final_low,
        hidden_low,
        activated,
        grad_pre,
        grad_ffn_out,
        grad_attn_out,
        grad_mixed,
        grad_resid,
        vec_grad,
        crop_sums,
        slope,
        hidden_one,
        normals,
        inverses,
        weights,
        sem,
    ) = refs[groups:]
    step = pl.program_id(0)

    def row(i):
        return vec[i : i + 1]

    def chunk(j):
        return weights[j * D : (j + 1) * D]

    def note(i, value):
        vec_grad[i : i + 1] += value

    @pl.when(step == 0)
    def _():
        vec_grad[...] = jnp.zeros_like(vec_grad)
        crop_sums[...] = jnp.zeros_like(crop_sums)
        fetch(read_here(me), refs[:groups], weights, sem)
        for first in range(0, ROW, MIDDLE_ROWS):
            at = slice(first, first + MIDDLE_ROWS)
            held = jnp.concatenate([ref[at] for ref in mixed], 1)
            resid_one = tokens[at].astype(F32) + (dot(held, w_out[...], 1, 0) + row(2))
            normal, inverse = normalise(resid_one)
            hidden = normal * row(3) + row(4)
            hidden_one[at] = hidden
            hidden_low[at] = hidden.astype(BF)
            normals[at] = normal
            inverses[at] = jnp.broadcast_to(inverse, (MIDDLE_ROWS, 128))
        for j in range(UP_CHUNKS):
            part = weights.at[pl.ds(j * D, D)]
            pltpu.make_async_copy(part, part, sem.at[j]).wait()
        part = weights.at[pl.ds(FF, FF)]
        pltpu.make_async_copy(part, part, sem.at[UP_CHUNKS]).wait()

    @pl.when(step > 0)
    def _():
        middle_tile(
            step - 1,
            count,
            seg_row,
            out_grad,
            w_out,
            row,
            chunk,
            note,
            final_low,
            hidden_low,
            activated,
            grad_pre,
            grad_ffn_out,
            grad_attn_out,
            grad_mixed,
            grad_resid,
            crop_sums,
            slope,
            hidden_one,
            normals,
            inverses,
        )


def middle_tile(
    step,
    count,
    seg_row,
    out_grad,
    w_out,
    row,
    chunk,
    note,
    final_low,
    hidden_low,
    activated,
    grad_pre,
    grad_ffn_out,
    grad_attn_out,
    grad_mixed,
    grad_resid,
    crop_sums,
    slope,
    hidden_one,
    normals,
    inverses,
):
    at = pl.ds(pl.multiple_of(step * MIDDLE_ROWS, MIDDLE_ROWS), MIDDLE_ROWS)
    low = hidden_low[at, :]
    total = hidden_one[at, :] + row(9)
    normal_one, inverse_one = normals[at, :], inverses[at, 0:1]
    ahead, act = dot(low, chunk(0), 1, 0), None
    for j in range(UP_CHUNKS):
        at = slice(j * D, (j + 1) * D)
        pre = ahead + row(5 + j)
        if j + 1 < UP_CHUNKS:
            ahead = dot(low, chunk(j + 1), 1, 0)
        if act is not None:
            total = total + dot(act, chunk(UP_CHUNKS + j - 1), 1, 0)
        share = 0.5 + 0.5 * lax.erf(pre * (0.5**0.5))
        density = jnp.exp(-0.5 * pre * pre) * 0.3989422804014327
        slope[:, at] = share + pre * density
        act = (pre * share).astype(BF)
        activated[:, at] = act
    total = total + dot(act, chunk(2 * UP_CHUNKS - 1), 1, 0)
    normal_two, inverse_two = normalise(total)
    final = normal_two * row(10) + row(11)
    final_low[...] = final.astype(BF)

    first = step * MIDDLE_ROWS
    across = (CROPS, MIDDLE_ROWS)
    position = first + lax.broadcasted_iota(jnp.int32, across, 1)
    crop = lax.broadcasted_iota(jnp.int32, across, 0)
    member = ((seg_row[...] == crop) & (position < count[0])).astype(BF)
    high = final.astype(BF)
    rest = final - high.astype(F32)
    mid = rest.astype(BF)
    tiny = (rest - mid.astype(F32)).astype(BF)
    crop_sums[...] += dot(member, high, 1, 0) + (dot(member, mid, 1, 0) + dot(member, tiny, 1, 0))

    position = first + lax.broadcasted_iota(jnp.int32, (MIDDLE_ROWS, 1), 0)
    valid = (position < count[0]).astype(F32)
    cotangent = out_grad[...].astype(F32) * valid
    note(10, column_sum(cotangent * normal_two))
    note(11, column_sum(cotangent))
    grad_two = normalise_back(cotangent, row(10), normal_two, inverse_two)
    grad_out = grad_two.astype(BF)
    grad_ffn_out[...] = grad_out
    note(9, column_sum(grad_out.astype(F32)))
    grad_hidden = grad_two
    ahead, back = dot(grad_out, chunk(UP_CHUNKS), 1, 1), None
    for j in range(UP_CHUNKS):
        at = slice(j * D, (j + 1) * D)
        grad_act = ahead
        if j + 1 < UP_CHUNKS:
            ahead = dot(grad_out, chunk(UP_CHUNKS + j + 1), 1, 1)
        if back is not None:
            grad_hidden = grad_hidden + dot(back, chunk(j - 1), 1, 1)
        back = (grad_act * slope[:, at]).astype(BF)
        grad_pre[:, at] = back
        note(5 + j, column_sum(back.astype(F32)))
    grad_hidden = grad_hidden + dot(back, chunk(UP_CHUNKS - 1), 1, 1)
    note(3, column_sum(grad_hidden * normal_one))
    note(4, column_sum(grad_hidden))
    grad_one = normalise_back(grad_hidden, row(3), normal_one, inverse_one)
    grad_resid[...] = grad_one
    grad_proj = grad_one.astype(BF)
    grad_attn_out[...] = grad_proj
    note(2, column_sum(grad_proj.astype(F32)))
    grad_mixed[...] = dot(grad_proj, w_out[...], 1, 1).astype(BF)


def middle(count, me, segments, mixed, tokens, out_grad, attn_whole, sources, fetch, vec):
    rows = tokens.shape[0]

    def tile_of(i):
        return jnp.maximum(i - 1, 0)

    def whole(width):
        return pl.BlockSpec((rows, width), lambda i: (0, 0), pipeline_mode=pl.Buffered(1))

    tile = pl.BlockSpec((MIDDLE_ROWS, D), lambda i: (tile_of(i), 0))
    wide = pl.BlockSpec((MIDDLE_ROWS, FF), lambda i: (tile_of(i), 0))
    small = pl.BlockSpec((VEC_ROWS, D), lambda i: (0, 0))

    def shape(width, kind):
        return jax.ShapeDtypeStruct((rows, width), kind)

    return pl.pallas_call(
        functools.partial(middle_kernel, fetch, len(sources)),
        grid=(rows // MIDDLE_ROWS + 1,),
        in_specs=[
            pl.BlockSpec(memory_space=pltpu.SMEM),
            pl.BlockSpec(memory_space=pltpu.SMEM),
            pl.BlockSpec((1, MIDDLE_ROWS), lambda i: (0, tile_of(i))),
            whole(D),
            tile,
            pl.BlockSpec((D, D), lambda i: (3, 0), pipeline_mode=pl.Buffered(1)),
            small,
        ]
        + [whole(2 * HEAD * p) for p in AHEAD_PAIRS]
        + [pl.BlockSpec(memory_space=pl.ANY)] * len(sources),
        out_specs=[tile, whole(D), wide, wide, tile, tile, tile, tile, small, small],
        out_shape=[
            shape(D, BF),
            shape(D, BF),
            shape(FF, BF),
            shape(FF, BF),
            shape(D, BF),
            shape(D, BF),
            shape(D, BF),
            shape(D, F32),
            jax.ShapeDtypeStruct((VEC_ROWS, D), F32),
            jax.ShapeDtypeStruct((CROPS, D), F32),
        ],
        scratch_shapes=[
            pltpu.VMEM((MIDDLE_ROWS, FF), F32),
            pltpu.VMEM((rows, D), F32),
            pltpu.VMEM((rows, D), F32),
            pltpu.VMEM((rows, 128), F32),
            pltpu.VMEM((FFN_ROWS, D), BF),
            pltpu.SemaphoreType.DMA((UP_CHUNKS + 1,)),
        ],
        compiler_params=pltpu.CompilerParams(vmem_limit_bytes=40 * MIB),
        cost_estimate=cost(40),
        name="middle",
    )(count, me, segments.reshape(1, rows), tokens, out_grad, attn_whole, vec, *mixed, *sources)


WIDTH = D // 3


def ffn_terms_kernel(shares, me, hidden, activated, *refs):
    pre, out = refs[:shares], refs[shares : 2 * shares]
    keep, give, hidden_t, block, sem = refs[-5:]
    step = pl.program_id(0)
    slot = lax.rem(step, 2)
    owners, rows = keep.shape[1], keep.shape[2]
    up_rows = rows // UP_CHUNKS
    per_chunk = D // rows

    @pl.when(step >= 2)
    def _():
        pltpu.make_async_copy(block.at[slot], block.at[slot], sem.at[slot]).wait()

    def to(core, y, start):
        @pl.when(core == me[1])
        def _():
            start(keep.at[y])

        @pl.when(core != me[1])
        def _():
            start(give.at[y])

    def down():
        right = jnp.concatenate([ref[...] for ref in out], 1)
        block[slot] = dot(activated[...], right, 0, 0).astype(BF)
        source = block.at[slot].reshape(per_chunk, rows, block.shape[2])

        def start(target):
            at = pl.ds(lax.rem(step, 2) * per_chunk, per_chunk)
            pltpu.make_async_copy(source, target.at[at], sem.at[slot]).start()

        to(lax.div(step, 2), 1, start)

    @pl.when(step < UP_CHUNKS - 1)
    def _():
        down()

    @pl.when(step == UP_CHUNKS - 1)
    def _():
        hidden_t[...] = hidden[...].T
        down()

    @pl.when(step >= UP_CHUNKS)
    def _():
        right = jnp.concatenate([ref[...] for ref in pre], 1)
        block[slot] = dot(hidden_t[...], right, 1, 0).astype(BF)
        chunk = step - UP_CHUNKS
        for core in range(2):
            source = block.at[slot, pl.ds(core * (D // 2), D // 2)]
            source = source.reshape(owners, up_rows, block.shape[2])

            def start(target):
                at = pl.ds(pl.multiple_of(chunk * up_rows, 16), up_rows)
                pltpu.make_async_copy(source, target.at[:, at], sem.at[slot]).start()

            to(core, 0, start)

    @pl.when(step == pl.num_programs(0) - 1)
    def _():
        for s in range(2):
            pltpu.make_async_copy(block.at[s], block.at[s], sem.at[s]).wait()


def ffn_terms(places, me, hidden, activated, grad_pre, grad_out, thirds, after):
    owners = places.wide
    rows = FFN_ROWS // places.count
    shares = len(thirds)
    width = shares * WIDTH
    shape = jax.ShapeDtypeStruct((2, owners, rows, width), BF)

    def pre_spec(third):
        return pl.BlockSpec((ROW, WIDTH), lambda i: (0, 3 * jnp.maximum(i - UP_CHUNKS, 0) + third))

    def out_spec(third):
        return pl.BlockSpec((ROW, WIDTH), lambda i: (0, third))

    def kernel(me_ref, hidden_ref, activated_ref, *refs):
        used = refs[: 2 * shares] + refs[2 * shares + len(after) :]
        ffn_terms_kernel(shares, me_ref, hidden_ref, activated_ref, *used)

    return pl.pallas_call(
        kernel,
        grid=(2 * UP_CHUNKS,),
        in_specs=[
            pl.BlockSpec(memory_space=pltpu.SMEM),
            pl.BlockSpec((ROW, D), lambda i: (0, 0), pipeline_mode=pl.Buffered(1)),
            pl.BlockSpec((ROW, D), lambda i: (0, jnp.minimum(i, UP_CHUNKS - 1))),
        ]
        + [pre_spec(t) for t in thirds]
        + [out_spec(t) for t in thirds]
        + [pl.BlockSpec(memory_space=pl.ANY)] * len(after),
        out_specs=[pl.BlockSpec(memory_space=pl.ANY)] * 2,
        out_shape=[shape] * 2,
        scratch_shapes=[
            pltpu.VMEM((D, ROW), BF),
            pltpu.VMEM((2, D, width), BF),
            pltpu.SemaphoreType.DMA((2,)),
        ],
        compiler_params=pltpu.CompilerParams(vmem_limit_bytes=FFN_VMEM),
        cost_estimate=cost(5 * shares),
        name="ffn_terms",
    )(me, hidden, activated, *([grad_pre] * shares), *([grad_out] * shares), *after)


def attn_terms(places, me, tokens, mixed, grads, grad_proj, vectors, after):
    owners = places.wide
    rows = ATTN_ROWS // places.count
    parts, extra = len(AHEAD_PAIRS), vectors.shape[0]
    shape = jax.ShapeDtypeStruct((2, owners, rows + extra, D), BF)

    def kernel(me_ref, tokens_ref, vectors_ref, proj_ref, *refs):
        mixed_refs, grad_refs, refs = refs[:parts], refs[parts : parts + len(PAIRS)], refs[parts + len(PAIRS) :]
        keep, give, tokens_t, block, below, sem, below_sem = refs[len(after) :]
        step = pl.program_id(0)
        slot = lax.rem(step, 2)

        @pl.when(step == 0)
        def _():
            tokens_t[...] = tokens_ref[...].T
            below[...] = jnp.broadcast_to(vectors_ref[...].astype(BF)[None], below.shape)
            for target in (keep, give):
                for y in range(2):
                    pltpu.make_async_copy(
                        below, target.at[y, :, pl.ds(rows, extra)], below_sem
                    ).start()

        @pl.when(step >= 2)
        def _():
            pltpu.make_async_copy(block.at[slot], block.at[slot], sem.at[slot]).wait()

        @pl.when(step < 3)
        def _():
            right = jnp.concatenate([ref[0] for ref in grad_refs], 1)
            block[slot] = dot(tokens_t[...], right, 1, 0).astype(BF)

        @pl.when(step == 3)
        def _():
            left = jnp.concatenate([ref[...] for ref in mixed_refs], 1)
            block[slot] = dot(left, proj_ref[...], 0, 0).astype(BF)

        source = block.at[slot].reshape(owners, rows, D)
        y, core = lax.div(step, 2), lax.rem(step, 2)

        @pl.when(core == me_ref[1])
        def _():
            pltpu.make_async_copy(source, keep.at[y, :, pl.ds(0, rows)], sem.at[slot]).start()

        @pl.when(core != me_ref[1])
        def _():
            pltpu.make_async_copy(source, give.at[y, :, pl.ds(0, rows)], sem.at[slot]).start()

        @pl.when(step == 3)
        def _():
            for s in range(2):
                pltpu.make_async_copy(block.at[s], block.at[s], sem.at[s]).wait()
            for _ in range(4):
                pltpu.make_async_copy(below, below, below_sem).wait()

    def whole(width):
        return pl.BlockSpec((ROW, width), lambda i: (0, 0), pipeline_mode=pl.Buffered(1))

    return pl.pallas_call(
        kernel,
        grid=(4,),
        in_specs=[
            pl.BlockSpec(memory_space=pltpu.SMEM),
            whole(D),
            pl.BlockSpec((extra, D), lambda i: (0, 0)),
            whole(D),
        ]
        + [whole(2 * HEAD * p) for p in AHEAD_PAIRS]
        + [pl.BlockSpec((1, ROW, 2 * HEAD * p), lambda i: (jnp.minimum(i, 2), 0, 0)) for p in PAIRS]
        + [pl.BlockSpec(memory_space=pl.ANY)] * len(after),
        out_specs=[pl.BlockSpec(memory_space=pl.ANY)] * 2,
        out_shape=[shape] * 2,
        scratch_shapes=[
            pltpu.VMEM((D, ROW), BF),
            pltpu.VMEM((2, D, D), BF),
            pltpu.VMEM((owners, extra, D), BF),
            pltpu.SemaphoreType.DMA((2,)),
            pltpu.SemaphoreType.DMA,
        ],
        compiler_params=pltpu.CompilerParams(vmem_limit_bytes=TERMS_VMEM),
        cost_estimate=cost(6),
        name="attn_terms",
    )(me, tokens, vectors, grad_proj, *mixed, *grads, *after)


def token_grad_kernel(resid, weights, *refs):
    out = refs[-1]
    total = resid[...]
    for m in range(3):
        grad = jnp.concatenate([ref[m] for ref in refs[: len(PAIRS)]], 1)
        total = total + dot(grad, weights[m * D : (m + 1) * D], 1, 1)
    out[...] = total.astype(BF)


def token_gradient(resid, weights, grads, after):
    step = 256
    tile = pl.BlockSpec((step, D), lambda i: (i, 0))
    return pl.pallas_call(
        token_grad_kernel,
        grid=(ROW // step,),
        in_specs=[tile, pl.BlockSpec((3 * D, D), lambda i: (0, 0), pipeline_mode=pl.Buffered(1))]
        + [pl.BlockSpec((3, step, 2 * HEAD * p), lambda i: (0, i, 0)) for p in PAIRS]
        + [pl.BlockSpec(memory_space=pl.ANY)] * len(after),
        out_specs=tile,
        out_shape=jax.ShapeDtypeStruct((ROW, D), BF),
        compiler_params=pltpu.CompilerParams(vmem_limit_bytes=TOKEN_VMEM),
        cost_estimate=cost(2),
        name="token_grad",
    )(resid, weights, *grads, *after)


def adam_update(param, gradient, moment, square, shadow):
    step_float = float(STEP)
    moment_next = MOMENT_DECAY * moment + (1.0 - MOMENT_DECAY) * gradient
    square_next = SQUARE_DECAY * square + (1.0 - SQUARE_DECAY) * gradient * gradient
    moment_hat = moment_next / (1.0 - MOMENT_DECAY**step_float)
    square_hat = square_next / (1.0 - SQUARE_DECAY**step_float)
    change = -LEARN_RATE * (
        moment_hat / (jnp.sqrt(square_hat) + ADAM_EPSILON) + WEIGHT_DECAY * param
    )
    updated = param + change
    drift = (1.0 - SHADOW_RATE) * (updated - shadow)
    return (change, moment_next, square_next, drift)


def contract_rows(left, right):
    return dot(left, right, 0, 0)


def on_device(
    places,
    tokens,
    segments,
    counts,
    out_grad,
    attn_param,
    attn_moment,
    attn_square,
    attn_shadow,
    ffn_param,
    ffn_moment,
    ffn_square,
    ffn_shadow,
):
    assert counts.shape[0] == 1 and tokens.shape[0] == ROW
    number = places.count
    here = places.here()
    place_list = jnp.stack([here[a] for a in ("y", "c", "z", "x")]).astype(jnp.int32)
    me = lax.axis_index("dp") * places.wide + lax.axis_index("wide")
    staged = places.staged()
    attn_rows, ffn_rows = ATTN_ROWS // number, FFN_ROWS // number
    up_rows = ffn_rows // UP_CHUNKS
    holds_up = me < number // 2

    last = me == number - 1
    ends = jnp.concatenate([attn_param[-ATTN_TAIL:], ffn_param[-FFN_TAIL:]]).astype(BF)
    ends = jnp.where(last, ends, jnp.zeros_like(ends))
    if staged:
        digits = [lax.rem(lax.shift_right_logical(counts[0], 3 * i), 8) for i in range(4)]
        count_row = jnp.concatenate([jnp.stack(digits).astype(BF), jnp.zeros((D - 4,), BF)])
        filler = jnp.zeros(((VEC_ROWS - COUNT_ROW - 1) * D,), BF)
        extra = jnp.concatenate([ends, count_row, filler]).reshape(VEC_ROWS, D)
        attn_own = to_rows(places, me, attn_param, ATTN_ROWS, ATTN_TAIL).astype(BF)
        attn_set = Gathered(places, attn_rows)
        blocks = attn_set.start_z(jnp.concatenate([attn_own, extra], 0))
        ffn_own = to_rows(places, me, order(ffn_param, blocks[1]), FFN_ROWS, FFN_TAIL).astype(BF)
        by_chunk = ffn_own.reshape(up_rows, UP_CHUNKS, D).transpose(1, 0, 2).reshape(ffn_rows, D)
        ffn_own = jnp.where(holds_up, by_chunk, ffn_own)
        column = attn_set.join_z(here, blocks)
        half_rows = ffn_rows // 2
        ffn_set = Gathered(places, half_rows)
        blocks = ffn_set.start_z(order(ffn_own[:half_rows], column))
        near = [ffn_set.join_parts(place_list, [blocks])]
        plane = order(attn_set.along_first(column), *blocks)
        blocks = ffn_set.start_z(order(ffn_own[half_rows:], plane, near[0]))
        aside = [places.send(near[0], "xy", 1)]
        crossed = [places.send(near[0], "c", 1)]
        near.append(ffn_set.join_parts(place_list, [blocks]))
        groups = [plane]
        groups += [order(g, aside[0], near[1]) for g in attn_set.along_second(plane)]
        attn_groups = groups + attn_set.from_core(groups)
        aside.append(places.send(near[1], "xy", 1))
        across = [places.send(near[0], "yx", 1)]
        corner = [places.send(aside[0], "yx", 1)]
        query, key, value, vec, attn_whole = project(
            tokens, place_list, attn_set, attn_groups, [aside[0], near[1], crossed[0]]
        )
        token_total = sum(vec[COUNT_ROW, i] * float(8**i) for i in range(4))
        aside = [order(a, query) for a in aside]
        near[1] = order(near[1], query)
        crossed += [places.send(near[1], "c", 1)] + [places.send(a, "c", 1) for a in aside]
        across.append(places.send(near[1], "yx", 1))
        corner.append(places.send(aside[1], "yx", 1))
        extent = places.size
        per_half = UP_CHUNKS // 2
        piece = (extent["z"], per_half, up_rows, D)
        half = extent["y"] // 2

        def fetch(place, refs, weights, sem):
            side = (half, 2, extent["z"], extent["x"])
            up = weights.at[pl.ds(0, FF)].reshape(*((UP_CHUNKS,) + side + (up_rows, D)))
            down = weights.at[pl.ds(FF, FF)].reshape(*(side + (UP_CHUNKS, up_rows, D)))
            ways = [(far, i, j) for far in range(2) for i in range(2) for j in range(2)]
            for i, ref in enumerate(refs):
                h, way = divmod(i, len(ways))
                y, core, x = ffn_set.place(place, *ways[way])

                @pl.when(y < half)
                def _():
                    for part in range(per_half):
                        chunk = h * per_half + part
                        pltpu.make_async_copy(
                            ref.at[:, part], up.at[chunk, y, core, :, x], sem.at[chunk]
                        ).start()

                @pl.when(y >= half)
                def _():
                    chunks = pl.ds(h * per_half, per_half)
                    pltpu.make_async_copy(
                        ref, down.at[y - half, core, :, x, chunks], sem.at[UP_CHUNKS]
                    ).start()

    else:
        token_total = lax.psum(counts[0].astype(F32), AXES)
        vec = lax.psum(ends.astype(F32), AXES).reshape(COUNT_ROW, D)
        vec = jnp.concatenate([vec, jnp.zeros((VEC_ROWS - COUNT_ROW, D), F32)], 0)
        flat = lax.all_gather(attn_param.astype(BF), AXES, axis=0, tiled=True)
        attn_whole = flat[: ATTN_ROWS * D].reshape(ATTN_ROWS, D)
        flat = lax.all_gather(ffn_param.astype(BF), AXES, axis=0, tiled=True)
        w_up = flat[: FF * D].reshape(D, UP_CHUNKS, D).transpose(1, 0, 2).reshape(FF, D)
        w_down = flat[FF * D : FFN_ROWS * D].reshape(FF, D)
        sources = [w_up, w_down]

        def fetch(place, refs, weights, sem):
            w_up, w_down = refs
            for j in range(UP_CHUNKS):
                rows = pl.ds(j * D, D)
                pltpu.make_async_copy(w_up.at[rows], weights.at[rows], sem.at[j]).start()
            down = weights.at[pl.ds(FF, FF)]
            pltpu.make_async_copy(w_down, down, sem.at[UP_CHUNKS]).start()

        query, key, value = project_whole(tokens, attn_whole, vec)

    ahead = []
    for i, pairs in enumerate(AHEAD_PAIRS):
        after = [aside[1]] if staged and i == 0 else []
        first = sum(AHEAD_PAIRS[:i])
        ahead.append(attend(query, key, value, segments, counts, first, pairs, after))
    mixed = [a[0] for a in ahead]
    log_total = jnp.concatenate([a[1] for a in ahead], 0)
    if staged:
        sources = []
        for h in range(2):
            across[h], corner[h] = order(across[h], mixed[h]), order(corner[h], mixed[h])
            mine = [near[h], across[h], aside[h], corner[h]]
            theirs = [crossed[h], places.send(across[h], "c", 1)]
            theirs += [crossed[2 + h], places.send(corner[h], "c", 1)]
            sources += [a.reshape(piece) for a in mine + theirs]
    (
        final_low,
        hidden_low,
        activated,
        grad_pre,
        grad_ffn_out,
        grad_attn_out,
        grad_mixed,
        grad_resid,
        vec_grad,
        crop_sums,
    ) = middle(
        counts,
        place_list,
        segments,
        mixed,
        tokens,
        out_grad,
        attn_whole,
        sources,
        fetch,
        vec,
    )
    is_valid = jnp.arange(ROW, dtype=jnp.int32) < counts[0]
    member = (segments[None, :] == jnp.arange(CROPS, dtype=jnp.int32)[:, None]) & is_valid[None, :]
    crop_sizes = jnp.sum(member.astype(F32), axis=1)
    pooled = crop_sums / jnp.maximum(crop_sizes, 1.0)[:, None]

    def back(i, after, micros):
        return attend_back(
            query,
            key,
            value,
            grad_mixed,
            log_total,
            segments,
            counts,
            sum(PAIRS[:i]),
            PAIRS[i],
            after,
            micros,
        )

    if staged:
        ffn_sums, attn_sums = Scattered(places, place_list, 1.2), Scattered(places, place_list, 0.5)

        def spread(terms):
            return terms.reshape(2, extent["z"], extent["x"], *terms.shape[2:])

        def ffn_side(thirds, after):
            operands = (hidden_low, activated, grad_pre, grad_ffn_out)
            terms = ffn_terms(places, place_list, *operands, thirds, after)
            return [spread(t) for t in terms]

        keep_a, give_a = ffn_side([0, 1, 2], [])
        core_a = ffn_sums.core(give_a)
        back_0 = back(0, [give_a], 12)
        own_a, cut_a = ffn_sums.first(keep_a, order(core_a, back_0[0]))
        first_a = ffn_sums.send(cut_a)
        back_1 = back(1, [cut_a], 15)
        vectors = jnp.concatenate([back_0[1], back_1[1]], 1)[:2]
        vec_grad = jnp.concatenate([vectors, vec_grad[2:]], 0)
        grads = [back_0[0], back_1[0]]
        operands = (tokens, mixed, grads, grad_attn_out, vec_grad)
        terms = attn_terms(places, place_list, *operands, [])
        keep_c, give_c = [spread(t) for t in terms]
        core_c = attn_sums.core(give_c)
        own_a, cut_a = ffn_sums.second(own_a, order(first_a, give_c))
        second_a = ffn_sums.send_second(cut_a)
        token_grad = token_gradient(grad_resid, attn_whole, grads, [give_c, cut_a])
        own_c, cut_c = attn_sums.first(keep_c, order(core_c, token_grad))
        own_a, cuts_a = ffn_sums.along_z(own_a, order(second_a, cut_c))
        up_z_a = ffn_sums.send_z(cuts_a)
        first_c = attn_sums.send(cut_c, *cuts_a)
        own_c, cut_c = attn_sums.second(own_c, order(first_c, up_z_a[1], up_z_a[0]))
        second_c = attn_sums.send_second(cut_c)
        own_c, cuts_c = attn_sums.along_z(own_c, second_c)
        up_z_c = attn_sums.send_z(cuts_c)
        ffn_block = ffn_sums.result(own_a, up_z_a)
        block_c = attn_sums.result(own_c, up_z_c)
        attn_block, vec_sum = block_c[:attn_rows], block_c[attn_rows:]
        by_row = ffn_block.reshape(UP_CHUNKS, up_rows, D).transpose(1, 0, 2).reshape(ffn_rows, D)
        ffn_block = jnp.where(holds_up, by_row, ffn_block)
        ffn_summed = to_flat(places, me, ffn_block, vec_sum[5:12], FFN_TAIL)
        attn_summed = to_flat(places, me, attn_block, vec_sum[:5], ATTN_TAIL)
    else:
        backs = [back(i, [], 12) for i in range(len(PAIRS))]
        grads = [b[0] for b in backs]
        token_grad = token_gradient(grad_resid, attn_whole, grads, [])
        grads = jnp.concatenate(grads, 2)
        mats = [contract_rows(tokens, grads[i]) for i in range(3)]
        mats.append(contract_rows(jnp.concatenate(mixed, 1), grad_attn_out))
        vectors = jnp.concatenate([b[1] for b in backs], 1)[:2]
        vec_grad = jnp.concatenate([vectors, vec_grad[2:]], 0)
        attn_full = jnp.concatenate([g.reshape(-1) for g in mats + [vec_grad[:5]]])
        up = contract_rows(hidden_low, grad_pre)
        down = contract_rows(activated, grad_ffn_out)
        ffn_full = jnp.concatenate([g.reshape(-1) for g in (up, down, vec_grad[5:12])])
        attn_summed = lax.psum_scatter(attn_full, AXES, scatter_dimension=0, tiled=True)
        ffn_summed = lax.psum_scatter(ffn_full, AXES, scatter_dimension=0, tiled=True)
    attn_grad = attn_summed / token_total
    ffn_grad = ffn_summed / token_total
    attn_change, moment_attn, square_attn, drift_attn = adam_update(
        attn_param, attn_grad, attn_moment, attn_square, attn_shadow
    )
    ffn_change, moment_ffn, square_ffn, drift_ffn = adam_update(
        ffn_param, ffn_grad, ffn_moment, ffn_square, ffn_shadow
    )
    return (
        final_low,
        pooled,
        token_grad,
        attn_grad,
        ffn_grad,
        attn_change,
        ffn_change,
        moment_attn,
        moment_ffn,
        square_attn,
        square_ffn,
        drift_attn,
        drift_ffn,
    )


def solution(mesh):
    rows, flat = P(AXES, None), P(AXES)
    return jax.shard_map(
        functools.partial(on_device, Places(mesh)),
        mesh=mesh,
        in_specs=(rows, flat, flat, rows) + (flat,) * 8,
        out_specs=(rows, rows, rows) + (flat,) * 10,
        check_vma=False,
    )
```

```python
import functools

import jax
import jax.numpy as jnp
from jax import lax
from jax.experimental import pallas as pl
from jax.experimental.pallas import tpu as pltpu
from jax.sharding import PartitionSpec as P

D = 768
FF = 3072
HEAD = 64
HEADS = 12
ROW = 1024
STEP = 10
CROPS = 16

NORM_EPSILON = 1e-12
NEGATIVE = -1e30
MOMENT_DECAY = 0.9
SQUARE_DECAY = 0.999
LEARN_RATE = 0.001
WEIGHT_DECAY = 0.01
ADAM_EPSILON = 1e-08
SHADOW_RATE = 0.9995
SCALE = HEAD ** (-0.5)

AXES = ("dp", "wide")
BF = jnp.bfloat16
F32 = jnp.float32
UP_CHUNKS = FF // D
ATTN_ROWS = 4 * D
FFN_ROWS = 2 * FF
ATTN_TAIL = 5 * D
FFN_TAIL = FF + 3 * D
AHEAD_PAIRS = (3, 2, 1)
PAIRS = (1, 5)
VEC_ROWS = 16
COUNT_ROW = 12
MIB = 1 << 20
BACK_VMEM = 24 * MIB
TERMS_VMEM = 24 * MIB
TOKEN_VMEM = 24 * MIB
FFN_VMEM = 30 * MIB
ADD_VMEM = 24 * MIB


def dot(left, right, left_dim, right_dim):
    return lax.dot_general(
        left, right, (((left_dim,), (right_dim,)), ((), ())), preferred_element_type=F32
    )


class Places:
    def __init__(self, mesh):
        self.dp, self.wide = mesh.shape["dp"], mesh.shape["wide"]
        self.count = self.dp * self.wide
        self.size = {"c": 2, "y": self.dp // 2}
        self.size["x"] = self.size["y"]
        self.size["z"] = self.wide // self.size["x"]

    def staged(self):
        exact = self.dp == 4 and self.wide % self.size["x"] == 0
        return exact and D % (16 * UP_CHUNKS * self.wide // 2) == 0

    def index(self, y, c, z, x):
        return (y * 2 + c) * self.wide + z * self.size["x"] + x

    def rotation(self, axis, step):
        pairs = []
        extent = self.size
        for y in range(extent["y"]):
            for c in range(2):
                along = axis if len(axis) == 1 else axis[c]
                for z in range(extent["z"]):
                    for x in range(extent["x"]):
                        at = {"y": y, "c": c, "z": z, "x": x}
                        to = dict(at)
                        to[along] = (at[along] + step) % extent[along]
                        pairs.append((self.index(**at), self.index(**to)))
        return pairs

    def send(self, array, axis, step):
        return lax.ppermute(array, AXES, self.rotation(axis, step))

    def here(self):
        outer, inner = lax.axis_index("dp"), lax.axis_index("wide")
        extent = self.size["x"]
        return {"y": outer // 2, "c": outer % 2, "z": inner // extent, "x": inner % extent}


def order(array, *before):
    return lax.optimization_barrier((array,) + before)[0]


class Gathered:
    def __init__(self, places, rows):
        self.places, self.rows = places, rows
        self.deep = places.size["z"] * rows

    def start_z(self, own):
        extent = self.places.size["z"]
        return [own] + [self.places.send(own, "z", k) for k in range(1, extent)]

    def join_z(self, here, blocks):
        rows, extent = self.rows, self.places.size["z"]
        near = jnp.zeros((self.deep, D), BF)
        for k, block in enumerate(blocks):
            at = lax.rem(here["z"] + (extent - k), extent) * rows
            near = lax.dynamic_update_slice_in_dim(near, block[:rows], at, 0)
        return jnp.concatenate([near, self.total([b[rows:] for b in blocks])], 0)

    def join_parts(self, me, parts):
        extent, count = self.places.size["z"], len(parts)
        share = self.rows // count

        def kernel(me_ref, *refs):
            out, sem = refs[-2:]
            for p in range(count):
                for k in range(extent):
                    at = lax.rem(me_ref[2] + (extent - k), extent)
                    pltpu.make_async_copy(
                        refs[p * extent + k], out.at[at, pl.ds(p * share, share)], sem
                    ).start()
            pltpu.make_async_copy(out, out, sem).wait()

        blocks = [b for part in parts for b in part]
        return pl.pallas_call(
            kernel,
            in_specs=[pl.BlockSpec(memory_space=pltpu.SMEM)]
            + [pl.BlockSpec(memory_space=pl.ANY)] * len(blocks),
            out_specs=pl.BlockSpec(memory_space=pltpu.VMEM),
            out_shape=jax.ShapeDtypeStruct((extent, self.rows, D), BF),
            scratch_shapes=[pltpu.SemaphoreType.DMA],
            compiler_params=pltpu.CompilerParams(vmem_limit_bytes=16 * MIB),
            cost_estimate=cost(2),
            name="join",
        )(me, *blocks).reshape(self.deep, D)

    def along_first(self, near):
        places, extent = self.places, self.places.size
        blocks = [near] + [places.send(near, "xy", k) for k in range(1, extent["x"])]
        parts = [b[: self.deep] for b in blocks]
        if near.shape[0] > self.deep:
            parts.append(self.total([b[self.deep :] for b in blocks]))
        return jnp.concatenate(parts, 0)

    def along_second(self, near):
        return [self.places.send(near, "yx", k) for k in range(1, self.places.size["x"])]

    def from_core(self, groups):
        return [self.places.send(g, "c", 1) for g in groups]

    def total(self, arrays):
        result = arrays[0].astype(F32)
        for a in arrays[1:]:
            result = result + a.astype(F32)
        return result.astype(BF)

    def place(self, here, far, first, second):
        extent = self.places.size

        def back(axis, step):
            return lax.rem(here[axis] + (extent[axis] - step), extent[axis])

        core = here["c"] if far == 0 else 1 - here["c"]
        y = jnp.where(core == 0, back("y", second), back("y", first))
        x = jnp.where(core == 0, back("x", first), back("x", second))
        return y, core, x


def read_here(me_ref):
    return {"y": me_ref[0], "c": me_ref[1], "z": me_ref[2], "x": me_ref[3]}


def add_routed(me, keep, arrived, grid, routes, source_block, target_block, target_lead, micros):
    rows, width = keep.shape[-2:]

    def kernel(me_ref, *refs):
        for i in range(len(routes)):
            total = refs[2 * i][...].astype(F32) + refs[2 * i + 1][...].astype(F32)
            refs[2 * len(routes) + i][...] = total.astype(BF)

    def source(route):
        return pl.BlockSpec(source_block + (rows, width), lambda *at: route(*at) + (0, 0))

    target = pl.BlockSpec(target_block[0] + (rows, width), lambda *at: target_block[1](*at) + (0, 0))
    return pl.pallas_call(
        kernel,
        grid_spec=pltpu.PrefetchScalarGridSpec(
            num_scalar_prefetch=1,
            grid=grid,
            in_specs=[source(r) for r in routes for _ in range(2)],
            out_specs=[target] * len(routes),
        ),
        out_shape=[jax.ShapeDtypeStruct(target_lead + (rows, width), BF)] * len(routes),
        compiler_params=pltpu.CompilerParams(vmem_limit_bytes=ADD_VMEM),
        cost_estimate=cost(micros),
        name="add_routed",
    )(me, *([keep, arrived] * len(routes)))


class Scattered:
    def __init__(self, places, me, micros):
        self.places, self.me, self.micros = places, me, micros
        self.z = places.size["z"]

    def core(self, give):
        return self.places.send(give, "c", 1)

    def first(self, keep, arrived):
        deep = 2

        def route(far):
            def pick_block(z, e, me):
                y, x = jnp.abs(me[0] - far), jnp.abs(me[3] - far)
                return jnp.where(me[1] == 0, e, y), z, jnp.where(me[1] == 0, x, e)

            return pick_block

        own, cut = add_routed(
            self.me,
            keep,
            arrived,
            (self.z // deep, 2),
            [route(0), route(1)],
            (None, deep, None),
            ((deep, None), lambda z, e, me: (z, e)),
            (self.z, 2),
            4 * self.micros,
        )
        return own, cut

    def second(self, keep, arrived):
        deep = 2

        def route(far):
            return lambda z, me: (z, jnp.abs(jnp.where(me[1] == 0, me[0], me[3]) - far))

        own, cut = add_routed(
            self.me,
            keep,
            arrived,
            (self.z // deep,),
            [route(0), route(1)],
            (deep, None),
            ((deep,), lambda z, me: (z,)),
            (self.z,),
            2 * self.micros,
        )
        return own, cut

    def along_z(self, keep, arrived):
        def route(k):
            return lambda i, me: (lax.rem(me[2] + k, self.z),)

        own, *cuts = add_routed(
            self.me,
            keep,
            arrived,
            (1,),
            [route(k) for k in range(self.z)],
            (None,),
            ((None,), lambda i, me: (0,)),
            (1,),
            self.micros,
        )
        return own, cuts

    def send(self, cut, *before):
        return self.places.send(order(cut, *before), "xy", 1)

    def send_second(self, cut, *before):
        return self.places.send(order(cut, *before), "yx", 1)

    def send_z(self, cuts, *before):
        return [self.places.send(order(c, *before), "z", k + 1) for k, c in enumerate(cuts)]

    def result(self, own, arrived):
        total = own[0].astype(F32)
        for a in arrived:
            total = total + a[0].astype(F32)
        return total


def to_rows(places, me, flat, rows, tail):
    count = places.count
    block = rows // count * D
    slack = tail // count
    before = lax.ppermute(flat[-tail:], AXES, [(i, i + 1) for i in range(count - 1)])
    joined = jnp.concatenate([before, flat])
    return lax.dynamic_slice_in_dim(joined, tail - me * slack, block).reshape(rows // count, D)


def to_flat(places, me, block, vectors, tail):
    count = places.count
    slack = tail // count
    after = lax.ppermute(block[: tail // D], AXES, [(i + 1, i) for i in range(count - 1)])
    after = jnp.where(me == count - 1, vectors, after)
    joined = jnp.concatenate([block, after], 0).reshape(-1)
    return lax.dynamic_slice_in_dim(joined, me * slack, block.size + slack)


def project_body(step, tokens, weights, vec, query, key, value):
    held = tokens[...]
    query[...] = (dot(held, weights[0:D], 1, 0) + vec[0:1]).astype(BF)
    key[...] = dot(held, weights[D : 2 * D], 1, 0).astype(BF)
    value[...] = (dot(held, weights[2 * D : 3 * D], 1, 0) + vec[1:2]).astype(BF)


def project_kernel(gathered, number, after, me, tokens, *refs):
    groups = refs[:number]
    query, key, value, vec, whole, weights, extras, sem, extra_sem, out_sem = refs[number + after :]
    step = pl.program_id(0)
    extent = gathered.places.size
    rows, deep = gathered.rows, gathered.rows * extent["z"]

    @pl.when(step == 0)
    def _():
        here = read_here(me)
        for g, ref in enumerate(groups):
            pltpu.make_async_copy(
                ref.at[pl.ds(extent["x"] * deep, VEC_ROWS)], extras.at[g], extra_sem
            ).start()
        shape = (extent["y"], 2, extent["z"], extent["x"], rows, D)
        for g, ref in enumerate(groups):
            far, second = divmod(g, extent["x"])
            for first in range(extent["x"]):
                y, core, x = gathered.place(here, far, first, second)
                pltpu.make_async_copy(
                    ref.at[pl.ds(first * deep, deep)].reshape(extent["z"], rows, D),
                    weights.reshape(*shape).at[y, core, :, x],
                    sem,
                ).start()
        pltpu.make_async_copy(extras, extras, extra_sem).wait()
        total = extras[0].astype(F32)
        for g in range(1, number):
            total = total + extras[g].astype(F32)
        vec[...] = total
        pltpu.make_async_copy(weights, weights, sem).wait()
        pltpu.make_async_copy(weights, whole, out_sem).start()

    project_body(step, tokens, weights, vec, query, key, value)

    @pl.when(step == pl.num_programs(0) - 1)
    def _():
        pltpu.make_async_copy(weights, whole, out_sem).wait()


PROJECT_ROWS = 256


def project(tokens, me, gathered, groups, after):
    rows = tokens.shape[0]
    tile = pl.BlockSpec((PROJECT_ROWS, D), lambda i: (i, 0))
    number = len(groups)
    return pl.pallas_call(
        functools.partial(project_kernel, gathered, number, len(after)),
        grid=(rows // PROJECT_ROWS,),
        in_specs=[pl.BlockSpec(memory_space=pltpu.SMEM), tile]
        + [pl.BlockSpec(memory_space=pl.ANY)] * (number + len(after)),
        out_specs=[tile] * 3
        + [pl.BlockSpec((VEC_ROWS, D), lambda i: (0, 0)), pl.BlockSpec(memory_space=pl.ANY)],
        out_shape=[jax.ShapeDtypeStruct((rows, D), BF)] * 3
        + [jax.ShapeDtypeStruct((VEC_ROWS, D), F32), jax.ShapeDtypeStruct((ATTN_ROWS, D), BF)],
        scratch_shapes=[
            pltpu.VMEM((ATTN_ROWS, D), BF),
            pltpu.VMEM((number, VEC_ROWS, D), BF),
            pltpu.SemaphoreType.DMA,
            pltpu.SemaphoreType.DMA,
            pltpu.SemaphoreType.DMA,
        ],
        compiler_params=pltpu.CompilerParams(vmem_limit_bytes=24 * MIB),
        cost_estimate=cost(8),
        name="project",
    )(me, tokens, *groups, *after)


def project_whole(tokens, weights, vec):
    rows = tokens.shape[0]
    tile = pl.BlockSpec((PROJECT_ROWS, D), lambda i: (i, 0))
    return pl.pallas_call(
        lambda *refs: project_body(None, *refs),
        grid=(rows // PROJECT_ROWS,),
        in_specs=[
            tile,
            pl.BlockSpec((ATTN_ROWS, D), lambda i: (0, 0), pipeline_mode=pl.Buffered(1)),
            pl.BlockSpec((VEC_ROWS, D), lambda i: (0, 0)),
        ],
        out_specs=[tile] * 3,
        out_shape=[jax.ShapeDtypeStruct((rows, D), BF)] * 3,
        compiler_params=pltpu.CompilerParams(vmem_limit_bytes=24 * MIB),
        name="project",
    )(tokens, weights, vec)


QUERY_BLOCK = 256
QUERY_BLOCKS = ROW // QUERY_BLOCK


def window(block):
    low = max(0, block - 1) * QUERY_BLOCK
    return low, min(QUERY_BLOCKS, block + 2) * QUERY_BLOCK


def fill_bias(bias, seg_column, seg_row, count):
    for block in range(QUERY_BLOCKS):
        low, high = window(block)
        at = slice(block * QUERY_BLOCK, (block + 1) * QUERY_BLOCK)
        shape = (high - low, QUERY_BLOCK)
        key_pos = low + lax.broadcasted_iota(jnp.int32, shape, 0)
        query_pos = block * QUERY_BLOCK + lax.broadcasted_iota(jnp.int32, shape, 1)
        same = seg_column[low:high, 0:1] == seg_row[0:1, at]
        allowed = (same & (key_pos < count)) | (key_pos == query_pos)
        bias[0 : high - low, at] = jnp.where(allowed, 0.0, NEGATIVE).astype(F32)


def one_head(transposed):
    zero = jnp.zeros((HEAD, transposed.shape[1]), transposed.dtype)
    return (
        jnp.concatenate([transposed[:HEAD], zero], 0),
        jnp.concatenate([zero, transposed[HEAD:]], 0),
    )


def attend_kernel(count, seg_column, seg_row, query, key, value, *refs):
    mixed, log_total, bias = refs[-3:]

    @pl.when(pl.program_id(0) == 0)
    def _():
        fill_bias(bias, seg_column, seg_row, count[0])

    value_t = value[...].T
    query_t = one_head((query[...] * jnp.asarray(SCALE, BF)).T)
    parts = []

    def score(block, h):
        low, high = window(block)
        at = slice(block * QUERY_BLOCK, (block + 1) * QUERY_BLOCK)
        return dot(key[low:high, :], query_t[h][:, at], 1, 0) + bias[0 : high - low, at]

    def mix(block, h, shifted, inverse):
        low, high = window(block)
        at = slice(block * QUERY_BLOCK, (block + 1) * QUERY_BLOCK)
        part = dot(value_t[h * HEAD : (h + 1) * HEAD, low:high], shifted, 1, 0)
        parts.append(part * inverse)
        if h == 1:
            mixed[at, :] = jnp.concatenate(parts, 0).T.astype(BF)
            parts.clear()

    items = [(block, h) for block in range(QUERY_BLOCKS) for h in range(2)]
    ahead, behind = score(*items[0]), None
    for n, (block, h) in enumerate(items):
        at = slice(block * QUERY_BLOCK, (block + 1) * QUERY_BLOCK)
        scores = ahead
        if n + 1 < len(items):
            ahead = score(*items[n + 1])
        if behind is not None:
            mix(*behind)
        top = jnp.max(scores, axis=0, keepdims=True)
        shifted = jnp.exp(scores - top)
        total = jnp.sum(shifted, axis=0, keepdims=True)
        log_total[0, h : h + 1, at] = top + jnp.log(total)
        behind = (block, h, shifted.astype(BF), 1.0 / total)
    mix(*behind)


def attend_specs():
    return [
        pl.BlockSpec(memory_space=pltpu.SMEM),
        pl.BlockSpec((ROW, 1), lambda h: (0, 0)),
        pl.BlockSpec((1, ROW), lambda h: (0, 0)),
    ]


def attend(query, key, value, segments, count, first, pairs, after):
    pair = pl.BlockSpec((ROW, 2 * HEAD), lambda h: (0, h + first))
    return pl.pallas_call(
        attend_kernel,
        grid=(pairs,),
        in_specs=attend_specs() + [pair] * 3 + [pl.BlockSpec(memory_space=pl.ANY)] * len(after),
        out_specs=[
            pl.BlockSpec((ROW, 2 * HEAD), lambda h: (0, h)),
            pl.BlockSpec((1, 8, ROW), lambda h: (h, 0, 0)),
        ],
        out_shape=[
            jax.ShapeDtypeStruct((ROW, pairs * 2 * HEAD), BF),
            jax.ShapeDtypeStruct((pairs, 8, ROW), F32),
        ],
        scratch_shapes=[pltpu.VMEM((3 * QUERY_BLOCK, ROW), F32)],
        compiler_params=pltpu.CompilerParams(vmem_limit_bytes=24 * MIB),
        cost_estimate=cost(25 * pairs / 6),
        name="attend",
    )(count, segments.reshape(ROW, 1), segments.reshape(1, ROW), query, key, value, *after)


def attend_back_kernel(
    count, seg_column, seg_row, query, key, value, grad, log_total, *refs
):
    grads, sums, bias, key_sum, value_sum = refs[-5:]

    @pl.when(pl.program_id(0) == 0)
    def _():
        fill_bias(bias, seg_column, seg_row, count[0])

    query_t = (query[...] * jnp.asarray(SCALE, BF)).T
    key_t = key[...].T
    grad_t = grad[...].T
    query_one, grad_one = one_head(query_t), one_head(grad_t)
    key_sum[...] = jnp.zeros_like(key_sum)
    value_sum[...] = jnp.zeros_like(value_sum)
    parts = []

    def score(block, h):
        low, high = window(block)
        at = slice(block * QUERY_BLOCK, (block + 1) * QUERY_BLOCK)
        scores = dot(key[low:high, :], query_one[h][:, at], 1, 0) + bias[0 : high - low, at]
        return scores, dot(value[low:high, :], grad_one[h][:, at], 1, 0)

    def spread(block, h, grad_scores, probs):
        low, high = window(block)
        at = slice(block * QUERY_BLOCK, (block + 1) * QUERY_BLOCK)
        rows = slice(h * HEAD, (h + 1) * HEAD)
        parts.append(dot(key_t[rows, low:high], grad_scores, 1, 0))
        key_sum[rows, low:high] += dot(query_t[rows, at], grad_scores, 1, 1)
        value_sum[rows, low:high] += dot(grad_t[rows, at], probs, 1, 1)
        if h == 1:
            grads[0, at, :] = (jnp.concatenate(parts, 0) * SCALE).T.astype(BF)
            parts.clear()

    items = [(block, h) for block in range(QUERY_BLOCKS) for h in range(2)]
    ahead, behind = score(*items[0]), None
    for n, (block, h) in enumerate(items):
        at = slice(block * QUERY_BLOCK, (block + 1) * QUERY_BLOCK)
        scores, grad_probs = ahead
        if n + 1 < len(items):
            ahead = score(*items[n + 1])
        if behind is not None:
            spread(*behind)
        probs = jnp.exp(scores - log_total[0, h : h + 1, at])
        weighted = probs * grad_probs
        total = jnp.sum(weighted, axis=0, keepdims=True)
        behind = (block, h, (weighted - probs * total).astype(BF), probs.astype(BF))
    spread(*behind)
    grads[1] = key_sum[...].T.astype(BF)
    grads[2] = value_sum[...].T.astype(BF)
    sums[...] = jnp.zeros_like(sums)
    sums[0:1] = column_sum(grads[0].astype(F32))
    sums[1:2] = column_sum(grads[2].astype(F32))


def attend_back(query, key, value, grad, log_total, segments, count, first, pairs, after, micros):
    pair = pl.BlockSpec((ROW, 2 * HEAD), lambda h: (0, h + first))
    return pl.pallas_call(
        attend_back_kernel,
        grid=(pairs,),
        in_specs=attend_specs()
        + [pair] * 4
        + [pl.BlockSpec((1, 8, ROW), lambda h: (h + first, 0, 0))]
        + [pl.BlockSpec(memory_space=pl.ANY)] * len(after),
        out_specs=[
            pl.BlockSpec((3, ROW, 2 * HEAD), lambda h: (0, 0, h)),
            pl.BlockSpec((8, 2 * HEAD), lambda h: (0, h)),
        ],
        out_shape=[
            jax.ShapeDtypeStruct((3, ROW, pairs * 2 * HEAD), BF),
            jax.ShapeDtypeStruct((8, pairs * 2 * HEAD), F32),
        ],
        scratch_shapes=[
            pltpu.VMEM((3 * QUERY_BLOCK, ROW), F32),
            pltpu.VMEM((2 * HEAD, ROW), F32),
            pltpu.VMEM((2 * HEAD, ROW), F32),
        ],
        compiler_params=pltpu.CompilerParams(vmem_limit_bytes=BACK_VMEM),
        cost_estimate=cost(micros),
        name="attend_back",
    )(
        count,
        segments.reshape(ROW, 1),
        segments.reshape(1, ROW),
        query,
        key,
        value,
        grad,
        log_total,
        *after,
    )


def normalise(resid):
    centred = resid - jnp.mean(resid, axis=-1, keepdims=True)
    spread = jnp.mean(centred * centred, axis=-1, keepdims=True)
    inverse = lax.rsqrt(spread + NORM_EPSILON)
    return centred * inverse, inverse


def normalise_back(cotangent, gain, normal, inverse):
    scaled = cotangent * gain
    mean = jnp.mean(scaled, axis=-1, keepdims=True)
    aligned = jnp.mean(scaled * normal, axis=-1, keepdims=True)
    return inverse * (scaled - mean - normal * aligned)


def cost(micros):
    return pl.CostEstimate(flops=int(micros * 1.1e9), bytes_accessed=MIB, transcendentals=0)


def column_sum(array):
    return jnp.sum(array, axis=0, keepdims=True)


MIDDLE_ROWS = 256


def middle_kernel(
    fetch,
    groups,
    count,
    me,
    seg_row,
    tokens,
    out_grad,
    w_out,
    vec,
    *refs,
):
    mixed, refs = refs[: len(AHEAD_PAIRS)], refs[len(AHEAD_PAIRS) :]
    (
        final_low,
        hidden_low,
        activated,
        grad_pre,
        grad_ffn_out,
        grad_attn_out,
        grad_mixed,
        grad_resid,
        vec_grad,
        crop_sums,
        slope,
        hidden_one,
        normals,
        inverses,
        weights,
        sem,
    ) = refs[groups:]
    step = pl.program_id(0)

    def row(i):
        return vec[i : i + 1]

    def chunk(j):
        return weights[j * D : (j + 1) * D]

    def note(i, value):
        vec_grad[i : i + 1] += value

    @pl.when(step == 0)
    def _():
        vec_grad[...] = jnp.zeros_like(vec_grad)
        crop_sums[...] = jnp.zeros_like(crop_sums)
        fetch(read_here(me), refs[:groups], weights, sem)
        for first in range(0, ROW, MIDDLE_ROWS):
            at = slice(first, first + MIDDLE_ROWS)
            held = jnp.concatenate([ref[at] for ref in mixed], 1)
            resid_one = tokens[at].astype(F32) + (dot(held, w_out[...], 1, 0) + row(2))
            normal, inverse = normalise(resid_one)
            hidden = normal * row(3) + row(4)
            hidden_one[at] = hidden
            hidden_low[at] = hidden.astype(BF)
            normals[at] = normal
            inverses[at] = jnp.broadcast_to(inverse, (MIDDLE_ROWS, 128))
        for j in range(UP_CHUNKS):
            part = weights.at[pl.ds(j * D, D)]
            pltpu.make_async_copy(part, part, sem.at[j]).wait()
        part = weights.at[pl.ds(FF, FF)]
        pltpu.make_async_copy(part, part, sem.at[UP_CHUNKS]).wait()

    @pl.when(step > 0)
    def _():
        middle_tile(
            step - 1,
            count,
            seg_row,
            out_grad,
            w_out,
            row,
            chunk,
            note,
            final_low,
            hidden_low,
            activated,
            grad_pre,
            grad_ffn_out,
            grad_attn_out,
            grad_mixed,
            grad_resid,
            crop_sums,
            slope,
            hidden_one,
            normals,
            inverses,
        )


def middle_tile(
    step,
    count,
    seg_row,
    out_grad,
    w_out,
    row,
    chunk,
    note,
    final_low,
    hidden_low,
    activated,
    grad_pre,
    grad_ffn_out,
    grad_attn_out,
    grad_mixed,
    grad_resid,
    crop_sums,
    slope,
    hidden_one,
    normals,
    inverses,
):
    at = pl.ds(pl.multiple_of(step * MIDDLE_ROWS, MIDDLE_ROWS), MIDDLE_ROWS)
    low = hidden_low[at, :]
    total = hidden_one[at, :] + row(9)
    normal_one, inverse_one = normals[at, :], inverses[at, 0:1]
    ahead, act = dot(low, chunk(0), 1, 0), None
    for j in range(UP_CHUNKS):
        at = slice(j * D, (j + 1) * D)
        pre = ahead + row(5 + j)
        if j + 1 < UP_CHUNKS:
            ahead = dot(low, chunk(j + 1), 1, 0)
        if act is not None:
            total = total + dot(act, chunk(UP_CHUNKS + j - 1), 1, 0)
        share = 0.5 + 0.5 * lax.erf(pre * (0.5**0.5))
        density = jnp.exp(-0.5 * pre * pre) * 0.3989422804014327
        slope[:, at] = share + pre * density
        act = (pre * share).astype(BF)
        activated[:, at] = act
    total = total + dot(act, chunk(2 * UP_CHUNKS - 1), 1, 0)
    normal_two, inverse_two = normalise(total)
    final = normal_two * row(10) + row(11)
    final_low[...] = final.astype(BF)

    first = step * MIDDLE_ROWS
    across = (CROPS, MIDDLE_ROWS)
    position = first + lax.broadcasted_iota(jnp.int32, across, 1)
    crop = lax.broadcasted_iota(jnp.int32, across, 0)
    member = ((seg_row[...] == crop) & (position < count[0])).astype(BF)
    high = final.astype(BF)
    rest = final - high.astype(F32)
    mid = rest.astype(BF)
    tiny = (rest - mid.astype(F32)).astype(BF)
    crop_sums[...] += dot(member, high, 1, 0) + (dot(member, mid, 1, 0) + dot(member, tiny, 1, 0))

    position = first + lax.broadcasted_iota(jnp.int32, (MIDDLE_ROWS, 1), 0)
    valid = (position < count[0]).astype(F32)
    cotangent = out_grad[...].astype(F32) * valid
    note(10, column_sum(cotangent * normal_two))
    note(11, column_sum(cotangent))
    grad_two = normalise_back(cotangent, row(10), normal_two, inverse_two)
    grad_out = grad_two.astype(BF)
    grad_ffn_out[...] = grad_out
    note(9, column_sum(grad_out.astype(F32)))
    grad_hidden = grad_two
    ahead, back = dot(grad_out, chunk(UP_CHUNKS), 1, 1), None
    for j in range(UP_CHUNKS):
        at = slice(j * D, (j + 1) * D)
        grad_act = ahead
        if j + 1 < UP_CHUNKS:
            ahead = dot(grad_out, chunk(UP_CHUNKS + j + 1), 1, 1)
        if back is not None:
            grad_hidden = grad_hidden + dot(back, chunk(j - 1), 1, 1)
        back = (grad_act * slope[:, at]).astype(BF)
        grad_pre[:, at] = back
        note(5 + j, column_sum(back.astype(F32)))
    grad_hidden = grad_hidden + dot(back, chunk(UP_CHUNKS - 1), 1, 1)
    note(3, column_sum(grad_hidden * normal_one))
    note(4, column_sum(grad_hidden))
    grad_one = normalise_back(grad_hidden, row(3), normal_one, inverse_one)
    grad_resid[...] = grad_one
    grad_proj = grad_one.astype(BF)
    grad_attn_out[...] = grad_proj
    note(2, column_sum(grad_proj.astype(F32)))
    grad_mixed[...] = dot(grad_proj, w_out[...], 1, 1).astype(BF)


def middle(count, me, segments, mixed, tokens, out_grad, attn_whole, sources, fetch, vec):
    rows = tokens.shape[0]

    def tile_of(i):
        return jnp.maximum(i - 1, 0)

    def whole(width):
        return pl.BlockSpec((rows, width), lambda i: (0, 0), pipeline_mode=pl.Buffered(1))

    tile = pl.BlockSpec((MIDDLE_ROWS, D), lambda i: (tile_of(i), 0))
    wide = pl.BlockSpec((MIDDLE_ROWS, FF), lambda i: (tile_of(i), 0))
    small = pl.BlockSpec((VEC_ROWS, D), lambda i: (0, 0))

    def shape(width, kind):
        return jax.ShapeDtypeStruct((rows, width), kind)

    return pl.pallas_call(
        functools.partial(middle_kernel, fetch, len(sources)),
        grid=(rows // MIDDLE_ROWS + 1,),
        in_specs=[
            pl.BlockSpec(memory_space=pltpu.SMEM),
            pl.BlockSpec(memory_space=pltpu.SMEM),
            pl.BlockSpec((1, MIDDLE_ROWS), lambda i: (0, tile_of(i))),
            whole(D),
            tile,
            pl.BlockSpec((D, D), lambda i: (3, 0), pipeline_mode=pl.Buffered(1)),
            small,
        ]
        + [whole(2 * HEAD * p) for p in AHEAD_PAIRS]
        + [pl.BlockSpec(memory_space=pl.ANY)] * len(sources),
        out_specs=[tile, whole(D), wide, wide, tile, tile, tile, tile, small, small],
        out_shape=[
            shape(D, BF),
            shape(D, BF),
            shape(FF, BF),
            shape(FF, BF),
            shape(D, BF),
            shape(D, BF),
            shape(D, BF),
            shape(D, F32),
            jax.ShapeDtypeStruct((VEC_ROWS, D), F32),
            jax.ShapeDtypeStruct((CROPS, D), F32),
        ],
        scratch_shapes=[
            pltpu.VMEM((MIDDLE_ROWS, FF), F32),
            pltpu.VMEM((rows, D), F32),
            pltpu.VMEM((rows, D), F32),
            pltpu.VMEM((rows, 128), F32),
            pltpu.VMEM((FFN_ROWS, D), BF),
            pltpu.SemaphoreType.DMA((UP_CHUNKS + 1,)),
        ],
        compiler_params=pltpu.CompilerParams(vmem_limit_bytes=40 * MIB),
        cost_estimate=cost(40),
        name="middle",
    )(count, me, segments.reshape(1, rows), tokens, out_grad, attn_whole, vec, *mixed, *sources)


WIDTH = D // 3


def ffn_terms_kernel(shares, me, hidden, activated, *refs):
    pre, out = refs[:shares], refs[shares : 2 * shares]
    keep, give, hidden_t, block, sem = refs[-5:]
    step = pl.program_id(0)
    slot = lax.rem(step, 2)
    owners, rows = keep.shape[1], keep.shape[2]
    up_rows = rows // UP_CHUNKS
    per_chunk = D // rows

    @pl.when(step >= 2)
    def _():
        pltpu.make_async_copy(block.at[slot], block.at[slot], sem.at[slot]).wait()

    def to(core, y, start):
        @pl.when(core == me[1])
        def _():
            start(keep.at[y])

        @pl.when(core != me[1])
        def _():
            start(give.at[y])

    def down():
        right = jnp.concatenate([ref[...] for ref in out], 1)
        block[slot] = dot(activated[...], right, 0, 0).astype(BF)
        source = block.at[slot].reshape(per_chunk, rows, block.shape[2])

        def start(target):
            at = pl.ds(lax.rem(step, 2) * per_chunk, per_chunk)
            pltpu.make_async_copy(source, target.at[at], sem.at[slot]).start()

        to(lax.div(step, 2), 1, start)

    @pl.when(step < UP_CHUNKS - 1)
    def _():
        down()

    @pl.when(step == UP_CHUNKS - 1)
    def _():
        hidden_t[...] = hidden[...].T
        down()

    @pl.when(step >= UP_CHUNKS)
    def _():
        right = jnp.concatenate([ref[...] for ref in pre], 1)
        block[slot] = dot(hidden_t[...], right, 1, 0).astype(BF)
        chunk = step - UP_CHUNKS
        for core in range(2):
            source = block.at[slot, pl.ds(core * (D // 2), D // 2)]
            source = source.reshape(owners, up_rows, block.shape[2])

            def start(target):
                at = pl.ds(pl.multiple_of(chunk * up_rows, 16), up_rows)
                pltpu.make_async_copy(source, target.at[:, at], sem.at[slot]).start()

            to(core, 0, start)

    @pl.when(step == pl.num_programs(0) - 1)
    def _():
        for s in range(2):
            pltpu.make_async_copy(block.at[s], block.at[s], sem.at[s]).wait()


def ffn_terms(places, me, hidden, activated, grad_pre, grad_out, thirds, after):
    owners = places.wide
    rows = FFN_ROWS // places.count
    shares = len(thirds)
    width = shares * WIDTH
    shape = jax.ShapeDtypeStruct((2, owners, rows, width), BF)

    def pre_spec(third):
        return pl.BlockSpec((ROW, WIDTH), lambda i: (0, 3 * jnp.maximum(i - UP_CHUNKS, 0) + third))

    def out_spec(third):
        return pl.BlockSpec((ROW, WIDTH), lambda i: (0, third))

    def kernel(me_ref, hidden_ref, activated_ref, *refs):
        used = refs[: 2 * shares] + refs[2 * shares + len(after) :]
        ffn_terms_kernel(shares, me_ref, hidden_ref, activated_ref, *used)

    return pl.pallas_call(
        kernel,
        grid=(2 * UP_CHUNKS,),
        in_specs=[
            pl.BlockSpec(memory_space=pltpu.SMEM),
            pl.BlockSpec((ROW, D), lambda i: (0, 0), pipeline_mode=pl.Buffered(1)),
            pl.BlockSpec((ROW, D), lambda i: (0, jnp.minimum(i, UP_CHUNKS - 1))),
        ]
        + [pre_spec(t) for t in thirds]
        + [out_spec(t) for t in thirds]
        + [pl.BlockSpec(memory_space=pl.ANY)] * len(after),
        out_specs=[pl.BlockSpec(memory_space=pl.ANY)] * 2,
        out_shape=[shape] * 2,
        scratch_shapes=[
            pltpu.VMEM((D, ROW), BF),
            pltpu.VMEM((2, D, width), BF),
            pltpu.SemaphoreType.DMA((2,)),
        ],
        compiler_params=pltpu.CompilerParams(vmem_limit_bytes=FFN_VMEM),
        cost_estimate=cost(5 * shares),
        name="ffn_terms",
    )(me, hidden, activated, *([grad_pre] * shares), *([grad_out] * shares), *after)


def attn_terms(places, me, tokens, mixed, grads, grad_proj, vectors, after):
    owners = places.wide
    rows = ATTN_ROWS // places.count
    parts, extra = len(AHEAD_PAIRS), vectors.shape[0]
    shape = jax.ShapeDtypeStruct((2, owners, rows + extra, D), BF)

    def kernel(me_ref, tokens_ref, vectors_ref, proj_ref, *refs):
        mixed_refs, grad_refs, refs = refs[:parts], refs[parts : parts + len(PAIRS)], refs[parts + len(PAIRS) :]
        keep, give, tokens_t, block, below, sem, below_sem = refs[len(after) :]
        step = pl.program_id(0)
        slot = lax.rem(step, 2)

        @pl.when(step == 0)
        def _():
            tokens_t[...] = tokens_ref[...].T
            below[...] = jnp.broadcast_to(vectors_ref[...].astype(BF)[None], below.shape)
            for target in (keep, give):
                for y in range(2):
                    pltpu.make_async_copy(
                        below, target.at[y, :, pl.ds(rows, extra)], below_sem
                    ).start()

        @pl.when(step >= 2)
        def _():
            pltpu.make_async_copy(block.at[slot], block.at[slot], sem.at[slot]).wait()

        @pl.when(step < 3)
        def _():
            right = jnp.concatenate([ref[0] for ref in grad_refs], 1)
            block[slot] = dot(tokens_t[...], right, 1, 0).astype(BF)

        @pl.when(step == 3)
        def _():
            left = jnp.concatenate([ref[...] for ref in mixed_refs], 1)
            block[slot] = dot(left, proj_ref[...], 0, 0).astype(BF)

        source = block.at[slot].reshape(owners, rows, D)
        y, core = lax.div(step, 2), lax.rem(step, 2)

        @pl.when(core == me_ref[1])
        def _():
            pltpu.make_async_copy(source, keep.at[y, :, pl.ds(0, rows)], sem.at[slot]).start()

        @pl.when(core != me_ref[1])
        def _():
            pltpu.make_async_copy(source, give.at[y, :, pl.ds(0, rows)], sem.at[slot]).start()

        @pl.when(step == 3)
        def _():
            for s in range(2):
                pltpu.make_async_copy(block.at[s], block.at[s], sem.at[s]).wait()
            for _ in range(4):
                pltpu.make_async_copy(below, below, below_sem).wait()

    def whole(width):
        return pl.BlockSpec((ROW, width), lambda i: (0, 0), pipeline_mode=pl.Buffered(1))

    return pl.pallas_call(
        kernel,
        grid=(4,),
        in_specs=[
            pl.BlockSpec(memory_space=pltpu.SMEM),
            whole(D),
            pl.BlockSpec((extra, D), lambda i: (0, 0)),
            whole(D),
        ]
        + [whole(2 * HEAD * p) for p in AHEAD_PAIRS]
        + [pl.BlockSpec((1, ROW, 2 * HEAD * p), lambda i: (jnp.minimum(i, 2), 0, 0)) for p in PAIRS]
        + [pl.BlockSpec(memory_space=pl.ANY)] * len(after),
        out_specs=[pl.BlockSpec(memory_space=pl.ANY)] * 2,
        out_shape=[shape] * 2,
        scratch_shapes=[
            pltpu.VMEM((D, ROW), BF),
            pltpu.VMEM((2, D, D), BF),
            pltpu.VMEM((owners, extra, D), BF),
            pltpu.SemaphoreType.DMA((2,)),
            pltpu.SemaphoreType.DMA,
        ],
        compiler_params=pltpu.CompilerParams(vmem_limit_bytes=TERMS_VMEM),
        cost_estimate=cost(6),
        name="attn_terms",
    )(me, tokens, vectors, grad_proj, *mixed, *grads, *after)


def token_grad_kernel(resid, weights, *refs):
    out = refs[-1]
    total = resid[...]
    for m in range(3):
        grad = jnp.concatenate([ref[m] for ref in refs[: len(PAIRS)]], 1)
        total = total + dot(grad, weights[m * D : (m + 1) * D], 1, 1)
    out[...] = total.astype(BF)


def token_gradient(resid, weights, grads, after):
    step = 256
    tile = pl.BlockSpec((step, D), lambda i: (i, 0))
    return pl.pallas_call(
        token_grad_kernel,
        grid=(ROW // step,),
        in_specs=[tile, pl.BlockSpec((3 * D, D), lambda i: (0, 0), pipeline_mode=pl.Buffered(1))]
        + [pl.BlockSpec((3, step, 2 * HEAD * p), lambda i: (0, i, 0)) for p in PAIRS]
        + [pl.BlockSpec(memory_space=pl.ANY)] * len(after),
        out_specs=tile,
        out_shape=jax.ShapeDtypeStruct((ROW, D), BF),
        compiler_params=pltpu.CompilerParams(vmem_limit_bytes=TOKEN_VMEM),
        cost_estimate=cost(2),
        name="token_grad",
    )(resid, weights, *grads, *after)


def adam_update(param, gradient, moment, square, shadow):
    step_float = float(STEP)
    moment_next = MOMENT_DECAY * moment + (1.0 - MOMENT_DECAY) * gradient
    square_next = SQUARE_DECAY * square + (1.0 - SQUARE_DECAY) * gradient * gradient
    moment_hat = moment_next / (1.0 - MOMENT_DECAY**step_float)
    square_hat = square_next / (1.0 - SQUARE_DECAY**step_float)
    change = -LEARN_RATE * (
        moment_hat / (jnp.sqrt(square_hat) + ADAM_EPSILON) + WEIGHT_DECAY * param
    )
    updated = param + change
    drift = (1.0 - SHADOW_RATE) * (updated - shadow)
    return (change, moment_next, square_next, drift)


def contract_rows(left, right):
    return dot(left, right, 0, 0)


def on_device(
    places,
    tokens,
    segments,
    counts,
    out_grad,
    attn_param,
    attn_moment,
    attn_square,
    attn_shadow,
    ffn_param,
    ffn_moment,
    ffn_square,
    ffn_shadow,
):
    assert counts.shape[0] == 1 and tokens.shape[0] == ROW
    number = places.count
    here = places.here()
    place_list = jnp.stack([here[a] for a in ("y", "c", "z", "x")]).astype(jnp.int32)
    me = lax.axis_index("dp") * places.wide + lax.axis_index("wide")
    staged = places.staged()
    attn_rows, ffn_rows = ATTN_ROWS // number, FFN_ROWS // number
    up_rows = ffn_rows // UP_CHUNKS
    holds_up = me < number // 2

    last = me == number - 1
    ends = jnp.concatenate([attn_param[-ATTN_TAIL:], ffn_param[-FFN_TAIL:]]).astype(BF)
    ends = jnp.where(last, ends, jnp.zeros_like(ends))
    if staged:
        digits = [lax.rem(lax.shift_right_logical(counts[0], 3 * i), 8) for i in range(4)]
        count_row = jnp.concatenate([jnp.stack(digits).astype(BF), jnp.zeros((D - 4,), BF)])
        filler = jnp.zeros(((VEC_ROWS - COUNT_ROW - 1) * D,), BF)
        extra = jnp.concatenate([ends, count_row, filler]).reshape(VEC_ROWS, D)
        attn_own = to_rows(places, me, attn_param, ATTN_ROWS, ATTN_TAIL).astype(BF)
        attn_set = Gathered(places, attn_rows)
        blocks = attn_set.start_z(jnp.concatenate([attn_own, extra], 0))
        ffn_own = to_rows(places, me, order(ffn_param, blocks[1]), FFN_ROWS, FFN_TAIL).astype(BF)
        by_chunk = ffn_own.reshape(up_rows, UP_CHUNKS, D).transpose(1, 0, 2).reshape(ffn_rows, D)
        ffn_own = jnp.where(holds_up, by_chunk, ffn_own)
        column = attn_set.join_z(here, blocks)
        half_rows = ffn_rows // 2
        ffn_set = Gathered(places, half_rows)
        blocks = ffn_set.start_z(order(ffn_own[:half_rows], column))
        near = [ffn_set.join_parts(place_list, [blocks])]
        plane = order(attn_set.along_first(column), *blocks)
        blocks = ffn_set.start_z(order(ffn_own[half_rows:], plane, near[0]))
        aside = [places.send(near[0], "xy", 1)]
        crossed = [places.send(near[0], "c", 1)]
        near.append(ffn_set.join_parts(place_list, [blocks]))
        groups = [plane]
        groups += [order(g, aside[0], near[1]) for g in attn_set.along_second(plane)]
        attn_groups = groups + attn_set.from_core(groups)
        aside.append(places.send(near[1], "xy", 1))
        across = [places.send(near[0], "yx", 1)]
        corner = [places.send(aside[0], "yx", 1)]
        query, key, value, vec, attn_whole = project(
            tokens, place_list, attn_set, attn_groups, [aside[0], near[1], crossed[0]]
        )
        token_total = sum(vec[COUNT_ROW, i] * float(8**i) for i in range(4))
        aside = [order(a, query) for a in aside]
        near[1] = order(near[1], query)
        crossed += [places.send(near[1], "c", 1)] + [places.send(a, "c", 1) for a in aside]
        across.append(places.send(near[1], "yx", 1))
        corner.append(places.send(aside[1], "yx", 1))
        extent = places.size
        per_half = UP_CHUNKS // 2
        piece = (extent["z"], per_half, up_rows, D)
        half = extent["y"] // 2

        def fetch(place, refs, weights, sem):
            side = (half, 2, extent["z"], extent["x"])
            up = weights.at[pl.ds(0, FF)].reshape(*((UP_CHUNKS,) + side + (up_rows, D)))
            down = weights.at[pl.ds(FF, FF)].reshape(*(side + (UP_CHUNKS, up_rows, D)))
            ways = [(far, i, j) for far in range(2) for i in range(2) for j in range(2)]
            for i, ref in enumerate(refs):
                h, way = divmod(i, len(ways))
                y, core, x = ffn_set.place(place, *ways[way])

                @pl.when(y < half)
                def _():
                    for part in range(per_half):
                        chunk = h * per_half + part
                        pltpu.make_async_copy(
                            ref.at[:, part], up.at[chunk, y, core, :, x], sem.at[chunk]
                        ).start()

                @pl.when(y >= half)
                def _():
                    chunks = pl.ds(h * per_half, per_half)
                    pltpu.make_async_copy(
                        ref, down.at[y - half, core, :, x, chunks], sem.at[UP_CHUNKS]
                    ).start()

    else:
        token_total = lax.psum(counts[0].astype(F32), AXES)
        vec = lax.psum(ends.astype(F32), AXES).reshape(COUNT_ROW, D)
        vec = jnp.concatenate([vec, jnp.zeros((VEC_ROWS - COUNT_ROW, D), F32)], 0)
        flat = lax.all_gather(attn_param.astype(BF), AXES, axis=0, tiled=True)
        attn_whole = flat[: ATTN_ROWS * D].reshape(ATTN_ROWS, D)
        flat = lax.all_gather(ffn_param.astype(BF), AXES, axis=0, tiled=True)
        w_up = flat[: FF * D].reshape(D, UP_CHUNKS, D).transpose(1, 0, 2).reshape(FF, D)
        w_down = flat[FF * D : FFN_ROWS * D].reshape(FF, D)
        sources = [w_up, w_down]

        def fetch(place, refs, weights, sem):
            w_up, w_down = refs
            for j in range(UP_CHUNKS):
                rows = pl.ds(j * D, D)
                pltpu.make_async_copy(w_up.at[rows], weights.at[rows], sem.at[j]).start()
            down = weights.at[pl.ds(FF, FF)]
            pltpu.make_async_copy(w_down, down, sem.at[UP_CHUNKS]).start()

        query, key, value = project_whole(tokens, attn_whole, vec)

    ahead = []
    for i, pairs in enumerate(AHEAD_PAIRS):
        after = [aside[1]] if staged and i == 0 else []
        first = sum(AHEAD_PAIRS[:i])
        ahead.append(attend(query, key, value, segments, counts, first, pairs, after))
    mixed = [a[0] for a in ahead]
    log_total = jnp.concatenate([a[1] for a in ahead], 0)
    if staged:
        sources = []
        for h in range(2):
            across[h], corner[h] = order(across[h], mixed[h]), order(corner[h], mixed[h])
            mine = [near[h], across[h], aside[h], corner[h]]
            theirs = [crossed[h], places.send(across[h], "c", 1)]
            theirs += [crossed[2 + h], places.send(corner[h], "c", 1)]
            sources += [a.reshape(piece) for a in mine + theirs]
    (
        final_low,
        hidden_low,
        activated,
        grad_pre,
        grad_ffn_out,
        grad_attn_out,
        grad_mixed,
        grad_resid,
        vec_grad,
        crop_sums,
    ) = middle(
        counts,
        place_list,
        segments,
        mixed,
        tokens,
        out_grad,
        attn_whole,
        sources,
        fetch,
        vec,
    )
    is_valid = jnp.arange(ROW, dtype=jnp.int32) < counts[0]
    member = (segments[None, :] == jnp.arange(CROPS, dtype=jnp.int32)[:, None]) & is_valid[None, :]
    crop_sizes = jnp.sum(member.astype(F32), axis=1)
    pooled = crop_sums / jnp.maximum(crop_sizes, 1.0)[:, None]

    def back(i, after, micros):
        return attend_back(
            query,
            key,
            value,
            grad_mixed,
            log_total,
            segments,
            counts,
            sum(PAIRS[:i]),
            PAIRS[i],
            after,
            micros,
        )

    if staged:
        ffn_sums, attn_sums = Scattered(places, place_list, 1.2), Scattered(places, place_list, 0.5)

        def spread(terms):
            return terms.reshape(2, extent["z"], extent["x"], *terms.shape[2:])

        def ffn_side(thirds, after):
            operands = (hidden_low, activated, grad_pre, grad_ffn_out)
            terms = ffn_terms(places, place_list, *operands, thirds, after)
            return [spread(t) for t in terms]

        keep_a, give_a = ffn_side([0, 1, 2], [])
        core_a = ffn_sums.core(give_a)
        back_0 = back(0, [give_a], 12)
        own_a, cut_a = ffn_sums.first(keep_a, order(core_a, back_0[0]))
        first_a = ffn_sums.send(cut_a)
        back_1 = back(1, [cut_a], 15)
        vectors = jnp.concatenate([back_0[1], back_1[1]], 1)[:2]
        vec_grad = jnp.concatenate([vectors, vec_grad[2:]], 0)
        grads = [back_0[0], back_1[0]]
        operands = (tokens, mixed, grads, grad_attn_out, vec_grad)
        terms = attn_terms(places, place_list, *operands, [])
        keep_c, give_c = [spread(t) for t in terms]
        core_c = attn_sums.core(give_c)
        own_a, cut_a = ffn_sums.second(own_a, order(first_a, give_c))
        second_a = ffn_sums.send_second(cut_a)
        token_grad = token_gradient(grad_resid, attn_whole, grads, [give_c, cut_a])
        own_c, cut_c = attn_sums.first(keep_c, order(core_c, token_grad))
        own_a, cuts_a = ffn_sums.along_z(own_a, order(second_a, cut_c))
        up_z_a = ffn_sums.send_z(cuts_a)
        first_c = attn_sums.send(cut_c, *cuts_a)
        own_c, cut_c = attn_sums.second(own_c, order(first_c, up_z_a[1], up_z_a[0]))
        second_c = attn_sums.send_second(cut_c)
        own_c, cuts_c = attn_sums.along_z(own_c, second_c)
        up_z_c = attn_sums.send_z(cuts_c)
        ffn_block = ffn_sums.result(own_a, up_z_a)
        block_c = attn_sums.result(own_c, up_z_c)
        attn_block, vec_sum = block_c[:attn_rows], block_c[attn_rows:]
        by_row = ffn_block.reshape(UP_CHUNKS, up_rows, D).transpose(1, 0, 2).reshape(ffn_rows, D)
        ffn_block = jnp.where(holds_up, by_row, ffn_block)
        ffn_summed = to_flat(places, me, ffn_block, vec_sum[5:12], FFN_TAIL)
        attn_summed = to_flat(places, me, attn_block, vec_sum[:5], ATTN_TAIL)
    else:
        backs = [back(i, [], 12) for i in range(len(PAIRS))]
        grads = [b[0] for b in backs]
        token_grad = token_gradient(grad_resid, attn_whole, grads, [])
        grads = jnp.concatenate(grads, 2)
        mats = [contract_rows(tokens, grads[i]) for i in range(3)]
        mats.append(contract_rows(jnp.concatenate(mixed, 1), grad_attn_out))
        vectors = jnp.concatenate([b[1] for b in backs], 1)[:2]
        vec_grad = jnp.concatenate([vectors, vec_grad[2:]], 0)
        attn_full = jnp.concatenate([g.reshape(-1) for g in mats + [vec_grad[:5]]])
        up = contract_rows(hidden_low, grad_pre)
        down = contract_rows(activated, grad_ffn_out)
        ffn_full = jnp.concatenate([g.reshape(-1) for g in (up, down, vec_grad[5:12])])
        attn_summed = lax.psum_scatter(attn_full, AXES, scatter_dimension=0, tiled=True)
        ffn_summed = lax.psum_scatter(ffn_full, AXES, scatter_dimension=0, tiled=True)
    attn_grad = attn_summed / token_total
    ffn_grad = ffn_summed / token_total
    attn_change, moment_attn, square_attn, drift_attn = adam_update(
        attn_param, attn_grad, attn_moment, attn_square, attn_shadow
    )
    ffn_change, moment_ffn, square_ffn, drift_ffn = adam_update(
        ffn_param, ffn_grad, ffn_moment, ffn_square, ffn_shadow
    )
    return (
        final_low,
        pooled,
        token_grad,
        attn_grad,
        ffn_grad,
        attn_change,
        ffn_change,
        moment_attn,
        moment_ffn,
        square_attn,
        square_ffn,
        drift_attn,
        drift_ffn,
    )


def solution(mesh):
    rows, flat = P(AXES, None), P(AXES)
    return jax.shard_map(
        functools.partial(on_device, Places(mesh)),
        mesh=mesh,
        in_specs=(rows, flat, flat, rows) + (flat,) * 8,
        out_specs=(rows, rows, rows) + (flat,) * 10,
        check_vma=False,
    )
```

```python
import functools

import jax
import jax.numpy as jnp
from jax import lax
from jax.experimental import pallas as pl
from jax.experimental.pallas import tpu as pltpu
from jax.sharding import PartitionSpec as P

D = 768
FF = 3072
HEAD = 64
HEADS = 12
ROW = 1024
STEP = 10
CROPS = 16

NORM_EPSILON = 1e-12
NEGATIVE = -1e30
MOMENT_DECAY = 0.9
SQUARE_DECAY = 0.999
LEARN_RATE = 0.001
WEIGHT_DECAY = 0.01
ADAM_EPSILON = 1e-08
SHADOW_RATE = 0.9995
SCALE = HEAD ** (-0.5)

AXES = ("dp", "wide")
BF = jnp.bfloat16
F32 = jnp.float32
UP_CHUNKS = FF // D
ATTN_ROWS = 4 * D
FFN_ROWS = 2 * FF
ATTN_TAIL = 5 * D
FFN_TAIL = FF + 3 * D
AHEAD_PAIRS = (3, 2, 1)
PAIRS = (1, 5)
VEC_ROWS = 16
COUNT_ROW = 12
MIB = 1 << 20
BACK_VMEM = 24 * MIB
TERMS_VMEM = 24 * MIB
TOKEN_VMEM = 24 * MIB
FFN_VMEM = 30 * MIB
ADD_VMEM = 24 * MIB


def dot(left, right, left_dim, right_dim):
    return lax.dot_general(
        left, right, (((left_dim,), (right_dim,)), ((), ())), preferred_element_type=F32
    )


class Places:
    def __init__(self, mesh):
        self.dp, self.wide = mesh.shape["dp"], mesh.shape["wide"]
        self.count = self.dp * self.wide
        self.size = {"c": 2, "y": self.dp // 2}
        self.size["x"] = self.size["y"]
        self.size["z"] = self.wide // self.size["x"]

    def staged(self):
        exact = self.dp == 4 and self.wide % self.size["x"] == 0
        return exact and D % (16 * UP_CHUNKS * self.wide // 2) == 0

    def index(self, y, c, z, x):
        return (y * 2 + c) * self.wide + z * self.size["x"] + x

    def rotation(self, axis, step):
        pairs = []
        extent = self.size
        for y in range(extent["y"]):
            for c in range(2):
                along = axis if len(axis) == 1 else axis[c]
                for z in range(extent["z"]):
                    for x in range(extent["x"]):
                        at = {"y": y, "c": c, "z": z, "x": x}
                        to = dict(at)
                        to[along] = (at[along] + step) % extent[along]
                        pairs.append((self.index(**at), self.index(**to)))
        return pairs

    def send(self, array, axis, step):
        return lax.ppermute(array, AXES, self.rotation(axis, step))

    def here(self):
        outer, inner = lax.axis_index("dp"), lax.axis_index("wide")
        extent = self.size["x"]
        return {"y": outer // 2, "c": outer % 2, "z": inner // extent, "x": inner % extent}


def order(array, *before):
    return lax.optimization_barrier((array,) + before)[0]


class Gathered:
    def __init__(self, places, rows):
        self.places, self.rows = places, rows
        self.deep = places.size["z"] * rows

    def start_z(self, own):
        extent = self.places.size["z"]
        return [own] + [self.places.send(own, "z", k) for k in range(1, extent)]

    def join_z(self, here, blocks):
        rows, extent = self.rows, self.places.size["z"]
        near = jnp.zeros((self.deep, D), BF)
        for k, block in enumerate(blocks):
            at = lax.rem(here["z"] + (extent - k), extent) * rows
            near = lax.dynamic_update_slice_in_dim(near, block[:rows], at, 0)
        return jnp.concatenate([near, self.total([b[rows:] for b in blocks])], 0)

    def join_parts(self, me, parts):
        extent, count = self.places.size["z"], len(parts)
        share = self.rows // count

        def kernel(me_ref, *refs):
            out, sem = refs[-2:]
            for p in range(count):
                for k in range(extent):
                    at = lax.rem(me_ref[2] + (extent - k), extent)
                    pltpu.make_async_copy(
                        refs[p * extent + k], out.at[at, pl.ds(p * share, share)], sem
                    ).start()
            pltpu.make_async_copy(out, out, sem).wait()

        blocks = [b for part in parts for b in part]
        return pl.pallas_call(
            kernel,
            in_specs=[pl.BlockSpec(memory_space=pltpu.SMEM)]
            + [pl.BlockSpec(memory_space=pl.ANY)] * len(blocks),
            out_specs=pl.BlockSpec(memory_space=pltpu.VMEM),
            out_shape=jax.ShapeDtypeStruct((extent, self.rows, D), BF),
            scratch_shapes=[pltpu.SemaphoreType.DMA],
            compiler_params=pltpu.CompilerParams(vmem_limit_bytes=16 * MIB),
            cost_estimate=cost(2),
            name="join",
        )(me, *blocks).reshape(self.deep, D)

    def along_first(self, near):
        places, extent = self.places, self.places.size
        blocks = [near] + [places.send(near, "xy", k) for k in range(1, extent["x"])]
        parts = [b[: self.deep] for b in blocks]
        if near.shape[0] > self.deep:
            parts.append(self.total([b[self.deep :] for b in blocks]))
        return jnp.concatenate(parts, 0)

    def along_second(self, near):
        return [self.places.send(near, "yx", k) for k in range(1, self.places.size["x"])]

    def from_core(self, groups):
        return [self.places.send(g, "c", 1) for g in groups]

    def total(self, arrays):
        result = arrays[0].astype(F32)
        for a in arrays[1:]:
            result = result + a.astype(F32)
        return result.astype(BF)

    def place(self, here, far, first, second):
        extent = self.places.size

        def back(axis, step):
            return lax.rem(here[axis] + (extent[axis] - step), extent[axis])

        core = here["c"] if far == 0 else 1 - here["c"]
        y = jnp.where(core == 0, back("y", second), back("y", first))
        x = jnp.where(core == 0, back("x", first), back("x", second))
        return y, core, x


def read_here(me_ref):
    return {"y": me_ref[0], "c": me_ref[1], "z": me_ref[2], "x": me_ref[3]}


def add_routed(me, keep, arrived, grid, routes, source_block, target_block, target_lead, micros):
    rows, width = keep.shape[-2:]

    def kernel(me_ref, *refs):
        for i in range(len(routes)):
            total = refs[2 * i][...].astype(F32) + refs[2 * i + 1][...].astype(F32)
            refs[2 * len(routes) + i][...] = total.astype(BF)

    def source(route):
        return pl.BlockSpec(source_block + (rows, width), lambda *at: route(*at) + (0, 0))

    target = pl.BlockSpec(target_block[0] + (rows, width), lambda *at: target_block[1](*at) + (0, 0))
    return pl.pallas_call(
        kernel,
        grid_spec=pltpu.PrefetchScalarGridSpec(
            num_scalar_prefetch=1,
            grid=grid,
            in_specs=[source(r) for r in routes for _ in range(2)],
            out_specs=[target] * len(routes),
        ),
        out_shape=[jax.ShapeDtypeStruct(target_lead + (rows, width), BF)] * len(routes),
        compiler_params=pltpu.CompilerParams(vmem_limit_bytes=ADD_VMEM),
        cost_estimate=cost(micros),
        name="add_routed",
    )(me, *([keep, arrived] * len(routes)))


class Scattered:
    def __init__(self, places, me, micros):
        self.places, self.me, self.micros = places, me, micros
        self.z = places.size["z"]

    def core(self, give):
        return self.places.send(give, "c", 1)

    def first(self, keep, arrived):
        deep = 1

        def route(far):
            def pick_block(z, e, me):
                y, x = jnp.abs(me[0] - far), jnp.abs(me[3] - far)
                return jnp.where(me[1] == 0, e, y), z, jnp.where(me[1] == 0, x, e)

            return pick_block

        own, cut = add_routed(
            self.me,
            keep,
            arrived,
            (self.z // deep, 2),
            [route(0), route(1)],
            (None, deep, None),
            ((deep, None), lambda z, e, me: (z, e)),
            (self.z, 2),
            4 * self.micros,
        )
        return own, cut

    def second(self, keep, arrived):
        deep = 2

        def route(far):
            return lambda z, me: (z, jnp.abs(jnp.where(me[1] == 0, me[0], me[3]) - far))

        own, cut = add_routed(
            self.me,
            keep,
            arrived,
            (self.z // deep,),
            [route(0), route(1)],
            (deep, None),
            ((deep,), lambda z, me: (z,)),
            (self.z,),
            2 * self.micros,
        )
        return own, cut

    def along_z(self, keep, arrived):
        def route(k):
            return lambda i, me: (lax.rem(me[2] + k, self.z),)

        own, *cuts = add_routed(
            self.me,
            keep,
            arrived,
            (1,),
            [route(k) for k in range(self.z)],
            (None,),
            ((None,), lambda i, me: (0,)),
            (1,),
            self.micros,
        )
        return own, cuts

    def send(self, cut, *before):
        return self.places.send(order(cut, *before), "xy", 1)

    def send_second(self, cut, *before):
        return self.places.send(order(cut, *before), "yx", 1)

    def send_z(self, cuts, *before):
        return [self.places.send(order(c, *before), "z", k + 1) for k, c in enumerate(cuts)]

    def result(self, own, arrived):
        total = own[0].astype(F32)
        for a in arrived:
            total = total + a[0].astype(F32)
        return total


def to_rows(places, me, flat, rows, tail):
    count = places.count
    block = rows // count * D
    slack = tail // count
    before = lax.ppermute(flat[-tail:], AXES, [(i, i + 1) for i in range(count - 1)])
    joined = jnp.concatenate([before, flat])
    return lax.dynamic_slice_in_dim(joined, tail - me * slack, block).reshape(rows // count, D)


def to_flat(places, me, block, vectors, tail):
    count = places.count
    slack = tail // count
    after = lax.ppermute(block[: tail // D], AXES, [(i + 1, i) for i in range(count - 1)])
    after = jnp.where(me == count - 1, vectors, after)
    joined = jnp.concatenate([block, after], 0).reshape(-1)
    return lax.dynamic_slice_in_dim(joined, me * slack, block.size + slack)


def project_body(step, tokens, weights, vec, query, key, value):
    held = tokens[...]
    query[...] = (dot(held, weights[0:D], 1, 0) + vec[0:1]).astype(BF)
    key[...] = dot(held, weights[D : 2 * D], 1, 0).astype(BF)
    value[...] = (dot(held, weights[2 * D : 3 * D], 1, 0) + vec[1:2]).astype(BF)


def project_kernel(gathered, number, after, me, tokens, *refs):
    groups = refs[:number]
    query, key, value, vec, whole, weights, extras, sem, extra_sem, out_sem = refs[number + after :]
    step = pl.program_id(0)
    extent = gathered.places.size
    rows, deep = gathered.rows, gathered.rows * extent["z"]

    @pl.when(step == 0)
    def _():
        here = read_here(me)
        for g, ref in enumerate(groups):
            pltpu.make_async_copy(
                ref.at[pl.ds(extent["x"] * deep, VEC_ROWS)], extras.at[g], extra_sem
            ).start()
        shape = (extent["y"], 2, extent["z"], extent["x"], rows, D)
        for g, ref in enumerate(groups):
            far, second = divmod(g, extent["x"])
            for first in range(extent["x"]):
                y, core, x = gathered.place(here, far, first, second)
                pltpu.make_async_copy(
                    ref.at[pl.ds(first * deep, deep)].reshape(extent["z"], rows, D),
                    weights.reshape(*shape).at[y, core, :, x],
                    sem,
                ).start()
        pltpu.make_async_copy(extras, extras, extra_sem).wait()
        total = extras[0].astype(F32)
        for g in range(1, number):
            total = total + extras[g].astype(F32)
        vec[...] = total
        pltpu.make_async_copy(weights, weights, sem).wait()
        pltpu.make_async_copy(weights, whole, out_sem).start()

    project_body(step, tokens, weights, vec, query, key, value)

    @pl.when(step == pl.num_programs(0) - 1)
    def _():
        pltpu.make_async_copy(weights, whole, out_sem).wait()


PROJECT_ROWS = 256


def project(tokens, me, gathered, groups, after):
    rows = tokens.shape[0]
    tile = pl.BlockSpec((PROJECT_ROWS, D), lambda i: (i, 0))
    number = len(groups)
    return pl.pallas_call(
        functools.partial(project_kernel, gathered, number, len(after)),
        grid=(rows // PROJECT_ROWS,),
        in_specs=[pl.BlockSpec(memory_space=pltpu.SMEM), tile]
        + [pl.BlockSpec(memory_space=pl.ANY)] * (number + len(after)),
        out_specs=[tile] * 3
        + [pl.BlockSpec((VEC_ROWS, D), lambda i: (0, 0)), pl.BlockSpec(memory_space=pl.ANY)],
        out_shape=[jax.ShapeDtypeStruct((rows, D), BF)] * 3
        + [jax.ShapeDtypeStruct((VEC_ROWS, D), F32), jax.ShapeDtypeStruct((ATTN_ROWS, D), BF)],
        scratch_shapes=[
            pltpu.VMEM((ATTN_ROWS, D), BF),
            pltpu.VMEM((number, VEC_ROWS, D), BF),
            pltpu.SemaphoreType.DMA,
            pltpu.SemaphoreType.DMA,
            pltpu.SemaphoreType.DMA,
        ],
        compiler_params=pltpu.CompilerParams(vmem_limit_bytes=24 * MIB),
        cost_estimate=cost(8),
        name="project",
    )(me, tokens, *groups, *after)


def project_whole(tokens, weights, vec):
    rows = tokens.shape[0]
    tile = pl.BlockSpec((PROJECT_ROWS, D), lambda i: (i, 0))
    return pl.pallas_call(
        lambda *refs: project_body(None, *refs),
        grid=(rows // PROJECT_ROWS,),
        in_specs=[
            tile,
            pl.BlockSpec((ATTN_ROWS, D), lambda i: (0, 0), pipeline_mode=pl.Buffered(1)),
            pl.BlockSpec((VEC_ROWS, D), lambda i: (0, 0)),
        ],
        out_specs=[tile] * 3,
        out_shape=[jax.ShapeDtypeStruct((rows, D), BF)] * 3,
        compiler_params=pltpu.CompilerParams(vmem_limit_bytes=24 * MIB),
        name="project",
    )(tokens, weights, vec)


QUERY_BLOCK = 256
QUERY_BLOCKS = ROW // QUERY_BLOCK


def window(block):
    low = max(0, block - 1) * QUERY_BLOCK
    return low, min(QUERY_BLOCKS, block + 2) * QUERY_BLOCK


def fill_bias(bias, seg_column, seg_row, count):
    for block in range(QUERY_BLOCKS):
        low, high = window(block)
        at = slice(block * QUERY_BLOCK, (block + 1) * QUERY_BLOCK)
        shape = (high - low, QUERY_BLOCK)
        key_pos = low + lax.broadcasted_iota(jnp.int32, shape, 0)
        query_pos = block * QUERY_BLOCK + lax.broadcasted_iota(jnp.int32, shape, 1)
        same = seg_column[low:high, 0:1] == seg_row[0:1, at]
        allowed = (same & (key_pos < count)) | (key_pos == query_pos)
        bias[0 : high - low, at] = jnp.where(allowed, 0.0, NEGATIVE).astype(F32)


def one_head(transposed):
    zero = jnp.zeros((HEAD, transposed.shape[1]), transposed.dtype)
    return (
        jnp.concatenate([transposed[:HEAD], zero], 0),
        jnp.concatenate([zero, transposed[HEAD:]], 0),
    )


def attend_kernel(count, seg_column, seg_row, query, key, value, *refs):
    mixed, log_total, bias = refs[-3:]

    @pl.when(pl.program_id(0) == 0)
    def _():
        fill_bias(bias, seg_column, seg_row, count[0])

    value_t = value[...].T
    query_t = one_head((query[...] * jnp.asarray(SCALE, BF)).T)
    parts = []

    def score(block, h):
        low, high = window(block)
        at = slice(block * QUERY_BLOCK, (block + 1) * QUERY_BLOCK)
        return dot(key[low:high, :], query_t[h][:, at], 1, 0) + bias[0 : high - low, at]

    def mix(block, h, shifted, inverse):
        low, high = window(block)
        at = slice(block * QUERY_BLOCK, (block + 1) * QUERY_BLOCK)
        part = dot(value_t[h * HEAD : (h + 1) * HEAD, low:high], shifted, 1, 0)
        parts.append(part * inverse)
        if h == 1:
            mixed[at, :] = jnp.concatenate(parts, 0).T.astype(BF)
            parts.clear()

    items = [(block, h) for block in range(QUERY_BLOCKS) for h in range(2)]
    ahead, behind = score(*items[0]), None
    for n, (block, h) in enumerate(items):
        at = slice(block * QUERY_BLOCK, (block + 1) * QUERY_BLOCK)
        scores = ahead
        if n + 1 < len(items):
            ahead = score(*items[n + 1])
        if behind is not None:
            mix(*behind)
        top = jnp.max(scores, axis=0, keepdims=True)
        shifted = jnp.exp(scores - top)
        total = jnp.sum(shifted, axis=0, keepdims=True)
        log_total[0, h : h + 1, at] = top + jnp.log(total)
        behind = (block, h, shifted.astype(BF), 1.0 / total)
    mix(*behind)


def attend_specs():
    return [
        pl.BlockSpec(memory_space=pltpu.SMEM),
        pl.BlockSpec((ROW, 1), lambda h: (0, 0)),
        pl.BlockSpec((1, ROW), lambda h: (0, 0)),
    ]


def attend(query, key, value, segments, count, first, pairs, after):
    pair = pl.BlockSpec((ROW, 2 * HEAD), lambda h: (0, h + first))
    return pl.pallas_call(
        attend_kernel,
        grid=(pairs,),
        in_specs=attend_specs() + [pair] * 3 + [pl.BlockSpec(memory_space=pl.ANY)] * len(after),
        out_specs=[
            pl.BlockSpec((ROW, 2 * HEAD), lambda h: (0, h)),
            pl.BlockSpec((1, 8, ROW), lambda h: (h, 0, 0)),
        ],
        out_shape=[
            jax.ShapeDtypeStruct((ROW, pairs * 2 * HEAD), BF),
            jax.ShapeDtypeStruct((pairs, 8, ROW), F32),
        ],
        scratch_shapes=[pltpu.VMEM((3 * QUERY_BLOCK, ROW), F32)],
        compiler_params=pltpu.CompilerParams(vmem_limit_bytes=24 * MIB),
        cost_estimate=cost(25 * pairs / 6),
        name="attend",
    )(count, segments.reshape(ROW, 1), segments.reshape(1, ROW), query, key, value, *after)


def attend_back_kernel(
    count, seg_column, seg_row, query, key, value, grad, log_total, *refs
):
    grads, sums, bias, key_sum, value_sum = refs[-5:]

    @pl.when(pl.program_id(0) == 0)
    def _():
        fill_bias(bias, seg_column, seg_row, count[0])

    query_t = (query[...] * jnp.asarray(SCALE, BF)).T
    key_t = key[...].T
    grad_t = grad[...].T
    query_one, grad_one = one_head(query_t), one_head(grad_t)
    key_sum[...] = jnp.zeros_like(key_sum)
    value_sum[...] = jnp.zeros_like(value_sum)
    parts = []

    def score(block, h):
        low, high = window(block)
        at = slice(block * QUERY_BLOCK, (block + 1) * QUERY_BLOCK)
        scores = dot(key[low:high, :], query_one[h][:, at], 1, 0) + bias[0 : high - low, at]
        return scores, dot(value[low:high, :], grad_one[h][:, at], 1, 0)

    def spread(block, h, grad_scores, probs):
        low, high = window(block)
        at = slice(block * QUERY_BLOCK, (block + 1) * QUERY_BLOCK)
        rows = slice(h * HEAD, (h + 1) * HEAD)
        parts.append(dot(key_t[rows, low:high], grad_scores, 1, 0))
        key_sum[rows, low:high] += dot(query_t[rows, at], grad_scores, 1, 1)
        value_sum[rows, low:high] += dot(grad_t[rows, at], probs, 1, 1)
        if h == 1:
            grads[0, at, :] = (jnp.concatenate(parts, 0) * SCALE).T.astype(BF)
            parts.clear()

    items = [(block, h) for block in range(QUERY_BLOCKS) for h in range(2)]
    ahead, behind = score(*items[0]), None
    for n, (block, h) in enumerate(items):
        at = slice(block * QUERY_BLOCK, (block + 1) * QUERY_BLOCK)
        scores, grad_probs = ahead
        if n + 1 < len(items):
            ahead = score(*items[n + 1])
        if behind is not None:
            spread(*behind)
        probs = jnp.exp(scores - log_total[0, h : h + 1, at])
        weighted = probs * grad_probs
        total = jnp.sum(weighted, axis=0, keepdims=True)
        behind = (block, h, (weighted - probs * total).astype(BF), probs.astype(BF))
    spread(*behind)
    grads[1] = key_sum[...].T.astype(BF)
    grads[2] = value_sum[...].T.astype(BF)
    sums[...] = jnp.zeros_like(sums)
    sums[0:1] = column_sum(grads[0].astype(F32))
    sums[1:2] = column_sum(grads[2].astype(F32))


def attend_back(query, key, value, grad, log_total, segments, count, first, pairs, after, micros):
    pair = pl.BlockSpec((ROW, 2 * HEAD), lambda h: (0, h + first))
    return pl.pallas_call(
        attend_back_kernel,
        grid=(pairs,),
        in_specs=attend_specs()
        + [pair] * 4
        + [pl.BlockSpec((1, 8, ROW), lambda h: (h + first, 0, 0))]
        + [pl.BlockSpec(memory_space=pl.ANY)] * len(after),
        out_specs=[
            pl.BlockSpec((3, ROW, 2 * HEAD), lambda h: (0, 0, h)),
            pl.BlockSpec((8, 2 * HEAD), lambda h: (0, h)),
        ],
        out_shape=[
            jax.ShapeDtypeStruct((3, ROW, pairs * 2 * HEAD), BF),
            jax.ShapeDtypeStruct((8, pairs * 2 * HEAD), F32),
        ],
        scratch_shapes=[
            pltpu.VMEM((3 * QUERY_BLOCK, ROW), F32),
            pltpu.VMEM((2 * HEAD, ROW), F32),
            pltpu.VMEM((2 * HEAD, ROW), F32),
        ],
        compiler_params=pltpu.CompilerParams(vmem_limit_bytes=BACK_VMEM),
        cost_estimate=cost(micros),
        name="attend_back",
    )(
        count,
        segments.reshape(ROW, 1),
        segments.reshape(1, ROW),
        query,
        key,
        value,
        grad,
        log_total,
        *after,
    )


def normalise(resid):
    centred = resid - jnp.mean(resid, axis=-1, keepdims=True)
    spread = jnp.mean(centred * centred, axis=-1, keepdims=True)
    inverse = lax.rsqrt(spread + NORM_EPSILON)
    return centred * inverse, inverse


def normalise_back(cotangent, gain, normal, inverse):
    scaled = cotangent * gain
    mean = jnp.mean(scaled, axis=-1, keepdims=True)
    aligned = jnp.mean(scaled * normal, axis=-1, keepdims=True)
    return inverse * (scaled - mean - normal * aligned)


def cost(micros):
    return pl.CostEstimate(flops=int(micros * 1.1e9), bytes_accessed=MIB, transcendentals=0)


def column_sum(array):
    return jnp.sum(array, axis=0, keepdims=True)


MIDDLE_ROWS = 256


def middle_kernel(
    fetch,
    groups,
    count,
    me,
    seg_row,
    tokens,
    out_grad,
    w_out,
    vec,
    *refs,
):
    mixed, refs = refs[: len(AHEAD_PAIRS)], refs[len(AHEAD_PAIRS) :]
    (
        final_low,
        hidden_low,
        activated,
        grad_pre,
        grad_ffn_out,
        grad_attn_out,
        grad_mixed,
        grad_resid,
        vec_grad,
        crop_sums,
        slope,
        hidden_one,
        normals,
        inverses,
        weights,
        sem,
    ) = refs[groups:]
    step = pl.program_id(0)

    def row(i):
        return vec[i : i + 1]

    def chunk(j):
        return weights[j * D : (j + 1) * D]

    def note(i, value):
        vec_grad[i : i + 1] += value

    @pl.when(step == 0)
    def _():
        vec_grad[...] = jnp.zeros_like(vec_grad)
        crop_sums[...] = jnp.zeros_like(crop_sums)
        fetch(read_here(me), refs[:groups], weights, sem)
        for first in range(0, ROW, MIDDLE_ROWS):
            at = slice(first, first + MIDDLE_ROWS)
            held = jnp.concatenate([ref[at] for ref in mixed], 1)
            resid_one = tokens[at].astype(F32) + (dot(held, w_out[...], 1, 0) + row(2))
            normal, inverse = normalise(resid_one)
            hidden = normal * row(3) + row(4)
            hidden_one[at] = hidden
            hidden_low[at] = hidden.astype(BF)
            normals[at] = normal
            inverses[at] = jnp.broadcast_to(inverse, (MIDDLE_ROWS, 128))
        for j in range(UP_CHUNKS):
            part = weights.at[pl.ds(j * D, D)]
            pltpu.make_async_copy(part, part, sem.at[j]).wait()
        part = weights.at[pl.ds(FF, FF)]
        pltpu.make_async_copy(part, part, sem.at[UP_CHUNKS]).wait()

    @pl.when(step > 0)
    def _():
        middle_tile(
            step - 1,
            count,
            seg_row,
            out_grad,
            w_out,
            row,
            chunk,
            note,
            final_low,
            hidden_low,
            activated,
            grad_pre,
            grad_ffn_out,
            grad_attn_out,
            grad_mixed,
            grad_resid,
            crop_sums,
            slope,
            hidden_one,
            normals,
            inverses,
        )


def middle_tile(
    step,
    count,
    seg_row,
    out_grad,
    w_out,
    row,
    chunk,
    note,
    final_low,
    hidden_low,
    activated,
    grad_pre,
    grad_ffn_out,
    grad_attn_out,
    grad_mixed,
    grad_resid,
    crop_sums,
    slope,
    hidden_one,
    normals,
    inverses,
):
    at = pl.ds(pl.multiple_of(step * MIDDLE_ROWS, MIDDLE_ROWS), MIDDLE_ROWS)
    low = hidden_low[at, :]
    total = hidden_one[at, :] + row(9)
    normal_one, inverse_one = normals[at, :], inverses[at, 0:1]
    ahead, act = dot(low, chunk(0), 1, 0), None
    for j in range(UP_CHUNKS):
        at = slice(j * D, (j + 1) * D)
        pre = ahead + row(5 + j)
        if j + 1 < UP_CHUNKS:
            ahead = dot(low, chunk(j + 1), 1, 0)
        if act is not None:
            total = total + dot(act, chunk(UP_CHUNKS + j - 1), 1, 0)
        share = 0.5 + 0.5 * lax.erf(pre * (0.5**0.5))
        density = jnp.exp(-0.5 * pre * pre) * 0.3989422804014327
        slope[:, at] = share + pre * density
        act = (pre * share).astype(BF)
        activated[:, at] = act
    total = total + dot(act, chunk(2 * UP_CHUNKS - 1), 1, 0)
    normal_two, inverse_two = normalise(total)
    final = normal_two * row(10) + row(11)
    final_low[...] = final.astype(BF)

    first = step * MIDDLE_ROWS
    across = (CROPS, MIDDLE_ROWS)
    position = first + lax.broadcasted_iota(jnp.int32, across, 1)
    crop = lax.broadcasted_iota(jnp.int32, across, 0)
    member = ((seg_row[...] == crop) & (position < count[0])).astype(BF)
    high = final.astype(BF)
    rest = final - high.astype(F32)
    mid = rest.astype(BF)
    tiny = (rest - mid.astype(F32)).astype(BF)
    crop_sums[...] += dot(member, high, 1, 0) + (dot(member, mid, 1, 0) + dot(member, tiny, 1, 0))

    position = first + lax.broadcasted_iota(jnp.int32, (MIDDLE_ROWS, 1), 0)
    valid = (position < count[0]).astype(F32)
    cotangent = out_grad[...].astype(F32) * valid
    note(10, column_sum(cotangent * normal_two))
    note(11, column_sum(cotangent))
    grad_two = normalise_back(cotangent, row(10), normal_two, inverse_two)
    grad_out = grad_two.astype(BF)
    grad_ffn_out[...] = grad_out
    note(9, column_sum(grad_out.astype(F32)))
    grad_hidden = grad_two
    ahead, back = dot(grad_out, chunk(UP_CHUNKS), 1, 1), None
    for j in range(UP_CHUNKS):
        at = slice(j * D, (j + 1) * D)
        grad_act = ahead
        if j + 1 < UP_CHUNKS:
            ahead = dot(grad_out, chunk(UP_CHUNKS + j + 1), 1, 1)
        if back is not None:
            grad_hidden = grad_hidden + dot(back, chunk(j - 1), 1, 1)
        back = (grad_act * slope[:, at]).astype(BF)
        grad_pre[:, at] = back
        note(5 + j, column_sum(back.astype(F32)))
    grad_hidden = grad_hidden + dot(back, chunk(UP_CHUNKS - 1), 1, 1)
    note(3, column_sum(grad_hidden * normal_one))
    note(4, column_sum(grad_hidden))
    grad_one = normalise_back(grad_hidden, row(3), normal_one, inverse_one)
    grad_resid[...] = grad_one
    grad_proj = grad_one.astype(BF)
    grad_attn_out[...] = grad_proj
    note(2, column_sum(grad_proj.astype(F32)))
    grad_mixed[...] = dot(grad_proj, w_out[...], 1, 1).astype(BF)


def middle(count, me, segments, mixed, tokens, out_grad, attn_whole, sources, fetch, vec):
    rows = tokens.shape[0]

    def tile_of(i):
        return jnp.maximum(i - 1, 0)

    def whole(width):
        return pl.BlockSpec((rows, width), lambda i: (0, 0), pipeline_mode=pl.Buffered(1))

    tile = pl.BlockSpec((MIDDLE_ROWS, D), lambda i: (tile_of(i), 0))
    wide = pl.BlockSpec((MIDDLE_ROWS, FF), lambda i: (tile_of(i), 0))
    small = pl.BlockSpec((VEC_ROWS, D), lambda i: (0, 0))

    def shape(width, kind):
        return jax.ShapeDtypeStruct((rows, width), kind)

    return pl.pallas_call(
        functools.partial(middle_kernel, fetch, len(sources)),
        grid=(rows // MIDDLE_ROWS + 1,),
        in_specs=[
            pl.BlockSpec(memory_space=pltpu.SMEM),
            pl.BlockSpec(memory_space=pltpu.SMEM),
            pl.BlockSpec((1, MIDDLE_ROWS), lambda i: (0, tile_of(i))),
            whole(D),
            tile,
            pl.BlockSpec((D, D), lambda i: (3, 0), pipeline_mode=pl.Buffered(1)),
            small,
        ]
        + [whole(2 * HEAD * p) for p in AHEAD_PAIRS]
        + [pl.BlockSpec(memory_space=pl.ANY)] * len(sources),
        out_specs=[tile, whole(D), wide, wide, tile, tile, tile, tile, small, small],
        out_shape=[
            shape(D, BF),
            shape(D, BF),
            shape(FF, BF),
            shape(FF, BF),
            shape(D, BF),
            shape(D, BF),
            shape(D, BF),
            shape(D, F32),
            jax.ShapeDtypeStruct((VEC_ROWS, D), F32),
            jax.ShapeDtypeStruct((CROPS, D), F32),
        ],
        scratch_shapes=[
            pltpu.VMEM((MIDDLE_ROWS, FF), F32),
            pltpu.VMEM((rows, D), F32),
            pltpu.VMEM((rows, D), F32),
            pltpu.VMEM((rows, 128), F32),
            pltpu.VMEM((FFN_ROWS, D), BF),
            pltpu.SemaphoreType.DMA((UP_CHUNKS + 1,)),
        ],
        compiler_params=pltpu.CompilerParams(vmem_limit_bytes=40 * MIB),
        cost_estimate=cost(40),
        name="middle",
    )(count, me, segments.reshape(1, rows), tokens, out_grad, attn_whole, vec, *mixed, *sources)


WIDTH = D // 3


def ffn_terms_kernel(shares, me, hidden, activated, *refs):
    pre, out = refs[:shares], refs[shares : 2 * shares]
    keep, give, hidden_t, block, sem = refs[-5:]
    step = pl.program_id(0)
    slot = lax.rem(step, 2)
    owners, rows = keep.shape[1], keep.shape[2]
    up_rows = rows // UP_CHUNKS
    per_chunk = D // rows

    @pl.when(step >= 2)
    def _():
        pltpu.make_async_copy(block.at[slot], block.at[slot], sem.at[slot]).wait()

    def to(core, y, start):
        @pl.when(core == me[1])
        def _():
            start(keep.at[y])

        @pl.when(core != me[1])
        def _():
            start(give.at[y])

    def down():
        right = jnp.concatenate([ref[...] for ref in out], 1)
        block[slot] = dot(activated[...], right, 0, 0).astype(BF)
        source = block.at[slot].reshape(per_chunk, rows, block.shape[2])

        def start(target):
            at = pl.ds(lax.rem(step, 2) * per_chunk, per_chunk)
            pltpu.make_async_copy(source, target.at[at], sem.at[slot]).start()

        to(lax.div(step, 2), 1, start)

    @pl.when(step < UP_CHUNKS - 1)
    def _():
        down()

    @pl.when(step == UP_CHUNKS - 1)
    def _():
        hidden_t[...] = hidden[...].T
        down()

    @pl.when(step >= UP_CHUNKS)
    def _():
        right = jnp.concatenate([ref[...] for ref in pre], 1)
        block[slot] = dot(hidden_t[...], right, 1, 0).astype(BF)
        chunk = step - UP_CHUNKS
        for core in range(2):
            source = block.at[slot, pl.ds(core * (D // 2), D // 2)]
            source = source.reshape(owners, up_rows, block.shape[2])

            def start(target):
                at = pl.ds(pl.multiple_of(chunk * up_rows, 16), up_rows)
                pltpu.make_async_copy(source, target.at[:, at], sem.at[slot]).start()

            to(core, 0, start)

    @pl.when(step == pl.num_programs(0) - 1)
    def _():
        for s in range(2):
            pltpu.make_async_copy(block.at[s], block.at[s], sem.at[s]).wait()


def ffn_terms(places, me, hidden, activated, grad_pre, grad_out, thirds, after):
    owners = places.wide
    rows = FFN_ROWS // places.count
    shares = len(thirds)
    width = shares * WIDTH
    shape = jax.ShapeDtypeStruct((2, owners, rows, width), BF)

    def pre_spec(third):
        return pl.BlockSpec((ROW, WIDTH), lambda i: (0, 3 * jnp.maximum(i - UP_CHUNKS, 0) + third))

    def out_spec(third):
        return pl.BlockSpec((ROW, WIDTH), lambda i: (0, third))

    def kernel(me_ref, hidden_ref, activated_ref, *refs):
        used = refs[: 2 * shares] + refs[2 * shares + len(after) :]
        ffn_terms_kernel(shares, me_ref, hidden_ref, activated_ref, *used)

    return pl.pallas_call(
        kernel,
        grid=(2 * UP_CHUNKS,),
        in_specs=[
            pl.BlockSpec(memory_space=pltpu.SMEM),
            pl.BlockSpec((ROW, D), lambda i: (0, 0), pipeline_mode=pl.Buffered(1)),
            pl.BlockSpec((ROW, D), lambda i: (0, jnp.minimum(i, UP_CHUNKS - 1))),
        ]
        + [pre_spec(t) for t in thirds]
        + [out_spec(t) for t in thirds]
        + [pl.BlockSpec(memory_space=pl.ANY)] * len(after),
        out_specs=[pl.BlockSpec(memory_space=pl.ANY)] * 2,
        out_shape=[shape] * 2,
        scratch_shapes=[
            pltpu.VMEM((D, ROW), BF),
            pltpu.VMEM((2, D, width), BF),
            pltpu.SemaphoreType.DMA((2,)),
        ],
        compiler_params=pltpu.CompilerParams(vmem_limit_bytes=FFN_VMEM),
        cost_estimate=cost(5 * shares),
        name="ffn_terms",
    )(me, hidden, activated, *([grad_pre] * shares), *([grad_out] * shares), *after)


def attn_terms(places, me, tokens, mixed, grads, grad_proj, vectors, after):
    owners = places.wide
    rows = ATTN_ROWS // places.count
    parts, extra = len(AHEAD_PAIRS), vectors.shape[0]
    shape = jax.ShapeDtypeStruct((2, owners, rows + extra, D), BF)

    def kernel(me_ref, tokens_ref, vectors_ref, proj_ref, *refs):
        mixed_refs, grad_refs, refs = refs[:parts], refs[parts : parts + len(PAIRS)], refs[parts + len(PAIRS) :]
        keep, give, tokens_t, block, below, sem, below_sem = refs[len(after) :]
        step = pl.program_id(0)
        slot = lax.rem(step, 2)

        @pl.when(step == 0)
        def _():
            tokens_t[...] = tokens_ref[...].T
            below[...] = jnp.broadcast_to(vectors_ref[...].astype(BF)[None], below.shape)
            for target in (keep, give):
                for y in range(2):
                    pltpu.make_async_copy(
                        below, target.at[y, :, pl.ds(rows, extra)], below_sem
                    ).start()

        @pl.when(step >= 2)
        def _():
            pltpu.make_async_copy(block.at[slot], block.at[slot], sem.at[slot]).wait()

        @pl.when(step < 3)
        def _():
            right = jnp.concatenate([ref[0] for ref in grad_refs], 1)
            block[slot] = dot(tokens_t[...], right, 1, 0).astype(BF)

        @pl.when(step == 3)
        def _():
            left = jnp.concatenate([ref[...] for ref in mixed_refs], 1)
            block[slot] = dot(left, proj_ref[...], 0, 0).astype(BF)

        source = block.at[slot].reshape(owners, rows, D)
        y, core = lax.div(step, 2), lax.rem(step, 2)

        @pl.when(core == me_ref[1])
        def _():
            pltpu.make_async_copy(source, keep.at[y, :, pl.ds(0, rows)], sem.at[slot]).start()

        @pl.when(core != me_ref[1])
        def _():
            pltpu.make_async_copy(source, give.at[y, :, pl.ds(0, rows)], sem.at[slot]).start()

        @pl.when(step == 3)
        def _():
            for s in range(2):
                pltpu.make_async_copy(block.at[s], block.at[s], sem.at[s]).wait()
            for _ in range(4):
                pltpu.make_async_copy(below, below, below_sem).wait()

    def whole(width):
        return pl.BlockSpec((ROW, width), lambda i: (0, 0), pipeline_mode=pl.Buffered(1))

    return pl.pallas_call(
        kernel,
        grid=(4,),
        in_specs=[
            pl.BlockSpec(memory_space=pltpu.SMEM),
            whole(D),
            pl.BlockSpec((extra, D), lambda i: (0, 0)),
            whole(D),
        ]
        + [whole(2 * HEAD * p) for p in AHEAD_PAIRS]
        + [pl.BlockSpec((1, ROW, 2 * HEAD * p), lambda i: (jnp.minimum(i, 2), 0, 0)) for p in PAIRS]
        + [pl.BlockSpec(memory_space=pl.ANY)] * len(after),
        out_specs=[pl.BlockSpec(memory_space=pl.ANY)] * 2,
        out_shape=[shape] * 2,
        scratch_shapes=[
            pltpu.VMEM((D, ROW), BF),
            pltpu.VMEM((2, D, D), BF),
            pltpu.VMEM((owners, extra, D), BF),
            pltpu.SemaphoreType.DMA((2,)),
            pltpu.SemaphoreType.DMA,
        ],
        compiler_params=pltpu.CompilerParams(vmem_limit_bytes=TERMS_VMEM),
        cost_estimate=cost(6),
        name="attn_terms",
    )(me, tokens, vectors, grad_proj, *mixed, *grads, *after)


def token_grad_kernel(resid, weights, *refs):
    out = refs[-1]
    total = resid[...]
    for m in range(3):
        grad = jnp.concatenate([ref[m] for ref in refs[: len(PAIRS)]], 1)
        total = total + dot(grad, weights[m * D : (m + 1) * D], 1, 1)
    out[...] = total.astype(BF)


def token_gradient(resid, weights, grads, after):
    step = 256
    tile = pl.BlockSpec((step, D), lambda i: (i, 0))
    return pl.pallas_call(
        token_grad_kernel,
        grid=(ROW // step,),
        in_specs=[tile, pl.BlockSpec((3 * D, D), lambda i: (0, 0), pipeline_mode=pl.Buffered(1))]
        + [pl.BlockSpec((3, step, 2 * HEAD * p), lambda i: (0, i, 0)) for p in PAIRS]
        + [pl.BlockSpec(memory_space=pl.ANY)] * len(after),
        out_specs=tile,
        out_shape=jax.ShapeDtypeStruct((ROW, D), BF),
        compiler_params=pltpu.CompilerParams(vmem_limit_bytes=TOKEN_VMEM),
        cost_estimate=cost(2),
        name="token_grad",
    )(resid, weights, *grads, *after)


def adam_update(param, gradient, moment, square, shadow):
    step_float = float(STEP)
    moment_next = MOMENT_DECAY * moment + (1.0 - MOMENT_DECAY) * gradient
    square_next = SQUARE_DECAY * square + (1.0 - SQUARE_DECAY) * gradient * gradient
    moment_hat = moment_next / (1.0 - MOMENT_DECAY**step_float)
    square_hat = square_next / (1.0 - SQUARE_DECAY**step_float)
    change = -LEARN_RATE * (
        moment_hat / (jnp.sqrt(square_hat) + ADAM_EPSILON) + WEIGHT_DECAY * param
    )
    updated = param + change
    drift = (1.0 - SHADOW_RATE) * (updated - shadow)
    return (change, moment_next, square_next, drift)


def contract_rows(left, right):
    return dot(left, right, 0, 0)


def on_device(
    places,
    tokens,
    segments,
    counts,
    out_grad,
    attn_param,
    attn_moment,
    attn_square,
    attn_shadow,
    ffn_param,
    ffn_moment,
    ffn_square,
    ffn_shadow,
):
    assert counts.shape[0] == 1 and tokens.shape[0] == ROW
    number = places.count
    here = places.here()
    place_list = jnp.stack([here[a] for a in ("y", "c", "z", "x")]).astype(jnp.int32)
    me = lax.axis_index("dp") * places.wide + lax.axis_index("wide")
    staged = places.staged()
    attn_rows, ffn_rows = ATTN_ROWS // number, FFN_ROWS // number
    up_rows = ffn_rows // UP_CHUNKS
    holds_up = me < number // 2

    last = me == number - 1
    ends = jnp.concatenate([attn_param[-ATTN_TAIL:], ffn_param[-FFN_TAIL:]]).astype(BF)
    ends = jnp.where(last, ends, jnp.zeros_like(ends))
    if staged:
        digits = [lax.rem(lax.shift_right_logical(counts[0], 3 * i), 8) for i in range(4)]
        count_row = jnp.concatenate([jnp.stack(digits).astype(BF), jnp.zeros((D - 4,), BF)])
        filler = jnp.zeros(((VEC_ROWS - COUNT_ROW - 1) * D,), BF)
        extra = jnp.concatenate([ends, count_row, filler]).reshape(VEC_ROWS, D)
        attn_own = to_rows(places, me, attn_param, ATTN_ROWS, ATTN_TAIL).astype(BF)
        attn_set = Gathered(places, attn_rows)
        blocks = attn_set.start_z(jnp.concatenate([attn_own, extra], 0))
        ffn_own = to_rows(places, me, order(ffn_param, blocks[1]), FFN_ROWS, FFN_TAIL).astype(BF)
        by_chunk = ffn_own.reshape(up_rows, UP_CHUNKS, D).transpose(1, 0, 2).reshape(ffn_rows, D)
        ffn_own = jnp.where(holds_up, by_chunk, ffn_own)
        column = attn_set.join_z(here, blocks)
        half_rows = ffn_rows // 2
        ffn_set = Gathered(places, half_rows)
        blocks = ffn_set.start_z(order(ffn_own[:half_rows], column))
        near = [ffn_set.join_parts(place_list, [blocks])]
        plane = order(attn_set.along_first(column), *blocks)
        blocks = ffn_set.start_z(order(ffn_own[half_rows:], plane, near[0]))
        aside = [places.send(near[0], "xy", 1)]
        crossed = [places.send(near[0], "c", 1)]
        near.append(ffn_set.join_parts(place_list, [blocks]))
        groups = [plane]
        groups += [order(g, aside[0], near[1]) for g in attn_set.along_second(plane)]
        attn_groups = groups + attn_set.from_core(groups)
        aside.append(places.send(near[1], "xy", 1))
        across = [places.send(near[0], "yx", 1)]
        corner = [places.send(aside[0], "yx", 1)]
        query, key, value, vec, attn_whole = project(
            tokens, place_list, attn_set, attn_groups, [aside[0], near[1], crossed[0]]
        )
        token_total = sum(vec[COUNT_ROW, i] * float(8**i) for i in range(4))
        aside = [order(a, query) for a in aside]
        near[1] = order(near[1], query)
        crossed += [places.send(near[1], "c", 1)] + [places.send(a, "c", 1) for a in aside]
        across.append(places.send(near[1], "yx", 1))
        corner.append(places.send(aside[1], "yx", 1))
        extent = places.size
        per_half = UP_CHUNKS // 2
        piece = (extent["z"], per_half, up_rows, D)
        half = extent["y"] // 2

        def fetch(place, refs, weights, sem):
            side = (half, 2, extent["z"], extent["x"])
            up = weights.at[pl.ds(0, FF)].reshape(*((UP_CHUNKS,) + side + (up_rows, D)))
            down = weights.at[pl.ds(FF, FF)].reshape(*(side + (UP_CHUNKS, up_rows, D)))
            ways = [(far, i, j) for far in range(2) for i in range(2) for j in range(2)]
            for i, ref in enumerate(refs):
                h, way = divmod(i, len(ways))
                y, core, x = ffn_set.place(place, *ways[way])

                @pl.when(y < half)
                def _():
                    for part in range(per_half):
                        chunk = h * per_half + part
                        pltpu.make_async_copy(
                            ref.at[:, part], up.at[chunk, y, core, :, x], sem.at[chunk]
                        ).start()

                @pl.when(y >= half)
                def _():
                    chunks = pl.ds(h * per_half, per_half)
                    pltpu.make_async_copy(
                        ref, down.at[y - half, core, :, x, chunks], sem.at[UP_CHUNKS]
                    ).start()

    else:
        token_total = lax.psum(counts[0].astype(F32), AXES)
        vec = lax.psum(ends.astype(F32), AXES).reshape(COUNT_ROW, D)
        vec = jnp.concatenate([vec, jnp.zeros((VEC_ROWS - COUNT_ROW, D), F32)], 0)
        flat = lax.all_gather(attn_param.astype(BF), AXES, axis=0, tiled=True)
        attn_whole = flat[: ATTN_ROWS * D].reshape(ATTN_ROWS, D)
        flat = lax.all_gather(ffn_param.astype(BF), AXES, axis=0, tiled=True)
        w_up = flat[: FF * D].reshape(D, UP_CHUNKS, D).transpose(1, 0, 2).reshape(FF, D)
        w_down = flat[FF * D : FFN_ROWS * D].reshape(FF, D)
        sources = [w_up, w_down]

        def fetch(place, refs, weights, sem):
            w_up, w_down = refs
            for j in range(UP_CHUNKS):
                rows = pl.ds(j * D, D)
                pltpu.make_async_copy(w_up.at[rows], weights.at[rows], sem.at[j]).start()
            down = weights.at[pl.ds(FF, FF)]
            pltpu.make_async_copy(w_down, down, sem.at[UP_CHUNKS]).start()

        query, key, value = project_whole(tokens, attn_whole, vec)

    ahead = []
    for i, pairs in enumerate(AHEAD_PAIRS):
        after = [aside[1]] if staged and i == 0 else []
        first = sum(AHEAD_PAIRS[:i])
        ahead.append(attend(query, key, value, segments, counts, first, pairs, after))
    mixed = [a[0] for a in ahead]
    log_total = jnp.concatenate([a[1] for a in ahead], 0)
    if staged:
        sources = []
        for h in range(2):
            across[h], corner[h] = order(across[h], mixed[h]), order(corner[h], mixed[h])
            mine = [near[h], across[h], aside[h], corner[h]]
            theirs = [crossed[h], places.send(across[h], "c", 1)]
            theirs += [crossed[2 + h], places.send(corner[h], "c", 1)]
            sources += [a.reshape(piece) for a in mine + theirs]
    (
        final_low,
        hidden_low,
        activated,
        grad_pre,
        grad_ffn_out,
        grad_attn_out,
        grad_mixed,
        grad_resid,
        vec_grad,
        crop_sums,
    ) = middle(
        counts,
        place_list,
        segments,
        mixed,
        tokens,
        out_grad,
        attn_whole,
        sources,
        fetch,
        vec,
    )
    is_valid = jnp.arange(ROW, dtype=jnp.int32) < counts[0]
    member = (segments[None, :] == jnp.arange(CROPS, dtype=jnp.int32)[:, None]) & is_valid[None, :]
    crop_sizes = jnp.sum(member.astype(F32), axis=1)
    pooled = crop_sums / jnp.maximum(crop_sizes, 1.0)[:, None]

    def back(i, after, micros):
        return attend_back(
            query,
            key,
            value,
            grad_mixed,
            log_total,
            segments,
            counts,
            sum(PAIRS[:i]),
            PAIRS[i],
            after,
            micros,
        )

    if staged:
        ffn_sums, attn_sums = Scattered(places, place_list, 1.2), Scattered(places, place_list, 0.5)

        def spread(terms):
            return terms.reshape(2, extent["z"], extent["x"], *terms.shape[2:])

        def ffn_side(thirds, after):
            operands = (hidden_low, activated, grad_pre, grad_ffn_out)
            terms = ffn_terms(places, place_list, *operands, thirds, after)
            return [spread(t) for t in terms]

        keep_a, give_a = ffn_side([0, 1, 2], [])
        core_a = ffn_sums.core(give_a)
        back_0 = back(0, [give_a], 12)
        own_a, cut_a = ffn_sums.first(keep_a, order(core_a, back_0[0]))
        first_a = ffn_sums.send(cut_a)
        back_1 = back(1, [cut_a], 15)
        vectors = jnp.concatenate([back_0[1], back_1[1]], 1)[:2]
        vec_grad = jnp.concatenate([vectors, vec_grad[2:]], 0)
        grads = [back_0[0], back_1[0]]
        operands = (tokens, mixed, grads, grad_attn_out, vec_grad)
        terms = attn_terms(places, place_list, *operands, [])
        keep_c, give_c = [spread(t) for t in terms]
        core_c = attn_sums.core(give_c)
        own_a, cut_a = ffn_sums.second(own_a, order(first_a, give_c))
        second_a = ffn_sums.send_second(cut_a)
        token_grad = token_gradient(grad_resid, attn_whole, grads, [give_c, cut_a])
        own_c, cut_c = attn_sums.first(keep_c, order(core_c, token_grad))
        own_a, cuts_a = ffn_sums.along_z(own_a, order(second_a, cut_c))
        up_z_a = ffn_sums.send_z(cuts_a)
        first_c = attn_sums.send(cut_c, *cuts_a)
        own_c, cut_c = attn_sums.second(own_c, order(first_c, up_z_a[1], up_z_a[0]))
        second_c = attn_sums.send_second(cut_c)
        own_c, cuts_c = attn_sums.along_z(own_c, second_c)
        up_z_c = attn_sums.send_z(cuts_c)
        ffn_block = ffn_sums.result(own_a, up_z_a)
        block_c = attn_sums.result(own_c, up_z_c)
        attn_block, vec_sum = block_c[:attn_rows], block_c[attn_rows:]
        by_row = ffn_block.reshape(UP_CHUNKS, up_rows, D).transpose(1, 0, 2).reshape(ffn_rows, D)
        ffn_block = jnp.where(holds_up, by_row, ffn_block)
        ffn_summed = to_flat(places, me, ffn_block, vec_sum[5:12], FFN_TAIL)
        attn_summed = to_flat(places, me, attn_block, vec_sum[:5], ATTN_TAIL)
    else:
        backs = [back(i, [], 12) for i in range(len(PAIRS))]
        grads = [b[0] for b in backs]
        token_grad = token_gradient(grad_resid, attn_whole, grads, [])
        grads = jnp.concatenate(grads, 2)
        mats = [contract_rows(tokens, grads[i]) for i in range(3)]
        mats.append(contract_rows(jnp.concatenate(mixed, 1), grad_attn_out))
        vectors = jnp.concatenate([b[1] for b in backs], 1)[:2]
        vec_grad = jnp.concatenate([vectors, vec_grad[2:]], 0)
        attn_full = jnp.concatenate([g.reshape(-1) for g in mats + [vec_grad[:5]]])
        up = contract_rows(hidden_low, grad_pre)
        down = contract_rows(activated, grad_ffn_out)
        ffn_full = jnp.concatenate([g.reshape(-1) for g in (up, down, vec_grad[5:12])])
        attn_summed = lax.psum_scatter(attn_full, AXES, scatter_dimension=0, tiled=True)
        ffn_summed = lax.psum_scatter(ffn_full, AXES, scatter_dimension=0, tiled=True)
    attn_grad = attn_summed / token_total
    ffn_grad = ffn_summed / token_total
    attn_change, moment_attn, square_attn, drift_attn = adam_update(
        attn_param, attn_grad, attn_moment, attn_square, attn_shadow
    )
    ffn_change, moment_ffn, square_ffn, drift_ffn = adam_update(
        ffn_param, ffn_grad, ffn_moment, ffn_square, ffn_shadow
    )
    return (
        final_low,
        pooled,
        token_grad,
        attn_grad,
        ffn_grad,
        attn_change,
        ffn_change,
        moment_attn,
        moment_ffn,
        square_attn,
        square_ffn,
        drift_attn,
        drift_ffn,
    )


def solution(mesh):
    rows, flat = P(AXES, None), P(AXES)
    return jax.shard_map(
        functools.partial(on_device, Places(mesh)),
        mesh=mesh,
        in_specs=(rows, flat, flat, rows) + (flat,) * 8,
        out_specs=(rows, rows, rows) + (flat,) * 10,
        check_vma=False,
    )
```
